32 devices in a mesh: tm: 16 (over z, y, core), batch: 2 (over x).
Axes of the slice: x: 2, y: 2, z: 4, core: 2. Of those that a mesh axis runs over, the one named last changes fastest.
Arguments:
- source_narrow: bfloat16 [3, 8, 2048, 256], P(None, 'batch', 'tm'), may hold values from -12 to 12
- source_wide: bfloat16 [2, 8, 2048, 384], P(None, 'batch', 'tm'), may hold values from -12 to 12
- lengths: int32 [8], P('batch'), may hold values from 512 to 2048, as said below
- cotangent: bfloat16 [8, 2048, 512], P('batch', 'tm'), may hold values from -6 to 6
- kernel_first: float32 [6528, 512], P('tm'), may hold values from -0.078125 to 0.078125
- kernel_rest: float32 [4, 8704, 512], P(None, 'tm'), may hold values from -0.0625 to 0.0625
- mixer_narrow: float32 [3, 256, 512], P(None, 'tm'), may hold values from -0.375 to 0.375
- mixer_wide: float32 [2, 384, 512], P(None, 'tm'), may hold values from -0.3125 to 0.3125
- norm_params: float32 [2, 10, 512], replicated, may hold values from -0.4 to 4, as said below
- moment_first: float32 [6528, 512], P('tm'), may hold values from -0.03125 to 0.03125
- square_first: float32 [6528, 512], P('tm'), may hold values from 2.2763695e-07 to 3.6421911e-06
- moment_rest: float32 [4, 8704, 512], P(None, 'tm'), may hold values from -0.03125 to 0.03125
- square_rest: float32 [4, 8704, 512], P(None, 'tm'), may hold values from 2.2763695e-07 to 3.6421911e-06
- moment_narrow: float32 [3, 256, 512], P(None, 'tm'), may hold values from -0.03125 to 0.03125
- square_narrow: float32 [3, 256, 512], P(None, 'tm'), may hold values from 2.2763695e-07 to 3.6421911e-06
- moment_wide: float32 [2, 384, 512], P(None, 'tm'), may hold values from -0.03125 to 0.03125
- square_wide: float32 [2, 384, 512], P(None, 'tm'), may hold values from 2.2763695e-07 to 3.6421911e-06
- moment_norm: float32 [2, 10, 512], replicated, may hold values from -0.0625 to 0.0625
- square_norm: float32 [2, 10, 512], replicated, may hold values from 9.105478e-08 to 3.6421912e-07
Outputs:
- mixed: bfloat16 [8, 2048, 512], P('batch', 'tm')
- grad_narrow: float32 [3, 8, 2048, 256], P(None, 'batch', 'tm')
- source_wide_gradient: float32 [2, 8, 2048, 384], P(None, 'batch', 'tm')
- grad_norm: float32 [], replicated
- new_first: float32 [6528, 512], P('tm')
- next_moment_first: float32 [6528, 512], P('tm')
- next_square_first: float32 [6528, 512], P('tm')
- new_rest: float32 [4, 8704, 512], P(None, 'tm')
- next_moment_rest: float32 [4, 8704, 512], P(None, 'tm')
- next_square_rest: float32 [4, 8704, 512], P(None, 'tm')
- new_narrow: float32 [3, 256, 512], P(None, 'tm')
- next_moment_narrow: float32 [3, 256, 512], P(None, 'tm')
- updated_square_mixer_narrow: float32 [3, 256, 512], P(None, 'tm')
- new_wide: float32 [2, 384, 512], P(None, 'tm')
- next_moment_wide: float32 [2, 384, 512], P(None, 'tm')
- next_square_wide: float32 [2, 384, 512], P(None, 'tm')
- new_norm: float32 [2, 10, 512], replicated
- next_moment_norm: float32 [2, 10, 512], replicated
- next_square_norm: float32 [2, 10, 512], replicated
The draws below stay inside these ranges and needn't reach their ends.
Inputs may be any that keep to these rules, and one draw needn't show every extreme that they name: `lengths`: in each aligned group of 4 sequences, one sequence drawn from the seed has length 2048. `norm_params`: row 0 holds gains, row 1 biases.
All inputs are finite; a program needn't handle non-finite values.
Results may differ from the reference program's by a relative error of at most 0.02.
Values may be sent and summed in bfloat16 or wider, within the bound.
A program may use at most 384 MiB of HBM per device.

```python
import math
import jax
import jax.numpy as jnp
from jax import lax

CO = 512
CW = 384
CN = 256
K = 17
STEP = 10
B_DEV = 4
SEQS = 8
FRAMES = 2048
PARAMS = 21964800


def draw_lengths(key, part):
    key = jax.random.fold_in(key, 1)
    first, second = jax.random.split(key)
    base = jax.random.randint(first, (SEQS,), FRAMES // 4, FRAMES + 1)
    pick = jax.random.randint(second, (SEQS // B_DEV, 1), 0, B_DEV)
    slots = jnp.arange(B_DEV, dtype=jnp.int32)[None, :]
    grouped = jnp.where(slots == pick, FRAMES, base.reshape(SEQS // B_DEV, B_DEV))
    return grouped.reshape(SEQS).astype(jnp.int32)


def channel_source(key, shape, low_end, rise):
    width = shape[-1]
    ramp = low_end + rise * jnp.arange(width, dtype=jnp.float32) / (width - 1)
    base = jnp.clip(jax.random.normal(key, shape, jnp.float32), -5.0, 5.0)
    return base * ramp


def draw_source_narrow(key, part):
    key = jax.random.fold_in(key, 3)
    return channel_source(key, (3, SEQS, FRAMES, CN), 0.5, 1.5).astype(jnp.bfloat16)


def draw_source_wide(key, part):
    key = jax.random.fold_in(key, 4)
    return channel_source(key, (2, SEQS, FRAMES, CW), 0.5, 1.5).astype(jnp.bfloat16)


def draw_norm_params(key, part):
    key = jax.random.fold_in(key, 2)
    first, second = jax.random.split(key)
    places = jnp.arange(CO, dtype=jnp.float32) / (CO - 1)
    ramp = 0.5 + 2.0 * places
    gains = jax.random.uniform(first, (1, 10, CO), jnp.float32, 0.6, 1.2) * ramp
    biases = jax.random.uniform(second, (1, 10, CO), jnp.float32, -0.4, 0.4)
    return jnp.concatenate([gains, biases], axis=0)


def level_of(stream_key, extent, pieces, smallest, largest):
    level, own = 1.0, jax.random.fold_in(stream_key, 6)
    for axis_at, parts in pieces:
        steps = jnp.exp(jax.random.uniform(jax.random.fold_in(own, axis_at), (parts,), jnp.float32, smallest / len(pieces), largest / len(pieces)))
        level = level * jnp.repeat(steps, extent[axis_at] // parts).reshape([-1 if axis == axis_at else 1 for axis in range(len(extent))])
    return level


def gaussian(rng, extent, scale, limit, cuts=(), held_as=jnp.bfloat16):
    level = level_of(rng, extent, cuts, -0.22, 0.18) if cuts else 1.0
    entries = jax.random.normal(rng, extent, jnp.float32) * scale * level
    return jnp.minimum(jnp.maximum(entries, -limit), limit).astype(held_as)


def setup_inputs(seed: int = 0) -> dict:
    keys = jax.random.split(jax.random.key(seed), 20)
    return {
        "source_narrow": draw_source_narrow(jax.random.fold_in(keys[19], 71), 0),
        "source_wide": draw_source_wide(jax.random.fold_in(keys[19], 71), 0),
        "lengths": draw_lengths(jax.random.fold_in(keys[19], 71), 0),
        "cotangent": gaussian(keys[3], (SEQS, FRAMES, CO), 1.0, 6.0, ((0, 2), (1, 16))),
        "kernel_first": gaussian(keys[4], (K * CW, CO), (K * CW) ** -0.5, 0.078125, ((0, 16),), jnp.float32),
        "kernel_rest": gaussian(keys[5], (4, K * CO, CO), (K * CO) ** -0.5, 0.0625, ((1, 16),), jnp.float32),
        "mixer_narrow": gaussian(keys[6], (3, CN, CO), CN ** -0.5, 0.375, ((1, 16),), jnp.float32),
        "mixer_wide": gaussian(keys[7], (2, CW, CO), CW ** -0.5, 0.3125, ((1, 16),), jnp.float32),
        "norm_params": draw_norm_params(jax.random.fold_in(keys[19], 71), 0),
        "moment_first": gaussian(keys[9], (K * CW, CO), (11.0 / PARAMS ** 0.5), 0.03125, ((0, 16),), jnp.float32),
        "square_first": jnp.clip(jnp.exp(math.log(3.6421911318029743e-06) - 2.7725887 * jax.random.uniform(keys[10], (K * CW, CO), jnp.float32) ** level_of(keys[10], (K * CW, CO), ((0, 16),), -0.2, 0.2)), 2.276369457376859e-07, 3.6421911318029743e-06),
        "moment_rest": gaussian(keys[11], (4, K * CO, CO), (11.0 / PARAMS ** 0.5), 0.03125, ((1, 16),), jnp.float32),
        "square_rest": jnp.clip(jnp.exp(math.log(3.6421911318029743e-06) - 2.7725887 * jax.random.uniform(keys[12], (4, K * CO, CO), jnp.float32) ** level_of(keys[12], (4, K * CO, CO), ((1, 16),), -0.2, 0.2)), 2.276369457376859e-07, 3.6421911318029743e-06),
        "moment_narrow": gaussian(keys[13], (3, CN, CO), (11.0 / PARAMS ** 0.5), 0.03125, ((1, 16),), jnp.float32),
        "square_narrow": jnp.clip(jnp.exp(math.log(3.6421911318029743e-06) - 2.7725887 * jax.random.uniform(keys[14], (3, CN, CO), jnp.float32) ** level_of(keys[14], (3, CN, CO), ((1, 16),), -0.2, 0.2)), 2.276369457376859e-07, 3.6421911318029743e-06),
        "moment_wide": gaussian(keys[15], (2, CW, CO), (11.0 / PARAMS ** 0.5), 0.03125, ((1, 16),), jnp.float32),
        "square_wide": jnp.clip(jnp.exp(math.log(3.6421911318029743e-06) - 2.7725887 * jax.random.uniform(keys[16], (2, CW, CO), jnp.float32) ** level_of(keys[16], (2, CW, CO), ((1, 16),), -0.2, 0.2)), 2.276369457376859e-07, 3.6421911318029743e-06),
        "moment_norm": gaussian(keys[17], (2, 10, CO), (22.0 / PARAMS ** 0.5), 0.0625, (), jnp.float32),
        "square_norm": jnp.clip(jnp.exp(jax.random.uniform(keys[18], (2, 10, CO), jnp.float32, math.log(9.105477971615983e-08), math.log(3.642191188646393e-07))), 9.105477971615983e-08, 3.642191188646393e-07),
    }


EPS = 1e-05
THRESHOLD = 100.0
BETA_ONE = 0.9
SECOND_DECAY = 0.999
ADAM_EPS = 1e-08
RATE_WEIGHT = 0.02
RATE_NORM = 0.4
DECAY = 0.01

@jax.custom_vjp
def low(v):
    return lax.optimization_barrier(v.astype(jnp.bfloat16)).astype(jnp.float32)

@jax.custom_vjp
def low_back(v):
    return v

def low_keep(v):
    return (low(v), None)

def low_pass(kept, grad):
    return (grad,)

def back_keep(v):
    return (v, None)

def back_low(kept, grad):
    return (low(grad),)
low.defvjp(low_keep, low_pass)
low_back.defvjp(back_keep, back_low)

def convolve(signal, kernel, width):
    taps = kernel.reshape(width, K, CO)
    padded = jnp.pad(signal, ((0, 0), (K // 2, K // 2), (0, 0)))
    total = jnp.zeros(signal.shape[:2] + (CO,), jnp.float32)
    for tap in range(K):
        total = total + jnp.einsum('btc,cd->btd', padded[:, tap:tap + FRAMES], taps[:, tap], precision=lax.Precision.HIGHEST)
    return total

def bnorm(value, valid, count, gain, bias):
    mean = lax.optimization_barrier(jnp.sum(value * valid, axis=(0, 1))) / count
    deviate = (value - mean) * valid
    variance = lax.optimization_barrier(jnp.sum(deviate * deviate, axis=(0, 1))) / count
    return gain * (value - mean) * lax.rsqrt(variance + EPS) + bias

def forward(source_narrow, source_wide, kernel_first, kernel_rest, mixer_narrow, mixer_wide, norm_params, valid, count):
    gains = norm_params[0]
    biases = norm_params[1]
    narrow = low(source_narrow * valid)
    wide = low(source_wide * valid)
    signal = wide[1]
    for index in range(5):
        if index == 0:
            kernel = low(kernel_first)
            width = CW
        else:
            kernel = low(kernel_rest[index - 1])
            width = CO
        field = low_back(convolve(signal, kernel, width))
        summed = bnorm(field, valid, count, gains[index], biases[index])
        if index == 4:
            for source in range(3):
                branch = low_back(jnp.einsum('btc,cd->btd', narrow[source], low(mixer_narrow[source]), precision=lax.Precision.HIGHEST))
                summed = summed + bnorm(branch, valid, count, gains[5 + source], biases[5 + source])
            for source in range(2):
                branch = low_back(jnp.einsum('btc,cd->btd', wide[source], low(mixer_wide[source]), precision=lax.Precision.HIGHEST))
                summed = summed + bnorm(branch, valid, count, gains[8 + source], biases[8 + source])
        active = jax.nn.silu(summed) * valid
        signal = low(active) if index < 4 else active
    return signal

def adamw(param, grad, first, second, rate, decay):
    first_new = BETA_ONE * first + (1.0 - BETA_ONE) * grad
    second_new = SECOND_DECAY * second + (1.0 - SECOND_DECAY) * grad * grad
    fix_one = 1.0 - BETA_ONE ** STEP
    fix_two = 1.0 - SECOND_DECAY ** STEP
    update = first_new / fix_one / (jnp.sqrt(second_new / fix_two) + ADAM_EPS)
    return (param - rate * (update + decay * param), first_new, second_new)

def reference(source_narrow, source_wide, lengths, cotangent, kernel_first, kernel_rest, mixer_narrow, mixer_wide, norm_params, moment_first, square_first, moment_rest, square_rest, moment_narrow, square_narrow, moment_wide, square_wide, moment_norm, square_norm):
    places = jnp.arange(FRAMES, dtype=jnp.int32)
    valid = (places[None, :] < lengths[:, None]).astype(jnp.float32)[:, :, None]
    count = jnp.sum(lengths).astype(jnp.float32)

    def wrapped(a, b, c, d, e, f, g):
        return forward(a, b, c, d, e, f, g, valid, count)
    output, pull = jax.vjp(wrapped, source_narrow.astype(jnp.float32), source_wide.astype(jnp.float32), kernel_first, kernel_rest, mixer_narrow, mixer_wide, norm_params)
    grads = pull(cotangent.astype(jnp.float32))
    params = (kernel_first, kernel_rest, mixer_narrow, mixer_wide, norm_params)
    weight_grads = grads[2:]
    total = jnp.zeros((), jnp.float32)
    for grad in weight_grads:
        total = total + jnp.sum(grad * grad)
    grad_norm = jnp.sqrt(total)
    clip = jnp.minimum(1.0, THRESHOLD / grad_norm)
    firsts = (moment_first, moment_rest, moment_narrow, moment_wide, moment_norm)
    seconds = (square_first, square_rest, square_narrow, square_wide, square_norm)
    results = []
    for slot in range(5):
        rate = RATE_NORM if slot == 4 else RATE_WEIGHT
        decay = 0.0 if slot == 4 else DECAY
        results.append(adamw(params[slot], clip * weight_grads[slot], firsts[slot], seconds[slot], rate, decay))
    return (output.astype(jnp.bfloat16), grads[0], grads[1], grad_norm, results[0][0], results[0][1], results[0][2], results[1][0], results[1][1], results[1][2], results[2][0], results[2][1], results[2][2], results[3][0], results[3][1], results[3][2], results[4][0], results[4][1], results[4][2])
```

```python
import numpy as np
import jax
import jax.numpy as jnp
from jax import lax
from jax.experimental import pallas as pl
from jax.experimental.pallas import tpu as pltpu
from jax.sharding import PartitionSpec as P

CO = 512
CW = 384
K = 17
STEP = 10


EPS = 1e-05
THRESHOLD = 100.0
BETA_ONE = 0.9
SECOND_DECAY = 0.999
ADAM_EPS = 1e-08
RATE_WEIGHT = 0.02
RATE_NORM = 0.4
DECAY = 0.01


def padded_2(shard, sides, width):
    for axis, dim in sides:
        devices, length = (lax.axis_size(axis), shard.shape[dim])
        up = [(i, (i + 1) % devices) for i in range(devices - 1)]
        down = [(j, i) for i, j in up]
        last = lax.slice_in_dim(shard, length - width, length, axis=dim)
        initial = lax.slice_in_dim(shard, 0, width, axis=dim)
        before = lax.ppermute(last, axis, up)
        after = lax.ppermute(initial, axis, down)
        shard = jnp.concatenate([before, shard, after], axis=dim)
    return shard


def adamw(param, grad, first, second, rate, decay):
    first_new = BETA_ONE * first + (1.0 - BETA_ONE) * grad
    second_new = SECOND_DECAY * second + (1.0 - SECOND_DECAY) * grad * grad
    fix_one = 1.0 - BETA_ONE**STEP
    fix_two = 1.0 - SECOND_DECAY**STEP
    update = first_new / fix_one / (jnp.sqrt(second_new / fix_two) + ADAM_EPS)
    return (param - rate * (update + decay * param), first_new, second_new)


def body(
    source_narrow,
    source_wide,
    lengths,
    cotangent,
    kernel_first,
    kernel_rest,
    mixer_narrow,
    mixer_wide,
    norm_params,
    moment_first,
    square_first,
    moment_rest,
    square_rest,
    moment_narrow,
    square_narrow,
    moment_wide,
    square_wide,
    moment_norm,
    square_norm,
):
    frames = source_wide.shape[2]
    half = K // 2
    places = lax.axis_index("tm") * frames + jnp.arange(frames, dtype=jnp.int32)
    valid = (places[None, :] < lengths[:, None]).astype(jnp.float32)[:, :, None]
    local_count = jnp.sum(valid)
    valid_low = valid.astype(jnp.bfloat16)
    narrow = source_narrow * valid_low[None]
    wide = source_wide * valid_low[None]
    full_first, full_rest, full_narrow, full_wide = (
        lax.all_gather(kernel_first.astype(jnp.bfloat16), "tm", axis=0, tiled=True),
        lax.all_gather(kernel_rest.astype(jnp.bfloat16), "tm", axis=1, tiled=True),
        lax.all_gather(mixer_narrow.astype(jnp.bfloat16), "tm", axis=1, tiled=True),
        lax.all_gather(mixer_wide.astype(jnp.bfloat16), "tm", axis=1, tiled=True),
    )
    kernels = [jnp.transpose(full_first.reshape(CW, K, CO), (1, 0, 2))] + [
        jnp.transpose(full_rest[layer].reshape(CO, K, CO), (1, 0, 2)) for layer in range(4)
    ]
    gains = norm_params[0]
    biases = norm_params[1]

    def batch_statistics(values, count):
        sums = tuple((jnp.sum(value * valid, axis=(0, 1)) for value in values))
        extra = (local_count,) if count is None else ()
        got = lax.psum(sums + extra, ("tm", "batch"))
        if count is None:
            count = got[-1]
        means = [total / count for total in got[: len(values)]]
        spreads = tuple(
            (
                jnp.sum(jnp.square((value - mean) * valid), axis=(0, 1))
                for value, mean in zip(values, means)
            )
        )
        second = lax.psum(spreads, ("tm", "batch"))
        variances = [total / count for total in second]
        scales = [lax.rsqrt(variance + EPS) for variance in variances]
        return (means, scales, count)

    signal = wide[1]
    kept = []
    count = None
    for index in range(5):
        padded = padded_2(signal, (("tm", 1),), half)
        field = jnp.zeros(signal.shape[:2] + (CO,), jnp.float32)
        for tap in range(K):
            field = field + jnp.einsum(
                "btc,cd->btd",
                padded[:, tap : tap + frames],
                kernels[index][tap],
                preferred_element_type=jnp.float32,
            )
        values = [field]
        indices = [index]
        if index == 4:
            for source in range(3):
                values.append(
                    jnp.einsum(
                        "btc,cd->btd",
                        narrow[source],
                        full_narrow[source],
                        preferred_element_type=jnp.float32,
                    )
                )
                indices.append(5 + source)
            for source in range(2):
                values.append(
                    jnp.einsum(
                        "btc,cd->btd",
                        wide[source],
                        full_wide[source],
                        preferred_element_type=jnp.float32,
                    )
                )
                indices.append(8 + source)
        means, scales, count = batch_statistics(values, count)
        normalized_values = [
            (value - mean) * scale for value, mean, scale in zip(values, means, scales)
        ]
        summed = jnp.zeros_like(field)
        for place in range(len(values)):
            summed = (
                summed + gains[indices[place]] * normalized_values[place] + biases[indices[place]]
            )
        kept.append((padded, normalized_values, scales, summed, indices))
        active = jax.nn.silu(summed) * valid
        signal = active.astype(jnp.bfloat16)
    grad_active = cotangent.astype(jnp.float32)
    kernel_grads = [None] * 5
    gain_grads = [None] * 10
    bias_grads = [None] * 10
    narrow_grads = []
    wide_grads = []
    narrow_inputs = []
    wide_inputs = []
    first_input = None
    for index in reversed(range(5)):
        padded, normalized_values, scales, summed, indices = kept[index]
        sigma = jax.nn.sigmoid(summed)
        gradient_total = grad_active * valid * sigma * (1.0 + summed * (1.0 - sigma))
        local_sums = (jnp.sum(gradient_total, axis=(0, 1)),) + tuple(
            (
                jnp.sum(gradient_total * standardized_input, axis=(0, 1))
                for standardized_input in normalized_values
            )
        )
        got = lax.psum(local_sums, ("tm", "batch"))
        bias_total = got[0]
        field_grads = []
        for place in range(len(normalized_values)):
            which = indices[place]
            gain = gains[which]
            gain_grads[which] = got[1 + place]
            bias_grads[which] = bias_total
            grad_field = scales[place] * (
                gain * gradient_total
                - valid * (gain * bias_total) / count
                - valid * normalized_values[place] * (gain * got[1 + place]) / count
            )
            field_grads.append(grad_field.astype(jnp.bfloat16))
        grad_conv = field_grads[0]
        tap_grads = [
            jnp.einsum(
                "btc,btd->cd",
                padded[:, tap : tap + frames],
                grad_conv,
                preferred_element_type=jnp.float32,
            )
            for tap in range(K)
        ]
        kernel_grads[index] = jnp.stack(tap_grads, axis=1).reshape(padded.shape[2] * K, CO)
        if index == 4:
            for source in range(3):
                branch = field_grads[1 + source]
                narrow_grads.append(
                    jnp.einsum(
                        "btc,btd->cd", narrow[source], branch, preferred_element_type=jnp.float32
                    )
                )
                narrow_inputs.append(
                    jnp.einsum(
                        "btd,cd->btc",
                        branch,
                        full_narrow[source],
                        preferred_element_type=jnp.float32,
                    )
                    * valid
                )
            for source in range(2):
                branch = field_grads[4 + source]
                wide_grads.append(
                    jnp.einsum(
                        "btc,btd->cd", wide[source], branch, preferred_element_type=jnp.float32
                    )
                )
                wide_inputs.append(
                    jnp.einsum(
                        "btd,cd->btc", branch, full_wide[source], preferred_element_type=jnp.float32
                    )
                    * valid
                )
        grad_padded = padded_2(grad_conv, (("tm", 1),), half)
        incoming = jnp.zeros(padded.shape[:1] + (frames, padded.shape[2]), jnp.float32)
        for tap in range(K):
            start = K - 1 - tap
            incoming = incoming + jnp.einsum(
                "btd,cd->btc",
                grad_padded[:, start : start + frames],
                kernels[index][tap],
                preferred_element_type=jnp.float32,
            )
        if index > 0:
            grad_active = incoming
        else:
            first_input = incoming
    grad_narrow = jnp.stack(narrow_inputs)
    source_wide_gradient = jnp.stack([wide_inputs[0], (first_input + wide_inputs[1]) * valid])
    shard_gradients = (
        kernel_grads[0],
        jnp.stack(kernel_grads[1:]),
        jnp.stack(narrow_grads),
        jnp.stack(wide_grads),
    )
    shards = (
        lax.psum_scatter(shard_gradients[0], "tm", scatter_dimension=0, tiled=True),
        lax.psum_scatter(shard_gradients[1], "tm", scatter_dimension=1, tiled=True),
        lax.psum_scatter(shard_gradients[2], "tm", scatter_dimension=1, tiled=True),
        lax.psum_scatter(shard_gradients[3], "tm", scatter_dimension=1, tiled=True),
    )
    norm_grad = jnp.stack([jnp.stack(gain_grads), jnp.stack(bias_grads)])
    params = (kernel_first, kernel_rest, mixer_narrow, mixer_wide)
    firsts = (moment_first, moment_rest, moment_narrow, moment_wide)
    seconds = (square_first, square_rest, square_narrow, square_wide)
    results = []
    shards = (
        lax.psum(shards[0].astype(jnp.bfloat16), "batch").astype(jnp.float32),
        lax.psum(shards[1].astype(jnp.bfloat16), "batch").astype(jnp.float32),
        lax.psum(shards[2].astype(jnp.bfloat16), "batch").astype(jnp.float32),
        lax.psum(shards[3].astype(jnp.bfloat16), "batch").astype(jnp.float32),
    )
    local_square = jnp.zeros((), jnp.float32)
    for shard in shards:
        local_square = local_square + jnp.sum(shard * shard)
    total = lax.psum(local_square, "tm") + jnp.sum(norm_grad * norm_grad)
    grad_norm = jnp.sqrt(total)
    clip = jnp.minimum(1.0, THRESHOLD / grad_norm)
    for slot in range(4):
        results.append(
            adamw(
                params[slot], clip * shards[slot], firsts[slot], seconds[slot], RATE_WEIGHT, DECAY
            )
        )
    results.append(adamw(norm_params, clip * norm_grad, moment_norm, square_norm, RATE_NORM, 0.0))
    return (
        signal,
        grad_narrow,
        source_wide_gradient,
        grad_norm,
        results[0][0],
        results[0][1],
        results[0][2],
        results[1][0],
        results[1][1],
        results[1][2],
        results[2][0],
        results[2][1],
        results[2][2],
        results[3][0],
        results[3][1],
        results[3][2],
        results[4][0],
        results[4][1],
        results[4][2],
    )


BF = jnp.bfloat16
F32 = jnp.float32
MESH = pl.DeviceIdType.MESH
ROWS = 1024
HALO = 64
HALF = 256
GROUPS = 34


def wait_on(ref, sem):
    pltpu.make_async_copy(ref, ref, sem).wait()


def remote(src, dst, send, recv, device):
    pltpu.make_async_remote_copy(
        src_ref=src,
        dst_ref=dst,
        send_sem=send,
        recv_sem=recv,
        device_id=device,
        device_id_type=MESH,
    ).start()


def position():
    x = lax.axis_index("batch")
    t = lax.axis_index("tm")
    return x, t, lax.div(t, 4), lax.rem(lax.div(t, 2), 2), lax.rem(t, 2)


def greet(x, t):
    barrier = pltpu.get_barrier_semaphore()

    def one(d, _):
        pl.semaphore_signal(
            barrier, inc=1, device_id=(lax.rem(t + d, 16), x), device_id_type=MESH
        )
        return 0

    lax.fori_loop(1, 16, one, 0)
    for d in (0, 1, 15):
        pl.semaphore_signal(
            barrier, inc=1, device_id=(lax.rem(t + d, 16), 1 - x), device_id_type=MESH
        )
    pl.semaphore_wait(barrier, 18)


def frame_mask(block, t, lens):
    frames = lax.broadcasted_iota(jnp.int32, (16, 8, HALF), 0) + (block * 16 + t * 128)
    return (frames.astype(F32) < lens[None]).astype(F32)


def share(box, at, t, x, send, recv):
    def one(d, _):
        remote(box.at[at, t], box.at[at, t], send, recv, (lax.rem(t + d, 16), x))
        return 0

    lax.fori_loop(1, 16, one, 0)


def forward_kernel(
    lens_in,
    norm,
    perm,
    src_n,
    src_w,
    cot,
    kf,
    kr,
    mn,
    mw,
    w_out,
    wmn_out,
    wmw_out,
    h_out,
    xh_out,
    y_out,
    nar_out,
    wid_out,
    cot_out,
    rs_out,
    len_out,
    W,
    G,
    wmn,
    wmw,
    hA,
    hB,
    z,
    zb,
    xhb,
    y5,
    stg,
    pf,
    pmn,
    pmw,
    raww,
    rawn,
    rawc,
    nar,
    wid,
    cotv,
    st,
    nv,
    lenr,
    lens,
    load_s,
    ag_s,
    rz,
    ry,
    rc,
    m_s,
    m_r,
    x_s,
    x_r,
    xr_s,
    xr_r,
    halo_s,
    halo_r,
    st_s,
    st_r,
    out_s,
):
    x, t, zi, yi, ci = position()
    cols = pl.ds(pl.multiple_of(x * HALF, HALF), HALF)
    partner = (t, 1 - x)
    sibling = (t + 1 - 2 * ci, x)
    across = (zi * 4 + (1 - yi) * 2 + ci, x)

    lanes = [pl.ds(pl.multiple_of(x * HALF + 128 * b, 128), 128) for b in range(2)]
    loads = [(kf.at[:, lanes[b]], pf.at[0, b, pl.ds(0, 408)]) for b in range(2)]
    loads += [(kr.at[i, :, lanes[b]], pf.at[1 + i, b]) for i in range(4) for b in range(2)]
    loads += [
        (mn.at[:, :, cols], pmn),
        (mw.at[:, :, cols], pmw),
        (src_w, raww.at[x]),
        (src_n, rawn.at[x]),
        (cot.at[:, :, cols], rawc.at[x]),
    ]
    copies = [pltpu.make_async_copy(a, b, load_s.at[i]) for i, (a, b) in enumerate(loads)]
    for copy in copies:
        copy.start()
    hA[:, :, pl.ds(1152, 16), :] = jnp.zeros((5, 2, 16, HALF), BF)

    @pl.when(t == 0)
    def _():
        hA[:, :, pl.ds(0, HALO), :] = jnp.zeros((5, 2, HALO, HALF), BF)

    @pl.when(t == 15)
    def _():
        hA[:, :, pl.ds(1088, HALO), :] = jnp.zeros((5, 2, HALO, HALF), BF)

    lenr[0] = lens_in[...]
    greet(x, t)

    other = pl.ds(pl.multiple_of((1 - x) * HALF, HALF), HALF)
    remote(lenr.at[0], lenr.at[1], xr_s.at[0], xr_r.at[0], partner)
    remote(src_w.at[1], raww.at[x, 1], xr_s.at[1], xr_r.at[1], partner)

    def prep(layer, count):
        for k in range(17):
            for b in range(2):
                v = pf[layer, b, pl.ds(k, count, stride=17), :]
                if count < 32:
                    v = jnp.concatenate([v, jnp.zeros((32 - count, 128), F32)], axis=0)
                W[17 * layer + k, t, :, pl.ds(128 * b, 128)] = v.astype(BF)

    def chunk(g, slot):
        return W.at[
            pl.ds(5 * lax.div(g, 2), 5), slot, pl.ds(pl.multiple_of(16 * lax.rem(g, 2), 16), 16)
        ]

    def amount(g, n):
        return W.at[
            pl.ds(5 * lax.div(g, 2), 5),
            pl.ds(0, n),
            pl.ds(pl.multiple_of(16 * lax.rem(g, 2), 16), 16),
        ]

    def along(dz):
        return lax.rem(zi + dz, 4) * 4 + yi * 2 + ci

    def own_sends(block, send, into_z, into_y, into_c):
        mine = block(t)
        for dz in (1, 2, 3):
            remote(mine, mine, send, into_z, (along(dz), x))
        remote(mine, mine, send, into_y, across)
        remote(mine, mine, send, into_c, sibling)

    def pass_z(block, send, into_y, into_c):
        for dz in (1, 2, 3):
            got = block(along(dz))
            remote(got, got, send, into_y, across)
            remote(got, got, send, into_c, sibling)

    def pass_y(block, send, into_c):
        for zz in range(4):
            got = block(zz * 4 + (1 - yi) * 2 + ci)
            remote(got, got, send, into_c, sibling)

    def service(g):
        @pl.when(g < GROUPS)
        def _():
            own_sends(lambda s: chunk(g, s), ag_s.at[g], rz.at[g], ry.at[g], rc.at[g])

        @pl.when((g >= 1) & (g <= GROUPS))
        def _():
            h = g - 1
            wait_on(amount(h, 3), rz.at[h])
            pass_z(lambda s: chunk(h, s), ag_s.at[h], ry.at[h], rc.at[h])

        @pl.when((g >= 2) & (g <= GROUPS + 1))
        def _():
            h = g - 2
            wait_on(amount(h, 4), ry.at[h])
            pass_y(lambda s: chunk(h, s), ag_s.at[h], rc.at[h])

        @pl.when((g >= 3) & (g <= GROUPS + 2))
        def _():
            h = g - 3
            wait_on(amount(h, 8), rc.at[h])

        mixer = lambda s: G.at[s]

        @pl.when(g == 8)
        def _():
            own_sends(mixer, m_s, m_r.at[0], m_r.at[1], m_r.at[2])

        @pl.when(g == 9)
        def _():
            wait_on(G.at[pl.ds(0, 3)], m_r.at[0])
            pass_z(mixer, m_s, m_r.at[1], m_r.at[2])

        @pl.when(g == 10)
        def _():
            wait_on(G.at[pl.ds(0, 4)], m_r.at[1])
            pass_y(mixer, m_s, m_r.at[2])

        @pl.when(g == 11)
        def _():
            wait_on(G.at[pl.ds(0, 8)], m_r.at[2])
            for j in range(3):
                for s in range(16):
                    wmn[j, pl.ds(16 * s, 16), :] = G[s, pl.ds(16 * j, 16), :]
            for j in range(2):
                for s in range(16):
                    wmw[j, pl.ds(32 * s, 32), :] = G[s, pl.ds(48 + 32 * j, 32), :]

    def serve(first, last):
        def one(g, _):
            service(g)
            return 0

        lax.fori_loop(first, last, one, 0)

    for copy in copies[:2]:
        copy.wait()
    prep(0, 24)
    service(jnp.int32(0))
    for copy in copies[2:12]:
        copy.wait()
    prep(1, 32)
    for layer in (2, 3, 4):
        prep(layer, 32)
    for j in range(3):
        G[t, pl.ds(16 * j, 16), :] = pmn[j].astype(BF)
    for j in range(2):
        G[t, pl.ds(48 + 32 * j, 32), :] = jnp.concatenate(
            [pmw[j], jnp.zeros((8, HALF), F32)], axis=0
        ).astype(BF)
    serve(1, 3)

    wait_on(lenr.at[1], xr_r.at[0])
    lens[...] = lenr[0] + lenr[1]
    len_out[...] = lens[...]
    for s in range(16):
        nv[s] = jnp.broadcast_to(
            jnp.sum(jnp.clip(lens[...] - 128.0 * s, 0.0, 128.0), axis=0, keepdims=True), (8, HALF)
        )

    def spread_wide(j):
        for s in range(8):
            v = jnp.dot(raww[s // 4, j, s % 4], perm[...], preferred_element_type=F32)
            for b in range(4):
                stg[b, pl.ds(s, 128, stride=8), :] = v[:, 128 * b : 128 * b + 128]

    def spread_half(v, s):
        for b in range(2):
            stg[b, pl.ds(s, 128, stride=8), :] = v[:, 128 * b : 128 * b + 128].astype(F32)

    def masked_block(b, h):
        rows = pl.ds(pl.multiple_of(b * 128, 128), 128)
        v = jnp.concatenate([stg[2 * h, rows, :], stg[2 * h + 1, rows, :]], axis=1)
        v = v.reshape(16, 8, HALF)
        return (v * frame_mask(b, t, lens[...])).reshape(128, HALF).astype(BF)

    copies[12].wait()
    wait_on(raww.at[0, 1], xr_r.at[1])
    spread_wide(1)

    def first_block(b, _):
        for h in range(2):
            hA[0, h, pl.ds(pl.multiple_of(HALO + b * 128, 64), 128), :] = masked_block(b, h)
        return 0

    lax.fori_loop(0, 8, first_block, 0)

    def halo_send(layer, half, to, side):
        a, b = ((HALO, 1088), (1024, 0))[side]
        remote(
            hA.at[layer, half, pl.ds(a, HALO)],
            hA.at[layer, half, pl.ds(b, HALO)],
            halo_s.at[layer, side, half if to is None else to],
            halo_r.at[layer, side, half],
            (t - 1 + 2 * side, x if to is None else jnp.where(to == 0, x, 1 - x)),
        )

    def halo_wait(layer, send):
        @pl.when(t > 0)
        def _():
            for h in range(2):
                wait_on(hA.at[layer, h, pl.ds(0, HALO)], (halo_s if send else halo_r).at[layer, 0 if send else 1, h])

        @pl.when(t < 15)
        def _():
            for h in range(2):
                wait_on(hA.at[layer, h, pl.ds(0, HALO)], (halo_s if send else halo_r).at[layer, 1 if send else 0, h])

    @pl.when(t > 0)
    def _():
        for h in range(2):
            halo_send(0, h, None, 0)

    @pl.when(t < 15)
    def _():
        for h in range(2):
            halo_send(0, h, None, 1)

    remote(src_n, rawn.at[x], xr_s.at[2], xr_r.at[2], partner)
    remote(src_w.at[0], raww.at[x, 0], xr_s.at[3], xr_r.at[3], partner)
    serve(3, 11)

    def shift_copy(layer):
        def one(b, _):
            for h in range(2):
                v = hA[layer, h, pl.ds(pl.multiple_of(b * 128, 128), 144), :].astype(F32)
                hB[h, pl.ds(pl.multiple_of(b * 128, 128), 128), :] = v[8:136].astype(BF)
            return 0

        lax.fori_loop(0, 9, one, 0)

    halo_wait(0, False)
    shift_copy(0)

    def rows_of(b):
        return pl.ds(pl.multiple_of(b * 128, 128), 128)

    def local_stats(ref):
        def total(b, acc):
            v = ref[rows_of(b), :].reshape(16, 8, HALF) * frame_mask(b, t, lens[...])
            return acc + jnp.sum(v, axis=0)

        s = jnp.sum(
            lax.fori_loop(0, 8, total, jnp.zeros((8, HALF), F32)), axis=0, keepdims=True
        )
        mean = s / jnp.maximum(nv[t, pl.ds(0, 1), :], 1.0)

        def spread(b, acc):
            v = (ref[rows_of(b), :].reshape(16, 8, HALF) - mean[None]) * frame_mask(
                b, t, lens[...]
            )
            return acc + jnp.sum(v * v, axis=0)

        m2 = jnp.sum(
            lax.fori_loop(0, 8, spread, jnp.zeros((8, HALF), F32)), axis=0, keepdims=True
        )
        return mean, m2

    def layer_step(layer, _):
        pltpu.make_async_copy(
            W.at[pl.ds(17 * layer, 17)], w_out.at[pl.ds(17 * layer, 17)], out_s.at[layer]
        ).start()
        pltpu.make_async_copy(
            hA.at[layer, :, pl.ds(HALO, ROWS)], h_out.at[layer], out_s.at[5 + layer]
        ).start()

        acc = jnp.zeros((ROWS, HALF), F32)
        for k in range(17):
            for h in range(2):
                lhs = (
                    hA[layer, h, pl.ds(8 * k, ROWS), :]
                    if k % 2 == 0
                    else hB[h, pl.ds(8 * (k - 1), ROWS), :]
                )
                acc = acc + jnp.dot(
                    lhs,
                    W[17 * layer + k, pl.ds(8 * h, 8)].reshape(HALF, HALF),
                    preferred_element_type=F32,
                )
        z[...] = acc

        @pl.when(layer == 1)
        def _():
            for j in range(3):
                zb[j] = jnp.dot(nar[j], wmn[j], preferred_element_type=F32)

        @pl.when(layer == 2)
        def _():
            zb[0] = jnp.dot(
                wid[0], wmw[0, pl.ds(0, HALF), :], preferred_element_type=F32
            ) + jnp.dot(wid[1], wmw[0, pl.ds(HALF, HALF), :], preferred_element_type=F32)
            zb[1] = jnp.dot(
                hA[0, 0, pl.ds(HALO, ROWS), :],
                wmw[1, pl.ds(0, HALF), :],
                preferred_element_type=F32,
            ) + jnp.dot(
                hA[0, 1, pl.ds(HALO, ROWS), :],
                wmw[1, pl.ds(HALF, HALF), :],
                preferred_element_type=F32,
            )

        def put_stats(ref, field):
            mean, m2 = local_stats(ref)
            st[layer, t, pl.ds(2 * field, 1), :] = mean
            st[layer, t, pl.ds(2 * field + 1, 1), :] = m2

        st[layer, t] = jnp.zeros((8, HALF), F32)
        put_stats(z, 0)
        for at, number in ((1, 3), (2, 2)):

            @pl.when(layer == at)
            def _():
                for j in range(number):
                    put_stats(zb.at[j], 1 + j)

        share(st, layer, t, x, st_s.at[layer], st_r.at[layer])
        wait_on(st.at[layer, pl.ds(0, 15)], st_r.at[layer])
        zero = jnp.zeros((8, HALF), F32)
        count = lax.fori_loop(0, 16, lambda s, a: a + nv[s], zero)
        mean = lax.fori_loop(0, 16, lambda s, a: a + nv[s] * st[layer, s], zero) / count

        def gather_spread(s, a):
            v = st[layer, s]
            d = v - mean
            return a[0] + nv[s] * d * d, a[1] + v

        between, inside = lax.fori_loop(0, 16, gather_spread, (zero, zero))

        def moments(field):
            m = mean[2 * field : 2 * field + 1]
            q = (inside[2 * field + 1 : 2 * field + 2] + between[2 * field : 2 * field + 1]) / count[:1]
            return m, lax.rsqrt(q + EPS)

        def branches(base, number):
            for j in range(number):
                m, r = moments(1 + j)
                field = base + j
                rs_out[field] = jnp.broadcast_to(r, (8, HALF))
                gain = norm[field, pl.ds(0, 1), :]
                bias = norm[field, pl.ds(1, 1), :]
                if j > 0:
                    wait_on(xhb.at[1], out_s.at[10])

                def one(b, _):
                    v = (zb[j, rows_of(b), :] - m) * r
                    xhb[1, rows_of(b), :] = v
                    y = gain * v + bias
                    if field > 5:
                        y = y + y5[rows_of(b), :]
                    y5[rows_of(b), :] = y
                    return 0

                lax.fori_loop(0, 8, one, 0)
                pltpu.make_async_copy(xhb.at[1], xh_out.at[field], out_s.at[10]).start()
            wait_on(xhb.at[1], out_s.at[10])

        m, r = moments(0)
        rs_out[layer] = jnp.broadcast_to(r, (8, HALF))
        gain = norm[layer, pl.ds(0, 1), :]
        bias = norm[layer, pl.ds(1, 1), :]

        @pl.when(layer > 0)
        def _():
            wait_on(xhb.at[0], out_s.at[11])

        @pl.when(layer < 4)
        def _():
            def one(b, _):
                v = (z[rows_of(b), :] - m) * r
                xhb[0, rows_of(b), :] = v
                y = gain * v + bias
                a = (y * jax.nn.sigmoid(y)).reshape(16, 8, HALF) * frame_mask(b, t, lens[...])
                hA[layer + 1, x, pl.ds(pl.multiple_of(HALO + b * 128, 64), 128), :] = a.reshape(
                    128, HALF
                ).astype(BF)
                return 0

            lax.fori_loop(0, 8, one, 0)

            @pl.when(t > 0)
            def _():
                for to in range(2):
                    a = hA.at[layer + 1, x, pl.ds(HALO, HALO)]
                    b = hA.at[layer + 1, x, pl.ds(1088, HALO)]
                    remote(
                        a,
                        b,
                        halo_s.at[layer + 1, 0, to],
                        halo_r.at[layer + 1, 0, x],
                        (t - 1, x if to == 0 else 1 - x),
                    )

            @pl.when(t < 15)
            def _():
                for to in range(2):
                    a = hA.at[layer + 1, x, pl.ds(1024, HALO)]
                    b = hA.at[layer + 1, x, pl.ds(0, HALO)]
                    remote(
                        a,
                        b,
                        halo_s.at[layer + 1, 1, to],
                        halo_r.at[layer + 1, 1, x],
                        (t + 1, x if to == 0 else 1 - x),
                    )

            inner = hA.at[layer + 1, x, pl.ds(HALO, ROWS)]
            remote(inner, inner, x_s.at[layer], x_r.at[layer], partner)

        @pl.when(layer == 4)
        def _():
            def one(b, _):
                v = (z[rows_of(b), :] - m) * r
                xhb[0, rows_of(b), :] = v
                y5[rows_of(b), :] = y5[rows_of(b), :] + gain * v + bias
                return 0

            lax.fori_loop(0, 8, one, 0)

        pltpu.make_async_copy(xhb.at[0], xh_out.at[layer], out_s.at[11]).start()

        @pl.when(layer < 4)
        def _():
            serve(11 + 7 * layer, 18 + 7 * layer)

        @pl.when(layer == 0)
        def _():
            copies[13].wait()
            wait_on(rawn.at[0], xr_r.at[2])
            for j in range(3):
                for s in range(8):
                    spread_half(rawn[s // 4, j, s % 4], s)

                def one(b, _):
                    nar[j, rows_of(b), :] = masked_block(b, 0)
                    return 0

                lax.fori_loop(0, 8, one, 0)

        @pl.when(layer == 1)
        def _():
            branches(5, 3)
            wait_on(raww.at[0, 0], xr_r.at[3])
            spread_wide(0)

            def one(b, _):
                for h in range(2):
                    wid[h, rows_of(b), :] = masked_block(b, h)
                return 0

            lax.fori_loop(0, 8, one, 0)

        @pl.when(layer == 2)
        def _():
            branches(8, 2)
            copies[14].wait()
            remote(cot.at[:, :, other], rawc.at[x], xr_s.at[4], xr_r.at[4], partner)

        @pl.when(layer == 3)
        def _():
            wait_on(rawc.at[0], xr_r.at[4])
            for s in range(8):
                spread_half(rawc[s // 4, s % 4], s)

            def one(b, _):
                cotv[rows_of(b), :] = masked_block(b, 0)
                return 0

            lax.fori_loop(0, 8, one, 0)

        @pl.when(layer < 4)
        def _():
            wait_on(hA.at[0, 0, pl.ds(HALO, ROWS)], x_r.at[layer])
            halo_wait(layer + 1, False)
            shift_copy(layer + 1)

        return 0

    lax.fori_loop(0, 5, layer_step, 0)

    last = [
        (wmn, wmn_out),
        (wmw, wmw_out),
        (y5, y_out),
        (nar, nar_out),
        (wid, wid_out),
        (cotv, cot_out),
    ]
    for i, (a, b) in enumerate(last):
        pltpu.make_async_copy(a, b, out_s.at[12 + i]).start()
    for i, (a, b) in enumerate(last):
        wait_on(a, out_s.at[12 + i])
    wait_on(xhb.at[0], out_s.at[11])
    for i in range(5):
        wait_on(W.at[pl.ds(0, 17)], out_s.at[i])
        wait_on(hA.at[0, :, pl.ds(HALO, ROWS)], out_s.at[5 + i])

    def drained(g, _):
        wait_on(amount(g, 15), ag_s.at[g])
        return 0

    lax.fori_loop(0, GROUPS, drained, 0)
    wait_on(G.at[pl.ds(0, 15)], m_s)
    wait_on(lenr.at[0], xr_s.at[0])
    wait_on(raww.at[0, 1], xr_s.at[1])
    wait_on(rawn.at[0], xr_s.at[2])
    wait_on(raww.at[0, 0], xr_s.at[3])
    wait_on(rawc.at[0], xr_s.at[4])

    def finish(layer, _):
        halo_wait(layer, True)
        wait_on(st.at[layer, pl.ds(0, 15)], st_s.at[layer])

        @pl.when(layer < 4)
        def _():
            wait_on(hA.at[0, 0, pl.ds(HALO, ROWS)], x_s.at[layer])

        return 0

    lax.fori_loop(0, 5, finish, 0)


def run_forward(lens, norm, perm, src_n, src_w, cot, kf, kr, mn, mw):
    vm = pl.BlockSpec(memory_space=pltpu.VMEM)
    hb = pl.BlockSpec(memory_space=pl.ANY)
    dma = pltpu.SemaphoreType.DMA
    S = jax.ShapeDtypeStruct
    return pl.pallas_call(
        forward_kernel,
        out_shape=(
            S((85, 16, 32, HALF), BF),
            S((3, HALF, HALF), BF),
            S((2, 512, HALF), BF),
            S((5, 2, ROWS, HALF), BF),
            S((10, ROWS, HALF), F32),
            S((ROWS, HALF), F32),
            S((3, ROWS, HALF), BF),
            S((2, ROWS, HALF), BF),
            S((ROWS, HALF), BF),
            S((10, 8, HALF), F32),
            S((8, HALF), F32),
        ),
        in_specs=[vm, vm, vm] + [hb] * 7,
        out_specs=[hb] * 9 + [vm, vm],
        scratch_shapes=[
            pltpu.VMEM((85, 16, 32, HALF), BF),
            pltpu.VMEM((16, 112, HALF), BF),
            pltpu.VMEM((3, HALF, HALF), BF),
            pltpu.VMEM((2, 512, HALF), BF),
            pltpu.VMEM((5, 2, 1168, HALF), BF),
            pltpu.VMEM((2, 1152, HALF), BF),
            pltpu.VMEM((ROWS, HALF), F32),
            pltpu.VMEM((3, ROWS, HALF), F32),
            pltpu.VMEM((2, ROWS, HALF), F32),
            pltpu.VMEM((ROWS, HALF), F32),
            pltpu.VMEM((4, ROWS, 128), F32),
            pltpu.VMEM((5, 2, 544, 128), F32),
            pltpu.VMEM((3, 16, HALF), F32),
            pltpu.VMEM((2, 24, HALF), F32),
            pltpu.VMEM((2, 2, 4, 128, 384), BF),
            pltpu.VMEM((2, 3, 4, 128, HALF), BF),
            pltpu.VMEM((2, 4, 128, HALF), BF),
            pltpu.VMEM((3, ROWS, HALF), BF),
            pltpu.VMEM((2, ROWS, HALF), BF),
            pltpu.VMEM((ROWS, HALF), BF),
            pltpu.VMEM((5, 16, 8, HALF), F32),
            pltpu.VMEM((16, 8, HALF), F32),
            pltpu.VMEM((2, 8, HALF), F32),
            pltpu.VMEM((8, HALF), F32),
            dma((15,)),
            dma((GROUPS,)),
            dma((GROUPS,)),
            dma((GROUPS,)),
            dma((GROUPS,)),
            dma,
            dma((3,)),
            dma((4,)),
            dma((4,)),
            dma((5,)),
            dma((5,)),
            dma((5, 2, 2)),
            dma((5, 2, 2)),
            dma((5,)),
            dma((5,)),
            dma((18,)),
        ],
        compiler_params=pltpu.CompilerParams(
            collective_id=0, has_side_effects=True, vmem_limit_bytes=62 << 20
        ),
        cost_estimate=pl.CostEstimate(flops=24 * 10**9, bytes_accessed=60 * 10**6, transcendentals=0),
    )(lens, norm, perm, src_n, src_w, cot, kf, kr, mn, mw)


def backward_kernel(
    lens_in,
    norm,
    rs,
    perm,
    w_in,
    wmn,
    wmw,
    h_in,
    xh_in,
    y_in,
    nar_in,
    wid_in,
    cot_in,
    mixed_out,
    gn_out,
    gw_out,
    gf_out,
    gr_out,
    gmn_out,
    gmw_out,
    ng_out,
    total_out,
    Wl,
    Hl,
    Xl,
    xb,
    sb,
    y5,
    da,
    dzA,
    dzB,
    dW,
    crecv,
    yrecv,
    zrecv,
    fin,
    xrecv,
    px,
    pxr,
    stg,
    own_n,
    own_w,
    snd_n,
    snd_w,
    rcv_n,
    rcv_w,
    mix_own,
    mix_rcv,
    Dm,
    cm,
    ym,
    zm,
    fm,
    xm,
    gst,
    gsm,
    bst,
    ngr,
    ngx,
    ss,
    fst,
    load_s,
    w_s,
    go,
    br_s,
    halo_s,
    halo_r,
    st_s,
    st_r,
    c_s,
    c_r,
    y_s,
    y_r,
    z_s,
    z_r,
    f_s,
    f_r,
    px_s,
    px_r,
    m_s,
    m_r,
    sn_s,
    sn_r,
    g_s,
    out_s,
    ng_s,
    ng_r,
):
    x, t, zi, yi, ci = position()
    partner = (t, 1 - x)
    sibling = (t + 1 - 2 * ci, x)
    across = (zi * 4 + (1 - yi) * 2 + ci, x)
    lens = lens_in[...]

    def when(cond, f):
        if isinstance(cond, bool):
            if cond:
                f()
        else:
            pl.when(cond)(f)

    def rows_of(b):
        return pl.ds(pl.multiple_of(b * 128, 128), 128)

    def copy_in(src, dst, sem):
        pltpu.make_async_copy(src, dst, sem).start()

    def load_w(layer):
        b2 = lax.rem(layer, 2)
        copy_in(w_in.at[pl.ds(17 * layer, 17)], Wl.at[b2], w_s.at[b2])

    def load_h(layer):
        copy_in(h_in.at[layer], Hl, load_s.at[1])

    def load_x(layer):
        copy_in(xh_in.at[layer], Xl, load_s.at[2])

    copy_in(y_in, y5, load_s.at[3])
    copy_in(cot_in, sb.at[0], load_s.at[4])
    load_x(4)
    copy_in(xh_in.at[5], xb.at[1], br_s.at[1])
    load_w(4)
    load_h(4)

    for edge, lo in ((0, 0), (15, 1088)):

        @pl.when(t == edge)
        def _():
            dzA[:, pl.ds(lo, HALO), :] = jnp.zeros((2, HALO, HALF), BF)

    dzA[:, pl.ds(1152, 16), :] = jnp.zeros((2, 16, HALF), BF)
    barrier = pltpu.get_barrier_semaphore()

    def greet_one(d, _):
        pl.semaphore_signal(
            barrier, inc=1, device_id=(lax.rem(t + d, 16), x), device_id_type=MESH
        )
        return 0

    lax.fori_loop(1, 16, greet_one, 0)
    pl.semaphore_signal(barrier, inc=1, device_id=partner, device_id_type=MESH)
    pl.semaphore_wait(barrier, 16)

    zero = jnp.zeros((8, HALF), F32)
    count = jnp.zeros((1, HALF), F32)
    for s in range(16):
        count = count + jnp.sum(jnp.clip(lens - 128.0 * s, 0.0, 128.0), axis=0, keepdims=True)

    def mask(b):
        return frame_mask(b, t, lens)

    def sequence(block, s):
        return stg[block, pl.ds(s, 128, stride=8), :]

    def unstage(blocks, own, send):
        for i in range(4):
            for b in range(blocks):
                own(i, b, sequence(b, 4 * x + i))
                send(i, b, sequence(b, 4 * (1 - x) + i))

    wait_on(y5, load_s.at[3])

    def out_block(b, _):
        y = y5[rows_of(b), :]
        a = (y * jax.nn.sigmoid(y)).reshape(16, 8, HALF) * mask(b)
        a = a.reshape(128, HALF)
        for i in range(2):
            stg[i, rows_of(b), :] = a[:, 128 * i : 128 * i + 128]
        return 0

    lax.fori_loop(0, 8, out_block, 0)

    def mix_put(ref):
        def put(i, b, v):
            ref[i, :, pl.ds(128 * b, 128)] = v.astype(BF)

        return put

    unstage(2, mix_put(mix_own.at[0]), mix_put(mix_own.at[1]))
    remote(mix_own.at[1], mix_rcv, sn_s.at[0], sn_r.at[0], partner)
    my_cols = pl.ds(pl.multiple_of(x * HALF, HALF), HALF)
    other_cols = pl.ds(pl.multiple_of((1 - x) * HALF, HALF), HALF)
    copy_in(mix_own.at[0], mixed_out.at[:, :, my_cols], out_s.at[0])

    wait_on(sb.at[0], load_s.at[4])

    def start_da(b, _):
        da[rows_of(b), :] = sb[0, rows_of(b), :].astype(F32)
        return 0

    lax.fori_loop(0, 8, start_da, 0)

    def slot_z(q):
        return lax.rem(zi + 1 + q, 4)

    def send_core(layer):
        b3, b2 = lax.rem(layer, 3), lax.rem(layer, 2)
        for q in range(4):
            zz = slot_z(q)
            remote(
                dW.at[b3, :, zz, :, 1 - ci],
                crecv.at[b2, :, zz],
                c_s.at[layer],
                c_r.at[layer, q],
                sibling,
            )

    def add_core(layer, q):
        b3, b2 = lax.rem(layer, 3), lax.rem(layer, 2)
        zz = slot_z(q)
        wait_on(crecv.at[b2, :, zz], c_r.at[layer, q])
        for yy in range(2):

            def one(k, _):
                dW[b3, k, zz, yy, ci] = (
                    dW[b3, k, zz, yy, ci].astype(F32) + crecv[b2, k, zz, yy].astype(F32)
                ).astype(BF)
                return 0

            lax.fori_loop(0, 17, one, 0)
        remote(
            dW.at[b3, :, zz, 1 - yi, ci],
            yrecv.at[b2, :, zz],
            y_s.at[layer],
            y_r.at[layer, q],
            across,
        )

    def add_across(layer, q):
        b3, b2 = lax.rem(layer, 3), lax.rem(layer, 2)
        zz = slot_z(q)
        wait_on(yrecv.at[b2, :, zz], y_r.at[layer, q])

        def one(k, _):
            dW[b3, k, zz, yi, ci] = (
                dW[b3, k, zz, yi, ci].astype(F32) + yrecv[b2, k, zz].astype(F32)
            ).astype(BF)
            return 0

        lax.fori_loop(0, 17, one, 0)
        if q < 3:
            remote(
                dW.at[b3, :, zz, yi, ci],
                zrecv.at[b2, q],
                z_s.at[layer],
                z_r.at[layer],
                (zz * 4 + yi * 2 + ci, x),
            )

    def finish_sum(layer):
        b3, b2 = lax.rem(layer, 3), lax.rem(layer, 2)
        wait_on(zrecv.at[b2], z_r.at[layer])
        when(layer + 2 <= 4, lambda: wait_on(fin.at[0], f_s.at[layer + 2]))

        def one(k, _):
            v = dW[b3, k, zi, yi, ci].astype(F32)
            for q in range(3):
                v = v + zrecv[b2, q, k].astype(F32)
            fin[b2, k] = v.astype(BF)
            return 0

        lax.fori_loop(0, 17, one, 0)
        remote(fin.at[b2], xrecv.at[layer], f_s.at[layer], f_r.at[layer], partner)

    def add_square(v):
        ss[...] += jnp.sum((v * v).reshape(-1, 8, 128), axis=0)

    def assemble(layer, rows, put):
        b2 = lax.rem(layer, 2)
        wait_on(xrecv.at[layer], f_r.at[layer])
        for k in range(17):
            for b in range(2):
                lanes = pl.ds(128 * b, 128)
                gst[2 * x + b, pl.ds(k, rows, stride=17), :] = fin[
                    b2, k, pl.ds(0, 32), lanes
                ].astype(F32)[:rows]
                gst[2 * (1 - x) + b, pl.ds(k, rows, stride=17), :] = xrecv[
                    layer, k, pl.ds(0, 32), lanes
                ].astype(F32)[:rows]
        for b in range(4):
            add_square(gst[b, pl.ds(0, rows * 17), :])
            copy_in(gst.at[b, pl.ds(0, rows * 17)], put(b), g_s)

    def wait_assembled(rows):
        wait_on(gst.at[:, pl.ds(0, rows * 17)], g_s)

    def drain_sums(layer):
        wait_on(crecv.at[0], c_s.at[layer])
        wait_on(yrecv.at[0], y_s.at[layer])
        wait_on(zrecv.at[0], z_s.at[layer])

    def put_rest(layer):
        return lambda b: gr_out.at[layer - 1, :, pl.ds(128 * b, 128)]

    def mixers_one():
        remote(Dm.at[:, :, 1 - ci], cm, m_s.at[0], m_r.at[0], sibling)

    def mixers_two():
        wait_on(cm, m_r.at[0])
        for zz in range(4):
            for yy in range(2):
                Dm[zz, yy, ci] = (Dm[zz, yy, ci].astype(F32) + cm[zz, yy].astype(F32)).astype(BF)
        remote(Dm.at[:, 1 - yi, ci], ym, m_s.at[1], m_r.at[1], across)

    def mixers_three():
        wait_on(ym, m_r.at[1])
        for zz in range(4):
            Dm[zz, yi, ci] = (Dm[zz, yi, ci].astype(F32) + ym[zz].astype(F32)).astype(BF)
        for q in range(3):
            zz = slot_z(q)
            remote(Dm.at[zz, yi, ci], zm.at[q], m_s.at[2], m_r.at[2], (zz * 4 + yi * 2 + ci, x))

    def mixers_four():
        wait_on(zm, m_r.at[2])
        v = Dm[zi, yi, ci].astype(F32)
        for q in range(3):
            v = v + zm[q].astype(F32)
        fm[...] = v.astype(BF)
        remote(fm, xm, m_s.at[3], m_r.at[3], partner)

    def mixers_five():
        wait_on(xm, m_r.at[3])
        for b in range(2):
            lanes = pl.ds(128 * b, 128)
            gsm[2 * x + b] = fm[:, lanes].astype(F32)
            gsm[2 * (1 - x) + b] = xm[:, lanes].astype(F32)
        for b in range(4):
            add_square(gsm[b])
            for j in range(3):
                copy_in(
                    gsm.at[b, pl.ds(16 * j, 16)],
                    gmn_out.at[j, :, pl.ds(128 * b, 128)],
                    out_s.at[1],
                )
            for j in range(2):
                copy_in(
                    gsm.at[b, pl.ds(48 + 32 * j, 24)],
                    gmw_out.at[j, :, pl.ds(128 * b, 128)],
                    out_s.at[2],
                )

    def halo_sent(layer):
        for side, edge in ((0, 0), (1, 15)):

            @pl.when(t != edge)
            def _():
                wait_on(dzA.at[0, pl.ds(0, HALO)], halo_s.at[layer, side])

    def norm_backward(layer, last):
        wait_on(Xl, load_s.at[2])
        gain = norm[layer, pl.ds(0, 1), :]
        bias = norm[layer, pl.ds(1, 1), :]

        def one(b, acc):
            xh = Xl[rows_of(b), :]
            y = y5[rows_of(b), :] if last else gain * xh + bias
            sg = jax.nn.sigmoid(y)
            v = da[rows_of(b), :] * sg * (1.0 + y * (1.0 - sg))
            v = v.reshape(16, 8, HALF) * mask(b)
            s0 = acc[0] + jnp.sum(v, axis=0)
            s1 = acc[1] + jnp.sum(v * xh.reshape(16, 8, HALF), axis=0)
            v = v.reshape(128, HALF)
            da[rows_of(b), :] = v
            if last:
                y5[rows_of(b), :] = v
            return s0, s1

        s0, s1 = lax.fori_loop(0, 8, one, (zero, zero))
        bst[layer, t] = zero
        bst[layer, t, pl.ds(0, 1), :] = jnp.sum(s0, axis=0, keepdims=True)
        bst[layer, t, pl.ds(1, 1), :] = jnp.sum(s1, axis=0, keepdims=True)
        if last:
            for j in range(5):
                at = (j + 1) % 2
                wait_on(xb.at[at], br_s.at[at])
                if j < 4:
                    copy_in(xh_in.at[6 + j], xb.at[1 - at], br_s.at[1 - at])

                def branch(b, acc):
                    return acc + jnp.sum(
                        (da[rows_of(b), :] * xb[at, rows_of(b), :]).reshape(16, 8, HALF), axis=0
                    )

                sj = lax.fori_loop(0, 8, branch, zero)
                bst[layer, t, pl.ds(2 + j, 1), :] = jnp.sum(sj, axis=0, keepdims=True)
        share(bst, layer, t, x, st_s.at[layer], st_r.at[layer])
        wait_on(bst.at[layer, pl.ds(0, 15)], st_r.at[layer])
        sums = lax.fori_loop(0, 16, lambda s, a: a + bst[layer, s], zero)
        ngr[layer, pl.ds(0, 1), :] = sums[1:2]
        ngr[layer, pl.ds(1, 1), :] = sums[0:1]
        if last:
            for j in range(5):
                ngr[5 + j, pl.ds(0, 1), :] = sums[2 + j : 3 + j]
                ngr[5 + j, pl.ds(1, 1), :] = sums[0:1]
        r = rs[layer, pl.ds(0, 1), :]
        c0 = gain * sums[0:1] / count
        c1 = gain * sums[1:2] / count
        b2 = lax.rem(layer, 2)

        def dz_block(b, _):
            m = mask(b)
            v = (gain * da[rows_of(b), :]).reshape(16, 8, HALF)
            xh = Xl[rows_of(b), :].reshape(16, 8, HALF)
            v = r * (v - m * c0 - m * xh * c1)
            dzA[b2, pl.ds(pl.multiple_of(HALO + b * 128, 64), 128), :] = v.reshape(
                128, HALF
            ).astype(BF)
            return 0

        when(layer + 2 <= 4, lambda: halo_sent(layer + 2))
        lax.fori_loop(0, 8, dz_block, 0)
        for side, edge, lo, to in ((0, 0, HALO, 1088), (1, 15, 1024, 0)):

            @pl.when(t != edge)
            def _():
                remote(
                    dzA.at[b2, pl.ds(lo, HALO)],
                    dzA.at[b2, pl.ds(to, HALO)],
                    halo_s.at[layer, side],
                    halo_r.at[layer, side],
                    (t - 1 + 2 * side, x),
                )

        return sums

    def halo_arrived(layer):
        b2 = lax.rem(layer, 2)
        for side, edge in ((1, 0), (0, 15)):

            @pl.when(t != edge)
            def _():
                wait_on(dzA.at[b2, pl.ds(0, HALO)], halo_r.at[layer, side])

        def one(b, _):
            v = dzA[b2, pl.ds(pl.multiple_of(b * 128, 128), 144), :].astype(F32)
            dzB[pl.ds(pl.multiple_of(b * 128, 128), 128), :] = v[8:136].astype(BF)
            return 0

        lax.fori_loop(0, 9, one, 0)

    def shifted(b2, k):
        o = 16 - k
        if o % 2 == 0:
            return dzA[b2, pl.ds(8 * o, ROWS), :]
        return dzB[pl.ds(8 * (o - 1), ROWS), :]

    def data_half(layer, half):
        b2 = lax.rem(layer, 2)
        acc = jnp.zeros((ROWS, HALF), F32)
        for k in range(17):
            acc = acc + lax.dot_general(
                shifted(b2, k),
                Wl[b2, k, pl.ds(8 * half, 8)].reshape(HALF, HALF),
                (((1,), (1,)), ((), ())),
                preferred_element_type=F32,
            )
        return acc

    def weight_gradient(layer):
        b3, b2 = lax.rem(layer, 3), lax.rem(layer, 2)
        wait_on(Hl, load_s.at[1])
        for k in range(17):
            for h in range(2):
                v = lax.dot_general(
                    Hl[h], shifted(b2, k), (((0,), (0,)), ((), ())), preferred_element_type=F32
                )
                dW[b3, k, pl.ds(2 * h, 2)] = v.reshape(2, 2, 2, 32, HALF).astype(BF)

    def branches(sums):
        own_first = True
        for j in range(5):
            field = 5 + j
            copy_in(xh_in.at[field], xb.at[0], br_s.at[0])
            if j < 3:
                copy_in(nar_in.at[j], sb.at[0], br_s.at[2])
            elif j == 3:
                copy_in(wid_in, sb, br_s.at[2])
            else:
                copy_in(h_in.at[0], sb, br_s.at[2])
            wait_on(xb.at[0], br_s.at[0])
            wait_on(sb.at[0] if j < 3 else sb, br_s.at[2])
            gain = norm[field, pl.ds(0, 1), :]
            r = rs[field, pl.ds(0, 1), :]
            c0 = gain * sums[0:1] / count
            c1 = gain * sums[2 + j : 3 + j] / count

            def one(b, _):
                m = mask(b)
                v = (gain * y5[rows_of(b), :]).reshape(16, 8, HALF)
                xh = xb[0, rows_of(b), :].reshape(16, 8, HALF)
                v = r * (v - m * c0 - m * xh * c1)
                px[1, rows_of(b), :] = v.reshape(128, HALF).astype(BF)
                return 0

            lax.fori_loop(0, 8, one, 0)
            dv = px[1]
            if j < 3:
                v = lax.dot_general(
                    sb[0], dv, (((0,), (0,)), ((), ())), preferred_element_type=F32
                )
                Dm[:, :, :, pl.ds(16 * j, 16), :] = v.reshape(4, 2, 2, 16, HALF).astype(BF)
                back = lax.dot_general(
                    dv, wmn[j], (((1,), (1,)), ((), ())), preferred_element_type=F32
                )
                blocks = 2
            else:
                i = j - 3
                for h in range(2):
                    v = lax.dot_general(
                        sb[h], dv, (((0,), (0,)), ((), ())), preferred_element_type=F32
                    )
                    Dm[pl.ds(2 * h, 2), :, :, pl.ds(48 + 32 * i, 32), :] = v.reshape(
                        2, 2, 2, 32, HALF
                    ).astype(BF)
                wu = jnp.dot(perm[...], wmw[i], preferred_element_type=F32).astype(BF)
                back = lax.dot_general(
                    dv, wu, (((1,), (1,)), ((), ())), preferred_element_type=F32
                )
                blocks = 3
            for b in range(blocks):
                stg[b] = back[:, 128 * b : 128 * b + 128]

            def masked(b, _):
                m = mask(b)[:, :, :128]
                for i in range(blocks):
                    stg[i, rows_of(b), :] = (
                        stg[i, rows_of(b), :].reshape(16, 8, 128) * m
                    ).reshape(128, 128)
                return 0

            lax.fori_loop(0, 8, masked, 0)
            if j < 3:

                def put_own(i, b, v):
                    own_n[j, i, :, pl.ds(128 * b, 128)] = v

                def put_send(i, b, v):
                    snd_n[j, i, :, pl.ds(128 * b, 128)] = v.astype(BF)

            else:

                def put_own(i, b, v):
                    own_w[j - 3, i, :, pl.ds(128 * b, 128)] = v

                def put_send(i, b, v):
                    snd_w[j - 3, i, :, pl.ds(128 * b, 128)] = v.astype(BF)

            unstage(blocks, put_own, put_send)
        remote(snd_n, rcv_n, sn_s.at[1], sn_r.at[1], partner)
        remote(snd_w.at[pl.ds(0, 2)], rcv_w.at[pl.ds(0, 2)], sn_s.at[2], sn_r.at[2], partner)

    def sources_narrow():
        wait_on(rcv_n, sn_r.at[1])
        own_n[...] = own_n[...] + rcv_n[...].astype(F32)
        copy_in(own_n, gn_out, out_s.at[3])

    def chain(layer, last, first):
        load_next = lambda f: when(layer > 0, lambda: f(layer - 1))
        b2 = lax.rem(layer, 2)
        load_next(load_w)
        sums = norm_backward(layer, last)
        load_next(load_x)
        halo_arrived(layer)

        if last is False:

            def finish_older():
                add_across(layer + 2, 2)
                add_across(layer + 2, 3)

            when(layer + 2 <= 4, finish_older)
            for q in range(4):
                add_core(layer + 1, q)
        wait_on(Wl.at[0], w_s.at[b2])
        if first is False:
            if last is False:
                wait_on(px.at[0], px_s)
            acc = data_half(layer, 1 - x)
            px[0] = acc.astype(BF)
            remote(px.at[0], pxr.at[b2], px_s, px_r.at[layer], partner)
            da[...] = data_half(layer, x)
        if last is False:
            when(layer + 2 <= 4, lambda: finish_sum(layer + 2))
            if first:
                for to in [across] + [(slot_z(q) * 4 + yi * 2 + ci, x) for q in range(3)]:
                    pl.semaphore_signal(go, inc=1, device_id=to, device_id_type=MESH)
            add_across(layer + 1, 0)
            when(layer + 3 <= 4, lambda: drain_sums(layer + 3))
        weight_gradient(layer)
        load_next(load_h)
        if last is False:
            add_across(layer + 1, 1)
        send_core(layer)
        if last is False:

            def older_out():
                when(layer + 3 <= 4, lambda: wait_assembled(32))
                assemble(layer + 2, 32, put_rest(layer + 2))

            when(layer + 2 <= 4, older_out)
        if last:
            branches(sums)
        if first is False:
            wait_on(pxr.at[0], px_r.at[layer])

            def one(b, _):
                da[rows_of(b), :] = da[rows_of(b), :] + pxr[b2, rows_of(b), :].astype(F32)
                return 0

            lax.fori_loop(0, 8, one, 0)

    ss[...] = jnp.zeros((8, 128), F32)
    chain(4, True, False)
    mixers_one()
    mixers_two()

    def middle(i, _):
        layer = 3 - i
        chain(layer, False, False)

        @pl.when(layer == 3)
        def _():
            mixers_three()
            wait_on(mix_rcv, sn_r.at[0])
            copy_in(mix_rcv, mixed_out.at[:, :, other_cols], out_s.at[4])

        @pl.when(layer == 2)
        def _():
            mixers_four()
            sources_narrow()

        @pl.when(layer == 1)
        def _():
            mixers_five()

        return 0

    lax.fori_loop(0, 3, middle, 0)
    chain(0, False, True)

    remote(ngr, ngx, ng_s, ng_r, partner)

    for k in range(17):
        Wl[1, k, pl.ds(0, 12)] = (
            jnp.dot(perm[...], Wl[0, k].reshape(512, HALF), preferred_element_type=F32)
            .astype(BF)
            .reshape(12, 32, HALF)
        )
    add_across(1, 2)
    pl.semaphore_wait(go, 4)
    add_core(0, 0)
    add_core(0, 1)
    add_across(1, 3)
    add_core(0, 2)
    add_core(0, 3)
    for part in range(4):
        acc = jnp.zeros((HALF, 384), F32)
        for k in range(17):
            o = 16 - k
            lo = part * HALF
            lhs = (
                dzA[0, pl.ds(8 * o + lo, HALF), :]
                if o % 2 == 0
                else dzB[pl.ds(8 * (o - 1) + lo, HALF), :]
            )
            acc = acc + lax.dot_general(
                lhs,
                Wl[1, k, pl.ds(0, 12)].reshape(384, HALF),
                (((1,), (1,)), ((), ())),
                preferred_element_type=F32,
            )
        for half in range(2):
            m = mask(2 * part + half)[:, :, :128]
            for b in range(3):
                stg[b, pl.ds(part * HALF + half * 128, 128), :] = (
                    acc[128 * half : 128 * half + 128, 128 * b : 128 * b + 128].reshape(
                        16, 8, 128
                    )
                    * m
                ).reshape(128, 128)

    def put_own(i, b, v):
        lanes = pl.ds(128 * b, 128)
        own_w[1, i, :, lanes] = own_w[1, i, :, lanes] + v

    def put_send(i, b, v):
        snd_w[2, i, :, pl.ds(128 * b, 128)] = v.astype(BF)

    unstage(3, put_own, put_send)
    remote(snd_w.at[2], rcv_w.at[2], sn_s.at[3], sn_r.at[3], partner)
    add_across(0, 0)
    finish_sum(1)
    add_across(0, 1)
    add_across(0, 2)
    add_across(0, 3)
    wait_assembled(32)
    assemble(1, 32, put_rest(1))
    wait_on(rcv_w.at[pl.ds(0, 2)], sn_r.at[2])
    wait_on(rcv_w.at[2], sn_r.at[3])
    for j in range(2):
        v = own_w[j] + rcv_w[j].astype(F32)
        if j == 1:
            v = v + rcv_w[2].astype(F32)
        own_w[j] = v
    copy_in(own_w, gw_out, out_s.at[5])
    wait_on(ngx, ng_r)
    finish_sum(0)
    wait_assembled(32)
    assemble(0, 24, lambda b: gf_out.at[:, pl.ds(128 * b, 128)])

    fst[t] = ss[...]

    def tell(d, _):
        remote(fst.at[t], fst.at[t], st_s.at[5], st_r.at[5], (lax.rem(t + d, 16), x))
        return 0

    lax.fori_loop(1, 16, tell, 0)
    mine, theirs = ngr[...], ngx[...]
    left = jnp.where(x == 0, mine, theirs)
    right = jnp.where(x == 0, theirs, mine)
    rows = lax.broadcasted_iota(jnp.int32, (10, 8, HALF), 1)
    left = jnp.where(rows < 2, left, 0.0)
    right = jnp.where(rows < 2, right, 0.0)
    ng_out[0] = left
    ng_out[1] = right
    norms = jnp.sum(left * left + right * right)
    wait_on(fst.at[pl.ds(0, 15)], st_r.at[5])
    every = lax.fori_loop(0, 16, lambda s, a: a + fst[s], jnp.zeros((8, 128), F32))
    total_out[...] = jnp.zeros((8, 128), F32) + (jnp.sum(every) + norms)

    wait_assembled(24)
    wait_on(mix_own.at[0], out_s.at[0])
    wait_on(mix_rcv, out_s.at[4])
    wait_on(own_n, out_s.at[3])
    wait_on(own_w, out_s.at[5])
    wait_on(gsm.at[:, pl.ds(0, 48)], out_s.at[1])
    wait_on(gsm.at[:, pl.ds(0, 48)], out_s.at[2])
    wait_on(px.at[0], px_s)
    wait_on(mix_own.at[1], sn_s.at[0])
    wait_on(snd_n, sn_s.at[1])
    wait_on(snd_w.at[pl.ds(0, 2)], sn_s.at[2])
    wait_on(snd_w.at[2], sn_s.at[3])
    wait_on(cm, m_s.at[0])
    wait_on(ym, m_s.at[1])
    wait_on(zm, m_s.at[2])
    wait_on(fm, m_s.at[3])
    wait_on(ngr, ng_s)
    wait_on(fst.at[pl.ds(0, 15)], st_s.at[5])
    for layer in (1, 0, 2):
        drain_sums(layer)

    for layer in range(2):
        wait_on(fin.at[0], f_s.at[layer])
        halo_sent(layer)

    def finish(layer, _):
        wait_on(bst.at[layer, pl.ds(0, 15)], st_s.at[layer])
        return 0

    lax.fori_loop(0, 5, finish, 0)


def run_backward(lens, norm, rs, perm, w, wmn, wmw, h, xh, y, nar, wid, cot):
    vm = pl.BlockSpec(memory_space=pltpu.VMEM)
    hb = pl.BlockSpec(memory_space=pl.ANY)
    dma = pltpu.SemaphoreType.DMA
    S = jax.ShapeDtypeStruct
    V = pltpu.VMEM
    return pl.pallas_call(
        backward_kernel,
        out_shape=(
            S((4, 128, 512), BF),
            S((3, 4, 128, HALF), F32),
            S((2, 4, 128, 384), F32),
            S((408, 512), F32),
            S((4, 544, 512), F32),
            S((3, 16, 512), F32),
            S((2, 24, 512), F32),
            S((2, 10, 8, HALF), F32),
            S((8, 128), F32),
        ),
        in_specs=[vm, vm, vm, vm, hb, vm, vm, hb, hb, hb, hb, hb, hb],
        out_specs=[hb] * 7 + [vm, vm],
        scratch_shapes=[
            V((2, 17, 16, 32, HALF), BF),
            V((2, ROWS, HALF), BF),
            V((ROWS, HALF), F32),
            V((2, ROWS, HALF), F32),
            V((2, ROWS, HALF), BF),
            V((ROWS, HALF), F32),
            V((ROWS, HALF), F32),
            V((2, 1168, HALF), BF),
            V((1152, HALF), BF),
            V((3, 17, 4, 2, 2, 32, HALF), BF),
            V((2, 17, 4, 2, 32, HALF), BF),
            V((2, 17, 4, 32, HALF), BF),
            V((2, 3, 17, 32, HALF), BF),
            V((2, 17, 32, HALF), BF),
            V((5, 17, 32, HALF), BF),
            V((2, ROWS, HALF), BF),
            V((2, ROWS, HALF), BF),
            V((3, ROWS, 128), F32),
            V((3, 4, 128, HALF), F32),
            V((2, 4, 128, 384), F32),
            V((3, 4, 128, HALF), BF),
            V((3, 4, 128, 384), BF),
            V((3, 4, 128, HALF), BF),
            V((3, 4, 128, 384), BF),
            V((2, 4, 128, HALF), BF),
            V((4, 128, HALF), BF),
            V((4, 2, 2, 112, HALF), BF),
            V((4, 2, 112, HALF), BF),
            V((4, 112, HALF), BF),
            V((3, 112, HALF), BF),
            V((112, HALF), BF),
            V((112, HALF), BF),
            V((4, 544, 128), F32),
            V((4, 112, 128), F32),
            V((5, 16, 8, HALF), F32),
            V((10, 8, HALF), F32),
            V((10, 8, HALF), F32),
            V((8, 128), F32),
            V((16, 8, 128), F32),
            dma((5,)),
            dma((2,)),
            pltpu.SemaphoreType.REGULAR,
            dma((3,)),
            dma((5, 2)),
            dma((5, 2)),
            dma((6,)),
            dma((6,)),
            dma((5,)),
            dma((5, 4)),
            dma((5,)),
            dma((5, 4)),
            dma((5,)),
            dma((5,)),
            dma((5,)),
            dma((5,)),
            dma,
            dma((5,)),
            dma((4,)),
            dma((4,)),
            dma((4,)),
            dma((4,)),
            dma,
            dma((6,)),
            dma,
            dma,
        ],
        compiler_params=pltpu.CompilerParams(
            collective_id=1, has_side_effects=True, vmem_limit_bytes=63 << 20
        ),
        cost_estimate=pl.CostEstimate(flops=46 * 10**9, bytes_accessed=60 * 10**6, transcendentals=0),
    )(lens, norm, rs, perm, w, wmn, wmw, h, xh, y, nar, wid, cot)


def prepare(lengths, norm_params):
    x = lax.axis_index("batch")
    mine = jnp.broadcast_to(lengths.astype(F32)[:, None], (4, HALF))
    lens = jnp.zeros((8, HALF), F32)
    lens = lax.dynamic_update_slice(lens, mine, (4 * x, 0))
    half = lax.dynamic_slice(norm_params, (0, 0, x * HALF), (2, 10, HALF))
    norm = jnp.pad(jnp.transpose(half, (1, 0, 2)), ((0, 0), (0, 6), (0, 0)))
    places = np.arange(384)
    perm = np.zeros((384, 512), np.float32)
    perm[places, (places // 24) * 32 + places % 24] = 1.0
    return lens, norm, jnp.asarray(perm, BF)


def body_split(
    source_narrow,
    source_wide,
    lengths,
    cotangent,
    kernel_first,
    kernel_rest,
    mixer_narrow,
    mixer_wide,
    norm_params,
    moment_first,
    square_first,
    moment_rest,
    square_rest,
    moment_narrow,
    square_narrow,
    moment_wide,
    square_wide,
    moment_norm,
    square_norm,
):
    lens, norm, perm = prepare(lengths, norm_params)
    w, wmn, wmw, h, xh, y, nar, wid, cot, rs, lens = run_forward(
        lens,
        norm,
        perm,
        source_narrow,
        source_wide,
        cotangent,
        kernel_first,
        kernel_rest,
        mixer_narrow,
        mixer_wide,
    )
    mixed, gn, gw, gf, gr, gmn, gmw, ng, total = run_backward(
        lens, norm, rs, perm, w, wmn, wmw, h, xh, y, nar, wid, cot
    )
    grad_norm = jnp.sqrt(total[0, 0])
    clip = jnp.minimum(1.0, THRESHOLD / grad_norm)
    norm_grad = jnp.transpose(ng[:, :, :2, :], (2, 1, 0, 3)).reshape(2, 10, CO)
    results = []
    for p, g, m, v in (
        (kernel_first, gf, moment_first, square_first),
        (kernel_rest, gr, moment_rest, square_rest),
        (mixer_narrow, gmn, moment_narrow, square_narrow),
        (mixer_wide, gmw, moment_wide, square_wide),
    ):
        results += adamw(p, clip * g, m, v, RATE_WEIGHT, DECAY)
    results += adamw(norm_params, clip * norm_grad, moment_norm, square_norm, RATE_NORM, 0.0)
    return (mixed, gn, gw, grad_norm, *results)


def solution(mesh):
    in_specs = (
        P(None, "batch", "tm", None),
        P(None, "batch", "tm", None),
        P("batch"),
        P("batch", "tm", None),
        P("tm", None),
        P(None, "tm", None),
        P(None, "tm", None),
        P(None, "tm", None),
        P(),
        P("tm", None),
        P("tm", None),
        P(None, "tm", None),
        P(None, "tm", None),
        P(None, "tm", None),
        P(None, "tm", None),
        P(None, "tm", None),
        P(None, "tm", None),
        P(),
        P(),
    )
    out_specs = (
        P("batch", "tm", None),
        P(None, "batch", "tm", None),
        P(None, "batch", "tm", None),
        P(),
        P("tm", None),
        P("tm", None),
        P("tm", None),
        P(None, "tm", None),
        P(None, "tm", None),
        P(None, "tm", None),
        P(None, "tm", None),
        P(None, "tm", None),
        P(None, "tm", None),
        P(None, "tm", None),
        P(None, "tm", None),
        P(None, "tm", None),
        P(),
        P(),
        P(),
    )
    fits = mesh.shape["tm"] == 16 and mesh.shape["batch"] == 2
    chosen = body_split if fits else body
    return jax.shard_map(chosen, mesh=mesh, in_specs=in_specs, out_specs=out_specs, check_vma=False)
```

```python
import numpy as np
import jax
import jax.numpy as jnp
from jax import lax
from jax.experimental import pallas as pl
from jax.experimental.pallas import tpu as pltpu
from jax.sharding import PartitionSpec as P

CO = 512
CW = 384
K = 17
STEP = 10


EPS = 1e-05
THRESHOLD = 100.0
BETA_ONE = 0.9
SECOND_DECAY = 0.999
ADAM_EPS = 1e-08
RATE_WEIGHT = 0.02
RATE_NORM = 0.4
DECAY = 0.01


def padded_2(shard, sides, width):
    for axis, dim in sides:
        devices, length = (lax.axis_size(axis), shard.shape[dim])
        up = [(i, (i + 1) % devices) for i in range(devices - 1)]
        down = [(j, i) for i, j in up]
        last = lax.slice_in_dim(shard, length - width, length, axis=dim)
        initial = lax.slice_in_dim(shard, 0, width, axis=dim)
        before = lax.ppermute(last, axis, up)
        after = lax.ppermute(initial, axis, down)
        shard = jnp.concatenate([before, shard, after], axis=dim)
    return shard


def adamw(param, grad, first, second, rate, decay):
    first_new = BETA_ONE * first + (1.0 - BETA_ONE) * grad
    second_new = SECOND_DECAY * second + (1.0 - SECOND_DECAY) * grad * grad
    fix_one = 1.0 - BETA_ONE**STEP
    fix_two = 1.0 - SECOND_DECAY**STEP
    update = first_new / fix_one / (jnp.sqrt(second_new / fix_two) + ADAM_EPS)
    return (param - rate * (update + decay * param), first_new, second_new)


def body(
    source_narrow,
    source_wide,
    lengths,
    cotangent,
    kernel_first,
    kernel_rest,
    mixer_narrow,
    mixer_wide,
    norm_params,
    moment_first,
    square_first,
    moment_rest,
    square_rest,
    moment_narrow,
    square_narrow,
    moment_wide,
    square_wide,
    moment_norm,
    square_norm,
):
    frames = source_wide.shape[2]
    half = K // 2
    places = lax.axis_index("tm") * frames + jnp.arange(frames, dtype=jnp.int32)
    valid = (places[None, :] < lengths[:, None]).astype(jnp.float32)[:, :, None]
    local_count = jnp.sum(valid)
    valid_low = valid.astype(jnp.bfloat16)
    narrow = source_narrow * valid_low[None]
    wide = source_wide * valid_low[None]
    full_first, full_rest, full_narrow, full_wide = (
        lax.all_gather(kernel_first.astype(jnp.bfloat16), "tm", axis=0, tiled=True),
        lax.all_gather(kernel_rest.astype(jnp.bfloat16), "tm", axis=1, tiled=True),
        lax.all_gather(mixer_narrow.astype(jnp.bfloat16), "tm", axis=1, tiled=True),
        lax.all_gather(mixer_wide.astype(jnp.bfloat16), "tm", axis=1, tiled=True),
    )
    kernels = [jnp.transpose(full_first.reshape(CW, K, CO), (1, 0, 2))] + [
        jnp.transpose(full_rest[layer].reshape(CO, K, CO), (1, 0, 2)) for layer in range(4)
    ]
    gains = norm_params[0]
    biases = norm_params[1]

    def batch_statistics(values, count):
        sums = tuple((jnp.sum(value * valid, axis=(0, 1)) for value in values))
        extra = (local_count,) if count is None else ()
        got = lax.psum(sums + extra, ("tm", "batch"))
        if count is None:
            count = got[-1]
        means = [total / count for total in got[: len(values)]]
        spreads = tuple(
            (
                jnp.sum(jnp.square((value - mean) * valid), axis=(0, 1))
                for value, mean in zip(values, means)
            )
        )
        second = lax.psum(spreads, ("tm", "batch"))
        variances = [total / count for total in second]
        scales = [lax.rsqrt(variance + EPS) for variance in variances]
        return (means, scales, count)

    signal = wide[1]
    kept = []
    count = None
    for index in range(5):
        padded = padded_2(signal, (("tm", 1),), half)
        field = jnp.zeros(signal.shape[:2] + (CO,), jnp.float32)
        for tap in range(K):
            field = field + jnp.einsum(
                "btc,cd->btd",
                padded[:, tap : tap + frames],
                kernels[index][tap],
                preferred_element_type=jnp.float32,
            )
        values = [field]
        indices = [index]
        if index == 4:
            for source in range(3):
                values.append(
                    jnp.einsum(
                        "btc,cd->btd",
                        narrow[source],
                        full_narrow[source],
                        preferred_element_type=jnp.float32,
                    )
                )
                indices.append(5 + source)
            for source in range(2):
                values.append(
                    jnp.einsum(
                        "btc,cd->btd",
                        wide[source],
                        full_wide[source],
                        preferred_element_type=jnp.float32,
                    )
                )
                indices.append(8 + source)
        means, scales, count = batch_statistics(values, count)
        normalized_values = [
            (value - mean) * scale for value, mean, scale in zip(values, means, scales)
        ]
        summed = jnp.zeros_like(field)
        for place in range(len(values)):
            summed = (
                summed + gains[indices[place]] * normalized_values[place] + biases[indices[place]]
            )
        kept.append((padded, normalized_values, scales, summed, indices))
        active = jax.nn.silu(summed) * valid
        signal = active.astype(jnp.bfloat16)
    grad_active = cotangent.astype(jnp.float32)
    kernel_grads = [None] * 5
    gain_grads = [None] * 10
    bias_grads = [None] * 10
    narrow_grads = []
    wide_grads = []
    narrow_inputs = []
    wide_inputs = []
    first_input = None
    for index in reversed(range(5)):
        padded, normalized_values, scales, summed, indices = kept[index]
        sigma = jax.nn.sigmoid(summed)
        gradient_total = grad_active * valid * sigma * (1.0 + summed * (1.0 - sigma))
        local_sums = (jnp.sum(gradient_total, axis=(0, 1)),) + tuple(
            (
                jnp.sum(gradient_total * standardized_input, axis=(0, 1))
                for standardized_input in normalized_values
            )
        )
        got = lax.psum(local_sums, ("tm", "batch"))
        bias_total = got[0]
        field_grads = []
        for place in range(len(normalized_values)):
            which = indices[place]
            gain = gains[which]
            gain_grads[which] = got[1 + place]
            bias_grads[which] = bias_total
            grad_field = scales[place] * (
                gain * gradient_total
                - valid * (gain * bias_total) / count
                - valid * normalized_values[place] * (gain * got[1 + place]) / count
            )
            field_grads.append(grad_field.astype(jnp.bfloat16))
        grad_conv = field_grads[0]
        tap_grads = [
            jnp.einsum(
                "btc,btd->cd",
                padded[:, tap : tap + frames],
                grad_conv,
                preferred_element_type=jnp.float32,
            )
            for tap in range(K)
        ]
        kernel_grads[index] = jnp.stack(tap_grads, axis=1).reshape(padded.shape[2] * K, CO)
        if index == 4:
            for source in range(3):
                branch = field_grads[1 + source]
                narrow_grads.append(
                    jnp.einsum(
                        "btc,btd->cd", narrow[source], branch, preferred_element_type=jnp.float32
                    )
                )
                narrow_inputs.append(
                    jnp.einsum(
                        "btd,cd->btc",
                        branch,
                        full_narrow[source],
                        preferred_element_type=jnp.float32,
                    )
                    * valid
                )
            for source in range(2):
                branch = field_grads[4 + source]
                wide_grads.append(
                    jnp.einsum(
                        "btc,btd->cd", wide[source], branch, preferred_element_type=jnp.float32
                    )
                )
                wide_inputs.append(
                    jnp.einsum(
                        "btd,cd->btc", branch, full_wide[source], preferred_element_type=jnp.float32
                    )
                    * valid
                )
        grad_padded = padded_2(grad_conv, (("tm", 1),), half)
        incoming = jnp.zeros(padded.shape[:1] + (frames, padded.shape[2]), jnp.float32)
        for tap in range(K):
            start = K - 1 - tap
            incoming = incoming + jnp.einsum(
                "btd,cd->btc",
                grad_padded[:, start : start + frames],
                kernels[index][tap],
                preferred_element_type=jnp.float32,
            )
        if index > 0:
            grad_active = incoming
        else:
            first_input = incoming
    grad_narrow = jnp.stack(narrow_inputs)
    source_wide_gradient = jnp.stack([wide_inputs[0], (first_input + wide_inputs[1]) * valid])
    shard_gradients = (
        kernel_grads[0],
        jnp.stack(kernel_grads[1:]),
        jnp.stack(narrow_grads),
        jnp.stack(wide_grads),
    )
    shards = (
        lax.psum_scatter(shard_gradients[0], "tm", scatter_dimension=0, tiled=True),
        lax.psum_scatter(shard_gradients[1], "tm", scatter_dimension=1, tiled=True),
        lax.psum_scatter(shard_gradients[2], "tm", scatter_dimension=1, tiled=True),
        lax.psum_scatter(shard_gradients[3], "tm", scatter_dimension=1, tiled=True),
    )
    norm_grad = jnp.stack([jnp.stack(gain_grads), jnp.stack(bias_grads)])
    params = (kernel_first, kernel_rest, mixer_narrow, mixer_wide)
    firsts = (moment_first, moment_rest, moment_narrow, moment_wide)
    seconds = (square_first, square_rest, square_narrow, square_wide)
    results = []
    shards = (
        lax.psum(shards[0].astype(jnp.bfloat16), "batch").astype(jnp.float32),
        lax.psum(shards[1].astype(jnp.bfloat16), "batch").astype(jnp.float32),
        lax.psum(shards[2].astype(jnp.bfloat16), "batch").astype(jnp.float32),
        lax.psum(shards[3].astype(jnp.bfloat16), "batch").astype(jnp.float32),
    )
    local_square = jnp.zeros((), jnp.float32)
    for shard in shards:
        local_square = local_square + jnp.sum(shard * shard)
    total = lax.psum(local_square, "tm") + jnp.sum(norm_grad * norm_grad)
    grad_norm = jnp.sqrt(total)
    clip = jnp.minimum(1.0, THRESHOLD / grad_norm)
    for slot in range(4):
        results.append(
            adamw(
                params[slot], clip * shards[slot], firsts[slot], seconds[slot], RATE_WEIGHT, DECAY
            )
        )
    results.append(adamw(norm_params, clip * norm_grad, moment_norm, square_norm, RATE_NORM, 0.0))
    return (
        signal,
        grad_narrow,
        source_wide_gradient,
        grad_norm,
        results[0][0],
        results[0][1],
        results[0][2],
        results[1][0],
        results[1][1],
        results[1][2],
        results[2][0],
        results[2][1],
        results[2][2],
        results[3][0],
        results[3][1],
        results[3][2],
        results[4][0],
        results[4][1],
        results[4][2],
    )


BF = jnp.bfloat16
F32 = jnp.float32
MESH = pl.DeviceIdType.MESH
ROWS = 1024
HALO = 64
HALF = 256
GROUPS = 34


def wait_on(ref, sem):
    pltpu.make_async_copy(ref, ref, sem).wait()


def remote(src, dst, send, recv, device):
    pltpu.make_async_remote_copy(
        src_ref=src,
        dst_ref=dst,
        send_sem=send,
        recv_sem=recv,
        device_id=device,
        device_id_type=MESH,
    ).start()


def position():
    x = lax.axis_index("batch")
    t = lax.axis_index("tm")
    return x, t, lax.div(t, 4), lax.rem(lax.div(t, 2), 2), lax.rem(t, 2)


def greet(x, t):
    barrier = pltpu.get_barrier_semaphore()

    def one(d, _):
        pl.semaphore_signal(
            barrier, inc=1, device_id=(lax.rem(t + d, 16), x), device_id_type=MESH
        )
        return 0

    lax.fori_loop(1, 16, one, 0)
    for d in (0, 1, 15):
        pl.semaphore_signal(
            barrier, inc=1, device_id=(lax.rem(t + d, 16), 1 - x), device_id_type=MESH
        )
    pl.semaphore_wait(barrier, 18)


def frame_mask(block, t, lens):
    frames = lax.broadcasted_iota(jnp.int32, (16, 8, HALF), 0) + (block * 16 + t * 128)
    return (frames.astype(F32) < lens[None]).astype(F32)


def share(box, at, rows, t, x, send, recv):
    mine = box.at[at, t, pl.ds(0, rows)]

    def one(d, _):
        remote(mine, mine, send, recv, (lax.rem(t + d, 16), x))
        return 0

    lax.fori_loop(1, 16, one, 0)


def forward_kernel(
    lens_in,
    norm,
    perm,
    src_n,
    src_w,
    cot,
    kf,
    kr,
    mn,
    mw,
    w_out,
    wmn_out,
    wmw_out,
    h_out,
    xh_out,
    y_out,
    nar_out,
    wid_out,
    cot_out,
    rs_out,
    len_out,
    W,
    G,
    wmn,
    wmw,
    hA,
    hB,
    z,
    zb,
    xhb,
    y5,
    stg,
    pf,
    pmn,
    pmw,
    raww,
    rawn,
    rawc,
    nar,
    wid,
    cotv,
    st,
    nv,
    lenr,
    lens,
    load_s,
    ag_s,
    rz,
    ry,
    rc,
    m_s,
    m_r,
    x_s,
    x_r,
    xr_s,
    xr_r,
    halo_s,
    halo_r,
    st_s,
    st_r,
    out_s,
):
    x, t, zi, yi, ci = position()
    cols = pl.ds(pl.multiple_of(x * HALF, HALF), HALF)
    partner = (t, 1 - x)
    sibling = (t + 1 - 2 * ci, x)
    across = (zi * 4 + (1 - yi) * 2 + ci, x)

    lanes = [pl.ds(pl.multiple_of(x * HALF + 128 * b, 128), 128) for b in range(2)]
    loads = [(kf.at[:, lanes[b]], pf.at[0, b, pl.ds(0, 408)]) for b in range(2)]
    loads += [(kr.at[i, :, lanes[b]], pf.at[1 + i, b]) for i in range(4) for b in range(2)]
    loads += [
        (mn.at[:, :, cols], pmn),
        (mw.at[:, :, cols], pmw),
        (src_w, raww.at[x]),
        (src_n, rawn.at[x]),
        (cot.at[:, :, cols], rawc.at[x]),
    ]
    copies = [pltpu.make_async_copy(a, b, load_s.at[i]) for i, (a, b) in enumerate(loads)]
    for copy in copies:
        copy.start()
    hA[:, :, pl.ds(1152, 16), :] = jnp.zeros((5, 2, 16, HALF), BF)

    @pl.when(t == 0)
    def _():
        hA[:, :, pl.ds(0, HALO), :] = jnp.zeros((5, 2, HALO, HALF), BF)

    @pl.when(t == 15)
    def _():
        hA[:, :, pl.ds(1088, HALO), :] = jnp.zeros((5, 2, HALO, HALF), BF)

    st[...] = jnp.zeros((7, 16, 8, HALF), F32)
    lenr[0] = lens_in[...]
    greet(x, t)

    other = pl.ds(pl.multiple_of((1 - x) * HALF, HALF), HALF)
    remote(lenr.at[0], lenr.at[1], xr_s.at[0], xr_r.at[0], partner)
    remote(src_w.at[1], raww.at[x, 1], xr_s.at[1], xr_r.at[1], partner)

    def prep(layer, count):
        for k in range(17):
            for b in range(2):
                v = pf[layer, b, pl.ds(k, count, stride=17), :]
                if count < 32:
                    v = jnp.concatenate([v, jnp.zeros((32 - count, 128), F32)], axis=0)
                W[17 * layer + k, zi, yi, ci, :, pl.ds(128 * b, 128)] = v.astype(BF)

    def taps(g):
        return pl.ds(5 * lax.div(g, 2), 5)

    def part(g):
        return pl.ds(pl.multiple_of(16 * lax.rem(g, 2), 16), 16)

    def first_sends(own, send, into_z):
        for dz in (1, 2, 3):
            remote(own, own, send, into_z, (lax.rem(zi + dz, 4) * 4 + yi * 2 + ci, x))

    def pass_z(line, send, into_y, into_c):
        remote(line, line, send, into_y, across)
        remote(line, line, send, into_c, sibling)

    def service(g):
        @pl.when(g < GROUPS)
        def _():
            first_sends(W.at[taps(g), zi, yi, ci, part(g)], ag_s.at[g], rz.at[g])

        @pl.when((g >= 2) & (g <= GROUPS + 1))
        def _():
            h = g - 2
            wait_on(W.at[taps(h), pl.ds(0, 3), 0, 0, part(h)], rz.at[h])
            pass_z(W.at[taps(h), :, yi, ci, part(h)], ag_s.at[h], ry.at[h], rc.at[h])

        @pl.when((g >= 4) & (g <= GROUPS + 3))
        def _():
            h = g - 4
            line = W.at[taps(h), :, 1 - yi, ci, part(h)]
            wait_on(line, ry.at[h])
            remote(line, line, ag_s.at[h], rc.at[h], sibling)

        @pl.when((g >= 5) & (g <= GROUPS + 4))
        def _():
            h = g - 5
            wait_on(W.at[taps(h), :, :, 0, part(h)], rc.at[h])

        @pl.when(g == 8)
        def _():
            first_sends(G.at[zi, yi, ci], m_s, m_r.at[0])

        @pl.when(g == 10)
        def _():
            wait_on(G.at[pl.ds(0, 3), 0, 0], m_r.at[0])
            pass_z(G.at[:, yi, ci], m_s, m_r.at[1], m_r.at[2])

        @pl.when(g == 12)
        def _():
            line = G.at[:, 1 - yi, ci]
            wait_on(line, m_r.at[1])
            remote(line, line, m_s, m_r.at[2], sibling)

        @pl.when(g == 13)
        def _():
            wait_on(G.at[:, :, 0], m_r.at[2])
            for s in range(16):
                got = G.at[s // 4, s // 2 % 2, s % 2]
                for j in range(3):
                    wmn[j, pl.ds(16 * s, 16), :] = got[pl.ds(16 * j, 16), :]
                for j in range(2):
                    wmw[j, pl.ds(32 * s, 32), :] = got[pl.ds(48 + 32 * j, 32), :]

    def serve(first, last):
        def one(g, _):
            service(g)
            return 0

        lax.fori_loop(first, last, one, 0)

    for copy in copies[:2]:
        copy.wait()
    prep(0, 24)
    service(jnp.int32(0))
    for copy in copies[2:12]:
        copy.wait()
    prep(1, 32)
    for layer in (2, 3, 4):
        prep(layer, 32)
    for j in range(3):
        G[zi, yi, ci, pl.ds(16 * j, 16), :] = pmn[j].astype(BF)
    for j in range(2):
        G[zi, yi, ci, pl.ds(48 + 32 * j, 32), :] = jnp.concatenate(
            [pmw[j], jnp.zeros((8, HALF), F32)], axis=0
        ).astype(BF)
    serve(1, 3)

    wait_on(lenr.at[1], xr_r.at[0])
    lens[...] = lenr[0] + lenr[1]
    len_out[...] = lens[...]
    for s in range(16):
        nv[s] = jnp.broadcast_to(
            jnp.sum(jnp.clip(lens[...] - 128.0 * s, 0.0, 128.0), axis=0, keepdims=True), (8, HALF)
        )

    def spread_wide(j):
        for s in range(8):
            v = jnp.dot(raww[s // 4, j, s % 4], perm[...], preferred_element_type=F32)
            for b in range(4):
                stg[b, pl.ds(s, 128, stride=8), :] = v[:, 128 * b : 128 * b + 128]

    def spread_half(v, s):
        for b in range(2):
            stg[b, pl.ds(s, 128, stride=8), :] = v[:, 128 * b : 128 * b + 128].astype(F32)

    def masked_block(b, h):
        rows = pl.ds(pl.multiple_of(b * 128, 128), 128)
        v = jnp.concatenate([stg[2 * h, rows, :], stg[2 * h + 1, rows, :]], axis=1)
        v = v.reshape(16, 8, HALF)
        return (v * frame_mask(b, t, lens[...])).reshape(128, HALF).astype(BF)

    copies[12].wait()
    wait_on(raww.at[0, 1], xr_r.at[1])
    spread_wide(1)

    def first_block(b, _):
        for h in range(2):
            hA[0, h, pl.ds(pl.multiple_of(HALO + b * 128, 64), 128), :] = masked_block(b, h)
        return 0

    lax.fori_loop(0, 8, first_block, 0)

    def halo_send(layer, half, to, side):
        a, b = ((HALO, 1088), (1024, 0))[side]
        remote(
            hA.at[layer, half, pl.ds(a, HALO)],
            hA.at[layer, half, pl.ds(b, HALO)],
            halo_s.at[layer, side, half if to is None else to],
            halo_r.at[layer, side, half],
            (t - 1 + 2 * side, x if to is None else jnp.where(to == 0, x, 1 - x)),
        )

    def halo_wait(layer, half, sems, sides):
        for side, edge in sides:

            @pl.when(t != edge)
            def _():
                wait_on(hA.at[layer, half, pl.ds(0, HALO)], sems.at[layer, side, half])

    ARRIVE = ((1, 0), (0, 15))
    DEPART = ((0, 0), (1, 15))

    @pl.when(t > 0)
    def _():
        for h in range(2):
            halo_send(0, h, None, 0)

    @pl.when(t < 15)
    def _():
        for h in range(2):
            halo_send(0, h, None, 1)

    remote(src_n, rawn.at[x], xr_s.at[2], xr_r.at[2], partner)
    remote(src_w.at[0], raww.at[x, 0], xr_s.at[3], xr_r.at[3], partner)
    serve(3, 13)

    def shift_copy(layer, half):
        def one(b, _):
            v = hA[layer, half, pl.ds(pl.multiple_of(b * 128, 128), 144), :].astype(F32)
            hB[half, pl.ds(pl.multiple_of(b * 128, 128), 128), :] = v[8:136].astype(BF)
            return 0

        lax.fori_loop(0, 9, one, 0)


    def rows_of(b):
        return pl.ds(pl.multiple_of(b * 128, 128), 128)

    def local_stats(ref):
        def total(b, acc):
            v = ref[rows_of(b), :].reshape(16, 8, HALF) * frame_mask(b, t, lens[...])
            return acc + jnp.sum(v, axis=0)

        s = jnp.sum(
            lax.fori_loop(0, 8, total, jnp.zeros((8, HALF), F32)), axis=0, keepdims=True
        )
        mean = s / jnp.maximum(nv[t, pl.ds(0, 1), :], 1.0)

        def spread(b, acc):
            v = (ref[rows_of(b), :].reshape(16, 8, HALF) - mean[None]) * frame_mask(
                b, t, lens[...]
            )
            return acc + jnp.sum(v * v, axis=0)

        m2 = jnp.sum(
            lax.fori_loop(0, 8, spread, jnp.zeros((8, HALF), F32)), axis=0, keepdims=True
        )
        return mean, m2

    def put_stats(ref, layer, field):
        mean, m2 = local_stats(ref)
        st[layer, t, pl.ds(2 * field, 1), :] = mean
        st[layer, t, pl.ds(2 * field + 1, 1), :] = m2

    def combine(at):
        zero = jnp.zeros((8, HALF), F32)
        count = lax.fori_loop(0, 16, lambda s, a: a + nv[s], zero)
        mean = lax.fori_loop(0, 16, lambda s, a: a + nv[s] * st[at, s], zero) / count

        def gather_spread(s, a):
            v = st[at, s]
            d = v - mean
            return a[0] + nv[s] * d * d, a[1] + v

        between, inside = lax.fori_loop(0, 16, gather_spread, (zero, zero))

        def moments(field):
            m = mean[2 * field : 2 * field + 1]
            q = inside[2 * field + 1 : 2 * field + 2] + between[2 * field : 2 * field + 1]
            return m, lax.rsqrt(q / count[:1] + EPS)

        return moments

    def branch_fields(at, number, inputs):
        for j in range(number):
            total = None
            for lhs, rhs in inputs(j):
                v = jnp.dot(lhs, rhs, preferred_element_type=F32)
                total = v if total is None else total + v
            zb[j] = total
            put_stats(zb.at[j], at, j)
        share(st, at, 8, t, x, st_s.at[at], st_r.at[at])

    def taps_of(layer, half, lo, rows):
        for k in range(17):
            lhs = (
                hA[layer, half, pl.ds(lo + 8 * k, rows), :]
                if k % 2 == 0
                else hB[half, pl.ds(lo + 8 * (k - 1), rows), :]
            )
            rhs = W[17 * layer + k, pl.ds(2 * half, 2)].reshape(HALF, HALF)
            yield jnp.dot(lhs, rhs, preferred_element_type=F32)

    PIECES = ((64, 320), (384, 256), (640, 256), (896, 192))

    def layer_step(layer, _):
        base = 13 + 7 * layer
        service(base)
        pltpu.make_async_copy(
            W.at[pl.ds(17 * layer, 17)], w_out.at[pl.ds(17 * layer, 17)], out_s.at[layer]
        ).start()

        halo_wait(layer, x, halo_r, ARRIVE)
        shift_copy(layer, x)
        acc = jnp.zeros((ROWS, HALF), F32)
        for v in taps_of(layer, x, 0, ROWS):
            acc = acc + v
        z[...] = acc
        service(base + 1)

        halo_wait(layer, 1 - x, halo_r, ARRIVE)
        for j, (lo, rows) in enumerate(PIECES):

            @pl.when(layer > 0)
            def _():
                wait_on(hA.at[layer, 1 - x, pl.ds(lo, rows)], x_r.at[layer, j])

            a = 0 if j == 0 else 256 * j + 112
            n = 368 if j == 0 else 256
            v = hA[layer, 1 - x, pl.ds(a, n + 16), :].astype(F32)
            hB[1 - x, pl.ds(a, n), :] = v[8 : n + 8].astype(BF)
            acc = z[pl.ds(256 * j, 256), :]
            for v in taps_of(layer, 1 - x, 256 * j, 256):
                acc = acc + v
            z[pl.ds(256 * j, 256), :] = acc
            if j == 1:
                service(base + 2)

        pltpu.make_async_copy(
            hA.at[layer, :, pl.ds(HALO, ROWS)], h_out.at[layer], out_s.at[5 + layer]
        ).start()
        put_stats(z, layer, 0)
        share(st, layer, 2, t, x, st_s.at[layer], st_r.at[layer])
        service(base + 3)
        service(base + 4)
        wait_on(st.at[layer, pl.ds(0, 15), pl.ds(0, 2)], st_r.at[layer])
        moments = combine(layer)

        def branches(at, base, number):
            wait_on(st.at[at, pl.ds(0, 15)], st_r.at[at])
            shares = combine(at)
            for j in range(number):
                m, r = shares(j)
                field = base + j
                rs_out[field] = jnp.broadcast_to(r, (8, HALF))
                gain = norm[field, pl.ds(0, 1), :]
                bias = norm[field, pl.ds(1, 1), :]
                if j > 0:
                    wait_on(xhb.at[1], out_s.at[10])

                def one(b, _):
                    v = (zb[j, rows_of(b), :] - m) * r
                    xhb[1, rows_of(b), :] = v
                    y = gain * v + bias
                    if field > 5:
                        y = y + y5[rows_of(b), :]
                    y5[rows_of(b), :] = y
                    return 0

                lax.fori_loop(0, 8, one, 0)
                pltpu.make_async_copy(xhb.at[1], xh_out.at[field], out_s.at[10]).start()
            wait_on(xhb.at[1], out_s.at[10])

        m, r = moments(0)
        rs_out[layer] = jnp.broadcast_to(r, (8, HALF))
        gain = norm[layer, pl.ds(0, 1), :]
        bias = norm[layer, pl.ds(1, 1), :]

        @pl.when(layer > 0)
        def _():
            wait_on(xhb.at[0], out_s.at[11])

        @pl.when(layer < 4)
        def _():
            def one(b, _):
                rows = pl.ds(pl.multiple_of(b * 64, 64), 64)
                v = (z[rows, :] - m) * r
                xhb[0, rows, :] = v
                y = gain * v + bias
                frames = lax.broadcasted_iota(jnp.int32, (8, 8, HALF), 0) + (b * 8 + t * 128)
                a = (y * jax.nn.sigmoid(y)).reshape(8, 8, HALF)
                a = jnp.where(frames.astype(F32) < lens[...][None], a, 0.0)
                hA[layer + 1, x, pl.ds(pl.multiple_of(HALO + b * 64, 64), 64), :] = a.reshape(
                    64, HALF
                ).astype(BF)
                return 0

            done = 0
            for j, (lo, rows) in enumerate(PIECES):
                last = (lo + rows - HALO) // 64
                lax.fori_loop(done, last, one, 0)
                done = last
                ref = hA.at[layer + 1, x, pl.ds(lo, rows)]
                remote(ref, ref, x_s.at[layer + 1, j], x_r.at[layer + 1, j], partner)
            for side, edge in DEPART:

                @pl.when(t != edge)
                def _():
                    lo, to = ((HALO, 1088), (1024, 0))[side]
                    for other in range(2):
                        remote(
                            hA.at[layer + 1, x, pl.ds(lo, HALO)],
                            hA.at[layer + 1, x, pl.ds(to, HALO)],
                            halo_s.at[layer + 1, side, other],
                            halo_r.at[layer + 1, side, x],
                            (t - 1 + 2 * side, x if other == 0 else 1 - x),
                        )

        @pl.when(layer == 4)
        def _():
            def one(b, _):
                v = (z[rows_of(b), :] - m) * r
                xhb[0, rows_of(b), :] = v
                y5[rows_of(b), :] = y5[rows_of(b), :] + gain * v + bias
                return 0

            lax.fori_loop(0, 8, one, 0)

        pltpu.make_async_copy(xhb.at[0], xh_out.at[layer], out_s.at[11]).start()

        service(base + 5)

        @pl.when(layer == 0)
        def _():
            copies[13].wait()
            wait_on(rawn.at[0], xr_r.at[2])
            for j in range(3):
                for s in range(8):
                    spread_half(rawn[s // 4, j, s % 4], s)

                def one(b, _):
                    nar[j, rows_of(b), :] = masked_block(b, 0)
                    return 0

                lax.fori_loop(0, 8, one, 0)
                if j == 0:
                    service(base + 6)

        @pl.when(layer == 1)
        def _():
            branches(5, 5, 3)
            service(base + 6)
            wait_on(raww.at[0, 0], xr_r.at[3])
            spread_wide(0)

            def one(b, _):
                for h in range(2):
                    wid[h, rows_of(b), :] = masked_block(b, h)
                return 0

            lax.fori_loop(0, 8, one, 0)

        @pl.when(layer == 2)
        def _():
            branches(6, 8, 2)
            service(base + 6)
            copies[14].wait()
            remote(cot.at[:, :, other], rawc.at[x], xr_s.at[4], xr_r.at[4], partner)

        @pl.when(layer == 3)
        def _():
            service(base + 6)
            wait_on(rawc.at[0], xr_r.at[4])
            for s in range(8):
                spread_half(rawc[s // 4, s % 4], s)

            def one(b, _):
                cotv[rows_of(b), :] = masked_block(b, 0)
                return 0

            lax.fori_loop(0, 8, one, 0)


        @pl.when(layer == 0)
        def _():
            branch_fields(5, 3, lambda j: [(nar[j], wmn[j])])

        @pl.when(layer == 1)
        def _():
            def inputs(j):
                for h in range(2):
                    lhs = wid[h] if j == 0 else hA[0, h, pl.ds(HALO, ROWS), :]
                    yield lhs, wmw[j, pl.ds(HALF * h, HALF), :]

            branch_fields(6, 2, inputs)

        return 0

    lax.fori_loop(0, 5, layer_step, 0)

    last = [
        (wmn, wmn_out),
        (wmw, wmw_out),
        (y5, y_out),
        (nar, nar_out),
        (wid, wid_out),
        (cotv, cot_out),
    ]
    for i, (a, b) in enumerate(last):
        pltpu.make_async_copy(a, b, out_s.at[12 + i]).start()
    for i, (a, b) in enumerate(last):
        wait_on(a, out_s.at[12 + i])
    wait_on(xhb.at[0], out_s.at[11])
    for i in range(5):
        wait_on(W.at[pl.ds(0, 17)], out_s.at[i])
        wait_on(hA.at[0, :, pl.ds(HALO, ROWS)], out_s.at[5 + i])

    def drained(g, _):
        wait_on(W.at[pl.ds(0, 75), 0, 0, 0, pl.ds(0, 16)], ag_s.at[g])
        return 0

    lax.fori_loop(0, GROUPS, drained, 0)
    wait_on(W.at[pl.ds(0, 35), pl.ds(0, 3), 0, 0, pl.ds(0, 16)], m_s)
    wait_on(lenr.at[0], xr_s.at[0])
    wait_on(raww.at[0, 1], xr_s.at[1])
    wait_on(rawn.at[0], xr_s.at[2])
    wait_on(raww.at[0, 0], xr_s.at[3])
    wait_on(rawc.at[0], xr_s.at[4])

    def finish(layer, _):
        for h in range(2):
            halo_wait(layer, h, halo_s, DEPART)
        wait_on(st.at[layer, pl.ds(0, 15), pl.ds(0, 2)], st_s.at[layer])

        @pl.when(layer > 0)
        def _():
            for j, (lo, rows) in enumerate(PIECES):
                wait_on(hA.at[0, 0, pl.ds(lo, rows)], x_s.at[layer, j])

        return 0

    lax.fori_loop(0, 5, finish, 0)
    for at in (5, 6):
        wait_on(st.at[at, pl.ds(0, 15)], st_s.at[at])


def run_forward(lens, norm, perm, src_n, src_w, cot, kf, kr, mn, mw):
    vm = pl.BlockSpec(memory_space=pltpu.VMEM)
    hb = pl.BlockSpec(memory_space=pl.ANY)
    dma = pltpu.SemaphoreType.DMA
    S = jax.ShapeDtypeStruct
    return pl.pallas_call(
        forward_kernel,
        out_shape=(
            S((85, 4, 2, 2, 32, HALF), BF),
            S((3, HALF, HALF), BF),
            S((2, 512, HALF), BF),
            S((5, 2, ROWS, HALF), BF),
            S((10, ROWS, HALF), F32),
            S((ROWS, HALF), F32),
            S((3, ROWS, HALF), BF),
            S((2, ROWS, HALF), BF),
            S((ROWS, HALF), BF),
            S((10, 8, HALF), F32),
            S((8, HALF), F32),
        ),
        in_specs=[vm, vm, vm] + [hb] * 7,
        out_specs=[hb] * 9 + [vm, vm],
        scratch_shapes=[
            pltpu.VMEM((85, 4, 2, 2, 32, HALF), BF),
            pltpu.VMEM((4, 2, 2, 112, HALF), BF),
            pltpu.VMEM((3, HALF, HALF), BF),
            pltpu.VMEM((2, 512, HALF), BF),
            pltpu.VMEM((5, 2, 1168, HALF), BF),
            pltpu.VMEM((2, 1152, HALF), BF),
            pltpu.VMEM((ROWS, HALF), F32),
            pltpu.VMEM((3, ROWS, HALF), F32),
            pltpu.VMEM((2, ROWS, HALF), F32),
            pltpu.VMEM((ROWS, HALF), F32),
            pltpu.VMEM((4, ROWS, 128), F32),
            pltpu.VMEM((5, 2, 544, 128), F32),
            pltpu.VMEM((3, 16, HALF), F32),
            pltpu.VMEM((2, 24, HALF), F32),
            pltpu.VMEM((2, 2, 4, 128, 384), BF),
            pltpu.VMEM((2, 3, 4, 128, HALF), BF),
            pltpu.VMEM((2, 4, 128, HALF), BF),
            pltpu.VMEM((3, ROWS, HALF), BF),
            pltpu.VMEM((2, ROWS, HALF), BF),
            pltpu.VMEM((ROWS, HALF), BF),
            pltpu.VMEM((7, 16, 8, HALF), F32),
            pltpu.VMEM((16, 8, HALF), F32),
            pltpu.VMEM((2, 8, HALF), F32),
            pltpu.VMEM((8, HALF), F32),
            dma((15,)),
            dma((GROUPS,)),
            dma((GROUPS,)),
            dma((GROUPS,)),
            dma((GROUPS,)),
            dma,
            dma((3,)),
            dma((5, 4)),
            dma((5, 4)),
            dma((5,)),
            dma((5,)),
            dma((5, 2, 2)),
            dma((5, 2, 2)),
            dma((7,)),
            dma((7,)),
            dma((18,)),
        ],
        compiler_params=pltpu.CompilerParams(
            collective_id=0, has_side_effects=True, vmem_limit_bytes=62 << 20
        ),
        cost_estimate=pl.CostEstimate(flops=24 * 10**9, bytes_accessed=60 * 10**6, transcendentals=0),
    )(lens, norm, perm, src_n, src_w, cot, kf, kr, mn, mw)


def backward_kernel(
    lens_in,
    norm,
    rs,
    perm,
    w_in,
    wmn,
    wmw,
    h_in,
    xh_in,
    y_in,
    nar_in,
    wid_in,
    cot_in,
    mixed_out,
    gn_out,
    gw_out,
    gf_out,
    gr_out,
    gmn_out,
    gmw_out,
    ng_out,
    total_out,
    Wl,
    Hl,
    Xl,
    xb,
    sb,
    y5,
    da,
    dzA,
    dzB,
    dW,
    crecv,
    yrecv,
    zrecv,
    fin,
    xrecv,
    px,
    pxr,
    stg,
    own_n,
    own_w,
    snd_n,
    snd_w,
    rcv_n,
    rcv_w,
    mix_own,
    mix_rcv,
    Dm,
    cm,
    ym,
    zm,
    fm,
    xm,
    gst,
    gsm,
    bst,
    sums4,
    ngr,
    ngx,
    ss,
    fst,
    load_s,
    w_s,
    br_s,
    halo_s,
    halo_r,
    st_s,
    st_r,
    c_s,
    c_r,
    y_s,
    y_r,
    z_s,
    z_r,
    f_s,
    f_r,
    px_s,
    px_r,
    m_s,
    m_r,
    sn_s,
    sn_r,
    g_s,
    out_s,
    ng_s,
    ng_r,
):
    x, t, zi, yi, ci = position()
    partner = (t, 1 - x)
    sibling = (t + 1 - 2 * ci, x)
    across = (zi * 4 + (1 - yi) * 2 + ci, x)
    lens = lens_in[...]

    def when(cond, f):
        if isinstance(cond, bool):
            if cond:
                f()
        else:
            pl.when(cond)(f)

    def rows_of(b):
        return pl.ds(pl.multiple_of(b * 128, 128), 128)

    def copy_in(src, dst, sem):
        pltpu.make_async_copy(src, dst, sem).start()

    def load_w(layer):
        b2 = lax.rem(layer, 2)
        copy_in(w_in.at[pl.ds(17 * layer, 17)], Wl.at[b2], w_s.at[b2])

    def load_h(layer):
        copy_in(h_in.at[layer], Hl, load_s.at[1])

    def load_x(layer):
        copy_in(xh_in.at[layer], Xl, load_s.at[2])

    copy_in(y_in, y5, load_s.at[3])
    copy_in(cot_in, sb.at[0], load_s.at[4])
    load_x(4)
    copy_in(xh_in.at[5], xb.at[1], br_s.at[1])
    load_w(4)
    load_h(4)

    for edge, lo in ((0, 0), (15, 1088)):

        @pl.when(t == edge)
        def _():
            dzA[:, pl.ds(lo, HALO), :] = jnp.zeros((2, HALO, HALF), BF)

    dzA[:, pl.ds(1152, 16), :] = jnp.zeros((2, 16, HALF), BF)
    bst[...] = jnp.zeros((5, 16, 8, HALF), F32)
    barrier = pltpu.get_barrier_semaphore()

    def greet_one(d, _):
        pl.semaphore_signal(
            barrier, inc=1, device_id=(lax.rem(t + d, 16), x), device_id_type=MESH
        )
        return 0

    lax.fori_loop(1, 16, greet_one, 0)
    pl.semaphore_signal(barrier, inc=1, device_id=partner, device_id_type=MESH)
    pl.semaphore_wait(barrier, 16)

    zero = jnp.zeros((8, HALF), F32)
    count = jnp.zeros((1, HALF), F32)
    for s in range(16):
        count = count + jnp.sum(jnp.clip(lens - 128.0 * s, 0.0, 128.0), axis=0, keepdims=True)

    def mask(b):
        return frame_mask(b, t, lens)

    def sequence(block, s):
        return stg[block, pl.ds(s, 128, stride=8), :]

    def unstage(blocks, own, send):
        for i in range(4):
            for b in range(blocks):
                own(i, b, sequence(b, 4 * x + i))
                send(i, b, sequence(b, 4 * (1 - x) + i))

    def mix_put(ref):
        def put(i, b, v):
            ref[i, :, pl.ds(128 * b, 128)] = v.astype(BF)

        return put

    my_cols = pl.ds(pl.multiple_of(x * HALF, HALF), HALF)
    other_cols = pl.ds(pl.multiple_of((1 - x) * HALF, HALF), HALF)

    def send_mixed():
        unstage(2, mix_put(mix_own.at[0]), mix_put(mix_own.at[1]))
        remote(mix_own.at[1], mix_rcv, sn_s.at[0], sn_r.at[0], partner)
        copy_in(mix_own.at[0], mixed_out.at[:, :, my_cols], out_s.at[0])

    ORDER = (0, 3, 1, 2)

    def send_core(layer, zs):
        b3, b2 = lax.rem(layer, 3), lax.rem(layer, 2)
        for zz in zs:
            remote(
                dW.at[b3, :, zz, :, 1 - ci],
                crecv.at[b2, :, zz],
                c_s.at[layer],
                c_r.at[layer, zz],
                sibling,
            )

    def add_core(layer, u, n=17):
        b3, b2 = lax.rem(layer, 3), lax.rem(layer, 2)
        zz, lo = ORDER[u // 2], n * (u % 2)
        if u % 2 == 0:
            wait_on(crecv.at[b2, :, zz], c_r.at[layer, zz])

        def one(k, _):
            for yy in range(2):
                dW[b3, k, zz, yy, ci] = (
                    dW[b3, k, zz, yy, ci].astype(F32) + crecv[b2, k, zz, yy].astype(F32)
                ).astype(BF)
            return 0

        lax.fori_loop(lo, lo + n, one, 0)
        remote(
            dW.at[b3, pl.ds(lo, n), zz, 1 - yi, ci],
            yrecv.at[b3, pl.ds(lo, n), zz],
            y_s.at[layer],
            y_r.at[layer, u],
            across,
        )

    def add_across(layer, u, n=17):
        b3 = lax.rem(layer, 3)
        zz, lo = ORDER[u // 2], n * (u % 2)
        wait_on(yrecv.at[b3, pl.ds(lo, n), zz], y_r.at[layer, u])

        def one(k, _):
            dW[b3, k, zz, yi, ci] = (
                dW[b3, k, zz, yi, ci].astype(F32) + yrecv[b3, k, zz].astype(F32)
            ).astype(BF)
            return 0

        lax.fori_loop(lo, lo + n, one, 0)

        @pl.when(zi != zz)
        def _():
            remote(
                dW.at[b3, pl.ds(lo, n), zz, yi, ci],
                zrecv.at[b3, lax.rem(zi + 3 - zz, 4), pl.ds(lo, n)],
                z_s.at[layer, u % 2],
                z_r.at[layer, u % 2],
                (zz * 4 + yi * 2 + ci, x),
            )

    def finish_sum(layer, half, n=17):
        b3, b2 = lax.rem(layer, 3), lax.rem(layer, 2)
        lo = n * half
        wait_on(zrecv.at[b3, :, pl.ds(lo, n)], z_r.at[layer, half])
        if half == 0:
            when(layer + 2 <= 4, lambda: wait_on(fin.at[0], f_s.at[layer + 2]))

        def one(k, _):
            v = dW[b3, k, zi, yi, ci].astype(F32)
            for q in range(3):
                v = v + zrecv[b3, q, k].astype(F32)
            fin[b2, k] = v.astype(BF)
            return 0

        lax.fori_loop(lo, lo + n, one, 0)
        mine = pl.ds(lo, n)
        remote(
            fin.at[b2, mine], xrecv.at[layer, mine], f_s.at[layer], f_r.at[layer, half], partner
        )

    def add_square(v):
        ss[...] += jnp.sum((v * v).reshape(-1, 8, 128), axis=0)

    def assemble(layer, put, n=17):
        b2 = lax.rem(layer, 2)
        rows = 32 if n == 17 else 24
        for half in range(2):
            wait_on(xrecv.at[layer, pl.ds(n * half, n)], f_r.at[layer, half])
        for source, side in ((fin.at[b2], x), (xrecv.at[layer], 1 - x)):
            for b in range(2):
                lanes = pl.ds(128 * b, 128)
                for k in range(17):
                    if n == 17:
                        v = source[pl.ds(2 * k, 2), :, lanes].astype(F32).reshape(32, 128)
                    else:
                        lo = 3 * (k // 2) + k % 2
                        v = source[pl.ds(lo, 2), :, lanes].astype(F32).reshape(32, 128)
                        v = v[8 * (k % 2) : 8 * (k % 2) + 24]
                    gst[2 * side + b, pl.ds(k, rows, stride=17), :] = v
        for b in range(4):
            add_square(gst[b, pl.ds(0, rows * 17), :])
            copy_in(gst.at[b, pl.ds(0, rows * 17)], put(b), g_s)

    def wait_assembled(rows):
        wait_on(gst.at[:, pl.ds(0, rows * 17)], g_s)

    def drain_sums(layer, n=17):
        wait_on(crecv.at[0], c_s.at[layer])
        wait_on(yrecv.at[0, pl.ds(0, 2 * n)], y_s.at[layer])
        for half in range(2):
            wait_on(zrecv.at[0, :, pl.ds(0, n)], z_s.at[layer, half])

    def put_rest(layer):
        return lambda b: gr_out.at[layer - 1, :, pl.ds(128 * b, 128)]

    def mixers_one():
        remote(Dm.at[:, :, 1 - ci], cm, m_s.at[0], m_r.at[0], sibling)

    def mixers_two():
        wait_on(cm, m_r.at[0])
        for zz in range(4):
            for yy in range(2):
                Dm[zz, yy, ci] = (Dm[zz, yy, ci].astype(F32) + cm[zz, yy].astype(F32)).astype(BF)
        remote(Dm.at[:, 1 - yi, ci], ym, m_s.at[1], m_r.at[1], across)

    def mixers_three():
        wait_on(ym, m_r.at[1])
        for zz in range(4):
            Dm[zz, yi, ci] = (Dm[zz, yi, ci].astype(F32) + ym[zz].astype(F32)).astype(BF)
        for q in range(3):
            zz = lax.rem(zi + 1 + q, 4)
            remote(Dm.at[zz, yi, ci], zm.at[q], m_s.at[2], m_r.at[2], (zz * 4 + yi * 2 + ci, x))

    def mixers_four():
        wait_on(zm, m_r.at[2])
        v = Dm[zi, yi, ci].astype(F32)
        for q in range(3):
            v = v + zm[q].astype(F32)
        fm[...] = v.astype(BF)
        remote(fm, xm, m_s.at[3], m_r.at[3], partner)

    def mixers_five():
        wait_on(xm, m_r.at[3])
        for b in range(2):
            lanes = pl.ds(128 * b, 128)
            gsm[2 * x + b] = fm[:, lanes].astype(F32)
            gsm[2 * (1 - x) + b] = xm[:, lanes].astype(F32)
        for b in range(4):
            add_square(gsm[b])
            for j in range(3):
                copy_in(
                    gsm.at[b, pl.ds(16 * j, 16)],
                    gmn_out.at[j, :, pl.ds(128 * b, 128)],
                    out_s.at[1],
                )
            for j in range(2):
                copy_in(
                    gsm.at[b, pl.ds(48 + 32 * j, 24)],
                    gmw_out.at[j, :, pl.ds(128 * b, 128)],
                    out_s.at[2],
                )

    def halo_sent(layer):
        for side, edge in ((0, 0), (1, 15)):

            @pl.when(t != edge)
            def _():
                wait_on(dzA.at[0, pl.ds(0, HALO)], halo_s.at[layer, side])

    def output_gradient(layer, last):
        wait_on(Xl, load_s.at[2])
        if last:
            wait_on(y5, load_s.at[3])
            wait_on(sb.at[0], load_s.at[4])
        gain = norm[layer, pl.ds(0, 1), :]
        bias = norm[layer, pl.ds(1, 1), :]

        def one(b, acc):
            xh = Xl[rows_of(b), :]
            if last:
                y = y5[rows_of(b), :]
                d = sb[0, rows_of(b), :].astype(F32)
            else:
                y = gain * xh + bias
                d = da[rows_of(b), :] + pxr[1 - lax.rem(layer, 2), rows_of(b), :].astype(F32)
            sg = jax.nn.sigmoid(y)
            m = mask(b)
            if last:
                a = ((y * sg).reshape(16, 8, HALF) * m).reshape(128, HALF)
                for i in range(2):
                    stg[i, rows_of(b), :] = a[:, 128 * i : 128 * i + 128]
            v = (d * sg * (1.0 + y * (1.0 - sg))).reshape(16, 8, HALF) * m
            s0 = acc[0] + jnp.sum(v, axis=0)
            s1 = acc[1] + jnp.sum(v * xh.reshape(16, 8, HALF), axis=0)
            v = v.reshape(128, HALF)
            da[rows_of(b), :] = v
            if last:
                y5[rows_of(b), :] = v
            return s0, s1

        if last:
            s0, s1 = lax.fori_loop(0, 8, one, (zero, zero))
        else:
            s0, s1 = zero, zero
            for j in range(4):
                wait_on(pxr.at[0, pl.ds(0, 256)], px_r.at[layer + 1, j])
                s0, s1 = lax.fori_loop(2 * j, 2 * j + 2, one, (s0, s1))
        bst[layer, t] = zero
        bst[layer, t, pl.ds(0, 1), :] = jnp.sum(s0, axis=0, keepdims=True)
        bst[layer, t, pl.ds(1, 1), :] = jnp.sum(s1, axis=0, keepdims=True)
        if last:
            for j in range(5):
                at = (j + 1) % 2
                wait_on(xb.at[at], br_s.at[at])
                if j < 4:
                    copy_in(xh_in.at[6 + j], xb.at[1 - at], br_s.at[1 - at])

                def branch(b, acc):
                    return acc + jnp.sum(
                        (da[rows_of(b), :] * xb[at, rows_of(b), :]).reshape(16, 8, HALF), axis=0
                    )

                sj = lax.fori_loop(0, 8, branch, zero)
                bst[layer, t, pl.ds(2 + j, 1), :] = jnp.sum(sj, axis=0, keepdims=True)
        share(bst, layer, 8 if last else 2, t, x, st_s.at[layer], st_r.at[layer])

    def field_gradient(layer, last):
        wait_on(bst.at[layer, pl.ds(0, 15), pl.ds(0, 8 if last else 2)], st_r.at[layer])
        gain = norm[layer, pl.ds(0, 1), :]
        sums = lax.fori_loop(0, 16, lambda s, a: a + bst[layer, s], zero)
        ngr[layer, pl.ds(0, 1), :] = sums[1:2]
        ngr[layer, pl.ds(1, 1), :] = sums[0:1]
        if last:
            sums4[...] = sums
            for j in range(5):
                ngr[5 + j, pl.ds(0, 1), :] = sums[2 + j : 3 + j]
                ngr[5 + j, pl.ds(1, 1), :] = sums[0:1]
        r = rs[layer, pl.ds(0, 1), :]
        c0 = gain * sums[0:1] / count
        c1 = gain * sums[1:2] / count
        b2 = lax.rem(layer, 2)

        def dz_block(b, _):
            m = mask(b)
            v = (gain * da[rows_of(b), :]).reshape(16, 8, HALF)
            xh = Xl[rows_of(b), :].reshape(16, 8, HALF)
            v = r * (v - m * c0 - m * xh * c1)
            dzA[b2, pl.ds(pl.multiple_of(HALO + b * 128, 64), 128), :] = v.reshape(
                128, HALF
            ).astype(BF)
            return 0

        when(layer + 2 <= 4, lambda: halo_sent(layer + 2))
        lax.fori_loop(0, 8, dz_block, 0)
        for side, edge, lo, to in ((0, 0, HALO, 1088), (1, 15, 1024, 0)):

            @pl.when(t != edge)
            def _():
                remote(
                    dzA.at[b2, pl.ds(lo, HALO)],
                    dzA.at[b2, pl.ds(to, HALO)],
                    halo_s.at[layer, side],
                    halo_r.at[layer, side],
                    (t - 1 + 2 * side, x),
                )

    def halo_arrived(layer):
        b2 = lax.rem(layer, 2)
        for side, edge in ((1, 0), (0, 15)):

            @pl.when(t != edge)
            def _():
                wait_on(dzA.at[b2, pl.ds(0, HALO)], halo_r.at[layer, side])

        def one(b, _):
            v = dzA[b2, pl.ds(pl.multiple_of(b * 128, 128), 144), :].astype(F32)
            dzB[pl.ds(pl.multiple_of(b * 128, 128), 128), :] = v[8:136].astype(BF)
            return 0

        lax.fori_loop(0, 9, one, 0)

    def shifted(b2, k, lo=0, rows=ROWS):
        o = 16 - k
        if o % 2 == 0:
            return dzA[b2, pl.ds(8 * o + lo, rows), :]
        return dzB[pl.ds(8 * (o - 1) + lo, rows), :]

    def data_half(layer, half, lo=0, rows=ROWS):
        b2 = lax.rem(layer, 2)
        acc = jnp.zeros((rows, HALF), F32)
        for k in range(17):
            acc = acc + lax.dot_general(
                shifted(b2, k, lo, rows),
                Wl[b2, k, pl.ds(2 * half, 2)].reshape(HALF, HALF),
                (((1,), (1,)), ((), ())),
                preferred_element_type=F32,
            )
        return acc

    def weight_tap(layer, h, k):
        return lax.dot_general(
            Hl[h],
            shifted(lax.rem(layer, 2), k),
            (((0,), (0,)), ((), ())),
            preferred_element_type=F32,
        ).reshape(2, 2, 2, 32, HALF)

    def weight_gradient(layer, h):
        b3 = lax.rem(layer, 3)
        for k in range(17):
            v = weight_tap(layer, h, k)
            for part in range(2):
                dW[b3, 2 * k + part, pl.ds(2 * h, 2)] = v[:, :, :, 16 * part : 16 * part + 16].astype(BF)

    def first_weight_gradient(h):
        for pair in range(9):
            v = weight_tap(0, h, 2 * pair)[:, :, :, :24]
            if pair < 8:
                v = jnp.concatenate([v, weight_tap(0, h, 2 * pair + 1)[:, :, :, :24]], axis=3)
            else:
                v = jnp.concatenate([v, jnp.zeros((2, 2, 2, 8, HALF), F32)], axis=3)
            for part in range(3 if pair < 8 else 2):
                dW[0, 3 * pair + part, pl.ds(2 * h, 2)] = v[
                    :, :, :, 16 * part : 16 * part + 16
                ].astype(BF)

    def load_branch(j):
        copy_in(xh_in.at[5 + j], xb.at[0], br_s.at[0])
        if j < 3:
            copy_in(nar_in.at[j], sb.at[0], br_s.at[2])
        elif j == 3:
            copy_in(wid_in, sb, br_s.at[2])
        else:
            copy_in(h_in.at[0], sb, br_s.at[2])

    def branch(j):
        field = 5 + j
        sums = sums4[...]
        wait_on(xb.at[0], br_s.at[0])
        wait_on(sb.at[0] if j < 3 else sb, br_s.at[2])
        gain = norm[field, pl.ds(0, 1), :]
        r = rs[field, pl.ds(0, 1), :]
        c0 = gain * sums[0:1] / count
        c1 = gain * sums[2 + j : 3 + j] / count

        def one(b, _):
            m = mask(b)
            v = (gain * y5[rows_of(b), :]).reshape(16, 8, HALF)
            xh = xb[0, rows_of(b), :].reshape(16, 8, HALF)
            v = r * (v - m * c0 - m * xh * c1)
            px[1, rows_of(b), :] = v.reshape(128, HALF).astype(BF)
            return 0

        lax.fori_loop(0, 8, one, 0)
        dv = px[1]
        if j < 3:
            v = lax.dot_general(
                sb[0], dv, (((0,), (0,)), ((), ())), preferred_element_type=F32
            )
            Dm[:, :, :, pl.ds(16 * j, 16), :] = v.reshape(4, 2, 2, 16, HALF).astype(BF)
            back = lax.dot_general(
                dv, wmn[j], (((1,), (1,)), ((), ())), preferred_element_type=F32
            )
            blocks = 2
        else:
            i = j - 3
            for h in range(2):
                v = lax.dot_general(
                    sb[h], dv, (((0,), (0,)), ((), ())), preferred_element_type=F32
                )
                Dm[pl.ds(2 * h, 2), :, :, pl.ds(48 + 32 * i, 32), :] = v.reshape(
                    2, 2, 2, 32, HALF
                ).astype(BF)
            wu = jnp.dot(perm[...], wmw[i], preferred_element_type=F32).astype(BF)
            back = lax.dot_general(
                dv, wu, (((1,), (1,)), ((), ())), preferred_element_type=F32
            )
            blocks = 3
        if j < 4:
            load_branch(j + 1)
        for b in range(8):
            m = mask(b)[:, :, :128]
            for i in range(blocks):
                v = back[128 * b : 128 * b + 128, 128 * i : 128 * i + 128]
                stg[i, pl.ds(128 * b, 128), :] = (v.reshape(16, 8, 128) * m).reshape(128, 128)
        if j < 3:

            def put_own(i, b, v):
                own_n[j, i, :, pl.ds(128 * b, 128)] = v

            def put_send(i, b, v):
                snd_n[j, i, :, pl.ds(128 * b, 128)] = v.astype(BF)

        else:

            def put_own(i, b, v):
                own_w[j - 3, i, :, pl.ds(128 * b, 128)] = v

            def put_send(i, b, v):
                snd_w[j - 3, i, :, pl.ds(128 * b, 128)] = v.astype(BF)

        unstage(blocks, put_own, put_send)
        if j < 3:
            remote(snd_n.at[j], rcv_n.at[j], sn_s.at[1 + j], sn_r.at[1 + j], partner)
        else:
            remote(snd_w.at[j - 3], rcv_w.at[j - 3], sn_s.at[1 + j], sn_r.at[1 + j], partner)

    def sources_narrow():
        for j in range(3):
            wait_on(rcv_n.at[j], sn_r.at[1 + j])
        own_n[...] = own_n[...] + rcv_n[...].astype(F32)
        copy_in(own_n, gn_out, out_s.at[3])

    def chain(layer, last):
        b2 = lax.rem(layer, 2)
        one = layer + 1
        two = lambda f: when(layer + 2 <= 4, lambda: f(layer + 2))
        load_w(layer - 1)
        output_gradient(layer, last)
        if last:
            send_mixed()
            load_branch(0)
        else:

            def two_a(older):
                add_across(older, 6)
                add_across(older, 7)

            two(two_a)
            add_core(one, 0)
            add_core(one, 1)
        field_gradient(layer, last)
        load_x(layer - 1)
        if not last:
            add_core(one, 2)
            add_across(one, 0)
        halo_arrived(layer)
        wait_on(Wl.at[0], w_s.at[b2])
        for j in range(4):
            if not last:
                wait_on(px.at[0, pl.ds(0, 256)], px_s.at[j])
            rows = pl.ds(256 * j, 256)
            px[0, rows, :] = data_half(layer, 1 - x, 256 * j, 256).astype(BF)
            remote(px.at[0, rows], pxr.at[b2, rows], px_s.at[j], px_r.at[layer, j], partner)
            if j == 1 and not last:
                add_core(one, 3)
                add_across(one, 1)
        if not last:
            two(lambda older: finish_sum(older, 0))
        da[...] = data_half(layer, x)
        if not last:
            add_core(one, 4)
            add_across(one, 2)
            two(lambda older: finish_sum(older, 1))
            when(layer + 3 <= 4, lambda: drain_sums(layer + 3))
        wait_on(Hl, load_s.at[1])
        weight_gradient(layer, 0)
        send_core(layer, (0, 1))
        if not last:
            add_core(one, 5)
            add_across(one, 3)
        weight_gradient(layer, 1)
        send_core(layer, (2, 3))
        load_h(layer - 1)
        if not last:
            add_core(one, 6)
            add_across(one, 4)
            add_core(one, 7)
            add_across(one, 5)

            def two_out(older):
                when(layer + 3 <= 4, lambda: wait_assembled(32))
                assemble(older, put_rest(older))

            two(two_out)

    ss[...] = jnp.zeros((8, 128), F32)
    chain(4, True)
    branch(0)

    def middle(i, _):
        layer = 3 - i
        chain(layer, False)

        @pl.when(layer == 3)
        def _():
            branch(1)
            branch(2)
            wait_on(mix_rcv, sn_r.at[0])
            copy_in(mix_rcv, mixed_out.at[:, :, other_cols], out_s.at[4])

        @pl.when(layer == 2)
        def _():
            branch(3)
            branch(4)
            mixers_one()
            sources_narrow()

        @pl.when(layer == 1)
        def _():
            mixers_two()

        return 0

    lax.fori_loop(0, 3, middle, 0)

    output_gradient(0, False)
    add_across(2, 6)
    add_across(2, 7)
    add_core(1, 0)
    add_core(1, 1)
    field_gradient(0, False)
    add_core(1, 2)
    add_across(1, 0)
    halo_arrived(0)
    wait_on(Hl, load_s.at[1])
    wait_on(Wl.at[0], w_s.at[0])
    drain_sums(3)
    first_weight_gradient(0)
    send_core(0, (0, 1))
    add_core(1, 3)
    add_across(1, 1)
    finish_sum(2, 0)
    add_core(1, 4)
    add_across(1, 2)
    first_weight_gradient(1)
    send_core(0, (2, 3))
    finish_sum(2, 1)
    add_core(1, 5)
    add_across(1, 3)
    mixers_three()

    remote(ngr, ngx, ng_s, ng_r, partner)

    for k in range(17):
        Wl[1, k, pl.ds(0, 3)] = (
            jnp.dot(perm[...], Wl[0, k].reshape(512, HALF), preferred_element_type=F32)
            .astype(BF)
            .reshape(3, 2, 2, 32, HALF)
        )
    add_core(1, 6)
    add_across(1, 4)
    add_core(1, 7)
    add_across(1, 5)
    wait_assembled(32)
    assemble(2, put_rest(2))
    mixers_four()
    for part in range(4):
        acc = jnp.zeros((HALF, 384), F32)
        for k in range(17):
            o = 16 - k
            lo = part * HALF
            lhs = (
                dzA[0, pl.ds(8 * o + lo, HALF), :]
                if o % 2 == 0
                else dzB[pl.ds(8 * (o - 1) + lo, HALF), :]
            )
            acc = acc + lax.dot_general(
                lhs,
                Wl[1, k, pl.ds(0, 3)].reshape(384, HALF),
                (((1,), (1,)), ((), ())),
                preferred_element_type=F32,
            )
        for half in range(2):
            m = mask(2 * part + half)[:, :, :128]
            for b in range(3):
                stg[b, pl.ds(part * HALF + half * 128, 128), :] = (
                    acc[128 * half : 128 * half + 128, 128 * b : 128 * b + 128].reshape(
                        16, 8, 128
                    )
                    * m
                ).reshape(128, 128)
        if part == 0:
            add_across(1, 6)
            add_core(0, 0, 13)
        if part == 1:
            add_across(1, 7)
            add_core(0, 1, 13)
        if part == 2:
            finish_sum(1, 0)
            add_core(0, 2, 13)
            add_across(0, 0, 13)
        if part == 3:
            finish_sum(1, 1)
            add_core(0, 3, 13)
            add_across(0, 1, 13)

    def put_own(i, b, v):
        lanes = pl.ds(128 * b, 128)
        own_w[1, i, :, lanes] = own_w[1, i, :, lanes] + v

    def put_send(i, b, v):
        snd_w[2, i, :, pl.ds(128 * b, 128)] = v.astype(BF)

    unstage(3, put_own, put_send)
    remote(snd_w.at[2], rcv_w.at[2], sn_s.at[6], sn_r.at[6], partner)
    add_core(0, 4, 13)
    add_across(0, 2, 13)
    wait_assembled(32)
    assemble(1, put_rest(1))
    add_core(0, 5, 13)
    add_across(0, 3, 13)
    mixers_five()
    add_core(0, 6, 13)
    add_across(0, 4, 13)
    for j in range(2):
        wait_on(rcv_w.at[j], sn_r.at[4 + j])
    wait_on(rcv_w.at[2], sn_r.at[6])
    for j in range(2):
        v = own_w[j] + rcv_w[j].astype(F32)
        if j == 1:
            v = v + rcv_w[2].astype(F32)
        own_w[j] = v
    copy_in(own_w, gw_out, out_s.at[5])
    add_core(0, 7, 13)
    add_across(0, 5, 13)
    add_across(0, 6, 13)
    finish_sum(0, 0, 13)
    add_across(0, 7, 13)
    finish_sum(0, 1, 13)
    wait_on(ngx, ng_r)
    wait_assembled(32)
    assemble(0, lambda b: gf_out.at[:, pl.ds(128 * b, 128)], 13)

    fst[t] = ss[...]

    def tell(d, _):
        remote(fst.at[t], fst.at[t], st_s.at[5], st_r.at[5], (lax.rem(t + d, 16), x))
        return 0

    lax.fori_loop(1, 16, tell, 0)
    mine, theirs = ngr[...], ngx[...]
    left = jnp.where(x == 0, mine, theirs)
    right = jnp.where(x == 0, theirs, mine)
    rows = lax.broadcasted_iota(jnp.int32, (10, 8, HALF), 1)
    left = jnp.where(rows < 2, left, 0.0)
    right = jnp.where(rows < 2, right, 0.0)
    ng_out[0] = left
    ng_out[1] = right
    norms = jnp.sum(left * left + right * right)
    wait_on(fst.at[pl.ds(0, 15)], st_r.at[5])
    every = lax.fori_loop(0, 16, lambda s, a: a + fst[s], jnp.zeros((8, 128), F32))
    total_out[...] = jnp.zeros((8, 128), F32) + (jnp.sum(every) + norms)

    wait_assembled(24)
    wait_on(mix_own.at[0], out_s.at[0])
    wait_on(mix_rcv, out_s.at[4])
    wait_on(own_n, out_s.at[3])
    wait_on(own_w, out_s.at[5])
    wait_on(gsm.at[:, pl.ds(0, 48)], out_s.at[1])
    wait_on(gsm.at[:, pl.ds(0, 48)], out_s.at[2])
    for j in range(4):
        wait_on(px.at[0, pl.ds(0, 256)], px_s.at[j])
    wait_on(mix_own.at[1], sn_s.at[0])
    for j in range(3):
        wait_on(snd_n.at[0], sn_s.at[1 + j])
        wait_on(snd_w.at[0], sn_s.at[4 + j])
    wait_on(cm, m_s.at[0])
    wait_on(ym, m_s.at[1])
    wait_on(zm, m_s.at[2])
    wait_on(fm, m_s.at[3])
    wait_on(ngr, ng_s)
    wait_on(fst.at[pl.ds(0, 15)], st_s.at[5])
    drain_sums(2)
    drain_sums(1)
    drain_sums(0, 13)

    for layer in range(2):
        wait_on(fin.at[0, pl.ds(0, 34 if layer else 26)], f_s.at[layer])
        halo_sent(layer)

    for layer in range(5):
        wait_on(bst.at[layer, pl.ds(0, 15), pl.ds(0, 8 if layer == 4 else 2)], st_s.at[layer])


def run_backward(lens, norm, rs, perm, w, wmn, wmw, h, xh, y, nar, wid, cot):
    vm = pl.BlockSpec(memory_space=pltpu.VMEM)
    hb = pl.BlockSpec(memory_space=pl.ANY)
    dma = pltpu.SemaphoreType.DMA
    S = jax.ShapeDtypeStruct
    V = pltpu.VMEM
    return pl.pallas_call(
        backward_kernel,
        out_shape=(
            S((4, 128, 512), BF),
            S((3, 4, 128, HALF), F32),
            S((2, 4, 128, 384), F32),
            S((408, 512), F32),
            S((4, 544, 512), F32),
            S((3, 16, 512), F32),
            S((2, 24, 512), F32),
            S((2, 10, 8, HALF), F32),
            S((8, 128), F32),
        ),
        in_specs=[vm, vm, vm, vm, hb, vm, vm, hb, hb, hb, hb, hb, hb],
        out_specs=[hb] * 7 + [vm, vm],
        scratch_shapes=[
            V((2, 17, 4, 2, 2, 32, HALF), BF),
            V((2, ROWS, HALF), BF),
            V((ROWS, HALF), F32),
            V((2, ROWS, HALF), F32),
            V((2, ROWS, HALF), BF),
            V((ROWS, HALF), F32),
            V((ROWS, HALF), F32),
            V((2, 1168, HALF), BF),
            V((1152, HALF), BF),
            V((3, 34, 4, 2, 2, 16, HALF), BF),
            V((2, 34, 4, 2, 16, HALF), BF),
            V((3, 34, 4, 16, HALF), BF),
            V((3, 3, 34, 16, HALF), BF),
            V((2, 34, 16, HALF), BF),
            V((5, 34, 16, HALF), BF),
            V((2, ROWS, HALF), BF),
            V((2, ROWS, HALF), BF),
            V((3, ROWS, 128), F32),
            V((3, 4, 128, HALF), F32),
            V((2, 4, 128, 384), F32),
            V((3, 4, 128, HALF), BF),
            V((3, 4, 128, 384), BF),
            V((3, 4, 128, HALF), BF),
            V((3, 4, 128, 384), BF),
            V((2, 4, 128, HALF), BF),
            V((4, 128, HALF), BF),
            V((4, 2, 2, 112, HALF), BF),
            V((4, 2, 112, HALF), BF),
            V((4, 112, HALF), BF),
            V((3, 112, HALF), BF),
            V((112, HALF), BF),
            V((112, HALF), BF),
            V((4, 544, 128), F32),
            V((4, 112, 128), F32),
            V((5, 16, 8, HALF), F32),
            V((8, HALF), F32),
            V((10, 8, HALF), F32),
            V((10, 8, HALF), F32),
            V((8, 128), F32),
            V((16, 8, 128), F32),
            dma((5,)),
            dma((2,)),
            dma((3,)),
            dma((5, 2)),
            dma((5, 2)),
            dma((6,)),
            dma((6,)),
            dma((5,)),
            dma((5, 4)),
            dma((5,)),
            dma((5, 8)),
            dma((5, 2)),
            dma((5, 2)),
            dma((5,)),
            dma((5, 2)),
            dma((4,)),
            dma((5, 4)),
            dma((4,)),
            dma((4,)),
            dma((7,)),
            dma((7,)),
            dma,
            dma((6,)),
            dma,
            dma,
        ],
        compiler_params=pltpu.CompilerParams(
            collective_id=1, has_side_effects=True, vmem_limit_bytes=63 << 20
        ),
        cost_estimate=pl.CostEstimate(flops=46 * 10**9, bytes_accessed=60 * 10**6, transcendentals=0),
    )(lens, norm, rs, perm, w, wmn, wmw, h, xh, y, nar, wid, cot)


def prepare(lengths, norm_params):
    x = lax.axis_index("batch")
    mine = jnp.broadcast_to(lengths.astype(F32)[:, None], (4, HALF))
    lens = jnp.zeros((8, HALF), F32)
    lens = lax.dynamic_update_slice(lens, mine, (4 * x, 0))
    half = lax.dynamic_slice(norm_params, (0, 0, x * HALF), (2, 10, HALF))
    norm = jnp.pad(jnp.transpose(half, (1, 0, 2)), ((0, 0), (0, 6), (0, 0)))
    places = np.arange(384)
    perm = np.zeros((384, 512), np.float32)
    perm[places, (places // 24) * 32 + places % 24] = 1.0
    return lens, norm, jnp.asarray(perm, BF)


def body_split(
    source_narrow,
    source_wide,
    lengths,
    cotangent,
    kernel_first,
    kernel_rest,
    mixer_narrow,
    mixer_wide,
    norm_params,
    moment_first,
    square_first,
    moment_rest,
    square_rest,
    moment_narrow,
    square_narrow,
    moment_wide,
    square_wide,
    moment_norm,
    square_norm,
):
    lens, norm, perm = prepare(lengths, norm_params)
    w, wmn, wmw, h, xh, y, nar, wid, cot, rs, lens = run_forward(
        lens,
        norm,
        perm,
        source_narrow,
        source_wide,
        cotangent,
        kernel_first,
        kernel_rest,
        mixer_narrow,
        mixer_wide,
    )
    mixed, gn, gw, gf, gr, gmn, gmw, ng, total = run_backward(
        lens, norm, rs, perm, w, wmn, wmw, h, xh, y, nar, wid, cot
    )
    grad_norm = jnp.sqrt(total[0, 0])
    clip = jnp.minimum(1.0, THRESHOLD / grad_norm)
    norm_grad = jnp.transpose(ng[:, :, :2, :], (2, 1, 0, 3)).reshape(2, 10, CO)
    results = []
    for p, g, m, v in (
        (kernel_first, gf, moment_first, square_first),
        (kernel_rest, gr, moment_rest, square_rest),
        (mixer_narrow, gmn, moment_narrow, square_narrow),
        (mixer_wide, gmw, moment_wide, square_wide),
    ):
        results += adamw(p, clip * g, m, v, RATE_WEIGHT, DECAY)
    results += adamw(norm_params, clip * norm_grad, moment_norm, square_norm, RATE_NORM, 0.0)
    return (mixed, gn, gw, grad_norm, *results)


def solution(mesh):
    in_specs = (
        P(None, "batch", "tm", None),
        P(None, "batch", "tm", None),
        P("batch"),
        P("batch", "tm", None),
        P("tm", None),
        P(None, "tm", None),
        P(None, "tm", None),
        P(None, "tm", None),
        P(),
        P("tm", None),
        P("tm", None),
        P(None, "tm", None),
        P(None, "tm", None),
        P(None, "tm", None),
        P(None, "tm", None),
        P(None, "tm", None),
        P(None, "tm", None),
        P(),
        P(),
    )
    out_specs = (
        P("batch", "tm", None),
        P(None, "batch", "tm", None),
        P(None, "batch", "tm", None),
        P(),
        P("tm", None),
        P("tm", None),
        P("tm", None),
        P(None, "tm", None),
        P(None, "tm", None),
        P(None, "tm", None),
        P(None, "tm", None),
        P(None, "tm", None),
        P(None, "tm", None),
        P(None, "tm", None),
        P(None, "tm", None),
        P(None, "tm", None),
        P(),
        P(),
        P(),
    )
    fits = mesh.shape["tm"] == 16 and mesh.shape["batch"] == 2
    chosen = body_split if fits else body
    return jax.shard_map(chosen, mesh=mesh, in_specs=in_specs, out_specs=out_specs, check_vma=False)
```

```python
import numpy as np
import jax
import jax.numpy as jnp
from jax import lax
from jax.experimental import pallas as pl
from jax.experimental.pallas import tpu as pltpu
from jax.sharding import PartitionSpec as P

CO = 512
CW = 384
K = 17
STEP = 10


EPS = 1e-05
THRESHOLD = 100.0
BETA_ONE = 0.9
SECOND_DECAY = 0.999
ADAM_EPS = 1e-08
RATE_WEIGHT = 0.02
RATE_NORM = 0.4
DECAY = 0.01


def padded_2(shard, sides, width):
    for axis, dim in sides:
        devices, length = (lax.axis_size(axis), shard.shape[dim])
        up = [(i, (i + 1) % devices) for i in range(devices - 1)]
        down = [(j, i) for i, j in up]
        last = lax.slice_in_dim(shard, length - width, length, axis=dim)
        initial = lax.slice_in_dim(shard, 0, width, axis=dim)
        before = lax.ppermute(last, axis, up)
        after = lax.ppermute(initial, axis, down)
        shard = jnp.concatenate([before, shard, after], axis=dim)
    return shard


def adamw(param, grad, first, second, rate, decay):
    first_new = BETA_ONE * first + (1.0 - BETA_ONE) * grad
    second_new = SECOND_DECAY * second + (1.0 - SECOND_DECAY) * grad * grad
    fix_one = 1.0 - BETA_ONE**STEP
    fix_two = 1.0 - SECOND_DECAY**STEP
    update = first_new / fix_one / (jnp.sqrt(second_new / fix_two) + ADAM_EPS)
    return (param - rate * (update + decay * param), first_new, second_new)


def body(
    source_narrow,
    source_wide,
    lengths,
    cotangent,
    kernel_first,
    kernel_rest,
    mixer_narrow,
    mixer_wide,
    norm_params,
    moment_first,
    square_first,
    moment_rest,
    square_rest,
    moment_narrow,
    square_narrow,
    moment_wide,
    square_wide,
    moment_norm,
    square_norm,
):
    frames = source_wide.shape[2]
    half = K // 2
    places = lax.axis_index("tm") * frames + jnp.arange(frames, dtype=jnp.int32)
    valid = (places[None, :] < lengths[:, None]).astype(jnp.float32)[:, :, None]
    local_count = jnp.sum(valid)
    valid_low = valid.astype(jnp.bfloat16)
    narrow = source_narrow * valid_low[None]
    wide = source_wide * valid_low[None]
    full_first, full_rest, full_narrow, full_wide = (
        lax.all_gather(kernel_first.astype(jnp.bfloat16), "tm", axis=0, tiled=True),
        lax.all_gather(kernel_rest.astype(jnp.bfloat16), "tm", axis=1, tiled=True),
        lax.all_gather(mixer_narrow.astype(jnp.bfloat16), "tm", axis=1, tiled=True),
        lax.all_gather(mixer_wide.astype(jnp.bfloat16), "tm", axis=1, tiled=True),
    )
    kernels = [jnp.transpose(full_first.reshape(CW, K, CO), (1, 0, 2))] + [
        jnp.transpose(full_rest[layer].reshape(CO, K, CO), (1, 0, 2)) for layer in range(4)
    ]
    gains = norm_params[0]
    biases = norm_params[1]

    def batch_statistics(values, count):
        sums = tuple((jnp.sum(value * valid, axis=(0, 1)) for value in values))
        extra = (local_count,) if count is None else ()
        got = lax.psum(sums + extra, ("tm", "batch"))
        if count is None:
            count = got[-1]
        means = [total / count for total in got[: len(values)]]
        spreads = tuple(
            (
                jnp.sum(jnp.square((value - mean) * valid), axis=(0, 1))
                for value, mean in zip(values, means)
            )
        )
        second = lax.psum(spreads, ("tm", "batch"))
        variances = [total / count for total in second]
        scales = [lax.rsqrt(variance + EPS) for variance in variances]
        return (means, scales, count)

    signal = wide[1]
    kept = []
    count = None
    for index in range(5):
        padded = padded_2(signal, (("tm", 1),), half)
        field = jnp.zeros(signal.shape[:2] + (CO,), jnp.float32)
        for tap in range(K):
            field = field + jnp.einsum(
                "btc,cd->btd",
                padded[:, tap : tap + frames],
                kernels[index][tap],
                preferred_element_type=jnp.float32,
            )
        values = [field]
        indices = [index]
        if index == 4:
            for source in range(3):
                values.append(
                    jnp.einsum(
                        "btc,cd->btd",
                        narrow[source],
                        full_narrow[source],
                        preferred_element_type=jnp.float32,
                    )
                )
                indices.append(5 + source)
            for source in range(2):
                values.append(
                    jnp.einsum(
                        "btc,cd->btd",
                        wide[source],
                        full_wide[source],
                        preferred_element_type=jnp.float32,
                    )
                )
                indices.append(8 + source)
        means, scales, count = batch_statistics(values, count)
        normalized_values = [
            (value - mean) * scale for value, mean, scale in zip(values, means, scales)
        ]
        summed = jnp.zeros_like(field)
        for place in range(len(values)):
            summed = (
                summed + gains[indices[place]] * normalized_values[place] + biases[indices[place]]
            )
        kept.append((padded, normalized_values, scales, summed, indices))
        active = jax.nn.silu(summed) * valid
        signal = active.astype(jnp.bfloat16)
    grad_active = cotangent.astype(jnp.float32)
    kernel_grads = [None] * 5
    gain_grads = [None] * 10
    bias_grads = [None] * 10
    narrow_grads = []
    wide_grads = []
    narrow_inputs = []
    wide_inputs = []
    first_input = None
    for index in reversed(range(5)):
        padded, normalized_values, scales, summed, indices = kept[index]
        sigma = jax.nn.sigmoid(summed)
        gradient_total = grad_active * valid * sigma * (1.0 + summed * (1.0 - sigma))
        local_sums = (jnp.sum(gradient_total, axis=(0, 1)),) + tuple(
            (
                jnp.sum(gradient_total * standardized_input, axis=(0, 1))
                for standardized_input in normalized_values
            )
        )
        got = lax.psum(local_sums, ("tm", "batch"))
        bias_total = got[0]
        field_grads = []
        for place in range(len(normalized_values)):
            which = indices[place]
            gain = gains[which]
            gain_grads[which] = got[1 + place]
            bias_grads[which] = bias_total
            grad_field = scales[place] * (
                gain * gradient_total
                - valid * (gain * bias_total) / count
                - valid * normalized_values[place] * (gain * got[1 + place]) / count
            )
            field_grads.append(grad_field.astype(jnp.bfloat16))
        grad_conv = field_grads[0]
        tap_grads = [
            jnp.einsum(
                "btc,btd->cd",
                padded[:, tap : tap + frames],
                grad_conv,
                preferred_element_type=jnp.float32,
            )
            for tap in range(K)
        ]
        kernel_grads[index] = jnp.stack(tap_grads, axis=1).reshape(padded.shape[2] * K, CO)
        if index == 4:
            for source in range(3):
                branch = field_grads[1 + source]
                narrow_grads.append(
                    jnp.einsum(
                        "btc,btd->cd", narrow[source], branch, preferred_element_type=jnp.float32
                    )
                )
                narrow_inputs.append(
                    jnp.einsum(
                        "btd,cd->btc",
                        branch,
                        full_narrow[source],
                        preferred_element_type=jnp.float32,
                    )
                    * valid
                )
            for source in range(2):
                branch = field_grads[4 + source]
                wide_grads.append(
                    jnp.einsum(
                        "btc,btd->cd", wide[source], branch, preferred_element_type=jnp.float32
                    )
                )
                wide_inputs.append(
                    jnp.einsum(
                        "btd,cd->btc", branch, full_wide[source], preferred_element_type=jnp.float32
                    )
                    * valid
                )
        grad_padded = padded_2(grad_conv, (("tm", 1),), half)
        incoming = jnp.zeros(padded.shape[:1] + (frames, padded.shape[2]), jnp.float32)
        for tap in range(K):
            start = K - 1 - tap
            incoming = incoming + jnp.einsum(
                "btd,cd->btc",
                grad_padded[:, start : start + frames],
                kernels[index][tap],
                preferred_element_type=jnp.float32,
            )
        if index > 0:
            grad_active = incoming
        else:
            first_input = incoming
    grad_narrow = jnp.stack(narrow_inputs)
    source_wide_gradient = jnp.stack([wide_inputs[0], (first_input + wide_inputs[1]) * valid])
    shard_gradients = (
        kernel_grads[0],
        jnp.stack(kernel_grads[1:]),
        jnp.stack(narrow_grads),
        jnp.stack(wide_grads),
    )
    shards = (
        lax.psum_scatter(shard_gradients[0], "tm", scatter_dimension=0, tiled=True),
        lax.psum_scatter(shard_gradients[1], "tm", scatter_dimension=1, tiled=True),
        lax.psum_scatter(shard_gradients[2], "tm", scatter_dimension=1, tiled=True),
        lax.psum_scatter(shard_gradients[3], "tm", scatter_dimension=1, tiled=True),
    )
    norm_grad = jnp.stack([jnp.stack(gain_grads), jnp.stack(bias_grads)])
    params = (kernel_first, kernel_rest, mixer_narrow, mixer_wide)
    firsts = (moment_first, moment_rest, moment_narrow, moment_wide)
    seconds = (square_first, square_rest, square_narrow, square_wide)
    results = []
    shards = (
        lax.psum(shards[0].astype(jnp.bfloat16), "batch").astype(jnp.float32),
        lax.psum(shards[1].astype(jnp.bfloat16), "batch").astype(jnp.float32),
        lax.psum(shards[2].astype(jnp.bfloat16), "batch").astype(jnp.float32),
        lax.psum(shards[3].astype(jnp.bfloat16), "batch").astype(jnp.float32),
    )
    local_square = jnp.zeros((), jnp.float32)
    for shard in shards:
        local_square = local_square + jnp.sum(shard * shard)
    total = lax.psum(local_square, "tm") + jnp.sum(norm_grad * norm_grad)
    grad_norm = jnp.sqrt(total)
    clip = jnp.minimum(1.0, THRESHOLD / grad_norm)
    for slot in range(4):
        results.append(
            adamw(
                params[slot], clip * shards[slot], firsts[slot], seconds[slot], RATE_WEIGHT, DECAY
            )
        )
    results.append(adamw(norm_params, clip * norm_grad, moment_norm, square_norm, RATE_NORM, 0.0))
    return (
        signal,
        grad_narrow,
        source_wide_gradient,
        grad_norm,
        results[0][0],
        results[0][1],
        results[0][2],
        results[1][0],
        results[1][1],
        results[1][2],
        results[2][0],
        results[2][1],
        results[2][2],
        results[3][0],
        results[3][1],
        results[3][2],
        results[4][0],
        results[4][1],
        results[4][2],
    )


BF = jnp.bfloat16
F32 = jnp.float32
MESH = pl.DeviceIdType.MESH
ROWS = 1024
HALO = 64
HALF = 256
GROUPS = 34
LEAD = 10
AHEAD = 3
LAG = AHEAD + 2


def wait_on(ref, sem):
    pltpu.make_async_copy(ref, ref, sem).wait()


def remote(src, dst, send, recv, device):
    pltpu.make_async_remote_copy(
        src_ref=src,
        dst_ref=dst,
        send_sem=send,
        recv_sem=recv,
        device_id=device,
        device_id_type=MESH,
    ).start()


def position():
    x = lax.axis_index("batch")
    t = lax.axis_index("tm")
    return x, t, lax.div(t, 4), lax.rem(lax.div(t, 2), 2), lax.rem(t, 2)


def greet(x, t):
    barrier = pltpu.get_barrier_semaphore()

    def one(d, _):
        pl.semaphore_signal(
            barrier, inc=1, device_id=(lax.rem(t + d, 16), x), device_id_type=MESH
        )
        return 0

    lax.fori_loop(1, 16, one, 0)
    for d in (0, 1, 2, 14, 15):
        pl.semaphore_signal(
            barrier, inc=1, device_id=(lax.rem(t + d, 16), 1 - x), device_id_type=MESH
        )
    pl.semaphore_wait(barrier, 20)


def frame_mask(block, t, lens):
    frames = lax.broadcasted_iota(jnp.int32, (16, 8, HALF), 0) + (block * 16 + t * 128)
    return (frames.astype(F32) < lens[None]).astype(F32)


def share(box, part, at, rows, sems):
    x, t, zi, yi, ci = position()
    chip = lax.div(t, 2)
    to_first, to_peer, to_second, first, peer, second = sems
    used = pl.ds(0, rows)

    @pl.when(ci == 1)
    def _():
        remote(
            part.at[at, used],
            box.at[at, chip, 1, used],
            to_first.at[at],
            first.at[at],
            (t - 1, x),
        )

    @pl.when(ci == 0)
    def _():
        box[at, chip, 0] = part[at]
        wait_on(box.at[at, chip, 1, used], first.at[at])
        mine = box.at[at, chip, :, used]

        def one(d, _):
            remote(mine, mine, to_peer.at[at], peer.at[at], (lax.rem(t + 2 * d, 16), x))
            return 0

        lax.fori_loop(1, 8, one, 0)


def shared(box, at, rows, sems):
    x, t, zi, yi, ci = position()
    to_first, to_peer, to_second, first, peer, second = sems
    used = pl.ds(0, rows)

    @pl.when(ci == 0)
    def _():
        wait_on(box.at[at, pl.ds(0, 7), :, used], peer.at[at])
        every = box.at[at, :, :, used]
        remote(every, every, to_second.at[at], second.at[at], (t + 1, x))

    @pl.when(ci == 1)
    def _():
        wait_on(box.at[at, :, :, used], second.at[at])


def share_drained(box, part, at, rows, sems):
    ci = position()[4]
    to_first, to_peer, to_second, first, peer, second = sems
    used = pl.ds(0, rows)

    @pl.when(ci == 1)
    def _():
        wait_on(part.at[at, used], to_first.at[at])

    @pl.when(ci == 0)
    def _():
        wait_on(box.at[at, pl.ds(0, 7), :, used], to_peer.at[at])
        wait_on(box.at[at, :, :, used], to_second.at[at])


def forward_kernel(
    lens_in,
    norm,
    perm,
    src_n,
    src_w,
    cot,
    kf,
    kr,
    mn,
    mw,
    w_out,
    wmn_out,
    wmw_out,
    h_out,
    xh_out,
    y_out,
    nar_out,
    wid_out,
    cot_out,
    rs_out,
    len_out,
    W,
    G,
    wmn,
    wmw,
    hA,
    hB,
    z,
    zb,
    xhb,
    y5,
    stg,
    pf,
    pmn,
    pmw,
    raww,
    rawn,
    rawc,
    nar,
    wid,
    cotv,
    st,
    sp,
    rel,
    nv,
    lenr,
    lens,
    load_s,
    dl_s,
    dl_r,
    ag_s,
    rz,
    rf,
    ry,
    rc,
    m_s,
    m_r,
    x_s,
    x_r,
    xr_s,
    xr_r,
    halo_s,
    halo_r,
    rel_s,
    rel_r,
    st_a,
    st_b,
    st_c,
    st_d,
    st_e,
    st_f,
    out_s,
):
    x, t, zi, yi, ci = position()
    cols = pl.ds(pl.multiple_of(x * HALF, HALF), HALF)
    partner = (t, 1 - x)
    sibling = (t + 1 - 2 * ci, x)
    across = (zi * 4 + (1 - yi) * 2 + ci, x)
    sems = (st_a, st_b, st_c, st_d, st_e, st_f)

    lanes = [pl.ds(pl.multiple_of(x * HALF + 128 * b, 128), 128) for b in range(2)]
    loads = [(kf.at[:, lanes[b]], pf.at[0, b, pl.ds(0, 408)]) for b in range(2)]
    loads += [(kr.at[i, :, lanes[b]], pf.at[1 + i, b]) for i in range(4) for b in range(2)]
    loads += [
        (mn.at[:, :, cols], pmn),
        (mw.at[:, :, cols], pmw),
        (src_w, raww.at[x]),
        (src_n, rawn.at[x]),
        (cot.at[:, :, cols], rawc.at[x]),
    ]
    copies = [pltpu.make_async_copy(a, b, load_s.at[i]) for i, (a, b) in enumerate(loads)]
    for copy in copies:
        copy.start()
    hA[:, :, pl.ds(1152, 16), :] = jnp.zeros((5, 2, 16, HALF), BF)

    @pl.when(t == 0)
    def _():
        hA[:, :, pl.ds(0, HALO), :] = jnp.zeros((5, 2, HALO, HALF), BF)

    @pl.when(t == 15)
    def _():
        hA[:, :, pl.ds(1088, HALO), :] = jnp.zeros((5, 2, HALO, HALF), BF)

    st[...] = jnp.zeros((7, 8, 2, 8, HALF), F32)
    sp[...] = jnp.zeros((7, 8, HALF), F32)
    lenr[0] = lens_in[...]
    greet(x, t)

    other = pl.ds(pl.multiple_of((1 - x) * HALF, HALF), HALF)
    remote(lenr.at[0], lenr.at[1], xr_s.at[0], xr_r.at[0], partner)
    remote(src_w.at[1], raww.at[x, 1], xr_s.at[1], xr_r.at[1], partner)

    def prep(layer, count):
        for k in range(17):
            for b in range(2):
                v = pf[layer, b, pl.ds(k, count, stride=17), :]
                if count < 32:
                    v = jnp.concatenate([v, jnp.zeros((32 - count, 128), F32)], axis=0)
                W[17 * layer + k, zi, yi, ci, :, pl.ds(128 * b, 128)] = v.astype(BF)

    def taps(g):
        return pl.ds(5 * lax.div(g, 2), 5)

    def part(g):
        return pl.ds(pl.multiple_of(16 * lax.rem(g, 2), 16), 16)

    def first_sends(pair, send, into_z):
        for dz in (1, 2, 3):
            remote(pair, pair, send, into_z, (lax.rem(zi + dz, 4) * 4 + yi * 2 + 1, x))

    def pass_z(block, send_y, send_c, into_y, into_c):
        line = block(slice(None), yi, slice(None))
        remote(line, line, send_y, into_y, across)
        line = block(slice(None), yi, 1)
        remote(line, line, send_c, into_c, sibling)
        for dz in (1, 2, 3):
            one = block(lax.rem(zi + dz, 4), yi, 0)
            remote(one, one, send_c, into_c, sibling)

    def pass_y(block, send_c, into_c):
        line = block(slice(None), 1 - yi, slice(None))
        remote(line, line, send_c, into_c, sibling)

    def chunk(g):
        return lambda zs, ys, cs: W.at[taps(g), zs, ys, cs, part(g)]

    def mixers(zs, ys, cs):
        return G.at[zs, ys, cs]

    ALL = slice(None)
    THREE = pl.ds(0, 3)

    inner = (zi == 1) | (zi == 2)
    far = jnp.where(zi == 1, 3, 0)

    def own_step(g):
        pair = chunk(g)(zi, yi, ALL)

        def to(zz, sems):
            remote(pair, pair, ag_s.at[g, 0], sems.at[g], (zz * 4 + yi * 2 + 1, x))

        @pl.when((ci == 1) & (g < GROUPS) & inner)
        def _():
            to(3 - zi, rz)
            to(jnp.where(zi == 1, 0, 3), rz)
            to(jnp.where(zi == 1, 3, 0), rz)

        @pl.when((ci == 1) & (g < GROUPS) & (zi == 0))
        def _():
            to(1, rz)
            to(2, rf)

        @pl.when((ci == 1) & (g < GROUPS) & (zi == 3))
        def _():
            to(2, rz)
            to(1, rf)

    def far_step(g):
        @pl.when((ci == 1) & (g < GROUPS) & inner)
        def _():
            pair = chunk(g)(far, yi, ALL)
            wait_on(pair, rf.at[g])
            remote(pair, pair, ag_s.at[g, 0], rz.at[g], ((3 - far) * 4 + yi * 2 + 1, x))

    def y_step(h):
        @pl.when((ci == 1) & (h >= 0) & (h < GROUPS))
        def _():
            wait_on(chunk(h)(ALL, 0, ALL), ry.at[h])
            pass_y(chunk(h), ag_s.at[h, 2], rc.at[h])

    def service(g, start):
        own_step(g + LEAD)
        far_step(g + 2)

        @pl.when((ci == 1) & (g < GROUPS) & inner)
        def _():
            wait_on(chunk(g)(pl.ds(0, 2), 0, ALL), rz.at[g])

        @pl.when((ci == 1) & (g < GROUPS) & jnp.logical_not(inner))
        def _():
            wait_on(chunk(g)(THREE, 0, ALL), rz.at[g])

        @pl.when((ci == 1) & (g < GROUPS))
        def _():
            pass_z(chunk(g), ag_s.at[g, 1], ag_s.at[g, 2], ry.at[g], rc.at[g])

        @pl.when(g - LAG >= start)
        def _():
            y_step(g - LAG)

        @pl.when((ci == 1) & (g == 8))
        def _():
            wait_on(mixers(THREE, 0, ALL), m_r.at[0])
            pass_z(mixers, m_s.at[1], m_s.at[2], m_r.at[1], m_r.at[2])

        @pl.when((ci == 1) & (g == 11))
        def _():
            wait_on(mixers(ALL, 0, ALL), m_r.at[1])
            pass_y(mixers, m_s.at[2], m_r.at[2])

    def mixers_arrived():
        @pl.when(ci == 0)
        def _():
            wait_on(W.at[pl.ds(0, 35), THREE, 0, 0, pl.ds(0, 16)], m_r.at[2])

        for s in range(16):
            got = G.at[s // 4, s // 2 % 2, s % 2]
            for j in range(3):
                wmn[j, pl.ds(16 * s, 16), :] = got[pl.ds(16 * j, 16), :]
            for j in range(2):
                wmw[j, pl.ds(32 * s, 32), :] = got[pl.ds(48 + 32 * j, 32), :]

    FIFTEEN = W.at[pl.ds(0, 75), 0, 0, 0, pl.ds(0, 16)]

    def weights_arrived(layer):
        def one(h, _):
            wait_on(FIFTEEN, rc.at[h])
            return 0

        for d in range(2):
            y_step(2 * lax.div(17 * layer + 16, 5) + d)

        @pl.when(ci == 0)
        def _():
            lo = jnp.where(layer == 0, 0, 2 * lax.div(17 * layer - 1, 5) + 2)
            lax.fori_loop(lo, 2 * lax.div(17 * layer + 16, 5) + 2, one, 0)

    def lend(layer):
        own = W.at[pl.ds(17 * layer, 17), zi, yi, 0]

        @pl.when(ci == 0)
        def _():
            remote(own, own, dl_s.at[layer], dl_r.at[layer], sibling)

    def lent(layer):
        @pl.when(ci == 1)
        def _():
            wait_on(W.at[pl.ds(0, 17), zi, yi, 0], dl_r.at[layer])

    def serve(first, last):
        def one(g, _):
            service(g, 0)
            return 0

        lax.fori_loop(first, last, one, 0)

    for copy in copies[:2]:
        copy.wait()
    prep(0, 24)
    lend(0)
    for copy in copies[2:12]:
        copy.wait()
    for layer in (1, 2, 3, 4):
        prep(layer, 32)
        lend(layer)
    for j in range(3):
        G[zi, yi, ci, pl.ds(16 * j, 16), :] = pmn[j].astype(BF)
    for j in range(2):
        G[zi, yi, ci, pl.ds(48 + 32 * j, 32), :] = jnp.concatenate(
            [pmw[j], jnp.zeros((8, HALF), F32)], axis=0
        ).astype(BF)

    @pl.when(ci == 0)
    def _():
        remote(G.at[zi, yi, 0], G.at[zi, yi, 0], dl_s.at[5], dl_r.at[5], sibling)

    for layer in range(5):
        lent(layer)

    @pl.when(ci == 1)
    def _():
        wait_on(G.at[zi, yi, 0], dl_r.at[5])


    def own_one(g, _):
        own_step(g)
        return 0

    lax.fori_loop(0, LEAD, own_one, 0)
    far_step(jnp.int32(0))
    far_step(jnp.int32(1))

    @pl.when(ci == 1)
    def _():
        first_sends(mixers(zi, yi, ALL), m_s.at[0], m_r.at[0])

    serve(0, 2)

    wait_on(lenr.at[1], xr_r.at[0])
    lens[...] = lenr[0] + lenr[1]
    len_out[...] = lens[...]
    for s in range(16):
        nv[s] = jnp.broadcast_to(
            jnp.sum(jnp.clip(lens[...] - 128.0 * s, 0.0, 128.0), axis=0, keepdims=True), (8, HALF)
        )

    def spread_wide(j):
        for s in range(8):
            v = jnp.dot(raww[s // 4, j, s % 4], perm[...], preferred_element_type=F32)
            for b in range(4):
                stg[b, pl.ds(s, 128, stride=8), :] = v[:, 128 * b : 128 * b + 128]

    def spread_half(v, s):
        for b in range(2):
            stg[b, pl.ds(s, 128, stride=8), :] = v[:, 128 * b : 128 * b + 128].astype(F32)

    def masked_block(b, h):
        rows = pl.ds(pl.multiple_of(b * 128, 128), 128)
        v = jnp.concatenate([stg[2 * h, rows, :], stg[2 * h + 1, rows, :]], axis=1)
        v = v.reshape(16, 8, HALF)
        return (v * frame_mask(b, t, lens[...])).reshape(128, HALF).astype(BF)

    copies[12].wait()
    wait_on(raww.at[0, 1], xr_r.at[1])
    spread_wide(1)

    def first_block(b, _):
        for h in range(2):
            hA[0, h, pl.ds(pl.multiple_of(HALO + b * 128, 64), 128), :] = masked_block(b, h)
        return 0

    lax.fori_loop(0, 8, first_block, 0)

    EDGE = ((HALO, 1088), (1024, 0))

    def halo_out(layer, half, side, at):
        lo, to = EDGE[side]
        goal = hA.at[layer, half, pl.ds(to, HALO)]
        source = hA.at[layer, half, pl.ds(lo, HALO)]
        step = 2 * side - 1
        for other in at:
            remote(
                source,
                goal,
                halo_s.at[layer, side, half if len(at) == 1 else other],
                halo_r.at[layer, side, half],
                (t + step, 1 - x if other else x),
            )

    def halos_out(layer, half, at, relay):
        @pl.when(t > 0)
        def _():
            halo_out(layer, half, 0, at)

        @pl.when(ci == 0)
        def _():
            halo_out(layer, half, 1, at)

        @pl.when((ci == 1) & (t < 15))
        def _():
            remote(
                hA.at[layer, half, pl.ds(1024, HALO)],
                rel.at[relay],
                rel_s.at[relay, 0],
                rel_r.at[relay],
                sibling,
            )

        @pl.when((ci == 0) & (t < 14))
        def _():
            wait_on(rel.at[relay], rel_r.at[relay])
            goal = hA.at[layer, half, pl.ds(0, HALO)]
            for other in at:
                remote(
                    rel.at[relay],
                    goal,
                    rel_s.at[relay, other],
                    halo_r.at[layer, 1, half],
                    (t + 2, 1 - x if other else x),
                )

    def halos_sent(layer, half, at, relay):
        @pl.when(t > 0)
        def _():
            for other in at:
                wait_on(rel.at[0], halo_s.at[layer, 0, half if len(at) == 1 else other])

        @pl.when(ci == 0)
        def _():
            for other in at:
                wait_on(rel.at[0], halo_s.at[layer, 1, half if len(at) == 1 else other])

        @pl.when((ci == 1) & (t < 15))
        def _():
            wait_on(rel.at[0], rel_s.at[relay, 0])

        @pl.when((ci == 0) & (t < 14))
        def _():
            for other in at:
                wait_on(rel.at[0], rel_s.at[relay, other])

    def halo_wait(layer, half, sems, sides):
        for side, edge in sides:

            @pl.when(t != edge)
            def _():
                wait_on(hA.at[layer, half, pl.ds(0, HALO)], sems.at[layer, side, half])

    ARRIVE = ((1, 0), (0, 15))
    for h in range(2):
        halos_out(0, h, (0,), h)

    remote(src_n, rawn.at[x], xr_s.at[2], xr_r.at[2], partner)
    remote(src_w.at[0], raww.at[x, 0], xr_s.at[3], xr_r.at[3], partner)
    serve(2, 8 + AHEAD)

    def shift_copy(layer, half):
        def one(b, _):
            v = hA[layer, half, pl.ds(pl.multiple_of(b * 128, 128), 144), :].astype(F32)
            hB[half, pl.ds(pl.multiple_of(b * 128, 128), 128), :] = v[8:136].astype(BF)
            return 0

        lax.fori_loop(0, 9, one, 0)


    def rows_of(b):
        return pl.ds(pl.multiple_of(b * 128, 128), 128)

    def local_stats(ref):
        def total(b, acc):
            v = ref[rows_of(b), :].reshape(16, 8, HALF) * frame_mask(b, t, lens[...])
            return acc + jnp.sum(v, axis=0)

        s = jnp.sum(
            lax.fori_loop(0, 8, total, jnp.zeros((8, HALF), F32)), axis=0, keepdims=True
        )
        mean = s / jnp.maximum(nv[t, pl.ds(0, 1), :], 1.0)

        def spread(b, acc):
            v = (ref[rows_of(b), :].reshape(16, 8, HALF) - mean[None]) * frame_mask(
                b, t, lens[...]
            )
            return acc + jnp.sum(v * v, axis=0)

        m2 = jnp.sum(
            lax.fori_loop(0, 8, spread, jnp.zeros((8, HALF), F32)), axis=0, keepdims=True
        )
        return mean, m2

    def put_stats(ref, layer, field):
        mean, m2 = local_stats(ref)
        sp[layer, pl.ds(2 * field, 1), :] = mean
        sp[layer, pl.ds(2 * field + 1, 1), :] = m2

    def combine(at):
        zero = jnp.zeros((8, HALF), F32)
        count = lax.fori_loop(0, 16, lambda s, a: a + nv[s], zero)
        of = lambda s: st[at, lax.div(s, 2), lax.rem(s, 2)]
        mean = lax.fori_loop(0, 16, lambda s, a: a + nv[s] * of(s), zero) / count

        def gather_spread(s, a):
            v = of(s)
            d = v - mean
            return a[0] + nv[s] * d * d, a[1] + v

        between, inside = lax.fori_loop(0, 16, gather_spread, (zero, zero))

        def moments(field):
            m = mean[2 * field : 2 * field + 1]
            q = inside[2 * field + 1 : 2 * field + 2] + between[2 * field : 2 * field + 1]
            return m, lax.rsqrt(q / count[:1] + EPS)

        return moments

    def branch_fields(at, number, inputs):
        for j in range(number):
            total = None
            for lhs, rhs in inputs(j):
                v = jnp.dot(lhs, rhs, preferred_element_type=F32)
                total = v if total is None else total + v
            zb[j] = total
            put_stats(zb.at[j], at, j)
        share(st, sp, at, 8, sems)

    def branches(at, base, number):
        shared(st, at, 8, sems)
        shares = combine(at)
        for j in range(number):
            m, r = shares(j)
            field = base + j
            rs_out[field] = jnp.broadcast_to(r, (8, HALF))
            gain = norm[field, pl.ds(0, 1), :]
            bias = norm[field, pl.ds(1, 1), :]
            if j > 0:
                wait_on(xhb.at[1], out_s.at[10])

            def one(b, _):
                v = (zb[j, rows_of(b), :] - m) * r
                xhb[1, rows_of(b), :] = v
                y = gain * v + bias
                if field > 5:
                    y = y + y5[rows_of(b), :]
                y5[rows_of(b), :] = y
                return 0

            lax.fori_loop(0, 8, one, 0)
            pltpu.make_async_copy(xhb.at[1], xh_out.at[field], out_s.at[10]).start()
        wait_on(xhb.at[1], out_s.at[10])

    def spread_narrow(j):
        for s in range(8):
            spread_half(rawn[s // 4, j, s % 4], s)

        def one(b, _):
            nar[j, rows_of(b), :] = masked_block(b, 0)
            return 0

        lax.fori_loop(0, 8, one, 0)

    def beside_statistics(layer):
        @pl.when(layer == 0)
        def _():
            copies[13].wait()
            wait_on(rawn.at[0], xr_r.at[2])
            spread_narrow(0)

        @pl.when(layer == 1)
        def _():
            mixers_arrived()
            branch_fields(5, 3, lambda j: [(nar[j], wmn[j])])

        @pl.when(layer == 2)
        def _():
            branches(5, 5, 3)

        @pl.when(layer == 3)
        def _():
            wait_on(rawc.at[0], xr_r.at[4])
            for s in range(8):
                spread_half(rawc[s // 4, s % 4], s)

            def one(b, _):
                cotv[rows_of(b), :] = masked_block(b, 0)
                return 0

            lax.fori_loop(0, 8, one, 0)

        @pl.when(layer == 4)
        def _():
            branches(6, 8, 2)

    def beside_exchange(layer):
        @pl.when(layer == 0)
        def _():
            spread_narrow(1)
            spread_narrow(2)

        @pl.when(layer == 1)
        def _():
            wait_on(raww.at[0, 0], xr_r.at[3])
            spread_wide(0)

            def one(b, _):
                for h in range(2):
                    wid[h, rows_of(b), :] = masked_block(b, h)
                return 0

            lax.fori_loop(0, 8, one, 0)

        @pl.when(layer == 2)
        def _():
            copies[14].wait()
            remote(cot.at[:, :, other], rawc.at[x], xr_s.at[4], xr_r.at[4], partner)

            def inputs(j):
                for h in range(2):
                    lhs = wid[h] if j == 0 else hA[0, h, pl.ds(HALO, ROWS), :]
                    yield lhs, wmw[j, pl.ds(HALF * h, HALF), :]

            branch_fields(6, 2, inputs)

    def taps_of(layer, half, lo, rows):
        for k in range(17):
            lhs = (
                hA[layer, half, pl.ds(lo + 8 * k, rows), :]
                if k % 2 == 0
                else hB[half, pl.ds(lo + 8 * (k - 1), rows), :]
            )
            rhs = W[17 * layer + k, pl.ds(2 * half, 2)].reshape(HALF, HALF)
            yield jnp.dot(lhs, rhs, preferred_element_type=F32)

    PIECES = ((64, 320), (384, 256), (640, 256), (896, 192))

    def layer_step(layer, _):
        base = 8 + 6 * layer + 2 * (layer > 1).astype(jnp.int32)
        weights_arrived(layer)
        pltpu.make_async_copy(
            W.at[pl.ds(17 * layer, 17)], w_out.at[pl.ds(17 * layer, 17)], out_s.at[layer]
        ).start()

        halo_wait(layer, x, halo_r, ARRIVE)
        shift_copy(layer, x)
        for half in range(2):

            @pl.when(x == half)
            def _():
                acc = jnp.zeros((ROWS, HALF), F32)
                for v in taps_of(layer, half, 0, ROWS):
                    acc = acc + v
                z[...] = acc

        service(base + AHEAD, base)

        halo_wait(layer, 1 - x, halo_r, ARRIVE)
        for j, (lo, rows) in enumerate(PIECES):

            @pl.when(layer > 0)
            def _():
                wait_on(hA.at[layer, 1 - x, pl.ds(lo, rows)], x_r.at[layer, j])

            a = 0 if j == 0 else 256 * j + 112
            n = 368 if j == 0 else 256
            for half in range(2):

                @pl.when(x == 1 - half)
                def _():
                    v = hA[layer, half, pl.ds(a, n + 16), :].astype(F32)
                    hB[half, pl.ds(a, n), :] = v[8 : n + 8].astype(BF)
                    acc = z[pl.ds(256 * j, 256), :]
                    for v in taps_of(layer, half, 256 * j, 256):
                        acc = acc + v
                    z[pl.ds(256 * j, 256), :] = acc

            if j == 1:
                service(base + AHEAD + 1, base)

        pltpu.make_async_copy(
            hA.at[layer, :, pl.ds(HALO, ROWS)], h_out.at[layer], out_s.at[5 + layer]
        ).start()
        put_stats(z, layer, 0)
        share(st, sp, layer, 2, sems)
        service(base + AHEAD + 2, base)
        service(base + AHEAD + 3, base)
        beside_statistics(layer)
        shared(st, layer, 2, sems)
        moments = combine(layer)

        m, r = moments(0)
        rs_out[layer] = jnp.broadcast_to(r, (8, HALF))
        gain = norm[layer, pl.ds(0, 1), :]
        bias = norm[layer, pl.ds(1, 1), :]

        @pl.when(layer > 0)
        def _():
            wait_on(xhb.at[0], out_s.at[11])

        @pl.when(layer < 4)
        def _():
            def one(b, _):
                rows = pl.ds(pl.multiple_of(b * 64, 64), 64)
                v = (z[rows, :] - m) * r
                xhb[0, rows, :] = v
                y = gain * v + bias
                frames = lax.broadcasted_iota(jnp.int32, (8, 8, HALF), 0) + (b * 8 + t * 128)
                a = (y * jax.nn.sigmoid(y)).reshape(8, 8, HALF)
                a = jnp.where(frames.astype(F32) < lens[...][None], a, 0.0)
                hA[layer + 1, x, pl.ds(pl.multiple_of(HALO + b * 64, 64), 64), :] = a.reshape(
                    64, HALF
                ).astype(BF)
                return 0

            lax.fori_loop(0, 16, one, 0)
            halos_out(layer + 1, x, (0, 1), layer + 2)
            for j, (lo, rows) in enumerate(PIECES):
                ref = hA.at[layer + 1, x, pl.ds(lo, rows)]
                remote(ref, ref, x_s.at[layer + 1, j], x_r.at[layer + 1, j], partner)
        @pl.when(layer == 4)
        def _():
            def one(b, _):
                v = (z[rows_of(b), :] - m) * r
                xhb[0, rows_of(b), :] = v
                y5[rows_of(b), :] = y5[rows_of(b), :] + gain * v + bias
                return 0

            lax.fori_loop(0, 8, one, 0)

        pltpu.make_async_copy(xhb.at[0], xh_out.at[layer], out_s.at[11]).start()

        service(base + AHEAD + 4, base)

        beside_exchange(layer)
        service(base + AHEAD + 5, base)

        @pl.when(layer == 1)
        def _():
            service(base + AHEAD + 6, base)
            service(base + AHEAD + 7, base)

        return 0

    lax.fori_loop(0, 5, layer_step, 0)

    last = [
        (wmn, wmn_out),
        (wmw, wmw_out),
        (y5, y_out),
        (nar, nar_out),
        (wid, wid_out),
        (cotv, cot_out),
    ]
    for i, (a, b) in enumerate(last):
        pltpu.make_async_copy(a, b, out_s.at[12 + i]).start()
    for i, (a, b) in enumerate(last):
        wait_on(a, out_s.at[12 + i])
    wait_on(xhb.at[0], out_s.at[11])
    for i in range(5):
        wait_on(W.at[pl.ds(0, 17)], out_s.at[i])
        wait_on(hA.at[0, :, pl.ds(HALO, ROWS)], out_s.at[5 + i])

    @pl.when(ci == 1)
    def _():
        def drained(g, _):

            @pl.when(inner)
            def _():
                wait_on(chunk(0)(ALL, 0, ALL), ag_s.at[g, 0])

            @pl.when(jnp.logical_not(inner))
            def _():
                wait_on(chunk(0)(pl.ds(0, 2), 0, ALL), ag_s.at[g, 0])

            wait_on(chunk(0)(ALL, 0, ALL), ag_s.at[g, 1])
            wait_on(FIFTEEN, ag_s.at[g, 2])
            return 0

        lax.fori_loop(0, GROUPS, drained, 0)
        wait_on(mixers(THREE, 0, ALL), m_s.at[0])
        wait_on(mixers(ALL, 0, ALL), m_s.at[1])
        wait_on(W.at[pl.ds(0, 35), THREE, 0, 0, pl.ds(0, 16)], m_s.at[2])

    @pl.when(ci == 0)
    def _():
        for layer in range(5):
            wait_on(W.at[pl.ds(0, 17), zi, yi, 0], dl_s.at[layer])
        wait_on(G.at[zi, yi, 0], dl_s.at[5])

    wait_on(lenr.at[0], xr_s.at[0])
    wait_on(raww.at[0, 1], xr_s.at[1])
    wait_on(rawn.at[0], xr_s.at[2])
    wait_on(raww.at[0, 0], xr_s.at[3])
    wait_on(rawc.at[0], xr_s.at[4])

    for h in range(2):
        halos_sent(0, h, (0,), h)

    def finish(layer, _):
        halos_sent(layer, x, (0, 1), layer + 1)
        for j, (lo, rows) in enumerate(PIECES):
            wait_on(hA.at[0, 0, pl.ds(lo, rows)], x_s.at[layer, j])
        return 0

    lax.fori_loop(1, 5, finish, 0)
    for at in range(7):
        share_drained(st, sp, at, 2 if at < 5 else 8, sems)


def run_forward(lens, norm, perm, src_n, src_w, cot, kf, kr, mn, mw):
    vm = pl.BlockSpec(memory_space=pltpu.VMEM)
    hb = pl.BlockSpec(memory_space=pl.ANY)
    dma = pltpu.SemaphoreType.DMA
    S = jax.ShapeDtypeStruct
    return pl.pallas_call(
        forward_kernel,
        out_shape=(
            S((85, 4, 2, 2, 32, HALF), BF),
            S((3, HALF, HALF), BF),
            S((2, 512, HALF), BF),
            S((5, 2, ROWS, HALF), BF),
            S((10, ROWS, HALF), F32),
            S((ROWS, HALF), F32),
            S((3, ROWS, HALF), BF),
            S((2, ROWS, HALF), BF),
            S((ROWS, HALF), BF),
            S((10, 8, HALF), F32),
            S((8, HALF), F32),
        ),
        in_specs=[vm, vm, vm] + [hb] * 7,
        out_specs=[hb] * 9 + [vm, vm],
        scratch_shapes=[
            pltpu.VMEM((85, 4, 2, 2, 32, HALF), BF),
            pltpu.VMEM((4, 2, 2, 112, HALF), BF),
            pltpu.VMEM((3, HALF, HALF), BF),
            pltpu.VMEM((2, 512, HALF), BF),
            pltpu.VMEM((5, 2, 1168, HALF), BF),
            pltpu.VMEM((2, 1152, HALF), BF),
            pltpu.VMEM((ROWS, HALF), F32),
            pltpu.VMEM((3, ROWS, HALF), F32),
            pltpu.VMEM((2, ROWS, HALF), F32),
            pltpu.VMEM((ROWS, HALF), F32),
            pltpu.VMEM((4, ROWS, 128), F32),
            pltpu.VMEM((5, 2, 544, 128), F32),
            pltpu.VMEM((3, 16, HALF), F32),
            pltpu.VMEM((2, 24, HALF), F32),
            pltpu.VMEM((2, 2, 4, 128, 384), BF),
            pltpu.VMEM((2, 3, 4, 128, HALF), BF),
            pltpu.VMEM((2, 4, 128, HALF), BF),
            pltpu.VMEM((3, ROWS, HALF), BF),
            pltpu.VMEM((2, ROWS, HALF), BF),
            pltpu.VMEM((ROWS, HALF), BF),
            pltpu.VMEM((7, 8, 2, 8, HALF), F32),
            pltpu.VMEM((7, 8, HALF), F32),
            pltpu.VMEM((6, HALO, HALF), BF),
            pltpu.VMEM((16, 8, HALF), F32),
            pltpu.VMEM((2, 8, HALF), F32),
            pltpu.VMEM((8, HALF), F32),
            dma((15,)),
            dma((6,)),
            dma((6,)),
            dma((GROUPS, 3)),
            dma((GROUPS,)),
            dma((GROUPS,)),
            dma((GROUPS,)),
            dma((GROUPS,)),
            dma((3,)),
            dma((3,)),
            dma((5, 4)),
            dma((5, 4)),
            dma((5,)),
            dma((5,)),
            dma((5, 2, 2)),
            dma((5, 2, 2)),
            dma((6, 2)),
            dma((6,)),
            dma((7,)),
            dma((7,)),
            dma((7,)),
            dma((7,)),
            dma((7,)),
            dma((7,)),
            dma((18,)),
        ],
        compiler_params=pltpu.CompilerParams(
            collective_id=0, has_side_effects=True, vmem_limit_bytes=62 << 20
        ),
        cost_estimate=pl.CostEstimate(flops=24 * 10**9, bytes_accessed=60 * 10**6, transcendentals=0),
    )(lens, norm, perm, src_n, src_w, cot, kf, kr, mn, mw)


def share_all(box, at, rows, t, x, send, recv):
    mine = box.at[at, t, pl.ds(0, rows)]

    def one(d, _):
        remote(mine, mine, send, recv, (lax.rem(t + d, 16), x))
        return 0

    lax.fori_loop(1, 16, one, 0)


def backward_kernel(
    lens_in,
    norm,
    rs,
    perm,
    w_in,
    wmn,
    wmw,
    h_in,
    xh_in,
    y_in,
    nar_in,
    wid_in,
    cot_in,
    mixed_out,
    gn_out,
    gw_out,
    gf_out,
    gr_out,
    gmn_out,
    gmw_out,
    ng_out,
    total_out,
    Wl,
    Hl,
    Xl,
    xb,
    sb,
    y5,
    da,
    dzA,
    dzB,
    dW,
    crecv,
    yrecv,
    zrecv,
    fin,
    xrecv,
    px,
    pxr,
    stg,
    own_n,
    own_w,
    snd_n,
    snd_w,
    rcv_n,
    rcv_w,
    mix_own,
    mix_rcv,
    Dm,
    cm,
    ym,
    zm,
    fm,
    xm,
    gst,
    gsm,
    bst,
    sums4,
    ngr,
    ngx,
    ss,
    fst,
    load_s,
    w_s,
    br_s,
    halo_s,
    halo_r,
    st_s,
    st_r,
    c_s,
    c_r,
    y_s,
    y_r,
    z_s,
    z_r,
    f_s,
    f_r,
    px_s,
    px_r,
    m_s,
    m_r,
    sn_s,
    sn_r,
    g_s,
    out_s,
    ng_s,
    ng_r,
):
    x, t, zi, yi, ci = position()
    partner = (t, 1 - x)
    sibling = (t + 1 - 2 * ci, x)
    across = (zi * 4 + (1 - yi) * 2 + ci, x)
    lens = lens_in[...]

    def when(cond, f):
        if isinstance(cond, bool):
            if cond:
                f()
        else:
            pl.when(cond)(f)

    def rows_of(b):
        return pl.ds(pl.multiple_of(b * 128, 128), 128)

    def copy_in(src, dst, sem):
        pltpu.make_async_copy(src, dst, sem).start()

    def load_w(layer):
        b2 = lax.rem(layer, 2)
        copy_in(w_in.at[pl.ds(17 * layer, 17)], Wl.at[b2], w_s.at[b2])

    def load_h(layer):
        copy_in(h_in.at[layer], Hl, load_s.at[1])

    def load_x(layer):
        copy_in(xh_in.at[layer], Xl, load_s.at[2])

    copy_in(y_in, y5, load_s.at[3])
    copy_in(cot_in, sb.at[0], load_s.at[4])
    load_x(4)
    copy_in(xh_in.at[5], xb.at[1], br_s.at[1])
    load_w(4)
    load_h(4)

    for edge, lo in ((0, 0), (15, 1088)):

        @pl.when(t == edge)
        def _():
            dzA[:, pl.ds(lo, HALO), :] = jnp.zeros((2, HALO, HALF), BF)

    dzA[:, pl.ds(1152, 16), :] = jnp.zeros((2, 16, HALF), BF)
    bst[...] = jnp.zeros((5, 16, 8, HALF), F32)
    barrier = pltpu.get_barrier_semaphore()

    def greet_one(d, _):
        pl.semaphore_signal(
            barrier, inc=1, device_id=(lax.rem(t + d, 16), x), device_id_type=MESH
        )
        return 0

    lax.fori_loop(1, 16, greet_one, 0)
    pl.semaphore_signal(barrier, inc=1, device_id=partner, device_id_type=MESH)
    pl.semaphore_wait(barrier, 16)

    zero = jnp.zeros((8, HALF), F32)
    count = jnp.zeros((1, HALF), F32)
    for s in range(16):
        count = count + jnp.sum(jnp.clip(lens - 128.0 * s, 0.0, 128.0), axis=0, keepdims=True)

    def mask(b):
        return frame_mask(b, t, lens)

    def sequence(block, s):
        return stg[block, pl.ds(s, 128, stride=8), :]

    def unstage(blocks, own, send):
        for i in range(4):
            for b in range(blocks):
                own(i, b, sequence(b, 4 * x + i))
                send(i, b, sequence(b, 4 * (1 - x) + i))

    def mix_put(ref):
        def put(i, b, v):
            ref[i, :, pl.ds(128 * b, 128)] = v.astype(BF)

        return put

    my_cols = pl.ds(pl.multiple_of(x * HALF, HALF), HALF)
    other_cols = pl.ds(pl.multiple_of((1 - x) * HALF, HALF), HALF)

    def send_mixed():
        unstage(2, mix_put(mix_own.at[0]), mix_put(mix_own.at[1]))
        remote(mix_own.at[1], mix_rcv, sn_s.at[0], sn_r.at[0], partner)
        copy_in(mix_own.at[0], mixed_out.at[:, :, my_cols], out_s.at[0])

    ORDER = (0, 3, 1, 2)

    def send_core(layer, zs):
        b3, b2 = lax.rem(layer, 3), lax.rem(layer, 2)
        for zz in zs:
            remote(
                dW.at[b3, :, zz, :, 1 - ci],
                crecv.at[b2, :, zz],
                c_s.at[layer],
                c_r.at[layer, zz],
                sibling,
            )

    def add_core(layer, u, n=17):
        b3, b2 = lax.rem(layer, 3), lax.rem(layer, 2)
        zz, lo = ORDER[u // 2], n * (u % 2)
        if u % 2 == 0:
            wait_on(crecv.at[b2, :, zz], c_r.at[layer, zz])

        def one(k, _):
            for yy in range(2):
                dW[b3, k, zz, yy, ci] = (
                    dW[b3, k, zz, yy, ci].astype(F32) + crecv[b2, k, zz, yy].astype(F32)
                ).astype(BF)
            return 0

        lax.fori_loop(lo, lo + n, one, 0)
        remote(
            dW.at[b3, pl.ds(lo, n), zz, 1 - yi, ci],
            yrecv.at[b3, pl.ds(lo, n), zz],
            y_s.at[layer],
            y_r.at[layer, u],
            across,
        )

    def add_across(layer, u, n=17):
        b3 = lax.rem(layer, 3)
        zz, lo = ORDER[u // 2], n * (u % 2)
        wait_on(yrecv.at[b3, pl.ds(lo, n), zz], y_r.at[layer, u])

        def one(k, _):
            dW[b3, k, zz, yi, ci] = (
                dW[b3, k, zz, yi, ci].astype(F32) + yrecv[b3, k, zz].astype(F32)
            ).astype(BF)
            return 0

        lax.fori_loop(lo, lo + n, one, 0)

        @pl.when(zi != zz)
        def _():
            remote(
                dW.at[b3, pl.ds(lo, n), zz, yi, ci],
                zrecv.at[b3, lax.rem(zi + 3 - zz, 4), pl.ds(lo, n)],
                z_s.at[layer, u % 2],
                z_r.at[layer, u % 2],
                (zz * 4 + yi * 2 + ci, x),
            )

    def finish_sum(layer, half, n=17):
        b3, b2 = lax.rem(layer, 3), lax.rem(layer, 2)
        lo = n * half
        wait_on(zrecv.at[b3, :, pl.ds(lo, n)], z_r.at[layer, half])
        if half == 0:
            when(layer + 2 <= 4, lambda: wait_on(fin.at[0], f_s.at[layer + 2]))

        def one(k, _):
            v = dW[b3, k, zi, yi, ci].astype(F32)
            for q in range(3):
                v = v + zrecv[b3, q, k].astype(F32)
            fin[b2, k] = v.astype(BF)
            return 0

        lax.fori_loop(lo, lo + n, one, 0)
        mine = pl.ds(lo, n)
        remote(
            fin.at[b2, mine], xrecv.at[layer, mine], f_s.at[layer], f_r.at[layer, half], partner
        )

    def add_square(v):
        ss[...] += jnp.sum((v * v).reshape(-1, 8, 128), axis=0)

    def assemble(layer, put, n=17):
        b2 = lax.rem(layer, 2)
        rows = 32 if n == 17 else 24
        for half in range(2):
            wait_on(xrecv.at[layer, pl.ds(n * half, n)], f_r.at[layer, half])
        for source, side in ((fin.at[b2], x), (xrecv.at[layer], 1 - x)):
            for b in range(2):
                lanes = pl.ds(128 * b, 128)
                for k in range(17):
                    if n == 17:
                        v = source[pl.ds(2 * k, 2), :, lanes].astype(F32).reshape(32, 128)
                    else:
                        lo = 3 * (k // 2) + k % 2
                        v = source[pl.ds(lo, 2), :, lanes].astype(F32).reshape(32, 128)
                        v = v[8 * (k % 2) : 8 * (k % 2) + 24]
                    gst[2 * side + b, pl.ds(k, rows, stride=17), :] = v
        for b in range(4):
            add_square(gst[b, pl.ds(0, rows * 17), :])
            copy_in(gst.at[b, pl.ds(0, rows * 17)], put(b), g_s)

    def wait_assembled(rows):
        wait_on(gst.at[:, pl.ds(0, rows * 17)], g_s)

    def drain_sums(layer, n=17):
        wait_on(crecv.at[0], c_s.at[layer])
        wait_on(yrecv.at[0, pl.ds(0, 2 * n)], y_s.at[layer])
        for half in range(2):
            wait_on(zrecv.at[0, :, pl.ds(0, n)], z_s.at[layer, half])

    def put_rest(layer):
        return lambda b: gr_out.at[layer - 1, :, pl.ds(128 * b, 128)]

    def mixers_one():
        remote(Dm.at[:, :, 1 - ci], cm, m_s.at[0], m_r.at[0], sibling)

    def mixers_two():
        wait_on(cm, m_r.at[0])
        for zz in range(4):
            for yy in range(2):
                Dm[zz, yy, ci] = (Dm[zz, yy, ci].astype(F32) + cm[zz, yy].astype(F32)).astype(BF)
        remote(Dm.at[:, 1 - yi, ci], ym, m_s.at[1], m_r.at[1], across)

    def mixers_three():
        wait_on(ym, m_r.at[1])
        for zz in range(4):
            Dm[zz, yi, ci] = (Dm[zz, yi, ci].astype(F32) + ym[zz].astype(F32)).astype(BF)
        for q in range(3):
            zz = lax.rem(zi + 1 + q, 4)
            remote(Dm.at[zz, yi, ci], zm.at[q], m_s.at[2], m_r.at[2], (zz * 4 + yi * 2 + ci, x))

    def mixers_four():
        wait_on(zm, m_r.at[2])
        v = Dm[zi, yi, ci].astype(F32)
        for q in range(3):
            v = v + zm[q].astype(F32)
        fm[...] = v.astype(BF)
        remote(fm, xm, m_s.at[3], m_r.at[3], partner)

    def mixers_five():
        wait_on(xm, m_r.at[3])
        for b in range(2):
            lanes = pl.ds(128 * b, 128)
            gsm[2 * x + b] = fm[:, lanes].astype(F32)
            gsm[2 * (1 - x) + b] = xm[:, lanes].astype(F32)
        for b in range(4):
            add_square(gsm[b])
            for j in range(3):
                copy_in(
                    gsm.at[b, pl.ds(16 * j, 16)],
                    gmn_out.at[j, :, pl.ds(128 * b, 128)],
                    out_s.at[1],
                )
            for j in range(2):
                copy_in(
                    gsm.at[b, pl.ds(48 + 32 * j, 24)],
                    gmw_out.at[j, :, pl.ds(128 * b, 128)],
                    out_s.at[2],
                )

    def halo_sent(layer):
        for side, edge in ((0, 0), (1, 15)):

            @pl.when(t != edge)
            def _():
                wait_on(dzA.at[0, pl.ds(0, HALO)], halo_s.at[layer, side])

    def output_gradient(layer, last):
        wait_on(Xl, load_s.at[2])
        if last:
            wait_on(y5, load_s.at[3])
            wait_on(sb.at[0], load_s.at[4])
        gain = norm[layer, pl.ds(0, 1), :]
        bias = norm[layer, pl.ds(1, 1), :]

        def one(b, acc):
            xh = Xl[rows_of(b), :]
            if last:
                y = y5[rows_of(b), :]
                d = sb[0, rows_of(b), :].astype(F32)
            else:
                y = gain * xh + bias
                d = da[rows_of(b), :] + pxr[1 - lax.rem(layer, 2), rows_of(b), :].astype(F32)
            sg = jax.nn.sigmoid(y)
            m = mask(b)
            if last:
                a = ((y * sg).reshape(16, 8, HALF) * m).reshape(128, HALF)
                for i in range(2):
                    stg[i, rows_of(b), :] = a[:, 128 * i : 128 * i + 128]
            v = (d * sg * (1.0 + y * (1.0 - sg))).reshape(16, 8, HALF) * m
            s0 = acc[0] + jnp.sum(v, axis=0)
            s1 = acc[1] + jnp.sum(v * xh.reshape(16, 8, HALF), axis=0)
            v = v.reshape(128, HALF)
            da[rows_of(b), :] = v
            if last:
                y5[rows_of(b), :] = v
            return s0, s1

        if last:
            s0, s1 = lax.fori_loop(0, 8, one, (zero, zero))
        else:
            s0, s1 = zero, zero
            for j in range(4):
                wait_on(pxr.at[0, pl.ds(0, 256)], px_r.at[layer + 1, j])
                s0, s1 = lax.fori_loop(2 * j, 2 * j + 2, one, (s0, s1))
        bst[layer, t] = zero
        bst[layer, t, pl.ds(0, 1), :] = jnp.sum(s0, axis=0, keepdims=True)
        bst[layer, t, pl.ds(1, 1), :] = jnp.sum(s1, axis=0, keepdims=True)
        if last:
            for j in range(5):
                at = (j + 1) % 2
                wait_on(xb.at[at], br_s.at[at])
                if j < 4:
                    copy_in(xh_in.at[6 + j], xb.at[1 - at], br_s.at[1 - at])

                def branch(b, acc):
                    return acc + jnp.sum(
                        (da[rows_of(b), :] * xb[at, rows_of(b), :]).reshape(16, 8, HALF), axis=0
                    )

                sj = lax.fori_loop(0, 8, branch, zero)
                bst[layer, t, pl.ds(2 + j, 1), :] = jnp.sum(sj, axis=0, keepdims=True)
        share_all(bst, layer, 8 if last else 2, t, x, st_s.at[layer], st_r.at[layer])

    def field_gradient(layer, last):
        wait_on(bst.at[layer, pl.ds(0, 15), pl.ds(0, 8 if last else 2)], st_r.at[layer])
        gain = norm[layer, pl.ds(0, 1), :]
        sums = lax.fori_loop(0, 16, lambda s, a: a + bst[layer, s], zero)
        ngr[layer, pl.ds(0, 1), :] = sums[1:2]
        ngr[layer, pl.ds(1, 1), :] = sums[0:1]
        if last:
            sums4[...] = sums
            for j in range(5):
                ngr[5 + j, pl.ds(0, 1), :] = sums[2 + j : 3 + j]
                ngr[5 + j, pl.ds(1, 1), :] = sums[0:1]
        r = rs[layer, pl.ds(0, 1), :]
        c0 = gain * sums[0:1] / count
        c1 = gain * sums[1:2] / count
        b2 = lax.rem(layer, 2)

        def dz_block(b, _):
            m = mask(b)
            v = (gain * da[rows_of(b), :]).reshape(16, 8, HALF)
            xh = Xl[rows_of(b), :].reshape(16, 8, HALF)
            v = r * (v - m * c0 - m * xh * c1)
            dzA[b2, pl.ds(pl.multiple_of(HALO + b * 128, 64), 128), :] = v.reshape(
                128, HALF
            ).astype(BF)
            return 0

        when(layer + 2 <= 4, lambda: halo_sent(layer + 2))
        lax.fori_loop(0, 8, dz_block, 0)
        for side, edge, lo, to in ((0, 0, HALO, 1088), (1, 15, 1024, 0)):

            @pl.when(t != edge)
            def _():
                remote(
                    dzA.at[b2, pl.ds(lo, HALO)],
                    dzA.at[b2, pl.ds(to, HALO)],
                    halo_s.at[layer, side],
                    halo_r.at[layer, side],
                    (t - 1 + 2 * side, x),
                )

    def halo_arrived(layer):
        b2 = lax.rem(layer, 2)
        for side, edge in ((1, 0), (0, 15)):

            @pl.when(t != edge)
            def _():
                wait_on(dzA.at[b2, pl.ds(0, HALO)], halo_r.at[layer, side])

        def one(b, _):
            v = dzA[b2, pl.ds(pl.multiple_of(b * 128, 128), 144), :].astype(F32)
            dzB[pl.ds(pl.multiple_of(b * 128, 128), 128), :] = v[8:136].astype(BF)
            return 0

        lax.fori_loop(0, 9, one, 0)

    def shifted(b2, k, lo=0, rows=ROWS):
        o = 16 - k
        if o % 2 == 0:
            return dzA[b2, pl.ds(8 * o + lo, rows), :]
        return dzB[pl.ds(8 * (o - 1) + lo, rows), :]

    def data_half(layer, half, lo=0, rows=ROWS):
        b2 = lax.rem(layer, 2)
        acc = jnp.zeros((rows, HALF), F32)
        for k in range(17):
            acc = acc + lax.dot_general(
                shifted(b2, k, lo, rows),
                Wl[b2, k, pl.ds(2 * half, 2)].reshape(HALF, HALF),
                (((1,), (1,)), ((), ())),
                preferred_element_type=F32,
            )
        return acc

    def weight_tap(layer, h, k):
        return lax.dot_general(
            Hl[h],
            shifted(lax.rem(layer, 2), k),
            (((0,), (0,)), ((), ())),
            preferred_element_type=F32,
        ).reshape(2, 2, 2, 32, HALF)

    def weight_gradient(layer, h):
        b3 = lax.rem(layer, 3)
        for k in range(17):
            v = weight_tap(layer, h, k)
            for part in range(2):
                dW[b3, 2 * k + part, pl.ds(2 * h, 2)] = v[:, :, :, 16 * part : 16 * part + 16].astype(BF)

    def first_weight_gradient(h):
        for pair in range(9):
            v = weight_tap(0, h, 2 * pair)[:, :, :, :24]
            if pair < 8:
                v = jnp.concatenate([v, weight_tap(0, h, 2 * pair + 1)[:, :, :, :24]], axis=3)
            else:
                v = jnp.concatenate([v, jnp.zeros((2, 2, 2, 8, HALF), F32)], axis=3)
            for part in range(3 if pair < 8 else 2):
                dW[0, 3 * pair + part, pl.ds(2 * h, 2)] = v[
                    :, :, :, 16 * part : 16 * part + 16
                ].astype(BF)

    def load_branch(j):
        copy_in(xh_in.at[5 + j], xb.at[0], br_s.at[0])
        if j < 3:
            copy_in(nar_in.at[j], sb.at[0], br_s.at[2])
        elif j == 3:
            copy_in(wid_in, sb, br_s.at[2])
        else:
            copy_in(h_in.at[0], sb, br_s.at[2])

    def branch(j):
        field = 5 + j
        sums = sums4[...]
        wait_on(xb.at[0], br_s.at[0])
        wait_on(sb.at[0] if j < 3 else sb, br_s.at[2])
        gain = norm[field, pl.ds(0, 1), :]
        r = rs[field, pl.ds(0, 1), :]
        c0 = gain * sums[0:1] / count
        c1 = gain * sums[2 + j : 3 + j] / count

        def one(b, _):
            m = mask(b)
            v = (gain * y5[rows_of(b), :]).reshape(16, 8, HALF)
            xh = xb[0, rows_of(b), :].reshape(16, 8, HALF)
            v = r * (v - m * c0 - m * xh * c1)
            px[1, rows_of(b), :] = v.reshape(128, HALF).astype(BF)
            return 0

        lax.fori_loop(0, 8, one, 0)
        dv = px[1]
        if j < 3:
            v = lax.dot_general(
                sb[0], dv, (((0,), (0,)), ((), ())), preferred_element_type=F32
            )
            Dm[:, :, :, pl.ds(16 * j, 16), :] = v.reshape(4, 2, 2, 16, HALF).astype(BF)
            back = lax.dot_general(
                dv, wmn[j], (((1,), (1,)), ((), ())), preferred_element_type=F32
            )
            blocks = 2
        else:
            i = j - 3
            for h in range(2):
                v = lax.dot_general(
                    sb[h], dv, (((0,), (0,)), ((), ())), preferred_element_type=F32
                )
                Dm[pl.ds(2 * h, 2), :, :, pl.ds(48 + 32 * i, 32), :] = v.reshape(
                    2, 2, 2, 32, HALF
                ).astype(BF)
            wu = jnp.dot(perm[...], wmw[i], preferred_element_type=F32).astype(BF)
            back = lax.dot_general(
                dv, wu, (((1,), (1,)), ((), ())), preferred_element_type=F32
            )
            blocks = 3
        if j < 4:
            load_branch(j + 1)
        for b in range(8):
            m = mask(b)[:, :, :128]
            for i in range(blocks):
                v = back[128 * b : 128 * b + 128, 128 * i : 128 * i + 128]
                stg[i, pl.ds(128 * b, 128), :] = (v.reshape(16, 8, 128) * m).reshape(128, 128)
        if j < 3:

            def put_own(i, b, v):
                own_n[j, i, :, pl.ds(128 * b, 128)] = v

            def put_send(i, b, v):
                snd_n[j, i, :, pl.ds(128 * b, 128)] = v.astype(BF)

        else:

            def put_own(i, b, v):
                own_w[j - 3, i, :, pl.ds(128 * b, 128)] = v

            def put_send(i, b, v):
                snd_w[j - 3, i, :, pl.ds(128 * b, 128)] = v.astype(BF)

        unstage(blocks, put_own, put_send)
        if j < 3:
            remote(snd_n.at[j], rcv_n.at[j], sn_s.at[1 + j], sn_r.at[1 + j], partner)
        else:
            remote(snd_w.at[j - 3], rcv_w.at[j - 3], sn_s.at[1 + j], sn_r.at[1 + j], partner)

    def sources_narrow():
        for j in range(3):
            wait_on(rcv_n.at[j], sn_r.at[1 + j])
        own_n[...] = own_n[...] + rcv_n[...].astype(F32)
        copy_in(own_n, gn_out, out_s.at[3])

    def chain(layer, last):
        b2 = lax.rem(layer, 2)
        one = layer + 1
        two = lambda f: when(layer + 2 <= 4, lambda: f(layer + 2))
        load_w(layer - 1)
        output_gradient(layer, last)
        if last:
            send_mixed()
            load_branch(0)
        else:

            def two_a(older):
                add_across(older, 6)
                add_across(older, 7)

            two(two_a)
            add_core(one, 0)
            add_core(one, 1)
        field_gradient(layer, last)
        load_x(layer - 1)
        if not last:
            add_core(one, 2)
            add_across(one, 0)
        halo_arrived(layer)
        wait_on(Wl.at[0], w_s.at[b2])
        for j in range(4):
            if not last:
                wait_on(px.at[0, pl.ds(0, 256)], px_s.at[j])
            rows = pl.ds(256 * j, 256)
            for half in range(2):

                @pl.when(x == 1 - half)
                def _():
                    px[0, rows, :] = data_half(layer, half, 256 * j, 256).astype(BF)

            remote(px.at[0, rows], pxr.at[b2, rows], px_s.at[j], px_r.at[layer, j], partner)
            if j == 1 and not last:
                add_core(one, 3)
                add_across(one, 1)
        if not last:
            two(lambda older: finish_sum(older, 0))
        for half in range(2):

            @pl.when(x == half)
            def _():
                da[...] = data_half(layer, half)

        if not last:
            add_core(one, 4)
            add_across(one, 2)
            two(lambda older: finish_sum(older, 1))
            when(layer + 3 <= 4, lambda: drain_sums(layer + 3))
        wait_on(Hl, load_s.at[1])
        weight_gradient(layer, 0)
        send_core(layer, (0, 1))
        if not last:
            add_core(one, 5)
            add_across(one, 3)
        weight_gradient(layer, 1)
        send_core(layer, (2, 3))
        load_h(layer - 1)
        if not last:
            add_core(one, 6)
            add_across(one, 4)
            add_core(one, 7)
            add_across(one, 5)

            def two_out(older):
                when(layer + 3 <= 4, lambda: wait_assembled(32))
                assemble(older, put_rest(older))

            two(two_out)

    ss[...] = jnp.zeros((8, 128), F32)
    chain(4, True)
    branch(0)

    def middle(i, _):
        layer = 3 - i
        chain(layer, False)

        @pl.when(layer == 3)
        def _():
            branch(1)
            branch(2)
            wait_on(mix_rcv, sn_r.at[0])
            copy_in(mix_rcv, mixed_out.at[:, :, other_cols], out_s.at[4])

        @pl.when(layer == 2)
        def _():
            branch(3)
            branch(4)
            mixers_one()
            sources_narrow()

        @pl.when(layer == 1)
        def _():
            mixers_two()

        return 0

    lax.fori_loop(0, 3, middle, 0)

    output_gradient(0, False)
    add_across(2, 6)
    add_across(2, 7)
    add_core(1, 0)
    add_core(1, 1)
    field_gradient(0, False)
    add_core(1, 2)
    add_across(1, 0)
    halo_arrived(0)
    wait_on(Hl, load_s.at[1])
    wait_on(Wl.at[0], w_s.at[0])
    drain_sums(3)
    first_weight_gradient(0)
    send_core(0, (0, 1))
    add_core(1, 3)
    add_across(1, 1)
    finish_sum(2, 0)
    add_core(1, 4)
    add_across(1, 2)
    first_weight_gradient(1)
    send_core(0, (2, 3))
    finish_sum(2, 1)
    add_core(1, 5)
    add_across(1, 3)
    mixers_three()

    remote(ngr, ngx, ng_s, ng_r, partner)

    for k in range(17):
        Wl[1, k, pl.ds(0, 3)] = (
            jnp.dot(perm[...], Wl[0, k].reshape(512, HALF), preferred_element_type=F32)
            .astype(BF)
            .reshape(3, 2, 2, 32, HALF)
        )
    add_core(1, 6)
    add_across(1, 4)
    add_core(1, 7)
    add_across(1, 5)
    wait_assembled(32)
    assemble(2, put_rest(2))
    mixers_four()
    for part in range(4):
        acc = jnp.zeros((HALF, 384), F32)
        for k in range(17):
            o = 16 - k
            lo = part * HALF
            lhs = (
                dzA[0, pl.ds(8 * o + lo, HALF), :]
                if o % 2 == 0
                else dzB[pl.ds(8 * (o - 1) + lo, HALF), :]
            )
            acc = acc + lax.dot_general(
                lhs,
                Wl[1, k, pl.ds(0, 3)].reshape(384, HALF),
                (((1,), (1,)), ((), ())),
                preferred_element_type=F32,
            )
        for half in range(2):
            m = mask(2 * part + half)[:, :, :128]
            for b in range(3):
                stg[b, pl.ds(part * HALF + half * 128, 128), :] = (
                    acc[128 * half : 128 * half + 128, 128 * b : 128 * b + 128].reshape(
                        16, 8, 128
                    )
                    * m
                ).reshape(128, 128)
        if part == 0:
            add_across(1, 6)
            add_core(0, 0, 13)
        if part == 1:
            add_across(1, 7)
            add_core(0, 1, 13)
        if part == 2:
            finish_sum(1, 0)
            add_core(0, 2, 13)
            add_across(0, 0, 13)
        if part == 3:
            finish_sum(1, 1)
            add_core(0, 3, 13)
            add_across(0, 1, 13)

    def put_own(i, b, v):
        lanes = pl.ds(128 * b, 128)
        own_w[1, i, :, lanes] = own_w[1, i, :, lanes] + v

    def put_send(i, b, v):
        snd_w[2, i, :, pl.ds(128 * b, 128)] = v.astype(BF)

    unstage(3, put_own, put_send)
    remote(snd_w.at[2], rcv_w.at[2], sn_s.at[6], sn_r.at[6], partner)
    add_core(0, 4, 13)
    add_across(0, 2, 13)
    wait_assembled(32)
    assemble(1, put_rest(1))
    add_core(0, 5, 13)
    add_across(0, 3, 13)
    mixers_five()
    add_core(0, 6, 13)
    add_across(0, 4, 13)
    for j in range(2):
        wait_on(rcv_w.at[j], sn_r.at[4 + j])
    wait_on(rcv_w.at[2], sn_r.at[6])
    for j in range(2):
        v = own_w[j] + rcv_w[j].astype(F32)
        if j == 1:
            v = v + rcv_w[2].astype(F32)
        own_w[j] = v
    copy_in(own_w, gw_out, out_s.at[5])
    add_core(0, 7, 13)
    add_across(0, 5, 13)
    add_across(0, 6, 13)
    finish_sum(0, 0, 13)
    add_across(0, 7, 13)
    finish_sum(0, 1, 13)
    wait_on(ngx, ng_r)
    wait_assembled(32)
    assemble(0, lambda b: gf_out.at[:, pl.ds(128 * b, 128)], 13)

    fst[t] = ss[...]

    def tell(d, _):
        remote(fst.at[t], fst.at[t], st_s.at[5], st_r.at[5], (lax.rem(t + d, 16), x))
        return 0

    lax.fori_loop(1, 16, tell, 0)
    mine, theirs = ngr[...], ngx[...]
    left = jnp.where(x == 0, mine, theirs)
    right = jnp.where(x == 0, theirs, mine)
    rows = lax.broadcasted_iota(jnp.int32, (10, 8, HALF), 1)
    left = jnp.where(rows < 2, left, 0.0)
    right = jnp.where(rows < 2, right, 0.0)
    ng_out[0] = left
    ng_out[1] = right
    norms = jnp.sum(left * left + right * right)
    wait_on(fst.at[pl.ds(0, 15)], st_r.at[5])
    every = lax.fori_loop(0, 16, lambda s, a: a + fst[s], jnp.zeros((8, 128), F32))
    total_out[...] = jnp.zeros((8, 128), F32) + (jnp.sum(every) + norms)

    wait_assembled(24)
    wait_on(mix_own.at[0], out_s.at[0])
    wait_on(mix_rcv, out_s.at[4])
    wait_on(own_n, out_s.at[3])
    wait_on(own_w, out_s.at[5])
    wait_on(gsm.at[:, pl.ds(0, 48)], out_s.at[1])
    wait_on(gsm.at[:, pl.ds(0, 48)], out_s.at[2])
    for j in range(4):
        wait_on(px.at[0, pl.ds(0, 256)], px_s.at[j])
    wait_on(mix_own.at[1], sn_s.at[0])
    for j in range(3):
        wait_on(snd_n.at[0], sn_s.at[1 + j])
        wait_on(snd_w.at[0], sn_s.at[4 + j])
    wait_on(cm, m_s.at[0])
    wait_on(ym, m_s.at[1])
    wait_on(zm, m_s.at[2])
    wait_on(fm, m_s.at[3])
    wait_on(ngr, ng_s)
    wait_on(fst.at[pl.ds(0, 15)], st_s.at[5])
    drain_sums(2)
    drain_sums(1)
    drain_sums(0, 13)

    for layer in range(2):
        wait_on(fin.at[0, pl.ds(0, 34 if layer else 26)], f_s.at[layer])
        halo_sent(layer)

    for layer in range(5):
        wait_on(bst.at[layer, pl.ds(0, 15), pl.ds(0, 8 if layer == 4 else 2)], st_s.at[layer])


def run_backward(lens, norm, rs, perm, w, wmn, wmw, h, xh, y, nar, wid, cot):
    vm = pl.BlockSpec(memory_space=pltpu.VMEM)
    hb = pl.BlockSpec(memory_space=pl.ANY)
    dma = pltpu.SemaphoreType.DMA
    S = jax.ShapeDtypeStruct
    V = pltpu.VMEM
    return pl.pallas_call(
        backward_kernel,
        out_shape=(
            S((4, 128, 512), BF),
            S((3, 4, 128, HALF), F32),
            S((2, 4, 128, 384), F32),
            S((408, 512), F32),
            S((4, 544, 512), F32),
            S((3, 16, 512), F32),
            S((2, 24, 512), F32),
            S((2, 10, 8, HALF), F32),
            S((8, 128), F32),
        ),
        in_specs=[vm, vm, vm, vm, hb, vm, vm, hb, hb, hb, hb, hb, hb],
        out_specs=[hb] * 7 + [vm, vm],
        scratch_shapes=[
            V((2, 17, 4, 2, 2, 32, HALF), BF),
            V((2, ROWS, HALF), BF),
            V((ROWS, HALF), F32),
            V((2, ROWS, HALF), F32),
            V((2, ROWS, HALF), BF),
            V((ROWS, HALF), F32),
            V((ROWS, HALF), F32),
            V((2, 1168, HALF), BF),
            V((1152, HALF), BF),
            V((3, 34, 4, 2, 2, 16, HALF), BF),
            V((2, 34, 4, 2, 16, HALF), BF),
            V((3, 34, 4, 16, HALF), BF),
            V((3, 3, 34, 16, HALF), BF),
            V((2, 34, 16, HALF), BF),
            V((5, 34, 16, HALF), BF),
            V((2, ROWS, HALF), BF),
            V((2, ROWS, HALF), BF),
            V((3, ROWS, 128), F32),
            V((3, 4, 128, HALF), F32),
            V((2, 4, 128, 384), F32),
            V((3, 4, 128, HALF), BF),
            V((3, 4, 128, 384), BF),
            V((3, 4, 128, HALF), BF),
            V((3, 4, 128, 384), BF),
            V((2, 4, 128, HALF), BF),
            V((4, 128, HALF), BF),
            V((4, 2, 2, 112, HALF), BF),
            V((4, 2, 112, HALF), BF),
            V((4, 112, HALF), BF),
            V((3, 112, HALF), BF),
            V((112, HALF), BF),
            V((112, HALF), BF),
            V((4, 544, 128), F32),
            V((4, 112, 128), F32),
            V((5, 16, 8, HALF), F32),
            V((8, HALF), F32),
            V((10, 8, HALF), F32),
            V((10, 8, HALF), F32),
            V((8, 128), F32),
            V((16, 8, 128), F32),
            dma((5,)),
            dma((2,)),
            dma((3,)),
            dma((5, 2)),
            dma((5, 2)),
            dma((6,)),
            dma((6,)),
            dma((5,)),
            dma((5, 4)),
            dma((5,)),
            dma((5, 8)),
            dma((5, 2)),
            dma((5, 2)),
            dma((5,)),
            dma((5, 2)),
            dma((4,)),
            dma((5, 4)),
            dma((4,)),
            dma((4,)),
            dma((7,)),
            dma((7,)),
            dma,
            dma((6,)),
            dma,
            dma,
        ],
        compiler_params=pltpu.CompilerParams(
            collective_id=1, has_side_effects=True, vmem_limit_bytes=63 << 20
        ),
        cost_estimate=pl.CostEstimate(flops=46 * 10**9, bytes_accessed=60 * 10**6, transcendentals=0),
    )(lens, norm, rs, perm, w, wmn, wmw, h, xh, y, nar, wid, cot)


def prepare(lengths, norm_params):
    x = lax.axis_index("batch")
    mine = jnp.broadcast_to(lengths.astype(F32)[:, None], (4, HALF))
    lens = jnp.zeros((8, HALF), F32)
    lens = lax.dynamic_update_slice(lens, mine, (4 * x, 0))
    half = lax.dynamic_slice(norm_params, (0, 0, x * HALF), (2, 10, HALF))
    norm = jnp.pad(jnp.transpose(half, (1, 0, 2)), ((0, 0), (0, 6), (0, 0)))
    places = np.arange(384)
    perm = np.zeros((384, 512), np.float32)
    perm[places, (places // 24) * 32 + places % 24] = 1.0
    return lens, norm, jnp.asarray(perm, BF)


def body_split(
    source_narrow,
    source_wide,
    lengths,
    cotangent,
    kernel_first,
    kernel_rest,
    mixer_narrow,
    mixer_wide,
    norm_params,
    moment_first,
    square_first,
    moment_rest,
    square_rest,
    moment_narrow,
    square_narrow,
    moment_wide,
    square_wide,
    moment_norm,
    square_norm,
):
    lens, norm, perm = prepare(lengths, norm_params)
    w, wmn, wmw, h, xh, y, nar, wid, cot, rs, lens = run_forward(
        lens,
        norm,
        perm,
        source_narrow,
        source_wide,
        cotangent,
        kernel_first,
        kernel_rest,
        mixer_narrow,
        mixer_wide,
    )
    mixed, gn, gw, gf, gr, gmn, gmw, ng, total = run_backward(
        lens, norm, rs, perm, w, wmn, wmw, h, xh, y, nar, wid, cot
    )
    grad_norm = jnp.sqrt(total[0, 0])
    clip = jnp.minimum(1.0, THRESHOLD / grad_norm)
    norm_grad = jnp.transpose(ng[:, :, :2, :], (2, 1, 0, 3)).reshape(2, 10, CO)
    results = []
    for p, g, m, v in (
        (kernel_first, gf, moment_first, square_first),
        (kernel_rest, gr, moment_rest, square_rest),
        (mixer_narrow, gmn, moment_narrow, square_narrow),
        (mixer_wide, gmw, moment_wide, square_wide),
    ):
        results += adamw(p, clip * g, m, v, RATE_WEIGHT, DECAY)
    results += adamw(norm_params, clip * norm_grad, moment_norm, square_norm, RATE_NORM, 0.0)
    return (mixed, gn, gw, grad_norm, *results)


def solution(mesh):
    in_specs = (
        P(None, "batch", "tm", None),
        P(None, "batch", "tm", None),
        P("batch"),
        P("batch", "tm", None),
        P("tm", None),
        P(None, "tm", None),
        P(None, "tm", None),
        P(None, "tm", None),
        P(),
        P("tm", None),
        P("tm", None),
        P(None, "tm", None),
        P(None, "tm", None),
        P(None, "tm", None),
        P(None, "tm", None),
        P(None, "tm", None),
        P(None, "tm", None),
        P(),
        P(),
    )
    out_specs = (
        P("batch", "tm", None),
        P(None, "batch", "tm", None),
        P(None, "batch", "tm", None),
        P(),
        P("tm", None),
        P("tm", None),
        P("tm", None),
        P(None, "tm", None),
        P(None, "tm", None),
        P(None, "tm", None),
        P(None, "tm", None),
        P(None, "tm", None),
        P(None, "tm", None),
        P(None, "tm", None),
        P(None, "tm", None),
        P(None, "tm", None),
        P(),
        P(),
        P(),
    )
    fits = mesh.shape["tm"] == 16 and mesh.shape["batch"] == 2
    chosen = body_split if fits else body
    return jax.shard_map(chosen, mesh=mesh, in_specs=in_specs, out_specs=out_specs, check_vma=False)
```

```python
import numpy as np
import jax
import jax.numpy as jnp
from jax import lax
from jax.experimental import pallas as pl
from jax.experimental.pallas import tpu as pltpu
from jax.sharding import PartitionSpec as P

CO = 512
CW = 384
K = 17
STEP = 10


EPS = 1e-05
THRESHOLD = 100.0
BETA_ONE = 0.9
SECOND_DECAY = 0.999
ADAM_EPS = 1e-08
RATE_WEIGHT = 0.02
RATE_NORM = 0.4
DECAY = 0.01


def padded_2(shard, sides, width):
    for axis, dim in sides:
        devices, length = (lax.axis_size(axis), shard.shape[dim])
        up = [(i, (i + 1) % devices) for i in range(devices - 1)]
        down = [(j, i) for i, j in up]
        last = lax.slice_in_dim(shard, length - width, length, axis=dim)
        initial = lax.slice_in_dim(shard, 0, width, axis=dim)
        before = lax.ppermute(last, axis, up)
        after = lax.ppermute(initial, axis, down)
        shard = jnp.concatenate([before, shard, after], axis=dim)
    return shard


def adamw(param, grad, first, second, rate, decay):
    first_new = BETA_ONE * first + (1.0 - BETA_ONE) * grad
    second_new = SECOND_DECAY * second + (1.0 - SECOND_DECAY) * grad * grad
    fix_one = 1.0 - BETA_ONE**STEP
    fix_two = 1.0 - SECOND_DECAY**STEP
    update = first_new / fix_one / (jnp.sqrt(second_new / fix_two) + ADAM_EPS)
    return (param - rate * (update + decay * param), first_new, second_new)


def body(
    source_narrow,
    source_wide,
    lengths,
    cotangent,
    kernel_first,
    kernel_rest,
    mixer_narrow,
    mixer_wide,
    norm_params,
    moment_first,
    square_first,
    moment_rest,
    square_rest,
    moment_narrow,
    square_narrow,
    moment_wide,
    square_wide,
    moment_norm,
    square_norm,
):
    frames = source_wide.shape[2]
    half = K // 2
    places = lax.axis_index("tm") * frames + jnp.arange(frames, dtype=jnp.int32)
    valid = (places[None, :] < lengths[:, None]).astype(jnp.float32)[:, :, None]
    local_count = jnp.sum(valid)
    valid_low = valid.astype(jnp.bfloat16)
    narrow = source_narrow * valid_low[None]
    wide = source_wide * valid_low[None]
    full_first, full_rest, full_narrow, full_wide = (
        lax.all_gather(kernel_first.astype(jnp.bfloat16), "tm", axis=0, tiled=True),
        lax.all_gather(kernel_rest.astype(jnp.bfloat16), "tm", axis=1, tiled=True),
        lax.all_gather(mixer_narrow.astype(jnp.bfloat16), "tm", axis=1, tiled=True),
        lax.all_gather(mixer_wide.astype(jnp.bfloat16), "tm", axis=1, tiled=True),
    )
    kernels = [jnp.transpose(full_first.reshape(CW, K, CO), (1, 0, 2))] + [
        jnp.transpose(full_rest[layer].reshape(CO, K, CO), (1, 0, 2)) for layer in range(4)
    ]
    gains = norm_params[0]
    biases = norm_params[1]

    def batch_statistics(values, count):
        sums = tuple((jnp.sum(value * valid, axis=(0, 1)) for value in values))
        extra = (local_count,) if count is None else ()
        got = lax.psum(sums + extra, ("tm", "batch"))
        if count is None:
            count = got[-1]
        means = [total / count for total in got[: len(values)]]
        spreads = tuple(
            (
                jnp.sum(jnp.square((value - mean) * valid), axis=(0, 1))
                for value, mean in zip(values, means)
            )
        )
        second = lax.psum(spreads, ("tm", "batch"))
        variances = [total / count for total in second]
        scales = [lax.rsqrt(variance + EPS) for variance in variances]
        return (means, scales, count)

    signal = wide[1]
    kept = []
    count = None
    for index in range(5):
        padded = padded_2(signal, (("tm", 1),), half)
        field = jnp.zeros(signal.shape[:2] + (CO,), jnp.float32)
        for tap in range(K):
            field = field + jnp.einsum(
                "btc,cd->btd",
                padded[:, tap : tap + frames],
                kernels[index][tap],
                preferred_element_type=jnp.float32,
            )
        values = [field]
        indices = [index]
        if index == 4:
            for source in range(3):
                values.append(
                    jnp.einsum(
                        "btc,cd->btd",
                        narrow[source],
                        full_narrow[source],
                        preferred_element_type=jnp.float32,
                    )
                )
                indices.append(5 + source)
            for source in range(2):
                values.append(
                    jnp.einsum(
                        "btc,cd->btd",
                        wide[source],
                        full_wide[source],
                        preferred_element_type=jnp.float32,
                    )
                )
                indices.append(8 + source)
        means, scales, count = batch_statistics(values, count)
        normalized_values = [
            (value - mean) * scale for value, mean, scale in zip(values, means, scales)
        ]
        summed = jnp.zeros_like(field)
        for place in range(len(values)):
            summed = (
                summed + gains[indices[place]] * normalized_values[place] + biases[indices[place]]
            )
        kept.append((padded, normalized_values, scales, summed, indices))
        active = jax.nn.silu(summed) * valid
        signal = active.astype(jnp.bfloat16)
    grad_active = cotangent.astype(jnp.float32)
    kernel_grads = [None] * 5
    gain_grads = [None] * 10
    bias_grads = [None] * 10
    narrow_grads = []
    wide_grads = []
    narrow_inputs = []
    wide_inputs = []
    first_input = None
    for index in reversed(range(5)):
        padded, normalized_values, scales, summed, indices = kept[index]
        sigma = jax.nn.sigmoid(summed)
        gradient_total = grad_active * valid * sigma * (1.0 + summed * (1.0 - sigma))
        local_sums = (jnp.sum(gradient_total, axis=(0, 1)),) + tuple(
            (
                jnp.sum(gradient_total * standardized_input, axis=(0, 1))
                for standardized_input in normalized_values
            )
        )
        got = lax.psum(local_sums, ("tm", "batch"))
        bias_total = got[0]
        field_grads = []
        for place in range(len(normalized_values)):
            which = indices[place]
            gain = gains[which]
            gain_grads[which] = got[1 + place]
            bias_grads[which] = bias_total
            grad_field = scales[place] * (
                gain * gradient_total
                - valid * (gain * bias_total) / count
                - valid * normalized_values[place] * (gain * got[1 + place]) / count
            )
            field_grads.append(grad_field.astype(jnp.bfloat16))
        grad_conv = field_grads[0]
        tap_grads = [
            jnp.einsum(
                "btc,btd->cd",
                padded[:, tap : tap + frames],
                grad_conv,
                preferred_element_type=jnp.float32,
            )
            for tap in range(K)
        ]
        kernel_grads[index] = jnp.stack(tap_grads, axis=1).reshape(padded.shape[2] * K, CO)
        if index == 4:
            for source in range(3):
                branch = field_grads[1 + source]
                narrow_grads.append(
                    jnp.einsum(
                        "btc,btd->cd", narrow[source], branch, preferred_element_type=jnp.float32
                    )
                )
                narrow_inputs.append(
                    jnp.einsum(
                        "btd,cd->btc",
                        branch,
                        full_narrow[source],
                        preferred_element_type=jnp.float32,
                    )
                    * valid
                )
            for source in range(2):
                branch = field_grads[4 + source]
                wide_grads.append(
                    jnp.einsum(
                        "btc,btd->cd", wide[source], branch, preferred_element_type=jnp.float32
                    )
                )
                wide_inputs.append(
                    jnp.einsum(
                        "btd,cd->btc", branch, full_wide[source], preferred_element_type=jnp.float32
                    )
                    * valid
                )
        grad_padded = padded_2(grad_conv, (("tm", 1),), half)
        incoming = jnp.zeros(padded.shape[:1] + (frames, padded.shape[2]), jnp.float32)
        for tap in range(K):
            start = K - 1 - tap
            incoming = incoming + jnp.einsum(
                "btd,cd->btc",
                grad_padded[:, start : start + frames],
                kernels[index][tap],
                preferred_element_type=jnp.float32,
            )
        if index > 0:
            grad_active = incoming
        else:
            first_input = incoming
    grad_narrow = jnp.stack(narrow_inputs)
    source_wide_gradient = jnp.stack([wide_inputs[0], (first_input + wide_inputs[1]) * valid])
    shard_gradients = (
        kernel_grads[0],
        jnp.stack(kernel_grads[1:]),
        jnp.stack(narrow_grads),
        jnp.stack(wide_grads),
    )
    shards = (
        lax.psum_scatter(shard_gradients[0], "tm", scatter_dimension=0, tiled=True),
        lax.psum_scatter(shard_gradients[1], "tm", scatter_dimension=1, tiled=True),
        lax.psum_scatter(shard_gradients[2], "tm", scatter_dimension=1, tiled=True),
        lax.psum_scatter(shard_gradients[3], "tm", scatter_dimension=1, tiled=True),
    )
    norm_grad = jnp.stack([jnp.stack(gain_grads), jnp.stack(bias_grads)])
    params = (kernel_first, kernel_rest, mixer_narrow, mixer_wide)
    firsts = (moment_first, moment_rest, moment_narrow, moment_wide)
    seconds = (square_first, square_rest, square_narrow, square_wide)
    results = []
    shards = (
        lax.psum(shards[0].astype(jnp.bfloat16), "batch").astype(jnp.float32),
        lax.psum(shards[1].astype(jnp.bfloat16), "batch").astype(jnp.float32),
        lax.psum(shards[2].astype(jnp.bfloat16), "batch").astype(jnp.float32),
        lax.psum(shards[3].astype(jnp.bfloat16), "batch").astype(jnp.float32),
    )
    local_square = jnp.zeros((), jnp.float32)
    for shard in shards:
        local_square = local_square + jnp.sum(shard * shard)
    total = lax.psum(local_square, "tm") + jnp.sum(norm_grad * norm_grad)
    grad_norm = jnp.sqrt(total)
    clip = jnp.minimum(1.0, THRESHOLD / grad_norm)
    for slot in range(4):
        results.append(
            adamw(
                params[slot], clip * shards[slot], firsts[slot], seconds[slot], RATE_WEIGHT, DECAY
            )
        )
    results.append(adamw(norm_params, clip * norm_grad, moment_norm, square_norm, RATE_NORM, 0.0))
    return (
        signal,
        grad_narrow,
        source_wide_gradient,
        grad_norm,
        results[0][0],
        results[0][1],
        results[0][2],
        results[1][0],
        results[1][1],
        results[1][2],
        results[2][0],
        results[2][1],
        results[2][2],
        results[3][0],
        results[3][1],
        results[3][2],
        results[4][0],
        results[4][1],
        results[4][2],
    )


BF = jnp.bfloat16
F32 = jnp.float32
MESH = pl.DeviceIdType.MESH
ROWS = 1024
HALO = 64
HALF = 256
GROUPS = 34
LEAD = 10
AHEAD = 3
LAG = AHEAD + 2


def wait_on(ref, sem):
    pltpu.make_async_copy(ref, ref, sem).wait()


def remote(src, dst, send, recv, device):
    pltpu.make_async_remote_copy(
        src_ref=src,
        dst_ref=dst,
        send_sem=send,
        recv_sem=recv,
        device_id=device,
        device_id_type=MESH,
    ).start()


def position():
    x = lax.axis_index("batch")
    t = lax.axis_index("tm")
    return x, t, lax.div(t, 4), lax.rem(lax.div(t, 2), 2), lax.rem(t, 2)


def greet(x, t):
    barrier = pltpu.get_barrier_semaphore()

    def one(d, _):
        pl.semaphore_signal(
            barrier, inc=1, device_id=(lax.rem(t + d, 16), x), device_id_type=MESH
        )
        return 0

    lax.fori_loop(1, 16, one, 0)
    for d in (0, 1, 2, 14, 15):
        pl.semaphore_signal(
            barrier, inc=1, device_id=(lax.rem(t + d, 16), 1 - x), device_id_type=MESH
        )
    pl.semaphore_wait(barrier, 20)


def frame_mask(block, t, lens):
    frames = lax.broadcasted_iota(jnp.int32, (16, 8, HALF), 0) + (block * 16 + t * 128)
    return (frames.astype(F32) < lens[None]).astype(F32)


def share(box, part, at, rows, sems):
    x, t, zi, yi, ci = position()
    chip = lax.div(t, 2)
    to_first, to_peer, to_second, first, peer, second = sems
    used = pl.ds(0, rows)

    @pl.when(ci == 1)
    def _():
        remote(
            part.at[at, used],
            box.at[at, chip, 1, used],
            to_first.at[at],
            first.at[at],
            (t - 1, x),
        )

    @pl.when(ci == 0)
    def _():
        box[at, chip, 0] = part[at]
        wait_on(box.at[at, chip, 1, used], first.at[at])
        mine = box.at[at, chip, :, used]

        def one(d, _):
            remote(mine, mine, to_peer.at[at], peer.at[at], (lax.rem(t + 2 * d, 16), x))
            return 0

        lax.fori_loop(1, 8, one, 0)


def shared(box, at, rows, sems):
    x, t, zi, yi, ci = position()
    to_first, to_peer, to_second, first, peer, second = sems
    used = pl.ds(0, rows)

    @pl.when(ci == 0)
    def _():
        wait_on(box.at[at, pl.ds(0, 7), :, used], peer.at[at])
        every = box.at[at, :, :, used]
        remote(every, every, to_second.at[at], second.at[at], (t + 1, x))

    @pl.when(ci == 1)
    def _():
        wait_on(box.at[at, :, :, used], second.at[at])


def share_drained(box, part, at, rows, sems):
    ci = position()[4]
    to_first, to_peer, to_second, first, peer, second = sems
    used = pl.ds(0, rows)

    @pl.when(ci == 1)
    def _():
        wait_on(part.at[at, used], to_first.at[at])

    @pl.when(ci == 0)
    def _():
        wait_on(box.at[at, pl.ds(0, 7), :, used], to_peer.at[at])
        wait_on(box.at[at, :, :, used], to_second.at[at])


def forward_kernel(
    lens_in,
    norm,
    perm,
    src_n,
    src_w,
    cot,
    kf,
    kr,
    mn,
    mw,
    w_out,
    wmn_out,
    wmw_out,
    h_out,
    xh_out,
    y_out,
    nar_out,
    wid_out,
    cot_out,
    rs_out,
    len_out,
    W,
    G,
    wmn,
    wmw,
    hA,
    hB,
    z,
    zb,
    xhb,
    y5,
    stg,
    pf,
    pmn,
    pmw,
    raww,
    rawn,
    rawc,
    nar,
    wid,
    cotv,
    st,
    sp,
    rel,
    nv,
    lenr,
    lens,
    load_s,
    dl_s,
    dl_r,
    ag_s,
    rz,
    rf,
    ry,
    rc,
    m_s,
    m_r,
    x_s,
    x_r,
    xr_s,
    xr_r,
    halo_s,
    halo_r,
    rel_s,
    rel_r,
    st_a,
    st_b,
    st_c,
    st_d,
    st_e,
    st_f,
    out_s,
):
    x, t, zi, yi, ci = position()
    cols = pl.ds(pl.multiple_of(x * HALF, HALF), HALF)
    partner = (t, 1 - x)
    sibling = (t + 1 - 2 * ci, x)
    across = (zi * 4 + (1 - yi) * 2 + ci, x)
    sems = (st_a, st_b, st_c, st_d, st_e, st_f)

    lanes = [pl.ds(pl.multiple_of(x * HALF + 128 * b, 128), 128) for b in range(2)]
    loads = [(kf.at[:, lanes[b]], pf.at[0, b, pl.ds(0, 408)]) for b in range(2)]
    loads += [(kr.at[i, :, lanes[b]], pf.at[1 + i, b]) for i in range(4) for b in range(2)]
    loads += [
        (mn.at[:, :, cols], pmn),
        (mw.at[:, :, cols], pmw),
        (src_w, raww.at[x]),
        (src_n, rawn.at[x]),
        (cot.at[:, :, cols], rawc.at[x]),
    ]
    copies = [pltpu.make_async_copy(a, b, load_s.at[i]) for i, (a, b) in enumerate(loads)]
    for copy in copies:
        copy.start()
    hA[:, :, pl.ds(1152, 16), :] = jnp.zeros((5, 2, 16, HALF), BF)

    @pl.when(t == 0)
    def _():
        hA[:, :, pl.ds(0, HALO), :] = jnp.zeros((5, 2, HALO, HALF), BF)

    @pl.when(t == 15)
    def _():
        hA[:, :, pl.ds(1088, HALO), :] = jnp.zeros((5, 2, HALO, HALF), BF)

    st[...] = jnp.zeros((7, 8, 2, 8, HALF), F32)
    sp[...] = jnp.zeros((7, 8, HALF), F32)
    lenr[0] = lens_in[...]
    greet(x, t)

    other = pl.ds(pl.multiple_of((1 - x) * HALF, HALF), HALF)
    remote(lenr.at[0], lenr.at[1], xr_s.at[0], xr_r.at[0], partner)
    remote(src_w.at[1], raww.at[x, 1], xr_s.at[1], xr_r.at[1], partner)

    def prep(layer, count):
        for k in range(17):
            for b in range(2):
                v = pf[layer, b, pl.ds(k, count, stride=17), :]
                if count < 32:
                    v = jnp.concatenate([v, jnp.zeros((32 - count, 128), F32)], axis=0)
                W[17 * layer + k, zi, yi, ci, :, pl.ds(128 * b, 128)] = v.astype(BF)

    def taps(g):
        return pl.ds(5 * lax.div(g, 2), 5)

    def part(g):
        return pl.ds(pl.multiple_of(16 * lax.rem(g, 2), 16), 16)

    def first_sends(pair, send, into_z):
        for dz in (1, 2, 3):
            remote(pair, pair, send, into_z, (lax.rem(zi + dz, 4) * 4 + yi * 2 + 1, x))

    def pass_z(block, send_y, send_c, into_y, into_c):
        line = block(slice(None), yi, slice(None))
        remote(line, line, send_y, into_y, across)
        line = block(slice(None), yi, 1)
        remote(line, line, send_c, into_c, sibling)
        for dz in (1, 2, 3):
            one = block(lax.rem(zi + dz, 4), yi, 0)
            remote(one, one, send_c, into_c, sibling)

    def pass_y(block, send_c, into_c):
        line = block(slice(None), 1 - yi, slice(None))
        remote(line, line, send_c, into_c, sibling)

    def chunk(g):
        return lambda zs, ys, cs: W.at[taps(g), zs, ys, cs, part(g)]

    def mixers(zs, ys, cs):
        return G.at[zs, ys, cs]

    ALL = slice(None)
    THREE = pl.ds(0, 3)

    inner = (zi == 1) | (zi == 2)
    far = jnp.where(zi == 1, 3, 0)

    def own_step(g):
        pair = chunk(g)(zi, yi, ALL)

        def to(zz, sems):
            remote(pair, pair, ag_s.at[g, 0], sems.at[g], (zz * 4 + yi * 2 + 1, x))

        @pl.when((ci == 1) & (g < GROUPS) & inner)
        def _():
            to(3 - zi, rz)
            to(jnp.where(zi == 1, 0, 3), rz)
            to(jnp.where(zi == 1, 3, 0), rz)

        @pl.when((ci == 1) & (g < GROUPS) & (zi == 0))
        def _():
            to(1, rz)
            to(2, rf)

        @pl.when((ci == 1) & (g < GROUPS) & (zi == 3))
        def _():
            to(2, rz)
            to(1, rf)

    def far_step(g):
        @pl.when((ci == 1) & (g < GROUPS) & inner)
        def _():
            pair = chunk(g)(far, yi, ALL)
            wait_on(pair, rf.at[g])
            remote(pair, pair, ag_s.at[g, 0], rz.at[g], ((3 - far) * 4 + yi * 2 + 1, x))

    def y_step(h):
        @pl.when((ci == 1) & (h >= 0) & (h < GROUPS))
        def _():
            wait_on(chunk(h)(ALL, 0, ALL), ry.at[h])
            pass_y(chunk(h), ag_s.at[h, 2], rc.at[h])

    def service(g, start):
        own_step(g + LEAD)
        far_step(g + 2)

        @pl.when((ci == 1) & (g < GROUPS) & inner)
        def _():
            wait_on(chunk(g)(pl.ds(0, 2), 0, ALL), rz.at[g])

        @pl.when((ci == 1) & (g < GROUPS) & jnp.logical_not(inner))
        def _():
            wait_on(chunk(g)(THREE, 0, ALL), rz.at[g])

        @pl.when((ci == 1) & (g < GROUPS))
        def _():
            pass_z(chunk(g), ag_s.at[g, 1], ag_s.at[g, 2], ry.at[g], rc.at[g])

        @pl.when(g - LAG >= start)
        def _():
            y_step(g - LAG)

        @pl.when((ci == 1) & (g == 8))
        def _():
            wait_on(mixers(THREE, 0, ALL), m_r.at[0])
            pass_z(mixers, m_s.at[1], m_s.at[2], m_r.at[1], m_r.at[2])

        @pl.when((ci == 1) & (g == 11))
        def _():
            wait_on(mixers(ALL, 0, ALL), m_r.at[1])
            pass_y(mixers, m_s.at[2], m_r.at[2])

    def mixers_arrived():
        @pl.when(ci == 0)
        def _():
            wait_on(W.at[pl.ds(0, 35), THREE, 0, 0, pl.ds(0, 16)], m_r.at[2])

        for s in range(16):
            got = G.at[s // 4, s // 2 % 2, s % 2]
            for j in range(3):
                wmn[j, pl.ds(16 * s, 16), :] = got[pl.ds(16 * j, 16), :]
            for j in range(2):
                wmw[j, pl.ds(32 * s, 32), :] = got[pl.ds(48 + 32 * j, 32), :]

    FIFTEEN = W.at[pl.ds(0, 75), 0, 0, 0, pl.ds(0, 16)]

    def weights_arrived(layer):
        def one(h, _):
            wait_on(FIFTEEN, rc.at[h])
            return 0

        for d in range(2):
            y_step(2 * lax.div(17 * layer + 16, 5) + d)

        @pl.when(ci == 0)
        def _():
            lo = jnp.where(layer == 0, 0, 2 * lax.div(17 * layer - 1, 5) + 2)
            lax.fori_loop(lo, 2 * lax.div(17 * layer + 16, 5) + 2, one, 0)

    def lend(layer):
        own = W.at[pl.ds(17 * layer, 17), zi, yi, 0]

        @pl.when(ci == 0)
        def _():
            remote(own, own, dl_s.at[layer], dl_r.at[layer], sibling)

    def lent(layer):
        @pl.when(ci == 1)
        def _():
            wait_on(W.at[pl.ds(0, 17), zi, yi, 0], dl_r.at[layer])

    def serve(first, last):
        def one(g, _):
            service(g, 0)
            return 0

        lax.fori_loop(first, last, one, 0)

    for copy in copies[:2]:
        copy.wait()
    prep(0, 24)
    lend(0)
    for copy in copies[2:12]:
        copy.wait()
    for layer in (1, 2, 3, 4):
        prep(layer, 32)
        lend(layer)
    for j in range(3):
        G[zi, yi, ci, pl.ds(16 * j, 16), :] = pmn[j].astype(BF)
    for j in range(2):
        G[zi, yi, ci, pl.ds(48 + 32 * j, 32), :] = jnp.concatenate(
            [pmw[j], jnp.zeros((8, HALF), F32)], axis=0
        ).astype(BF)

    @pl.when(ci == 0)
    def _():
        remote(G.at[zi, yi, 0], G.at[zi, yi, 0], dl_s.at[5], dl_r.at[5], sibling)

    for layer in range(5):
        lent(layer)

    @pl.when(ci == 1)
    def _():
        wait_on(G.at[zi, yi, 0], dl_r.at[5])


    def own_one(g, _):
        own_step(g)
        return 0

    lax.fori_loop(0, LEAD, own_one, 0)
    far_step(jnp.int32(0))
    far_step(jnp.int32(1))

    @pl.when(ci == 1)
    def _():
        first_sends(mixers(zi, yi, ALL), m_s.at[0], m_r.at[0])

    serve(0, 2)

    wait_on(lenr.at[1], xr_r.at[0])
    lens[...] = lenr[0] + lenr[1]
    len_out[...] = lens[...]
    for s in range(16):
        nv[s] = jnp.broadcast_to(
            jnp.sum(jnp.clip(lens[...] - 128.0 * s, 0.0, 128.0), axis=0, keepdims=True), (8, HALF)
        )

    def spread_wide(j):
        for s in range(8):
            v = jnp.dot(raww[s // 4, j, s % 4], perm[...], preferred_element_type=F32)
            for b in range(4):
                stg[b, pl.ds(s, 128, stride=8), :] = v[:, 128 * b : 128 * b + 128]

    def spread_half(v, s):
        for b in range(2):
            stg[b, pl.ds(s, 128, stride=8), :] = v[:, 128 * b : 128 * b + 128].astype(F32)

    def masked_block(b, h):
        rows = pl.ds(pl.multiple_of(b * 128, 128), 128)
        v = jnp.concatenate([stg[2 * h, rows, :], stg[2 * h + 1, rows, :]], axis=1)
        v = v.reshape(16, 8, HALF)
        return (v * frame_mask(b, t, lens[...])).reshape(128, HALF).astype(BF)

    copies[12].wait()
    wait_on(raww.at[0, 1], xr_r.at[1])
    spread_wide(1)

    def first_block(b, _):
        for h in range(2):
            hA[0, h, pl.ds(pl.multiple_of(HALO + b * 128, 64), 128), :] = masked_block(b, h)
        return 0

    lax.fori_loop(0, 8, first_block, 0)

    EDGE = ((HALO, 1088), (1024, 0))

    def halo_out(layer, half, side, at):
        lo, to = EDGE[side]
        goal = hA.at[layer, half, pl.ds(to, HALO)]
        source = hA.at[layer, half, pl.ds(lo, HALO)]
        step = 2 * side - 1
        for other in at:
            remote(
                source,
                goal,
                halo_s.at[layer, side, half if len(at) == 1 else other],
                halo_r.at[layer, side, half],
                (t + step, 1 - x if other else x),
            )

    def halos_out(layer, half, at, relay):
        @pl.when(t > 0)
        def _():
            halo_out(layer, half, 0, at)

        @pl.when(ci == 0)
        def _():
            halo_out(layer, half, 1, at)

        @pl.when((ci == 1) & (t < 15))
        def _():
            remote(
                hA.at[layer, half, pl.ds(1024, HALO)],
                rel.at[relay],
                rel_s.at[relay, 0],
                rel_r.at[relay],
                sibling,
            )

        @pl.when((ci == 0) & (t < 14))
        def _():
            wait_on(rel.at[relay], rel_r.at[relay])
            goal = hA.at[layer, half, pl.ds(0, HALO)]
            for other in at:
                remote(
                    rel.at[relay],
                    goal,
                    rel_s.at[relay, other],
                    halo_r.at[layer, 1, half],
                    (t + 2, 1 - x if other else x),
                )

    def halos_sent(layer, half, at, relay):
        @pl.when(t > 0)
        def _():
            for other in at:
                wait_on(rel.at[0], halo_s.at[layer, 0, half if len(at) == 1 else other])

        @pl.when(ci == 0)
        def _():
            for other in at:
                wait_on(rel.at[0], halo_s.at[layer, 1, half if len(at) == 1 else other])

        @pl.when((ci == 1) & (t < 15))
        def _():
            wait_on(rel.at[0], rel_s.at[relay, 0])

        @pl.when((ci == 0) & (t < 14))
        def _():
            for other in at:
                wait_on(rel.at[0], rel_s.at[relay, other])

    def halo_wait(layer, half, sems, sides):
        for side, edge in sides:

            @pl.when(t != edge)
            def _():
                wait_on(hA.at[layer, half, pl.ds(0, HALO)], sems.at[layer, side, half])

    ARRIVE = ((1, 0), (0, 15))
    for h in range(2):
        halos_out(0, h, (0,), h)

    remote(src_n, rawn.at[x], xr_s.at[2], xr_r.at[2], partner)
    remote(src_w.at[0], raww.at[x, 0], xr_s.at[3], xr_r.at[3], partner)
    serve(2, 8 + AHEAD)

    def shift_copy(layer, half):
        def one(b, _):
            v = hA[layer, half, pl.ds(pl.multiple_of(b * 128, 128), 144), :].astype(F32)
            hB[half, pl.ds(pl.multiple_of(b * 128, 128), 128), :] = v[8:136].astype(BF)
            return 0

        lax.fori_loop(0, 9, one, 0)


    def rows_of(b):
        return pl.ds(pl.multiple_of(b * 128, 128), 128)

    def local_stats(ref):
        def total(b, acc):
            v = ref[rows_of(b), :].reshape(16, 8, HALF) * frame_mask(b, t, lens[...])
            return acc + jnp.sum(v, axis=0)

        s = jnp.sum(
            lax.fori_loop(0, 8, total, jnp.zeros((8, HALF), F32)), axis=0, keepdims=True
        )
        mean = s / jnp.maximum(nv[t, pl.ds(0, 1), :], 1.0)

        def spread(b, acc):
            v = (ref[rows_of(b), :].reshape(16, 8, HALF) - mean[None]) * frame_mask(
                b, t, lens[...]
            )
            return acc + jnp.sum(v * v, axis=0)

        m2 = jnp.sum(
            lax.fori_loop(0, 8, spread, jnp.zeros((8, HALF), F32)), axis=0, keepdims=True
        )
        return mean, m2

    def put_stats(ref, layer, field):
        mean, m2 = local_stats(ref)
        sp[layer, pl.ds(2 * field, 1), :] = mean
        sp[layer, pl.ds(2 * field + 1, 1), :] = m2

    def combine(at):
        zero = jnp.zeros((8, HALF), F32)
        count = lax.fori_loop(0, 16, lambda s, a: a + nv[s], zero)
        of = lambda s: st[at, lax.div(s, 2), lax.rem(s, 2)]
        mean = lax.fori_loop(0, 16, lambda s, a: a + nv[s] * of(s), zero) / count

        def gather_spread(s, a):
            v = of(s)
            d = v - mean
            return a[0] + nv[s] * d * d, a[1] + v

        between, inside = lax.fori_loop(0, 16, gather_spread, (zero, zero))

        def moments(field):
            m = mean[2 * field : 2 * field + 1]
            q = inside[2 * field + 1 : 2 * field + 2] + between[2 * field : 2 * field + 1]
            return m, lax.rsqrt(q / count[:1] + EPS)

        return moments

    def branch_fields(at, number, inputs):
        for j in range(number):
            total = None
            for lhs, rhs in inputs(j):
                v = jnp.dot(lhs, rhs, preferred_element_type=F32)
                total = v if total is None else total + v
            zb[j] = total
            put_stats(zb.at[j], at, j)
        share(st, sp, at, 8, sems)

    def branches(at, base, number):
        shared(st, at, 8, sems)
        shares = combine(at)
        for j in range(number):
            m, r = shares(j)
            field = base + j
            rs_out[field] = jnp.broadcast_to(r, (8, HALF))
            gain = norm[field, pl.ds(0, 1), :]
            bias = norm[field, pl.ds(1, 1), :]
            if j > 0:
                wait_on(xhb.at[1], out_s.at[10])

            def one(b, _):
                v = (zb[j, rows_of(b), :] - m) * r
                xhb[1, rows_of(b), :] = v
                y = gain * v + bias
                if field > 5:
                    y = y + y5[rows_of(b), :]
                y5[rows_of(b), :] = y
                return 0

            lax.fori_loop(0, 8, one, 0)
            pltpu.make_async_copy(xhb.at[1], xh_out.at[field], out_s.at[10]).start()
        wait_on(xhb.at[1], out_s.at[10])

    def spread_narrow(j):
        for s in range(8):
            spread_half(rawn[s // 4, j, s % 4], s)

        def one(b, _):
            nar[j, rows_of(b), :] = masked_block(b, 0)
            return 0

        lax.fori_loop(0, 8, one, 0)

    def beside_statistics(layer):
        @pl.when(layer == 0)
        def _():
            copies[13].wait()
            wait_on(rawn.at[0], xr_r.at[2])
            spread_narrow(0)

        @pl.when(layer == 1)
        def _():
            mixers_arrived()
            branch_fields(5, 3, lambda j: [(nar[j], wmn[j])])

        @pl.when(layer == 2)
        def _():
            branches(5, 5, 3)

        @pl.when(layer == 3)
        def _():
            wait_on(rawc.at[0], xr_r.at[4])
            for s in range(8):
                spread_half(rawc[s // 4, s % 4], s)

            def one(b, _):
                cotv[rows_of(b), :] = masked_block(b, 0)
                return 0

            lax.fori_loop(0, 8, one, 0)

        @pl.when(layer == 4)
        def _():
            branches(6, 8, 2)

    def beside_exchange(layer):
        @pl.when(layer == 0)
        def _():
            spread_narrow(1)
            spread_narrow(2)

        @pl.when(layer == 1)
        def _():
            wait_on(raww.at[0, 0], xr_r.at[3])
            spread_wide(0)

            def one(b, _):
                for h in range(2):
                    wid[h, rows_of(b), :] = masked_block(b, h)
                return 0

            lax.fori_loop(0, 8, one, 0)

        @pl.when(layer == 2)
        def _():
            copies[14].wait()
            remote(cot.at[:, :, other], rawc.at[x], xr_s.at[4], xr_r.at[4], partner)

            def inputs(j):
                for h in range(2):
                    lhs = wid[h] if j == 0 else hA[0, h, pl.ds(HALO, ROWS), :]
                    yield lhs, wmw[j, pl.ds(HALF * h, HALF), :]

            branch_fields(6, 2, inputs)

    def tile_of(layer, half, at):
        at = pl.multiple_of(at, 256)
        acc = jnp.zeros((256, HALF), F32)
        for k in range(17):
            lhs = (
                hA[layer, half, pl.ds(at + 8 * k, 256), :]
                if k % 2 == 0
                else hB[half, pl.ds(at + 8 * (k - 1), 256), :]
            )
            rhs = W[17 * layer + k, pl.ds(2 * half, 2)].reshape(HALF, HALF)
            acc = acc + jnp.dot(lhs, rhs, preferred_element_type=F32)
        return acc

    PIECES = ((64, 320), (384, 256), (640, 256), (896, 192))

    def layer_step(layer, _):
        base = 8 + 6 * layer + 2 * (layer > 1).astype(jnp.int32)
        weights_arrived(layer)
        pltpu.make_async_copy(
            W.at[pl.ds(17 * layer, 17)], w_out.at[pl.ds(17 * layer, 17)], out_s.at[layer]
        ).start()

        halo_wait(layer, x, halo_r, ARRIVE)
        shift_copy(layer, x)
        def own_tile(j, _):
            z[pl.ds(pl.multiple_of(256 * j, 256), 256), :] = tile_of(layer, x, 256 * j)
            return 0

        lax.fori_loop(0, 4, own_tile, 0)
        service(base + AHEAD, base)

        halo_wait(layer, 1 - x, halo_r, ARRIVE)
        def other_tile(j, _):
            for i, (lo, rows) in enumerate(PIECES):

                @pl.when((layer > 0) & (j == i))
                def _():
                    wait_on(hA.at[layer, 1 - x, pl.ds(lo, rows)], x_r.at[layer, i])

            @pl.when(j == 0)
            def _():
                v = hA[layer, 1 - x, pl.ds(0, 128), :].astype(F32)
                hB[1 - x, pl.ds(0, 112), :] = v[8:120].astype(BF)

            a = pl.multiple_of(256 * j + 112, 16)
            v = hA[layer, 1 - x, pl.ds(a, 272), :].astype(F32)
            hB[1 - x, pl.ds(a, 256), :] = v[8:264].astype(BF)
            rows = pl.ds(pl.multiple_of(256 * j, 256), 256)
            z[rows, :] = z[rows, :] + tile_of(layer, 1 - x, 256 * j)

            @pl.when(j == 1)
            def _():
                service(base + AHEAD + 1, base)

            return 0

        lax.fori_loop(0, 4, other_tile, 0)

        pltpu.make_async_copy(
            hA.at[layer, :, pl.ds(HALO, ROWS)], h_out.at[layer], out_s.at[5 + layer]
        ).start()
        put_stats(z, layer, 0)
        share(st, sp, layer, 2, sems)
        service(base + AHEAD + 2, base)
        service(base + AHEAD + 3, base)
        beside_statistics(layer)
        shared(st, layer, 2, sems)
        moments = combine(layer)

        m, r = moments(0)
        rs_out[layer] = jnp.broadcast_to(r, (8, HALF))
        gain = norm[layer, pl.ds(0, 1), :]
        bias = norm[layer, pl.ds(1, 1), :]

        @pl.when(layer > 0)
        def _():
            wait_on(xhb.at[0], out_s.at[11])

        @pl.when(layer < 4)
        def _():
            def one(b, _):
                rows = pl.ds(pl.multiple_of(b * 64, 64), 64)
                v = (z[rows, :] - m) * r
                xhb[0, rows, :] = v
                y = gain * v + bias
                frames = lax.broadcasted_iota(jnp.int32, (8, 8, HALF), 0) + (b * 8 + t * 128)
                a = (y * jax.nn.sigmoid(y)).reshape(8, 8, HALF)
                a = jnp.where(frames.astype(F32) < lens[...][None], a, 0.0)
                hA[layer + 1, x, pl.ds(pl.multiple_of(HALO + b * 64, 64), 64), :] = a.reshape(
                    64, HALF
                ).astype(BF)
                return 0

            lax.fori_loop(0, 16, one, 0)
            halos_out(layer + 1, x, (0, 1), layer + 2)
            for j, (lo, rows) in enumerate(PIECES):
                ref = hA.at[layer + 1, x, pl.ds(lo, rows)]
                remote(ref, ref, x_s.at[layer + 1, j], x_r.at[layer + 1, j], partner)
        @pl.when(layer == 4)
        def _():
            def one(b, _):
                v = (z[rows_of(b), :] - m) * r
                xhb[0, rows_of(b), :] = v
                y5[rows_of(b), :] = y5[rows_of(b), :] + gain * v + bias
                return 0

            lax.fori_loop(0, 8, one, 0)

        pltpu.make_async_copy(xhb.at[0], xh_out.at[layer], out_s.at[11]).start()

        service(base + AHEAD + 4, base)

        beside_exchange(layer)
        service(base + AHEAD + 5, base)

        @pl.when(layer == 1)
        def _():
            service(base + AHEAD + 6, base)
            service(base + AHEAD + 7, base)

        return 0

    lax.fori_loop(0, 5, layer_step, 0)

    last = [
        (wmn, wmn_out),
        (wmw, wmw_out),
        (y5, y_out),
        (nar, nar_out),
        (wid, wid_out),
        (cotv, cot_out),
    ]
    for i, (a, b) in enumerate(last):
        pltpu.make_async_copy(a, b, out_s.at[12 + i]).start()
    for i, (a, b) in enumerate(last):
        wait_on(a, out_s.at[12 + i])
    wait_on(xhb.at[0], out_s.at[11])
    for i in range(5):
        wait_on(W.at[pl.ds(0, 17)], out_s.at[i])
        wait_on(hA.at[0, :, pl.ds(HALO, ROWS)], out_s.at[5 + i])

    @pl.when(ci == 1)
    def _():
        def drained(g, _):

            @pl.when(inner)
            def _():
                wait_on(chunk(0)(ALL, 0, ALL), ag_s.at[g, 0])

            @pl.when(jnp.logical_not(inner))
            def _():
                wait_on(chunk(0)(pl.ds(0, 2), 0, ALL), ag_s.at[g, 0])

            wait_on(chunk(0)(ALL, 0, ALL), ag_s.at[g, 1])
            wait_on(FIFTEEN, ag_s.at[g, 2])
            return 0

        lax.fori_loop(0, GROUPS, drained, 0)
        wait_on(mixers(THREE, 0, ALL), m_s.at[0])
        wait_on(mixers(ALL, 0, ALL), m_s.at[1])
        wait_on(W.at[pl.ds(0, 35), THREE, 0, 0, pl.ds(0, 16)], m_s.at[2])

    @pl.when(ci == 0)
    def _():
        for layer in range(5):
            wait_on(W.at[pl.ds(0, 17), zi, yi, 0], dl_s.at[layer])
        wait_on(G.at[zi, yi, 0], dl_s.at[5])

    wait_on(lenr.at[0], xr_s.at[0])
    wait_on(raww.at[0, 1], xr_s.at[1])
    wait_on(rawn.at[0], xr_s.at[2])
    wait_on(raww.at[0, 0], xr_s.at[3])
    wait_on(rawc.at[0], xr_s.at[4])

    for h in range(2):
        halos_sent(0, h, (0,), h)

    def finish(layer, _):
        halos_sent(layer, x, (0, 1), layer + 1)
        for j, (lo, rows) in enumerate(PIECES):
            wait_on(hA.at[0, 0, pl.ds(lo, rows)], x_s.at[layer, j])
        return 0

    lax.fori_loop(1, 5, finish, 0)
    for at in range(7):
        share_drained(st, sp, at, 2 if at < 5 else 8, sems)


def run_forward(lens, norm, perm, src_n, src_w, cot, kf, kr, mn, mw):
    vm = pl.BlockSpec(memory_space=pltpu.VMEM)
    hb = pl.BlockSpec(memory_space=pl.ANY)
    dma = pltpu.SemaphoreType.DMA
    S = jax.ShapeDtypeStruct
    return pl.pallas_call(
        forward_kernel,
        out_shape=(
            S((85, 4, 2, 2, 32, HALF), BF),
            S((3, HALF, HALF), BF),
            S((2, 512, HALF), BF),
            S((5, 2, ROWS, HALF), BF),
            S((10, ROWS, HALF), F32),
            S((ROWS, HALF), F32),
            S((3, ROWS, HALF), BF),
            S((2, ROWS, HALF), BF),
            S((ROWS, HALF), BF),
            S((10, 8, HALF), F32),
            S((8, HALF), F32),
        ),
        in_specs=[vm, vm, vm] + [hb] * 7,
        out_specs=[hb] * 9 + [vm, vm],
        scratch_shapes=[
            pltpu.VMEM((85, 4, 2, 2, 32, HALF), BF),
            pltpu.VMEM((4, 2, 2, 112, HALF), BF),
            pltpu.VMEM((3, HALF, HALF), BF),
            pltpu.VMEM((2, 512, HALF), BF),
            pltpu.VMEM((5, 2, 1168, HALF), BF),
            pltpu.VMEM((2, 1152, HALF), BF),
            pltpu.VMEM((ROWS, HALF), F32),
            pltpu.VMEM((3, ROWS, HALF), F32),
            pltpu.VMEM((2, ROWS, HALF), F32),
            pltpu.VMEM((ROWS, HALF), F32),
            pltpu.VMEM((4, ROWS, 128), F32),
            pltpu.VMEM((5, 2, 544, 128), F32),
            pltpu.VMEM((3, 16, HALF), F32),
            pltpu.VMEM((2, 24, HALF), F32),
            pltpu.VMEM((2, 2, 4, 128, 384), BF),
            pltpu.VMEM((2, 3, 4, 128, HALF), BF),
            pltpu.VMEM((2, 4, 128, HALF), BF),
            pltpu.VMEM((3, ROWS, HALF), BF),
            pltpu.VMEM((2, ROWS, HALF), BF),
            pltpu.VMEM((ROWS, HALF), BF),
            pltpu.VMEM((7, 8, 2, 8, HALF), F32),
            pltpu.VMEM((7, 8, HALF), F32),
            pltpu.VMEM((6, HALO, HALF), BF),
            pltpu.VMEM((16, 8, HALF), F32),
            pltpu.VMEM((2, 8, HALF), F32),
            pltpu.VMEM((8, HALF), F32),
            dma((15,)),
            dma((6,)),
            dma((6,)),
            dma((GROUPS, 3)),
            dma((GROUPS,)),
            dma((GROUPS,)),
            dma((GROUPS,)),
            dma((GROUPS,)),
            dma((3,)),
            dma((3,)),
            dma((5, 4)),
            dma((5, 4)),
            dma((5,)),
            dma((5,)),
            dma((5, 2, 2)),
            dma((5, 2, 2)),
            dma((6, 2)),
            dma((6,)),
            dma((7,)),
            dma((7,)),
            dma((7,)),
            dma((7,)),
            dma((7,)),
            dma((7,)),
            dma((18,)),
        ],
        compiler_params=pltpu.CompilerParams(
            collective_id=0, has_side_effects=True, vmem_limit_bytes=62 << 20
        ),
        cost_estimate=pl.CostEstimate(flops=24 * 10**9, bytes_accessed=60 * 10**6, transcendentals=0),
    )(lens, norm, perm, src_n, src_w, cot, kf, kr, mn, mw)


def backward_kernel(
    lens_in,
    norm,
    rs,
    perm,
    w_in,
    wmn,
    wmw,
    h_in,
    xh_in,
    y_in,
    nar_in,
    wid_in,
    cot_in,
    mixed_out,
    gn_out,
    gw_out,
    gf_out,
    gr_out,
    gmn_out,
    gmw_out,
    ng_out,
    total_out,
    Wl,
    Hl,
    Xl,
    xb,
    sb,
    y5,
    da,
    dzA,
    dzB,
    dW,
    crecv,
    yrecv,
    zrecv,
    fin,
    xrecv,
    px,
    pxr,
    stg,
    own_n,
    own_w,
    snd_n,
    snd_w,
    rcv_n,
    rcv_w,
    mix_own,
    mix_rcv,
    Dm,
    cm,
    ym,
    zm,
    fm,
    xm,
    gst,
    gsm,
    bst,
    bsp,
    rel,
    fin0,
    sums4,
    ngr,
    ngx,
    ss,
    load_s,
    w_s,
    br_s,
    halo_s,
    halo_r,
    rel_s,
    rel_r,
    st_a,
    st_b,
    st_c,
    st_d,
    st_e,
    st_f,
    free,
    c_s,
    c_r,
    y_s,
    y_r,
    z_s,
    z_r,
    f_s,
    f_r,
    n_r,
    px_s,
    px_r,
    m_s,
    m_r,
    sn_s,
    sn_r,
    g_s,
    out_s,
    ng_s,
    ng_r,
):
    x, t, zi, yi, ci = position()
    partner = (t, 1 - x)
    sibling = (t + 1 - 2 * ci, x)
    across = (zi * 4 + (1 - yi) * 2 + ci, x)
    sems = (st_a, st_b, st_c, st_d, st_e, st_f)
    lens = lens_in[...]

    def when(cond, f):
        if isinstance(cond, bool):
            if cond:
                f()
        else:
            pl.when(cond)(f)

    def rows_of(b):
        return pl.ds(pl.multiple_of(b * 128, 128), 128)

    def copy_in(src, dst, sem):
        pltpu.make_async_copy(src, dst, sem).start()

    def load_w(layer):
        b2 = lax.rem(layer, 2)
        copy_in(w_in.at[pl.ds(17 * layer, 17)], Wl.at[b2], w_s.at[b2])

    def load_h(layer):
        copy_in(h_in.at[layer], Hl, load_s.at[1])

    def load_x(layer):
        copy_in(xh_in.at[layer], Xl, load_s.at[2])

    copy_in(y_in, y5, load_s.at[3])
    copy_in(cot_in, sb.at[0], load_s.at[4])
    load_x(4)
    copy_in(xh_in.at[5], xb.at[0], br_s.at[0])
    load_w(4)
    load_h(4)

    for edge, lo in ((0, 0), (15, 1088)):

        @pl.when(t == edge)
        def _():
            dzA[:, pl.ds(lo, HALO), :] = jnp.zeros((2, HALO, HALF), BF)

    dzA[:, pl.ds(1152, 16), :] = jnp.zeros((2, 16, HALF), BF)
    bst[...] = jnp.zeros((6, 8, 2, 8, HALF), F32)
    bsp[...] = jnp.zeros((6, 8, HALF), F32)
    greet(x, t)

    zero = jnp.zeros((8, HALF), F32)
    count = jnp.zeros((1, HALF), F32)
    for s in range(16):
        count = count + jnp.sum(jnp.clip(lens - 128.0 * s, 0.0, 128.0), axis=0, keepdims=True)

    def mask(b):
        return frame_mask(b, t, lens)

    def sequence(block, s):
        return stg[block, pl.ds(s, 128, stride=8), :]

    def unstage(blocks, own, send):
        for i in range(4):
            for b in range(blocks):
                own(i, b, sequence(b, 4 * x + i))
                send(i, b, sequence(b, 4 * (1 - x) + i))

    def mix_put(ref):
        def put(i, b, v):
            ref[i, :, pl.ds(128 * b, 128)] = v.astype(BF)

        return put

    my_cols = pl.ds(pl.multiple_of(x * HALF, HALF), HALF)
    other_cols = pl.ds(pl.multiple_of((1 - x) * HALF, HALF), HALF)

    def send_mixed():
        unstage(2, mix_put(mix_own), mix_put(snd_w.at[2]))
        remote(
            snd_w.at[2, :, :, pl.ds(0, HALF)], mix_rcv, sn_s.at[0], sn_r.at[0], partner
        )
        copy_in(mix_own, mixed_out.at[:, :, my_cols], out_s.at[0])

    ORDER = (0, 3, 1, 2)

    def on_second(f):
        pl.when(ci == 1)(f)

    def send_core(layer, zs):
        b2 = lax.rem(layer, 2)

        @pl.when(ci == 0)
        def _():
            for zz in zs:
                when(layer < 4, lambda: pl.semaphore_wait(free.at[zz], 1))
                remote(dW.at[b2, :, zz], crecv.at[:, zz], c_s.at[layer], c_r.at[layer, zz], sibling)

    def add_core(layer, u, n=17):
        b3, b2 = lax.rem(layer, 3), lax.rem(layer, 2)
        zz, lo = ORDER[u // 2], n * (u % 2)

        @on_second
        def _():
            if u % 2 == 0:
                wait_on(crecv.at[:, zz], c_r.at[layer, zz])

            def one(k, _):
                for yy in range(2):
                    for cc in range(2):
                        dW[b2, k, zz, yy, cc] = (
                            dW[b2, k, zz, yy, cc].astype(F32) + crecv[k, zz, yy, cc].astype(F32)
                        ).astype(BF)
                return 0

            lax.fori_loop(lo, lo + n, one, 0)
            remote(
                dW.at[b2, pl.ds(lo, n), zz, 1 - yi],
                yrecv.at[b3, pl.ds(lo, n), zz],
                y_s.at[layer],
                y_r.at[layer, u],
                across,
            )
            if u % 2 == 1:

                def give():
                    pl.semaphore_signal(
                        free.at[zz], inc=1, device_id=sibling, device_id_type=MESH
                    )

                when(layer > 0, give)

    def add_across(layer, u, n=17):
        b3, b2 = lax.rem(layer, 3), lax.rem(layer, 2)
        zz, lo = ORDER[u // 2], n * (u % 2)

        @on_second
        def _():
            wait_on(yrecv.at[b3, pl.ds(lo, n), zz], y_r.at[layer, u])

            def one(k, _):
                for cc in range(2):
                    dW[b2, k, zz, yi, cc] = (
                        dW[b2, k, zz, yi, cc].astype(F32) + yrecv[b3, k, zz, cc].astype(F32)
                    ).astype(BF)
                return 0

            lax.fori_loop(lo, lo + n, one, 0)

            @pl.when(zi != zz)
            def _():
                remote(
                    dW.at[b2, pl.ds(lo, n), zz, yi],
                    zrecv.at[b3, lax.rem(zi + 3 - zz, 4), pl.ds(lo, n)],
                    z_s.at[layer, u % 2],
                    z_r.at[layer, u % 2],
                    (zz * 4 + yi * 2 + 1, x),
                )

    def finish_sum(layer, half, n=17):
        b3, b2 = lax.rem(layer, 3), lax.rem(layer, 2)
        lo = n * half

        @on_second
        def _():
            wait_on(zrecv.at[b3, :, pl.ds(lo, n)], z_r.at[layer, half])
            if half == 0:

                def sent():
                    wait_on(fin.at[0], f_s.at[layer + 2, 0])
                    wait_on(fin.at[0], f_s.at[layer + 2, 1])
                    wait_on(fin.at[0], f_s.at[layer + 2, 2])

                when(layer + 2 <= 4, sent)

            def one(k, _):
                for cc in range(2):
                    v = dW[b2, k, zi, yi, cc].astype(F32)
                    for q in range(3):
                        v = v + zrecv[b3, q, k, cc].astype(F32)
                    if cc == 1:
                        fin[b3, k] = v.astype(BF)
                    else:
                        fin0[b2, k] = v.astype(BF)
                return 0

            lax.fori_loop(lo, lo + n, one, 0)
            mine = pl.ds(lo, n)
            remote(
                fin0.at[b2, mine],
                fin.at[b3, mine],
                f_s.at[layer, 0],
                n_r.at[layer, half],
                sibling,
            )
            remote(
                fin.at[b3, mine],
                xrecv.at[layer, mine],
                f_s.at[layer, 1],
                f_r.at[layer, half],
                partner,
            )
            remote(
                fin0.at[b2, mine],
                xrecv.at[layer, mine],
                f_s.at[layer, 2],
                f_r.at[layer, half],
                (t - 1, 1 - x),
            )

    def add_square(v):
        ss[...] += jnp.sum((v * v).reshape(-1, 8, 128), axis=0)

    def assemble(layer, put, n=17):
        rows = 32 if n == 17 else 24
        for half in range(2):

            @pl.when(ci == 0)
            def _():
                wait_on(fin.at[0, pl.ds(n * half, n)], n_r.at[layer, half])

            wait_on(xrecv.at[layer, pl.ds(n * half, n)], f_r.at[layer, half])
        for source, side in ((fin.at[lax.rem(layer, 3)], x), (xrecv.at[layer], 1 - x)):
            for b in range(2):
                lanes = pl.ds(128 * b, 128)
                def rest_row(k, _):
                    v = source[pl.ds(2 * k, 2), :, lanes].astype(F32).reshape(32, 128)
                    gst[2 * side + b, pl.ds(k, 32, stride=17), :] = v
                    return 0

                if n == 17:
                    lax.fori_loop(0, 17, rest_row, 0)
                else:
                    for k in range(17):
                        lo = 3 * (k // 2) + k % 2
                        v = source[pl.ds(lo, 2), :, lanes].astype(F32).reshape(32, 128)
                        v = v[8 * (k % 2) : 8 * (k % 2) + 24]
                        gst[2 * side + b, pl.ds(k, rows, stride=17), :] = v
        for b in range(4):
            add_square(gst[b, pl.ds(0, rows * 17), :])
            copy_in(gst.at[b, pl.ds(0, rows * 17)], put(b), g_s)

    def wait_assembled(rows):
        wait_on(gst.at[:, pl.ds(0, rows * 17)], g_s)

    def drain_sums(layer, n=17):
        @pl.when(ci == 0)
        def _():
            wait_on(crecv, c_s.at[layer])

        @on_second
        def _():
            wait_on(yrecv.at[0, pl.ds(0, 2 * n)], y_s.at[layer])
            for half in range(2):
                wait_on(zrecv.at[0, :, pl.ds(0, n)], z_s.at[layer, half])

    def put_rest(layer):
        return lambda b: gr_out.at[layer - 1, :, pl.ds(128 * b, 128)]

    def mixers_one():
        remote(Dm.at[:, :, 1 - ci], cm, m_s.at[0], m_r.at[0], sibling)

    def mixers_two():
        wait_on(cm, m_r.at[0])
        for zz in range(4):
            for yy in range(2):
                Dm[zz, yy, ci] = (Dm[zz, yy, ci].astype(F32) + cm[zz, yy].astype(F32)).astype(BF)
        remote(Dm.at[:, 1 - yi, ci], ym, m_s.at[1], m_r.at[1], across)

    def mixers_three():
        wait_on(ym, m_r.at[1])
        for zz in range(4):
            Dm[zz, yi, ci] = (Dm[zz, yi, ci].astype(F32) + ym[zz].astype(F32)).astype(BF)
        for q in range(3):
            zz = lax.rem(zi + 1 + q, 4)
            remote(Dm.at[zz, yi, ci], zm.at[q], m_s.at[2], m_r.at[2], (zz * 4 + yi * 2 + ci, x))

    def mixers_four():
        wait_on(zm, m_r.at[2])
        v = Dm[zi, yi, ci].astype(F32)
        for q in range(3):
            v = v + zm[q].astype(F32)
        fm[...] = v.astype(BF)
        remote(fm, xm, m_s.at[3], m_r.at[3], partner)

    def mixers_five():
        wait_on(xm, m_r.at[3])
        for b in range(2):
            lanes = pl.ds(128 * b, 128)
            gsm[2 * x + b] = fm[:, lanes].astype(F32)
            gsm[2 * (1 - x) + b] = xm[:, lanes].astype(F32)
        for b in range(4):
            add_square(gsm[b])
            for j in range(3):
                copy_in(
                    gsm.at[b, pl.ds(16 * j, 16)],
                    gmn_out.at[j, :, pl.ds(128 * b, 128)],
                    out_s.at[1],
                )
            for j in range(2):
                copy_in(
                    gsm.at[b, pl.ds(48 + 32 * j, 24)],
                    gmw_out.at[j, :, pl.ds(128 * b, 128)],
                    out_s.at[2],
                )

    def halos_out(layer):
        b2 = lax.rem(layer, 2)
        low, high = dzA.at[b2, pl.ds(HALO, HALO)], dzA.at[b2, pl.ds(1024, HALO)]
        above, below = dzA.at[b2, pl.ds(1088, HALO)], dzA.at[b2, pl.ds(0, HALO)]

        @pl.when(ci == 1)
        def _():
            remote(low, above, halo_s.at[layer, 0], halo_r.at[layer, 0], sibling)

        @pl.when((ci == 1) & (t < 15))
        def _():
            remote(high, rel.at[layer], halo_s.at[layer, 1], rel_r.at[layer], sibling)

        @pl.when((ci == 0) & (t > 0))
        def _():
            remote(low, above, halo_s.at[layer, 0], halo_r.at[layer, 0], (t - 1, x))

        @pl.when(ci == 0)
        def _():
            remote(high, below, halo_s.at[layer, 1], halo_r.at[layer, 1], sibling)

        @pl.when((ci == 0) & (t < 14))
        def _():
            wait_on(rel.at[layer], rel_r.at[layer])
            remote(rel.at[layer], below, rel_s.at[layer], halo_r.at[layer, 1], (t + 2, x))

    def halo_sent(layer):
        for side, edge in ((0, 0), (1, 15)):

            @pl.when(t != edge)
            def _():
                wait_on(dzA.at[0, pl.ds(0, HALO)], halo_s.at[layer, side])

    def output_gradient(layer, last):
        wait_on(Xl, load_s.at[2])
        if last:
            wait_on(y5, load_s.at[3])
            wait_on(sb.at[0], load_s.at[4])
        gain = norm[layer, pl.ds(0, 1), :]
        bias = norm[layer, pl.ds(1, 1), :]

        def one(b, acc):
            xh = Xl[rows_of(b), :]
            if last:
                y = y5[rows_of(b), :]
                d = sb[0, rows_of(b), :].astype(F32)
            else:
                y = gain * xh + bias
                d = da[rows_of(b), :] + pxr[1 - lax.rem(layer, 2), rows_of(b), :].astype(F32)
            sg = jax.nn.sigmoid(y)
            m = mask(b)
            if last:
                a = ((y * sg).reshape(16, 8, HALF) * m).reshape(128, HALF)
                for i in range(2):
                    stg[i, rows_of(b), :] = a[:, 128 * i : 128 * i + 128]
            v = (d * sg * (1.0 + y * (1.0 - sg))).reshape(16, 8, HALF) * m
            s0 = acc[0] + jnp.sum(v, axis=0)
            s1 = acc[1] + jnp.sum(v * xh.reshape(16, 8, HALF), axis=0)
            v = v.reshape(128, HALF)
            da[rows_of(b), :] = v
            if last:
                y5[rows_of(b), :] = v
            return s0, s1

        if last:
            s0, s1 = lax.fori_loop(0, 8, one, (zero, zero))
        else:
            s0, s1 = zero, zero
            for j in range(4):
                wait_on(pxr.at[0, pl.ds(0, 256)], px_r.at[layer + 1, j])
                s0, s1 = lax.fori_loop(2 * j, 2 * j + 2, one, (s0, s1))
        bsp[layer, pl.ds(0, 1), :] = jnp.sum(s0, axis=0, keepdims=True)
        bsp[layer, pl.ds(1, 1), :] = jnp.sum(s1, axis=0, keepdims=True)
        if last:
            for j in range(5):
                wait_on(xb.at[0], br_s.at[0])

                def branch(b, acc):
                    return acc + jnp.sum(
                        (da[rows_of(b), :] * xb[0, rows_of(b), :]).reshape(16, 8, HALF), axis=0
                    )

                sj = lax.fori_loop(0, 8, branch, zero)
                if j < 4:
                    copy_in(xh_in.at[6 + j], xb.at[0], br_s.at[0])
                bsp[layer, pl.ds(2 + j, 1), :] = jnp.sum(sj, axis=0, keepdims=True)
        share(bst, bsp, layer, 8 if last else 2, sems)

    def field_gradient(layer, last):
        shared(bst, layer, 8 if last else 2, sems)
        gain = norm[layer, pl.ds(0, 1), :]
        sums = lax.fori_loop(
            0, 16, lambda s, a: a + bst[layer, lax.div(s, 2), lax.rem(s, 2)], zero
        )
        ngr[layer, pl.ds(0, 1), :] = sums[1:2]
        ngr[layer, pl.ds(1, 1), :] = sums[0:1]
        if last:
            sums4[...] = sums
            for j in range(5):
                ngr[5 + j, pl.ds(0, 1), :] = sums[2 + j : 3 + j]
                ngr[5 + j, pl.ds(1, 1), :] = sums[0:1]
        r = rs[layer, pl.ds(0, 1), :]
        c0 = gain * sums[0:1] / count
        c1 = gain * sums[1:2] / count
        b2 = lax.rem(layer, 2)

        def dz_block(b, _):
            m = mask(b)
            v = (gain * da[rows_of(b), :]).reshape(16, 8, HALF)
            xh = Xl[rows_of(b), :].reshape(16, 8, HALF)
            v = r * (v - m * c0 - m * xh * c1)
            dzA[b2, pl.ds(pl.multiple_of(HALO + b * 128, 64), 128), :] = v.reshape(
                128, HALF
            ).astype(BF)
            return 0

        when(layer + 2 <= 4, lambda: halo_sent(layer + 2))
        lax.fori_loop(0, 8, dz_block, 0)
        halos_out(layer)

    def halo_arrived(layer):
        b2 = lax.rem(layer, 2)
        for side, edge in ((1, 0), (0, 15)):

            @pl.when(t != edge)
            def _():
                wait_on(dzA.at[b2, pl.ds(0, HALO)], halo_r.at[layer, side])

        def one(b, _):
            v = dzA[b2, pl.ds(pl.multiple_of(b * 128, 128), 144), :].astype(F32)
            dzB[pl.ds(pl.multiple_of(b * 128, 128), 128), :] = v[8:136].astype(BF)
            return 0

        lax.fori_loop(0, 9, one, 0)

    def shifted(b2, k, lo=0, rows=ROWS):
        o = 16 - k
        if o % 2 == 0:
            return dzA[b2, pl.ds(8 * o + lo, rows), :]
        return dzB[pl.ds(8 * (o - 1) + lo, rows), :]

    def data_tile(layer, half, j):
        b2 = lax.rem(layer, 2)
        lo = pl.multiple_of(256 * j, 256)
        acc = jnp.zeros((256, HALF), F32)
        for k in range(17):
            acc = acc + lax.dot_general(
                shifted(b2, k, lo, 256),
                Wl[b2, k, pl.ds(2 * half, 2)].reshape(HALF, HALF),
                (((1,), (1,)), ((), ())),
                preferred_element_type=F32,
            )
        return acc

    def weight_tap(h, dz):
        return lax.dot_general(
            Hl[h], dz, (((0,), (0,)), ((), ())), preferred_element_type=F32
        ).reshape(2, 2, 2, 32, HALF)

    def even_tap(b2, i):
        return dzA[b2, pl.ds(pl.multiple_of(128 - 16 * i, 16), ROWS), :]

    def odd_tap(i):
        return dzB[pl.ds(pl.multiple_of(112 - 16 * i, 16), ROWS), :]

    def weight_gradient(layer, h):
        b2 = lax.rem(layer, 2)

        def put(k, v):
            for part in range(2):
                dW[b2, 2 * k + part, pl.ds(2 * h, 2)] = v[
                    :, :, :, 16 * part : 16 * part + 16
                ].astype(BF)

        def pair(i, _):
            put(2 * i, weight_tap(h, even_tap(b2, i)))
            put(2 * i + 1, weight_tap(h, odd_tap(i)))
            return 0

        lax.fori_loop(0, 8, pair, 0)
        put(16, weight_tap(h, even_tap(b2, 8)))

    def first_weight_gradient(h):
        def put(at, v, blocks):
            for part in range(blocks):
                dW[0, at + part, pl.ds(2 * h, 2)] = v[
                    :, :, :, 16 * part : 16 * part + 16
                ].astype(BF)

        def pair(i, _):
            v = [weight_tap(h, dz)[:, :, :, :24] for dz in (even_tap(0, i), odd_tap(i))]
            put(3 * i, jnp.concatenate(v, axis=3), 3)
            return 0

        lax.fori_loop(0, 8, pair, 0)
        v = weight_tap(h, even_tap(0, 8))[:, :, :, :24]
        put(24, jnp.concatenate([v, jnp.zeros((2, 2, 2, 8, HALF), F32)], axis=3), 2)

    def load_branch(j):
        copy_in(xh_in.at[5 + j], xb.at[0], br_s.at[0])
        if j < 3:
            copy_in(nar_in.at[j], sb.at[0], br_s.at[2])
        elif j == 3:
            copy_in(wid_in, sb, br_s.at[2])
        else:
            copy_in(h_in.at[0], sb, br_s.at[2])

    def branch(j):
        field = 5 + j
        sums = sums4[...]
        wait_on(xb.at[0], br_s.at[0])
        wait_on(sb.at[0] if j < 3 else sb, br_s.at[2])
        gain = norm[field, pl.ds(0, 1), :]
        r = rs[field, pl.ds(0, 1), :]
        c0 = gain * sums[0:1] / count
        c1 = gain * sums[2 + j : 3 + j] / count

        def one(b, _):
            m = mask(b)
            v = (gain * y5[rows_of(b), :]).reshape(16, 8, HALF)
            xh = xb[0, rows_of(b), :].reshape(16, 8, HALF)
            v = r * (v - m * c0 - m * xh * c1)
            px[1, rows_of(b), :] = v.reshape(128, HALF).astype(BF)
            return 0

        lax.fori_loop(0, 8, one, 0)
        dv = px[1]
        if j < 3:
            v = lax.dot_general(
                sb[0], dv, (((0,), (0,)), ((), ())), preferred_element_type=F32
            )
            Dm[:, :, :, pl.ds(16 * j, 16), :] = v.reshape(4, 2, 2, 16, HALF).astype(BF)
            back = lax.dot_general(
                dv, wmn[j], (((1,), (1,)), ((), ())), preferred_element_type=F32
            )
            blocks = 2
        else:
            i = j - 3
            for h in range(2):
                v = lax.dot_general(
                    sb[h], dv, (((0,), (0,)), ((), ())), preferred_element_type=F32
                )
                Dm[pl.ds(2 * h, 2), :, :, pl.ds(48 + 32 * i, 32), :] = v.reshape(
                    2, 2, 2, 32, HALF
                ).astype(BF)
            wu = jnp.dot(perm[...], wmw[i], preferred_element_type=F32).astype(BF)
            back = lax.dot_general(
                dv, wu, (((1,), (1,)), ((), ())), preferred_element_type=F32
            )
            blocks = 3
        if j < 4:
            load_branch(j + 1)
        for b in range(8):
            m = mask(b)[:, :, :128]
            for i in range(blocks):
                v = back[128 * b : 128 * b + 128, 128 * i : 128 * i + 128]
                stg[i, pl.ds(128 * b, 128), :] = (v.reshape(16, 8, 128) * m).reshape(128, 128)
        if j < 3:

            def put_own(i, b, v):
                own_n[j, i, :, pl.ds(128 * b, 128)] = v

            def put_send(i, b, v):
                snd_n[j, i, :, pl.ds(128 * b, 128)] = v.astype(BF)

        else:

            def put_own(i, b, v):
                own_w[j - 3, i, :, pl.ds(128 * b, 128)] = v

            def put_send(i, b, v):
                snd_w[j - 3, i, :, pl.ds(128 * b, 128)] = v.astype(BF)

        unstage(blocks, put_own, put_send)
        if j < 3:
            remote(snd_n.at[j], rcv_n.at[j], sn_s.at[1 + j], sn_r.at[1 + j], partner)
        else:
            remote(snd_w.at[j - 3], rcv_w.at[j - 3], sn_s.at[1 + j], sn_r.at[1 + j], partner)

    def sources_narrow():
        for j in range(3):
            wait_on(rcv_n.at[j], sn_r.at[1 + j])
        own_n[...] = own_n[...] + rcv_n[...].astype(F32)
        copy_in(own_n, gn_out, out_s.at[3])

    def chain(layer, last):
        b2 = lax.rem(layer, 2)
        one = layer + 1
        two = lambda f: when(layer + 2 <= 4, lambda: f(layer + 2))
        load_w(layer - 1)
        output_gradient(layer, last)
        if last:
            send_mixed()
            load_branch(0)
        else:

            def two_a(older):
                add_across(older, 6)
                add_across(older, 7)

            two(two_a)
            add_core(one, 0)
            add_core(one, 1)
        field_gradient(layer, last)
        load_x(layer - 1)
        if not last:
            add_core(one, 2)
            add_core(one, 3)
        halo_arrived(layer)
        wait_on(Wl.at[0], w_s.at[b2])
        def other_tile(j, _):
            if not last:
                wait_on(px.at[0, pl.ds(0, 256)], px_s.at[j])
            rows = pl.ds(pl.multiple_of(256 * j, 256), 256)
            px[0, rows, :] = data_tile(layer, 1 - x, j).astype(BF)
            remote(px.at[0, rows], pxr.at[b2, rows], px_s.at[j], px_r.at[layer, j], partner)
            if not last:

                @pl.when(j == 1)
                def _():
                    add_core(one, 4)
                    add_core(one, 5)
                    add_across(one, 0)

            return 0

        lax.fori_loop(0, 4, other_tile, 0)
        if not last:
            two(lambda older: finish_sum(older, 0))
        def own_tile(j, _):
            da[pl.ds(pl.multiple_of(256 * j, 256), 256), :] = data_tile(layer, x, j)
            return 0

        lax.fori_loop(0, 4, own_tile, 0)
        if not last:
            add_core(one, 6)
            add_core(one, 7)
            add_across(one, 1)
            add_across(one, 2)
            two(lambda older: finish_sum(older, 1))
            two(drain_sums)
        wait_on(Hl, load_s.at[1])
        weight_gradient(layer, 0)
        send_core(layer, (0, 1))
        if not last:
            add_across(one, 3)
        weight_gradient(layer, 1)
        send_core(layer, (2, 3))
        load_h(layer - 1)
        if not last:
            add_across(one, 4)
            add_across(one, 5)

            def two_out(older):
                when(layer + 3 <= 4, lambda: wait_assembled(32))
                assemble(older, put_rest(older))

            two(two_out)

    ss[...] = jnp.zeros((8, 128), F32)
    chain(4, True)
    branch(0)

    def middle(i, _):
        layer = 3 - i
        chain(layer, False)

        @pl.when(layer == 3)
        def _():
            branch(1)
            branch(2)
            wait_on(mix_rcv, sn_r.at[0])
            copy_in(mix_rcv, mixed_out.at[:, :, other_cols], out_s.at[4])

        @pl.when(layer == 2)
        def _():
            branch(3)
            branch(4)
            mixers_one()
            sources_narrow()

        @pl.when(layer == 1)
        def _():
            mixers_two()

        return 0

    lax.fori_loop(0, 3, middle, 0)

    output_gradient(0, False)
    add_across(2, 6)
    add_across(2, 7)
    add_core(1, 0)
    add_core(1, 1)
    field_gradient(0, False)
    add_core(1, 2)
    add_core(1, 3)
    halo_arrived(0)
    wait_on(Hl, load_s.at[1])
    wait_on(Wl.at[0], w_s.at[0])
    add_core(1, 4)
    add_core(1, 5)
    add_across(1, 0)
    finish_sum(2, 0)
    finish_sum(2, 1)
    drain_sums(2)
    add_core(1, 6)
    add_core(1, 7)
    first_weight_gradient(0)
    send_core(0, (0, 1))
    add_across(1, 1)
    add_across(1, 2)
    first_weight_gradient(1)
    send_core(0, (2, 3))
    add_across(1, 3)
    mixers_three()

    remote(ngr, ngx, ng_s, ng_r, partner)

    for k in range(17):
        Wl[1, k, pl.ds(0, 3)] = (
            jnp.dot(perm[...], Wl[0, k].reshape(512, HALF), preferred_element_type=F32)
            .astype(BF)
            .reshape(3, 2, 2, 32, HALF)
        )
    add_across(1, 4)
    add_core(0, 0, 13)
    add_across(1, 5)
    add_core(0, 1, 13)
    mixers_four()
    for part in range(4):
        acc = jnp.zeros((HALF, 384), F32)
        for k in range(17):
            o = 16 - k
            lo = part * HALF
            lhs = (
                dzA[0, pl.ds(8 * o + lo, HALF), :]
                if o % 2 == 0
                else dzB[pl.ds(8 * (o - 1) + lo, HALF), :]
            )
            acc = acc + lax.dot_general(
                lhs,
                Wl[1, k, pl.ds(0, 3)].reshape(384, HALF),
                (((1,), (1,)), ((), ())),
                preferred_element_type=F32,
            )
        for half in range(2):
            m = mask(2 * part + half)[:, :, :128]
            for b in range(3):
                stg[b, pl.ds(part * HALF + half * 128, 128), :] = (
                    acc[128 * half : 128 * half + 128, 128 * b : 128 * b + 128].reshape(
                        16, 8, 128
                    )
                    * m
                ).reshape(128, 128)
        if part == 0:
            add_across(1, 6)
            add_core(0, 2, 13)
            add_core(0, 3, 13)
        if part == 1:
            add_across(1, 7)
            add_core(0, 4, 13)
            add_core(0, 5, 13)
        if part == 2:
            add_across(0, 0, 13)
            add_core(0, 6, 13)
            add_core(0, 7, 13)
        if part == 3:
            add_across(0, 1, 13)
            finish_sum(1, 0)
            finish_sum(1, 1)

    def put_own(i, b, v):
        lanes = pl.ds(128 * b, 128)
        own_w[1, i, :, lanes] = own_w[1, i, :, lanes] + v

    def put_send(i, b, v):
        snd_w[2, i, :, pl.ds(128 * b, 128)] = v.astype(BF)

    wait_on(mix_own, sn_s.at[0])
    unstage(3, put_own, put_send)
    remote(snd_w.at[2], rcv_w.at[2], sn_s.at[6], sn_r.at[6], partner)
    add_across(0, 2, 13)
    wait_assembled(32)
    assemble(2, put_rest(2))
    add_across(0, 3, 13)
    mixers_five()
    add_across(0, 4, 13)
    wait_assembled(32)
    assemble(1, put_rest(1))
    for j in range(2):
        wait_on(rcv_w.at[j], sn_r.at[4 + j])
    wait_on(rcv_w.at[2], sn_r.at[6])
    for j in range(2):
        v = own_w[j] + rcv_w[j].astype(F32)
        if j == 1:
            v = v + rcv_w[2].astype(F32)
        own_w[j] = v
    copy_in(own_w, gw_out, out_s.at[5])
    add_across(0, 5, 13)
    add_across(0, 6, 13)
    finish_sum(0, 0, 13)
    add_across(0, 7, 13)
    finish_sum(0, 1, 13)
    wait_on(ngx, ng_r)
    wait_assembled(32)
    assemble(0, lambda b: gf_out.at[:, pl.ds(128 * b, 128)], 13)

    bsp[5, :, pl.ds(0, 128)] = ss[...]
    share(bst, bsp, 5, 8, sems)
    mine, theirs = ngr[...], ngx[...]
    left = jnp.where(x == 0, mine, theirs)
    right = jnp.where(x == 0, theirs, mine)
    rows = lax.broadcasted_iota(jnp.int32, (10, 8, HALF), 1)
    left = jnp.where(rows < 2, left, 0.0)
    right = jnp.where(rows < 2, right, 0.0)
    ng_out[0] = left
    ng_out[1] = right
    norms = jnp.sum(left * left + right * right)
    shared(bst, 5, 8, sems)
    every = lax.fori_loop(0, 16, lambda s, a: a + bst[5, lax.div(s, 2), lax.rem(s, 2)], zero)
    total_out[...] = jnp.zeros((8, 128), F32) + (jnp.sum(every) + norms)

    wait_assembled(24)
    wait_on(mix_own, out_s.at[0])
    wait_on(mix_rcv, out_s.at[4])
    wait_on(own_n, out_s.at[3])
    wait_on(own_w, out_s.at[5])
    wait_on(gsm.at[:, pl.ds(0, 48)], out_s.at[1])
    wait_on(gsm.at[:, pl.ds(0, 48)], out_s.at[2])
    for j in range(4):
        wait_on(px.at[0, pl.ds(0, 256)], px_s.at[j])
    for j in range(3):
        wait_on(snd_n.at[0], sn_s.at[1 + j])
        wait_on(snd_w.at[0], sn_s.at[4 + j])
    wait_on(cm, m_s.at[0])
    wait_on(ym, m_s.at[1])
    wait_on(zm, m_s.at[2])
    wait_on(fm, m_s.at[3])
    wait_on(ngr, ng_s)
    drain_sums(1)
    drain_sums(0, 13)

    for layer in range(2):
        halo_sent(layer)

        @on_second
        def _():
            for i in range(3):
                wait_on(fin.at[0, pl.ds(0, 34 if layer else 26)], f_s.at[layer, i])

    for layer in range(5):

        @pl.when((ci == 0) & (t < 14))
        def _():
            wait_on(rel.at[0], rel_s.at[layer])

    for layer in range(6):
        share_drained(bst, bsp, layer, 2 if layer < 4 else 8, sems)


def run_backward(lens, norm, rs, perm, w, wmn, wmw, h, xh, y, nar, wid, cot):
    vm = pl.BlockSpec(memory_space=pltpu.VMEM)
    hb = pl.BlockSpec(memory_space=pl.ANY)
    dma = pltpu.SemaphoreType.DMA
    S = jax.ShapeDtypeStruct
    V = pltpu.VMEM
    return pl.pallas_call(
        backward_kernel,
        out_shape=(
            S((4, 128, 512), BF),
            S((3, 4, 128, HALF), F32),
            S((2, 4, 128, 384), F32),
            S((408, 512), F32),
            S((4, 544, 512), F32),
            S((3, 16, 512), F32),
            S((2, 24, 512), F32),
            S((2, 10, 8, HALF), F32),
            S((8, 128), F32),
        ),
        in_specs=[vm, vm, vm, vm, hb, vm, vm, hb, hb, hb, hb, hb, hb],
        out_specs=[hb] * 7 + [vm, vm],
        scratch_shapes=[
            V((2, 17, 4, 2, 2, 32, HALF), BF),
            V((2, ROWS, HALF), BF),
            V((ROWS, HALF), F32),
            V((1, ROWS, HALF), F32),
            V((2, ROWS, HALF), BF),
            V((ROWS, HALF), F32),
            V((ROWS, HALF), F32),
            V((2, 1168, HALF), BF),
            V((1152, HALF), BF),
            V((2, 34, 4, 2, 2, 16, HALF), BF),
            V((34, 4, 2, 2, 16, HALF), BF),
            V((3, 34, 4, 2, 16, HALF), BF),
            V((3, 3, 34, 2, 16, HALF), BF),
            V((3, 34, 16, HALF), BF),
            V((5, 34, 16, HALF), BF),
            V((2, ROWS, HALF), BF),
            V((2, ROWS, HALF), BF),
            V((3, ROWS, 128), F32),
            V((3, 4, 128, HALF), F32),
            V((2, 4, 128, 384), F32),
            V((3, 4, 128, HALF), BF),
            V((3, 4, 128, 384), BF),
            V((3, 4, 128, HALF), BF),
            V((3, 4, 128, 384), BF),
            V((4, 128, HALF), BF),
            V((4, 128, HALF), BF),
            V((4, 2, 2, 112, HALF), BF),
            V((4, 2, 112, HALF), BF),
            V((4, 112, HALF), BF),
            V((3, 112, HALF), BF),
            V((112, HALF), BF),
            V((112, HALF), BF),
            V((4, 544, 128), F32),
            V((4, 112, 128), F32),
            V((6, 8, 2, 8, HALF), F32),
            V((6, 8, HALF), F32),
            V((5, HALO, HALF), BF),
            V((2, 34, 16, HALF), BF),
            V((8, HALF), F32),
            V((10, 8, HALF), F32),
            V((10, 8, HALF), F32),
            V((8, 128), F32),
            dma((5,)),
            dma((2,)),
            dma((3,)),
            dma((5, 2)),
            dma((5, 2)),
            dma((5,)),
            dma((5,)),
            dma((6,)),
            dma((6,)),
            dma((6,)),
            dma((6,)),
            dma((6,)),
            dma((6,)),
            pltpu.SemaphoreType.REGULAR((4,)),
            dma((5,)),
            dma((5, 4)),
            dma((5,)),
            dma((5, 8)),
            dma((5, 2)),
            dma((5, 2)),
            dma((5, 3)),
            dma((5, 2)),
            dma((5, 2)),
            dma((4,)),
            dma((5, 4)),
            dma((4,)),
            dma((4,)),
            dma((7,)),
            dma((7,)),
            dma,
            dma((6,)),
            dma,
            dma,
        ],
        compiler_params=pltpu.CompilerParams(
            collective_id=1, has_side_effects=True, vmem_limit_bytes=63 << 20
        ),
        cost_estimate=pl.CostEstimate(flops=46 * 10**9, bytes_accessed=60 * 10**6, transcendentals=0),
    )(lens, norm, rs, perm, w, wmn, wmw, h, xh, y, nar, wid, cot)


def prepare(lengths, norm_params):
    x = lax.axis_index("batch")
    mine = jnp.broadcast_to(lengths.astype(F32)[:, None], (4, HALF))
    lens = jnp.zeros((8, HALF), F32)
    lens = lax.dynamic_update_slice(lens, mine, (4 * x, 0))
    half = lax.dynamic_slice(norm_params, (0, 0, x * HALF), (2, 10, HALF))
    norm = jnp.pad(jnp.transpose(half, (1, 0, 2)), ((0, 0), (0, 6), (0, 0)))
    places = np.arange(384)
    perm = np.zeros((384, 512), np.float32)
    perm[places, (places // 24) * 32 + places % 24] = 1.0
    return lens, norm, jnp.asarray(perm, BF)


def body_split(
    source_narrow,
    source_wide,
    lengths,
    cotangent,
    kernel_first,
    kernel_rest,
    mixer_narrow,
    mixer_wide,
    norm_params,
    moment_first,
    square_first,
    moment_rest,
    square_rest,
    moment_narrow,
    square_narrow,
    moment_wide,
    square_wide,
    moment_norm,
    square_norm,
):
    lens, norm, perm = prepare(lengths, norm_params)
    w, wmn, wmw, h, xh, y, nar, wid, cot, rs, lens = run_forward(
        lens,
        norm,
        perm,
        source_narrow,
        source_wide,
        cotangent,
        kernel_first,
        kernel_rest,
        mixer_narrow,
        mixer_wide,
    )
    mixed, gn, gw, gf, gr, gmn, gmw, ng, total = run_backward(
        lens, norm, rs, perm, w, wmn, wmw, h, xh, y, nar, wid, cot
    )
    grad_norm = jnp.sqrt(total[0, 0])
    clip = jnp.minimum(1.0, THRESHOLD / grad_norm)
    norm_grad = jnp.transpose(ng[:, :, :2, :], (2, 1, 0, 3)).reshape(2, 10, CO)
    results = []
    for p, g, m, v in (
        (kernel_first, gf, moment_first, square_first),
        (kernel_rest, gr, moment_rest, square_rest),
        (mixer_narrow, gmn, moment_narrow, square_narrow),
        (mixer_wide, gmw, moment_wide, square_wide),
    ):
        results += adamw(p, clip * g, m, v, RATE_WEIGHT, DECAY)
    results += adamw(norm_params, clip * norm_grad, moment_norm, square_norm, RATE_NORM, 0.0)
    return (mixed, gn, gw, grad_norm, *results)


def solution(mesh):
    in_specs = (
        P(None, "batch", "tm", None),
        P(None, "batch", "tm", None),
        P("batch"),
        P("batch", "tm", None),
        P("tm", None),
        P(None, "tm", None),
        P(None, "tm", None),
        P(None, "tm", None),
        P(),
        P("tm", None),
        P("tm", None),
        P(None, "tm", None),
        P(None, "tm", None),
        P(None, "tm", None),
        P(None, "tm", None),
        P(None, "tm", None),
        P(None, "tm", None),
        P(),
        P(),
    )
    out_specs = (
        P("batch", "tm", None),
        P(None, "batch", "tm", None),
        P(None, "batch", "tm", None),
        P(),
        P("tm", None),
        P("tm", None),
        P("tm", None),
        P(None, "tm", None),
        P(None, "tm", None),
        P(None, "tm", None),
        P(None, "tm", None),
        P(None, "tm", None),
        P(None, "tm", None),
        P(None, "tm", None),
        P(None, "tm", None),
        P(None, "tm", None),
        P(),
        P(),
        P(),
    )
    fits = mesh.shape["tm"] == 16 and mesh.shape["batch"] == 2
    chosen = body_split if fits else body
    return jax.shard_map(chosen, mesh=mesh, in_specs=in_specs, out_specs=out_specs, check_vma=False)
```

```python
import numpy as np
import jax
import jax.numpy as jnp
from jax import lax
from jax.experimental import pallas as pl
from jax.experimental.pallas import tpu as pltpu
from jax.sharding import PartitionSpec as P

CO = 512
CW = 384
K = 17
STEP = 10


EPS = 1e-05
THRESHOLD = 100.0
BETA_ONE = 0.9
SECOND_DECAY = 0.999
ADAM_EPS = 1e-08
RATE_WEIGHT = 0.02
RATE_NORM = 0.4
DECAY = 0.01


def padded_2(shard, sides, width):
    for axis, dim in sides:
        devices, length = (lax.axis_size(axis), shard.shape[dim])
        up = [(i, (i + 1) % devices) for i in range(devices - 1)]
        down = [(j, i) for i, j in up]
        last = lax.slice_in_dim(shard, length - width, length, axis=dim)
        initial = lax.slice_in_dim(shard, 0, width, axis=dim)
        before = lax.ppermute(last, axis, up)
        after = lax.ppermute(initial, axis, down)
        shard = jnp.concatenate([before, shard, after], axis=dim)
    return shard


def adamw(param, grad, first, second, rate, decay):
    first_new = BETA_ONE * first + (1.0 - BETA_ONE) * grad
    second_new = SECOND_DECAY * second + (1.0 - SECOND_DECAY) * grad * grad
    fix_one = 1.0 - BETA_ONE**STEP
    fix_two = 1.0 - SECOND_DECAY**STEP
    update = first_new / fix_one / (jnp.sqrt(second_new / fix_two) + ADAM_EPS)
    return (param - rate * (update + decay * param), first_new, second_new)


def body(
    source_narrow,
    source_wide,
    lengths,
    cotangent,
    kernel_first,
    kernel_rest,
    mixer_narrow,
    mixer_wide,
    norm_params,
    moment_first,
    square_first,
    moment_rest,
    square_rest,
    moment_narrow,
    square_narrow,
    moment_wide,
    square_wide,
    moment_norm,
    square_norm,
):
    frames = source_wide.shape[2]
    half = K // 2
    places = lax.axis_index("tm") * frames + jnp.arange(frames, dtype=jnp.int32)
    valid = (places[None, :] < lengths[:, None]).astype(jnp.float32)[:, :, None]
    local_count = jnp.sum(valid)
    valid_low = valid.astype(jnp.bfloat16)
    narrow = source_narrow * valid_low[None]
    wide = source_wide * valid_low[None]
    full_first, full_rest, full_narrow, full_wide = (
        lax.all_gather(kernel_first.astype(jnp.bfloat16), "tm", axis=0, tiled=True),
        lax.all_gather(kernel_rest.astype(jnp.bfloat16), "tm", axis=1, tiled=True),
        lax.all_gather(mixer_narrow.astype(jnp.bfloat16), "tm", axis=1, tiled=True),
        lax.all_gather(mixer_wide.astype(jnp.bfloat16), "tm", axis=1, tiled=True),
    )
    kernels = [jnp.transpose(full_first.reshape(CW, K, CO), (1, 0, 2))] + [
        jnp.transpose(full_rest[layer].reshape(CO, K, CO), (1, 0, 2)) for layer in range(4)
    ]
    gains = norm_params[0]
    biases = norm_params[1]

    def batch_statistics(values, count):
        sums = tuple((jnp.sum(value * valid, axis=(0, 1)) for value in values))
        extra = (local_count,) if count is None else ()
        got = lax.psum(sums + extra, ("tm", "batch"))
        if count is None:
            count = got[-1]
        means = [total / count for total in got[: len(values)]]
        spreads = tuple(
            (
                jnp.sum(jnp.square((value - mean) * valid), axis=(0, 1))
                for value, mean in zip(values, means)
            )
        )
        second = lax.psum(spreads, ("tm", "batch"))
        variances = [total / count for total in second]
        scales = [lax.rsqrt(variance + EPS) for variance in variances]
        return (means, scales, count)

    signal = wide[1]
    kept = []
    count = None
    for index in range(5):
        padded = padded_2(signal, (("tm", 1),), half)
        field = jnp.zeros(signal.shape[:2] + (CO,), jnp.float32)
        for tap in range(K):
            field = field + jnp.einsum(
                "btc,cd->btd",
                padded[:, tap : tap + frames],
                kernels[index][tap],
                preferred_element_type=jnp.float32,
            )
        values = [field]
        indices = [index]
        if index == 4:
            for source in range(3):
                values.append(
                    jnp.einsum(
                        "btc,cd->btd",
                        narrow[source],
                        full_narrow[source],
                        preferred_element_type=jnp.float32,
                    )
                )
                indices.append(5 + source)
            for source in range(2):
                values.append(
                    jnp.einsum(
                        "btc,cd->btd",
                        wide[source],
                        full_wide[source],
                        preferred_element_type=jnp.float32,
                    )
                )
                indices.append(8 + source)
        means, scales, count = batch_statistics(values, count)
        normalized_values = [
            (value - mean) * scale for value, mean, scale in zip(values, means, scales)
        ]
        summed = jnp.zeros_like(field)
        for place in range(len(values)):
            summed = (
                summed + gains[indices[place]] * normalized_values[place] + biases[indices[place]]
            )
        kept.append((padded, normalized_values, scales, summed, indices))
        active = jax.nn.silu(summed) * valid
        signal = active.astype(jnp.bfloat16)
    grad_active = cotangent.astype(jnp.float32)
    kernel_grads = [None] * 5
    gain_grads = [None] * 10
    bias_grads = [None] * 10
    narrow_grads = []
    wide_grads = []
    narrow_inputs = []
    wide_inputs = []
    first_input = None
    for index in reversed(range(5)):
        padded, normalized_values, scales, summed, indices = kept[index]
        sigma = jax.nn.sigmoid(summed)
        gradient_total = grad_active * valid * sigma * (1.0 + summed * (1.0 - sigma))
        local_sums = (jnp.sum(gradient_total, axis=(0, 1)),) + tuple(
            (
                jnp.sum(gradient_total * standardized_input, axis=(0, 1))
                for standardized_input in normalized_values
            )
        )
        got = lax.psum(local_sums, ("tm", "batch"))
        bias_total = got[0]
        field_grads = []
        for place in range(len(normalized_values)):
            which = indices[place]
            gain = gains[which]
            gain_grads[which] = got[1 + place]
            bias_grads[which] = bias_total
            grad_field = scales[place] * (
                gain * gradient_total
                - valid * (gain * bias_total) / count
                - valid * normalized_values[place] * (gain * got[1 + place]) / count
            )
            field_grads.append(grad_field.astype(jnp.bfloat16))
        grad_conv = field_grads[0]
        tap_grads = [
            jnp.einsum(
                "btc,btd->cd",
                padded[:, tap : tap + frames],
                grad_conv,
                preferred_element_type=jnp.float32,
            )
            for tap in range(K)
        ]
        kernel_grads[index] = jnp.stack(tap_grads, axis=1).reshape(padded.shape[2] * K, CO)
        if index == 4:
            for source in range(3):
                branch = field_grads[1 + source]
                narrow_grads.append(
                    jnp.einsum(
                        "btc,btd->cd", narrow[source], branch, preferred_element_type=jnp.float32
                    )
                )
                narrow_inputs.append(
                    jnp.einsum(
                        "btd,cd->btc",
                        branch,
                        full_narrow[source],
                        preferred_element_type=jnp.float32,
                    )
                    * valid
                )
            for source in range(2):
                branch = field_grads[4 + source]
                wide_grads.append(
                    jnp.einsum(
                        "btc,btd->cd", wide[source], branch, preferred_element_type=jnp.float32
                    )
                )
                wide_inputs.append(
                    jnp.einsum(
                        "btd,cd->btc", branch, full_wide[source], preferred_element_type=jnp.float32
                    )
                    * valid
                )
        grad_padded = padded_2(grad_conv, (("tm", 1),), half)
        incoming = jnp.zeros(padded.shape[:1] + (frames, padded.shape[2]), jnp.float32)
        for tap in range(K):
            start = K - 1 - tap
            incoming = incoming + jnp.einsum(
                "btd,cd->btc",
                grad_padded[:, start : start + frames],
                kernels[index][tap],
                preferred_element_type=jnp.float32,
            )
        if index > 0:
            grad_active = incoming
        else:
            first_input = incoming
    grad_narrow = jnp.stack(narrow_inputs)
    source_wide_gradient = jnp.stack([wide_inputs[0], (first_input + wide_inputs[1]) * valid])
    shard_gradients = (
        kernel_grads[0],
        jnp.stack(kernel_grads[1:]),
        jnp.stack(narrow_grads),
        jnp.stack(wide_grads),
    )
    shards = (
        lax.psum_scatter(shard_gradients[0], "tm", scatter_dimension=0, tiled=True),
        lax.psum_scatter(shard_gradients[1], "tm", scatter_dimension=1, tiled=True),
        lax.psum_scatter(shard_gradients[2], "tm", scatter_dimension=1, tiled=True),
        lax.psum_scatter(shard_gradients[3], "tm", scatter_dimension=1, tiled=True),
    )
    norm_grad = jnp.stack([jnp.stack(gain_grads), jnp.stack(bias_grads)])
    params = (kernel_first, kernel_rest, mixer_narrow, mixer_wide)
    firsts = (moment_first, moment_rest, moment_narrow, moment_wide)
    seconds = (square_first, square_rest, square_narrow, square_wide)
    results = []
    shards = (
        lax.psum(shards[0].astype(jnp.bfloat16), "batch").astype(jnp.float32),
        lax.psum(shards[1].astype(jnp.bfloat16), "batch").astype(jnp.float32),
        lax.psum(shards[2].astype(jnp.bfloat16), "batch").astype(jnp.float32),
        lax.psum(shards[3].astype(jnp.bfloat16), "batch").astype(jnp.float32),
    )
    local_square = jnp.zeros((), jnp.float32)
    for shard in shards:
        local_square = local_square + jnp.sum(shard * shard)
    total = lax.psum(local_square, "tm") + jnp.sum(norm_grad * norm_grad)
    grad_norm = jnp.sqrt(total)
    clip = jnp.minimum(1.0, THRESHOLD / grad_norm)
    for slot in range(4):
        results.append(
            adamw(
                params[slot], clip * shards[slot], firsts[slot], seconds[slot], RATE_WEIGHT, DECAY
            )
        )
    results.append(adamw(norm_params, clip * norm_grad, moment_norm, square_norm, RATE_NORM, 0.0))
    return (
        signal,
        grad_narrow,
        source_wide_gradient,
        grad_norm,
        results[0][0],
        results[0][1],
        results[0][2],
        results[1][0],
        results[1][1],
        results[1][2],
        results[2][0],
        results[2][1],
        results[2][2],
        results[3][0],
        results[3][1],
        results[3][2],
        results[4][0],
        results[4][1],
        results[4][2],
    )


BF = jnp.bfloat16
F32 = jnp.float32
MESH = pl.DeviceIdType.MESH
ROWS = 1024
HALO = 64
HALF = 256
GROUPS = 34
LEAD = 10
AHEAD = 3
LAG = AHEAD + 2


def wait_on(ref, sem):
    pltpu.make_async_copy(ref, ref, sem).wait()


def remote(src, dst, send, recv, device):
    pltpu.make_async_remote_copy(
        src_ref=src,
        dst_ref=dst,
        send_sem=send,
        recv_sem=recv,
        device_id=device,
        device_id_type=MESH,
    ).start()


def position():
    x = lax.axis_index("batch")
    t = lax.axis_index("tm")
    return x, t, lax.div(t, 4), lax.rem(lax.div(t, 2), 2), lax.rem(t, 2)


def greet(x, t):
    barrier = pltpu.get_barrier_semaphore()

    def one(d, _):
        pl.semaphore_signal(
            barrier, inc=1, device_id=(lax.rem(t + d, 16), x), device_id_type=MESH
        )
        return 0

    lax.fori_loop(1, 16, one, 0)
    for d in (0, 1, 2, 14, 15):
        pl.semaphore_signal(
            barrier, inc=1, device_id=(lax.rem(t + d, 16), 1 - x), device_id_type=MESH
        )
    pl.semaphore_wait(barrier, 20)


def frame_mask(block, t, lens):
    frames = lax.broadcasted_iota(jnp.int32, (16, 8, HALF), 0) + (block * 16 + t * 128)
    return (frames.astype(F32) < lens[None]).astype(F32)


def share(box, part, at, rows, sems):
    x, t, zi, yi, ci = position()
    chip = lax.div(t, 2)
    to_first, to_peer, to_second, first, peer, second = sems
    used = pl.ds(0, rows)

    @pl.when(ci == 1)
    def _():
        remote(
            part.at[at, used],
            box.at[at, chip, 1, used],
            to_first.at[at],
            first.at[at],
            (t - 1, x),
        )

    @pl.when(ci == 0)
    def _():
        box[at, chip, 0] = part[at]
        wait_on(box.at[at, chip, 1, used], first.at[at])
        mine = box.at[at, chip, :, used]

        def one(d, _):
            remote(mine, mine, to_peer.at[at], peer.at[at], (lax.rem(t + 2 * d, 16), x))
            return 0

        lax.fori_loop(1, 8, one, 0)


def shared(box, at, rows, sems):
    x, t, zi, yi, ci = position()
    to_first, to_peer, to_second, first, peer, second = sems
    used = pl.ds(0, rows)

    @pl.when(ci == 0)
    def _():
        wait_on(box.at[at, pl.ds(0, 7), :, used], peer.at[at])
        every = box.at[at, :, :, used]
        remote(every, every, to_second.at[at], second.at[at], (t + 1, x))

    @pl.when(ci == 1)
    def _():
        wait_on(box.at[at, :, :, used], second.at[at])


def share_drained(box, part, at, rows, sems):
    ci = position()[4]
    to_first, to_peer, to_second, first, peer, second = sems
    used = pl.ds(0, rows)

    @pl.when(ci == 1)
    def _():
        wait_on(part.at[at, used], to_first.at[at])

    @pl.when(ci == 0)
    def _():
        wait_on(box.at[at, pl.ds(0, 7), :, used], to_peer.at[at])
        wait_on(box.at[at, :, :, used], to_second.at[at])


def forward_kernel(
    lens_in,
    norm,
    perm,
    src_n,
    src_w,
    cot,
    kf,
    kr,
    mn,
    mw,
    w_out,
    wmn_out,
    wmw_out,
    h_out,
    xh_out,
    y_out,
    nar_out,
    wid_out,
    cot_out,
    rs_out,
    len_out,
    W,
    G,
    wmn,
    wmw,
    hA,
    hB,
    z,
    zb,
    xhb,
    y5,
    stg,
    pf,
    pmn,
    pmw,
    raww,
    rawn,
    rawc,
    nar,
    wid,
    cotv,
    st,
    sp,
    rel,
    nv,
    lenr,
    lens,
    load_s,
    dl_s,
    dl_r,
    ag_s,
    rz,
    rf,
    ry,
    rc,
    m_s,
    m_r,
    x_s,
    x_r,
    xr_s,
    xr_r,
    halo_s,
    halo_r,
    rel_s,
    rel_r,
    st_a,
    st_b,
    st_c,
    st_d,
    st_e,
    st_f,
    out_s,
):
    x, t, zi, yi, ci = position()
    cols = pl.ds(pl.multiple_of(x * HALF, HALF), HALF)
    partner = (t, 1 - x)
    sibling = (t + 1 - 2 * ci, x)
    across = (zi * 4 + (1 - yi) * 2 + ci, x)
    sems = (st_a, st_b, st_c, st_d, st_e, st_f)

    lanes = [pl.ds(pl.multiple_of(x * HALF + 128 * b, 128), 128) for b in range(2)]
    loads = [(kf.at[:, lanes[b]], pf.at[0, b, pl.ds(0, 408)]) for b in range(2)]
    loads += [(kr.at[i, :, lanes[b]], pf.at[1 + i, b]) for i in range(4) for b in range(2)]
    loads += [
        (mn.at[:, :, cols], pmn),
        (mw.at[:, :, cols], pmw),
        (src_w, raww.at[x]),
        (src_n, rawn.at[x]),
        (cot.at[:, :, cols], rawc.at[x]),
    ]
    copies = [pltpu.make_async_copy(a, b, load_s.at[i]) for i, (a, b) in enumerate(loads)]
    for copy in copies:
        copy.start()
    hA[:, :, pl.ds(1152, 16), :] = jnp.zeros((5, 2, 16, HALF), BF)

    @pl.when(t == 0)
    def _():
        hA[:, :, pl.ds(0, HALO), :] = jnp.zeros((5, 2, HALO, HALF), BF)

    @pl.when(t == 15)
    def _():
        hA[:, :, pl.ds(1088, HALO), :] = jnp.zeros((5, 2, HALO, HALF), BF)

    st[...] = jnp.zeros((7, 8, 2, 8, HALF), F32)
    sp[...] = jnp.zeros((7, 8, HALF), F32)
    lenr[0] = lens_in[...]
    greet(x, t)

    other = pl.ds(pl.multiple_of((1 - x) * HALF, HALF), HALF)
    remote(lenr.at[0], lenr.at[1], xr_s.at[0], xr_r.at[0], partner)
    remote(src_w.at[1], raww.at[x, 1], xr_s.at[1], xr_r.at[1], partner)

    def prep(layer, count):
        for k in range(17):
            for b in range(2):
                v = pf[layer, b, pl.ds(k, count, stride=17), :]
                if count < 32:
                    v = jnp.concatenate([v, jnp.zeros((32 - count, 128), F32)], axis=0)
                W[17 * layer + k, zi, yi, ci, :, pl.ds(128 * b, 128)] = v.astype(BF)

    def taps(g):
        return pl.ds(5 * lax.div(g, 2), 5)

    def part(g):
        return pl.ds(pl.multiple_of(16 * lax.rem(g, 2), 16), 16)

    def first_sends(pair, send, into_z):
        for dz in (1, 2, 3):
            remote(pair, pair, send, into_z, (lax.rem(zi + dz, 4) * 4 + yi * 2 + 1, x))

    def pass_z(block, send_y, send_c, into_y, into_c):
        line = block(slice(None), yi, slice(None))
        remote(line, line, send_y, into_y, across)
        line = block(slice(None), yi, 1)
        remote(line, line, send_c, into_c, sibling)
        for dz in (1, 2, 3):
            one = block(lax.rem(zi + dz, 4), yi, 0)
            remote(one, one, send_c, into_c, sibling)

    def pass_y(block, send_c, into_c):
        line = block(slice(None), 1 - yi, slice(None))
        remote(line, line, send_c, into_c, sibling)

    def chunk(g):
        return lambda zs, ys, cs: W.at[taps(g), zs, ys, cs, part(g)]

    def mixers(zs, ys, cs):
        return G.at[zs, ys, cs]

    ALL = slice(None)
    THREE = pl.ds(0, 3)

    inner = (zi == 1) | (zi == 2)
    far = jnp.where(zi == 1, 3, 0)

    def own_step(g):
        pair = chunk(g)(zi, yi, ALL)

        def to(zz, sems):
            remote(pair, pair, ag_s.at[g, 0], sems.at[g], (zz * 4 + yi * 2 + 1, x))

        @pl.when((ci == 1) & (g < GROUPS) & inner)
        def _():
            to(3 - zi, rz)
            to(jnp.where(zi == 1, 0, 3), rz)
            to(jnp.where(zi == 1, 3, 0), rz)

        @pl.when((ci == 1) & (g < GROUPS) & (zi == 0))
        def _():
            to(1, rz)
            to(2, rf)

        @pl.when((ci == 1) & (g < GROUPS) & (zi == 3))
        def _():
            to(2, rz)
            to(1, rf)

    def far_step(g):
        @pl.when((ci == 1) & (g < GROUPS) & inner)
        def _():
            pair = chunk(g)(far, yi, ALL)
            wait_on(pair, rf.at[g])
            remote(pair, pair, ag_s.at[g, 0], rz.at[g], ((3 - far) * 4 + yi * 2 + 1, x))

    def y_step(h):
        @pl.when((ci == 1) & (h >= 0) & (h < GROUPS))
        def _():
            wait_on(chunk(h)(ALL, 0, ALL), ry.at[h])
            pass_y(chunk(h), ag_s.at[h, 2], rc.at[h])

    def service(g, start):
        own_step(g + LEAD)
        far_step(g + 2)

        @pl.when((ci == 1) & (g < GROUPS) & inner)
        def _():
            wait_on(chunk(g)(pl.ds(0, 2), 0, ALL), rz.at[g])

        @pl.when((ci == 1) & (g < GROUPS) & jnp.logical_not(inner))
        def _():
            wait_on(chunk(g)(THREE, 0, ALL), rz.at[g])

        @pl.when((ci == 1) & (g < GROUPS))
        def _():
            pass_z(chunk(g), ag_s.at[g, 1], ag_s.at[g, 2], ry.at[g], rc.at[g])

        @pl.when(g - LAG >= start)
        def _():
            y_step(g - LAG)

        @pl.when((ci == 1) & (g == 8))
        def _():
            wait_on(mixers(THREE, 0, ALL), m_r.at[0])
            pass_z(mixers, m_s.at[1], m_s.at[2], m_r.at[1], m_r.at[2])

        @pl.when((ci == 1) & (g == 11))
        def _():
            wait_on(mixers(ALL, 0, ALL), m_r.at[1])
            pass_y(mixers, m_s.at[2], m_r.at[2])

    def mixers_arrived():
        @pl.when(ci == 0)
        def _():
            wait_on(W.at[pl.ds(0, 35), THREE, 0, 0, pl.ds(0, 16)], m_r.at[2])

        for s in range(16):
            got = G.at[s // 4, s // 2 % 2, s % 2]
            for j in range(3):
                wmn[j, pl.ds(16 * s, 16), :] = got[pl.ds(16 * j, 16), :]
            for j in range(2):
                wmw[j, pl.ds(32 * s, 32), :] = got[pl.ds(48 + 32 * j, 32), :]

    FIFTEEN = W.at[pl.ds(0, 75), 0, 0, 0, pl.ds(0, 16)]

    def weights_arrived(layer):
        def one(h, _):
            wait_on(FIFTEEN, rc.at[h])
            return 0

        for d in range(2):
            y_step(2 * lax.div(17 * layer + 16, 5) + d)

        @pl.when(ci == 0)
        def _():
            lo = jnp.where(layer == 0, 0, 2 * lax.div(17 * layer - 1, 5) + 2)
            lax.fori_loop(lo, 2 * lax.div(17 * layer + 16, 5) + 2, one, 0)

    def lend(layer):
        own = W.at[pl.ds(17 * layer, 17), zi, yi, 0]

        @pl.when(ci == 0)
        def _():
            remote(own, own, dl_s.at[layer], dl_r.at[layer], sibling)

    def lent(layer):
        @pl.when(ci == 1)
        def _():
            wait_on(W.at[pl.ds(0, 17), zi, yi, 0], dl_r.at[layer])

    def serve(first, last):
        def one(g, _):
            service(g, 0)
            return 0

        lax.fori_loop(first, last, one, 0)

    for copy in copies[:2]:
        copy.wait()
    prep(0, 24)
    lend(0)
    for copy in copies[2:12]:
        copy.wait()
    for layer in (1, 2, 3, 4):
        prep(layer, 32)
        lend(layer)
    for j in range(3):
        G[zi, yi, ci, pl.ds(16 * j, 16), :] = pmn[j].astype(BF)
    for j in range(2):
        G[zi, yi, ci, pl.ds(48 + 32 * j, 32), :] = jnp.concatenate(
            [pmw[j], jnp.zeros((8, HALF), F32)], axis=0
        ).astype(BF)

    @pl.when(ci == 0)
    def _():
        remote(G.at[zi, yi, 0], G.at[zi, yi, 0], dl_s.at[5], dl_r.at[5], sibling)

    for layer in range(5):
        lent(layer)

    @pl.when(ci == 1)
    def _():
        wait_on(G.at[zi, yi, 0], dl_r.at[5])


    def own_one(g, _):
        own_step(g)
        return 0

    lax.fori_loop(0, LEAD, own_one, 0)
    far_step(jnp.int32(0))
    far_step(jnp.int32(1))

    @pl.when(ci == 1)
    def _():
        first_sends(mixers(zi, yi, ALL), m_s.at[0], m_r.at[0])

    serve(0, 2)

    wait_on(lenr.at[1], xr_r.at[0])
    lens[...] = lenr[0] + lenr[1]
    len_out[...] = lens[...]
    for s in range(16):
        nv[s] = jnp.broadcast_to(
            jnp.sum(jnp.clip(lens[...] - 128.0 * s, 0.0, 128.0), axis=0, keepdims=True), (8, HALF)
        )

    def spread_wide(j):
        for s in range(8):
            v = jnp.dot(raww[s // 4, j, s % 4], perm[...], preferred_element_type=F32)
            for b in range(4):
                stg[b, pl.ds(s, 128, stride=8), :] = v[:, 128 * b : 128 * b + 128]

    def spread_half(v, s):
        for b in range(2):
            stg[b, pl.ds(s, 128, stride=8), :] = v[:, 128 * b : 128 * b + 128].astype(F32)

    def masked_block(b, h):
        rows = pl.ds(pl.multiple_of(b * 128, 128), 128)
        v = jnp.concatenate([stg[2 * h, rows, :], stg[2 * h + 1, rows, :]], axis=1)
        v = v.reshape(16, 8, HALF)
        return (v * frame_mask(b, t, lens[...])).reshape(128, HALF).astype(BF)

    copies[12].wait()
    wait_on(raww.at[0, 1], xr_r.at[1])
    spread_wide(1)

    def first_block(b, _):
        for h in range(2):
            hA[0, h, pl.ds(pl.multiple_of(HALO + b * 128, 64), 128), :] = masked_block(b, h)
        return 0

    lax.fori_loop(0, 8, first_block, 0)

    EDGE = ((HALO, 1088), (1024, 0))

    def halo_out(layer, half, side, at):
        lo, to = EDGE[side]
        goal = hA.at[layer, half, pl.ds(to, HALO)]
        source = hA.at[layer, half, pl.ds(lo, HALO)]
        step = 2 * side - 1
        for other in at:
            remote(
                source,
                goal,
                halo_s.at[layer, side, half if len(at) == 1 else other],
                halo_r.at[layer, side, half],
                (t + step, 1 - x if other else x),
            )

    def halos_out(layer, half, at, relay):
        @pl.when(t > 0)
        def _():
            halo_out(layer, half, 0, at)

        @pl.when(ci == 0)
        def _():
            halo_out(layer, half, 1, at)

        @pl.when((ci == 1) & (t < 15))
        def _():
            remote(
                hA.at[layer, half, pl.ds(1024, HALO)],
                rel.at[relay],
                rel_s.at[relay, 0],
                rel_r.at[relay],
                sibling,
            )

        @pl.when((ci == 0) & (t < 14))
        def _():
            wait_on(rel.at[relay], rel_r.at[relay])
            goal = hA.at[layer, half, pl.ds(0, HALO)]
            for other in at:
                remote(
                    rel.at[relay],
                    goal,
                    rel_s.at[relay, other],
                    halo_r.at[layer, 1, half],
                    (t + 2, 1 - x if other else x),
                )

    def halos_sent(layer, half, at, relay):
        @pl.when(t > 0)
        def _():
            for other in at:
                wait_on(rel.at[0], halo_s.at[layer, 0, half if len(at) == 1 else other])

        @pl.when(ci == 0)
        def _():
            for other in at:
                wait_on(rel.at[0], halo_s.at[layer, 1, half if len(at) == 1 else other])

        @pl.when((ci == 1) & (t < 15))
        def _():
            wait_on(rel.at[0], rel_s.at[relay, 0])

        @pl.when((ci == 0) & (t < 14))
        def _():
            for other in at:
                wait_on(rel.at[0], rel_s.at[relay, other])

    def halo_wait(layer, half, sems, sides):
        for side, edge in sides:

            @pl.when(t != edge)
            def _():
                wait_on(hA.at[layer, half, pl.ds(0, HALO)], sems.at[layer, side, half])

    ARRIVE = ((1, 0), (0, 15))
    for h in range(2):
        halos_out(0, h, (0,), h)

    remote(src_n, rawn.at[x], xr_s.at[2], xr_r.at[2], partner)
    remote(src_w.at[0], raww.at[x, 0], xr_s.at[3], xr_r.at[3], partner)
    serve(2, 8 + AHEAD)

    def shift_copy(layer, half):
        def one(b, _):
            v = hA[layer, half, pl.ds(pl.multiple_of(b * 128, 128), 144), :].astype(F32)
            hB[half, pl.ds(pl.multiple_of(b * 128, 128), 128), :] = v[8:136].astype(BF)
            return 0

        lax.fori_loop(0, 9, one, 0)


    def rows_of(b):
        return pl.ds(pl.multiple_of(b * 128, 128), 128)

    def local_stats(ref):
        def total(b, acc):
            v = ref[rows_of(b), :].reshape(16, 8, HALF) * frame_mask(b, t, lens[...])
            return acc + jnp.sum(v, axis=0)

        s = jnp.sum(
            lax.fori_loop(0, 8, total, jnp.zeros((8, HALF), F32)), axis=0, keepdims=True
        )
        mean = s / jnp.maximum(nv[t, pl.ds(0, 1), :], 1.0)

        def spread(b, acc):
            v = (ref[rows_of(b), :].reshape(16, 8, HALF) - mean[None]) * frame_mask(
                b, t, lens[...]
            )
            return acc + jnp.sum(v * v, axis=0)

        m2 = jnp.sum(
            lax.fori_loop(0, 8, spread, jnp.zeros((8, HALF), F32)), axis=0, keepdims=True
        )
        return mean, m2

    def put_stats(ref, layer, field):
        mean, m2 = local_stats(ref)
        sp[layer, pl.ds(2 * field, 1), :] = mean
        sp[layer, pl.ds(2 * field + 1, 1), :] = m2

    def combine(at):
        zero = jnp.zeros((8, HALF), F32)
        count = lax.fori_loop(0, 16, lambda s, a: a + nv[s], zero)
        of = lambda s: st[at, lax.div(s, 2), lax.rem(s, 2)]
        mean = lax.fori_loop(0, 16, lambda s, a: a + nv[s] * of(s), zero) / count

        def gather_spread(s, a):
            v = of(s)
            d = v - mean
            return a[0] + nv[s] * d * d, a[1] + v

        between, inside = lax.fori_loop(0, 16, gather_spread, (zero, zero))

        def moments(field):
            m = mean[2 * field : 2 * field + 1]
            q = inside[2 * field + 1 : 2 * field + 2] + between[2 * field : 2 * field + 1]
            return m, lax.rsqrt(q / count[:1] + EPS)

        return moments

    def branch_fields(at, number, inputs):
        for j in range(number):
            total = None
            for lhs, rhs in inputs(j):
                v = jnp.dot(lhs, rhs, preferred_element_type=F32)
                total = v if total is None else total + v
            zb[j] = total
            put_stats(zb.at[j], at, j)
        share(st, sp, at, 8, sems)

    def branches(at, base, number):
        shared(st, at, 8, sems)
        shares = combine(at)
        for j in range(number):
            m, r = shares(j)
            field = base + j
            rs_out[field] = jnp.broadcast_to(r, (8, HALF))
            gain = norm[field, pl.ds(0, 1), :]
            bias = norm[field, pl.ds(1, 1), :]
            if j > 0:
                wait_on(xhb.at[1], out_s.at[10])

            def one(b, _):
                v = (zb[j, rows_of(b), :] - m) * r
                xhb[1, rows_of(b), :] = v
                y = gain * v + bias
                if field > 5:
                    y = y + y5[rows_of(b), :]
                y5[rows_of(b), :] = y
                return 0

            lax.fori_loop(0, 8, one, 0)
            pltpu.make_async_copy(xhb.at[1], xh_out.at[field], out_s.at[10]).start()
        wait_on(xhb.at[1], out_s.at[10])

    def spread_narrow(j):
        for s in range(8):
            spread_half(rawn[s // 4, j, s % 4], s)

        def one(b, _):
            nar[j, rows_of(b), :] = masked_block(b, 0)
            return 0

        lax.fori_loop(0, 8, one, 0)

    def beside_statistics(layer):
        @pl.when(layer == 0)
        def _():
            copies[13].wait()
            wait_on(rawn.at[0], xr_r.at[2])
            spread_narrow(0)

        @pl.when(layer == 1)
        def _():
            mixers_arrived()
            branch_fields(5, 3, lambda j: [(nar[j], wmn[j])])

        @pl.when(layer == 2)
        def _():
            branches(5, 5, 3)

        @pl.when(layer == 3)
        def _():
            wait_on(rawc.at[0], xr_r.at[4])
            for s in range(8):
                spread_half(rawc[s // 4, s % 4], s)

            def one(b, _):
                cotv[rows_of(b), :] = masked_block(b, 0)
                return 0

            lax.fori_loop(0, 8, one, 0)

        @pl.when(layer == 4)
        def _():
            branches(6, 8, 2)

    def beside_exchange(layer):
        @pl.when(layer == 0)
        def _():
            spread_narrow(1)
            spread_narrow(2)

        @pl.when(layer == 1)
        def _():
            wait_on(raww.at[0, 0], xr_r.at[3])
            spread_wide(0)

            def one(b, _):
                for h in range(2):
                    wid[h, rows_of(b), :] = masked_block(b, h)
                return 0

            lax.fori_loop(0, 8, one, 0)

        @pl.when(layer == 2)
        def _():
            copies[14].wait()
            remote(cot.at[:, :, other], rawc.at[x], xr_s.at[4], xr_r.at[4], partner)

            def inputs(j):
                for h in range(2):
                    lhs = wid[h] if j == 0 else hA[0, h, pl.ds(HALO, ROWS), :]
                    yield lhs, wmw[j, pl.ds(HALF * h, HALF), :]

            branch_fields(6, 2, inputs)

    def tile_of(layer, half, at):
        at = pl.multiple_of(at, 256)
        acc = jnp.zeros((256, HALF), F32)
        for k in range(17):
            lhs = (
                hA[layer, half, pl.ds(at + 8 * k, 256), :]
                if k % 2 == 0
                else hB[half, pl.ds(at + 8 * (k - 1), 256), :]
            )
            rhs = W[17 * layer + k, pl.ds(2 * half, 2)].reshape(HALF, HALF)
            acc = acc + jnp.dot(lhs, rhs, preferred_element_type=F32)
        return acc

    PIECES = ((64, 320), (384, 256), (640, 256), (896, 192))

    def layer_step(layer, _):
        base = 8 + 6 * layer + 2 * (layer > 1).astype(jnp.int32)
        weights_arrived(layer)
        pltpu.make_async_copy(
            W.at[pl.ds(17 * layer, 17)], w_out.at[pl.ds(17 * layer, 17)], out_s.at[layer]
        ).start()

        halo_wait(layer, x, halo_r, ARRIVE)
        shift_copy(layer, x)
        def own_tile(j, _):
            z[pl.ds(pl.multiple_of(256 * j, 256), 256), :] = tile_of(layer, x, 256 * j)
            return 0

        lax.fori_loop(0, 4, own_tile, 0)
        service(base + AHEAD, base)

        halo_wait(layer, 1 - x, halo_r, ARRIVE)
        def other_tile(j, _):
            for i, (lo, rows) in enumerate(PIECES):

                @pl.when((layer > 0) & (j == i))
                def _():
                    wait_on(hA.at[layer, 1 - x, pl.ds(lo, rows)], x_r.at[layer, i])

            @pl.when(j == 0)
            def _():
                v = hA[layer, 1 - x, pl.ds(0, 128), :].astype(F32)
                hB[1 - x, pl.ds(0, 112), :] = v[8:120].astype(BF)

            a = pl.multiple_of(256 * j + 112, 16)
            v = hA[layer, 1 - x, pl.ds(a, 272), :].astype(F32)
            hB[1 - x, pl.ds(a, 256), :] = v[8:264].astype(BF)
            rows = pl.ds(pl.multiple_of(256 * j, 256), 256)
            z[rows, :] = z[rows, :] + tile_of(layer, 1 - x, 256 * j)

            @pl.when(j == 1)
            def _():
                service(base + AHEAD + 1, base)

            return 0

        lax.fori_loop(0, 4, other_tile, 0)

        pltpu.make_async_copy(
            hA.at[layer, :, pl.ds(HALO, ROWS)], h_out.at[layer], out_s.at[5 + layer]
        ).start()
        put_stats(z, layer, 0)
        share(st, sp, layer, 2, sems)
        service(base + AHEAD + 2, base)
        service(base + AHEAD + 3, base)
        beside_statistics(layer)
        shared(st, layer, 2, sems)
        moments = combine(layer)

        m, r = moments(0)
        rs_out[layer] = jnp.broadcast_to(r, (8, HALF))
        gain = norm[layer, pl.ds(0, 1), :]
        bias = norm[layer, pl.ds(1, 1), :]

        @pl.when(layer > 0)
        def _():
            wait_on(xhb.at[0], out_s.at[11])

        @pl.when(layer < 4)
        def _():
            def one(b, _):
                rows = pl.ds(pl.multiple_of(b * 64, 64), 64)
                v = (z[rows, :] - m) * r
                xhb[0, rows, :] = v
                y = gain * v + bias
                frames = lax.broadcasted_iota(jnp.int32, (8, 8, HALF), 0) + (b * 8 + t * 128)
                a = (y * jax.nn.sigmoid(y)).reshape(8, 8, HALF)
                a = jnp.where(frames.astype(F32) < lens[...][None], a, 0.0)
                hA[layer + 1, x, pl.ds(pl.multiple_of(HALO + b * 64, 64), 64), :] = a.reshape(
                    64, HALF
                ).astype(BF)
                return 0

            lax.fori_loop(0, 16, one, 0)
            halos_out(layer + 1, x, (0, 1), layer + 2)
            for j, (lo, rows) in enumerate(PIECES):
                ref = hA.at[layer + 1, x, pl.ds(lo, rows)]
                remote(ref, ref, x_s.at[layer + 1, j], x_r.at[layer + 1, j], partner)
        @pl.when(layer == 4)
        def _():
            def one(b, _):
                v = (z[rows_of(b), :] - m) * r
                xhb[0, rows_of(b), :] = v
                y5[rows_of(b), :] = y5[rows_of(b), :] + gain * v + bias
                return 0

            lax.fori_loop(0, 8, one, 0)

        pltpu.make_async_copy(xhb.at[0], xh_out.at[layer], out_s.at[11]).start()

        service(base + AHEAD + 4, base)

        beside_exchange(layer)
        service(base + AHEAD + 5, base)

        @pl.when(layer == 1)
        def _():
            service(base + AHEAD + 6, base)
            service(base + AHEAD + 7, base)

        return 0

    lax.fori_loop(0, 5, layer_step, 0)

    last = [
        (wmn, wmn_out),
        (wmw, wmw_out),
        (y5, y_out),
        (nar, nar_out),
        (wid, wid_out),
        (cotv, cot_out),
    ]
    for i, (a, b) in enumerate(last):
        pltpu.make_async_copy(a, b, out_s.at[12 + i]).start()
    for i, (a, b) in enumerate(last):
        wait_on(a, out_s.at[12 + i])
    wait_on(xhb.at[0], out_s.at[11])
    for i in range(5):
        wait_on(W.at[pl.ds(0, 17)], out_s.at[i])
        wait_on(hA.at[0, :, pl.ds(HALO, ROWS)], out_s.at[5 + i])

    @pl.when(ci == 1)
    def _():
        def drained(g, _):

            @pl.when(inner)
            def _():
                wait_on(chunk(0)(ALL, 0, ALL), ag_s.at[g, 0])

            @pl.when(jnp.logical_not(inner))
            def _():
                wait_on(chunk(0)(pl.ds(0, 2), 0, ALL), ag_s.at[g, 0])

            wait_on(chunk(0)(ALL, 0, ALL), ag_s.at[g, 1])
            wait_on(FIFTEEN, ag_s.at[g, 2])
            return 0

        lax.fori_loop(0, GROUPS, drained, 0)
        wait_on(mixers(THREE, 0, ALL), m_s.at[0])
        wait_on(mixers(ALL, 0, ALL), m_s.at[1])
        wait_on(W.at[pl.ds(0, 35), THREE, 0, 0, pl.ds(0, 16)], m_s.at[2])

    @pl.when(ci == 0)
    def _():
        for layer in range(5):
            wait_on(W.at[pl.ds(0, 17), zi, yi, 0], dl_s.at[layer])
        wait_on(G.at[zi, yi, 0], dl_s.at[5])

    wait_on(lenr.at[0], xr_s.at[0])
    wait_on(raww.at[0, 1], xr_s.at[1])
    wait_on(rawn.at[0], xr_s.at[2])
    wait_on(raww.at[0, 0], xr_s.at[3])
    wait_on(rawc.at[0], xr_s.at[4])

    for h in range(2):
        halos_sent(0, h, (0,), h)

    def finish(layer, _):
        halos_sent(layer, x, (0, 1), layer + 1)
        for j, (lo, rows) in enumerate(PIECES):
            wait_on(hA.at[0, 0, pl.ds(lo, rows)], x_s.at[layer, j])
        return 0

    lax.fori_loop(1, 5, finish, 0)
    for at in range(7):
        share_drained(st, sp, at, 2 if at < 5 else 8, sems)


def run_forward(lens, norm, perm, src_n, src_w, cot, kf, kr, mn, mw):
    vm = pl.BlockSpec(memory_space=pltpu.VMEM)
    hb = pl.BlockSpec(memory_space=pl.ANY)
    dma = pltpu.SemaphoreType.DMA
    S = jax.ShapeDtypeStruct
    return pl.pallas_call(
        forward_kernel,
        out_shape=(
            S((85, 4, 2, 2, 32, HALF), BF),
            S((3, HALF, HALF), BF),
            S((2, 512, HALF), BF),
            S((5, 2, ROWS, HALF), BF),
            S((10, ROWS, HALF), F32),
            S((ROWS, HALF), F32),
            S((3, ROWS, HALF), BF),
            S((2, ROWS, HALF), BF),
            S((ROWS, HALF), BF),
            S((10, 8, HALF), F32),
            S((8, HALF), F32),
        ),
        in_specs=[vm, vm, vm] + [hb] * 7,
        out_specs=[hb] * 9 + [vm, vm],
        scratch_shapes=[
            pltpu.VMEM((85, 4, 2, 2, 32, HALF), BF),
            pltpu.VMEM((4, 2, 2, 112, HALF), BF),
            pltpu.VMEM((3, HALF, HALF), BF),
            pltpu.VMEM((2, 512, HALF), BF),
            pltpu.VMEM((5, 2, 1168, HALF), BF),
            pltpu.VMEM((2, 1152, HALF), BF),
            pltpu.VMEM((ROWS, HALF), F32),
            pltpu.VMEM((3, ROWS, HALF), F32),
            pltpu.VMEM((2, ROWS, HALF), F32),
            pltpu.VMEM((ROWS, HALF), F32),
            pltpu.VMEM((4, ROWS, 128), F32),
            pltpu.VMEM((5, 2, 544, 128), F32),
            pltpu.VMEM((3, 16, HALF), F32),
            pltpu.VMEM((2, 24, HALF), F32),
            pltpu.VMEM((2, 2, 4, 128, 384), BF),
            pltpu.VMEM((2, 3, 4, 128, HALF), BF),
            pltpu.VMEM((2, 4, 128, HALF), BF),
            pltpu.VMEM((3, ROWS, HALF), BF),
            pltpu.VMEM((2, ROWS, HALF), BF),
            pltpu.VMEM((ROWS, HALF), BF),
            pltpu.VMEM((7, 8, 2, 8, HALF), F32),
            pltpu.VMEM((7, 8, HALF), F32),
            pltpu.VMEM((6, HALO, HALF), BF),
            pltpu.VMEM((16, 8, HALF), F32),
            pltpu.VMEM((2, 8, HALF), F32),
            pltpu.VMEM((8, HALF), F32),
            dma((15,)),
            dma((6,)),
            dma((6,)),
            dma((GROUPS, 3)),
            dma((GROUPS,)),
            dma((GROUPS,)),
            dma((GROUPS,)),
            dma((GROUPS,)),
            dma((3,)),
            dma((3,)),
            dma((5, 4)),
            dma((5, 4)),
            dma((5,)),
            dma((5,)),
            dma((5, 2, 2)),
            dma((5, 2, 2)),
            dma((6, 2)),
            dma((6,)),
            dma((7,)),
            dma((7,)),
            dma((7,)),
            dma((7,)),
            dma((7,)),
            dma((7,)),
            dma((18,)),
        ],
        compiler_params=pltpu.CompilerParams(
            collective_id=0, has_side_effects=True, vmem_limit_bytes=62 << 20
        ),
        cost_estimate=pl.CostEstimate(flops=24 * 10**9, bytes_accessed=60 * 10**6, transcendentals=0),
    )(lens, norm, perm, src_n, src_w, cot, kf, kr, mn, mw)


def backward_kernel(
    lens_in,
    norm,
    rs,
    perm,
    w_in,
    wmn,
    wmw,
    h_in,
    xh_in,
    y_in,
    nar_in,
    wid_in,
    cot_in,
    mixed_out,
    gn_out,
    gw_out,
    gf_out,
    gr_out,
    gmn_out,
    gmw_out,
    ng_out,
    total_out,
    Wl,
    Hl,
    Xl,
    xb,
    sb,
    y5,
    da,
    dzA,
    dzB,
    dW,
    crecv,
    yrecv,
    zrecv,
    fin,
    xrecv,
    px,
    pxr,
    stg,
    own_n,
    own_w,
    snd_n,
    snd_w,
    rcv_n,
    rcv_w,
    mix_own,
    mix_rcv,
    Dm,
    cm,
    ym,
    zm,
    fm,
    xm,
    gst,
    gsm,
    bst,
    bsp,
    rel,
    fin0,
    sums4,
    ngr,
    ngx,
    ss,
    load_s,
    w_s,
    br_s,
    halo_s,
    halo_r,
    rel_s,
    rel_r,
    st_a,
    st_b,
    st_c,
    st_d,
    st_e,
    st_f,
    free,
    c_s,
    c_r,
    y_s,
    y_r,
    z_s,
    z_r,
    f_s,
    f_r,
    n_r,
    px_s,
    px_r,
    m_s,
    m_r,
    sn_s,
    sn_r,
    g_s,
    out_s,
    ng_s,
    ng_r,
):
    x, t, zi, yi, ci = position()
    partner = (t, 1 - x)
    sibling = (t + 1 - 2 * ci, x)
    across = (zi * 4 + (1 - yi) * 2 + ci, x)
    sems = (st_a, st_b, st_c, st_d, st_e, st_f)
    lens = lens_in[...]

    def when(cond, f):
        if isinstance(cond, bool):
            if cond:
                f()
        else:
            pl.when(cond)(f)

    def rows_of(b):
        return pl.ds(pl.multiple_of(b * 128, 128), 128)

    def copy_in(src, dst, sem):
        pltpu.make_async_copy(src, dst, sem).start()

    def load_w(layer):
        b2 = lax.rem(layer, 2)
        copy_in(w_in.at[pl.ds(17 * layer, 17)], Wl.at[b2], w_s.at[b2])

    def load_h(layer):
        copy_in(h_in.at[layer], Hl, load_s.at[1])

    def load_x(layer):
        copy_in(xh_in.at[layer], Xl, load_s.at[2])

    copy_in(y_in, y5, load_s.at[3])
    copy_in(cot_in, sb.at[0], load_s.at[4])
    load_x(4)
    copy_in(xh_in.at[5], xb.at[0], br_s.at[0])
    load_w(4)
    load_h(4)

    for edge, lo in ((0, 0), (15, 1088)):

        @pl.when(t == edge)
        def _():
            dzA[:, pl.ds(lo, HALO), :] = jnp.zeros((2, HALO, HALF), BF)

    dzA[:, pl.ds(1152, 16), :] = jnp.zeros((2, 16, HALF), BF)
    bst[...] = jnp.zeros((6, 8, 2, 8, HALF), F32)
    bsp[...] = jnp.zeros((6, 8, HALF), F32)
    greet(x, t)

    zero = jnp.zeros((8, HALF), F32)
    count = jnp.zeros((1, HALF), F32)
    for s in range(16):
        count = count + jnp.sum(jnp.clip(lens - 128.0 * s, 0.0, 128.0), axis=0, keepdims=True)

    def mask(b):
        return frame_mask(b, t, lens)

    def sequence(block, s):
        return stg[block, pl.ds(s, 128, stride=8), :]

    def unstage(blocks, own, send):
        for i in range(4):
            for b in range(blocks):
                own(i, b, sequence(b, 4 * x + i))
                send(i, b, sequence(b, 4 * (1 - x) + i))

    def mix_put(ref):
        def put(i, b, v):
            ref[i, :, pl.ds(128 * b, 128)] = v.astype(BF)

        return put

    my_cols = pl.ds(pl.multiple_of(x * HALF, HALF), HALF)
    other_cols = pl.ds(pl.multiple_of((1 - x) * HALF, HALF), HALF)

    def send_mixed():
        unstage(2, mix_put(mix_own), mix_put(snd_w.at[2]))
        remote(
            snd_w.at[2, :, :, pl.ds(0, HALF)], mix_rcv, sn_s.at[0], sn_r.at[0], partner
        )
        copy_in(mix_own, mixed_out.at[:, :, my_cols], out_s.at[0])

    ORDER = (0, 3, 1, 2)

    def on_second(f):
        pl.when(ci == 1)(f)

    def send_core(layer, zs):
        b2 = lax.rem(layer, 2)

        @pl.when(ci == 0)
        def _():
            for zz in zs:
                when(layer < 4, lambda: pl.semaphore_wait(free.at[zz], 1))
                remote(dW.at[b2, :, zz], crecv.at[:, zz], c_s.at[layer], c_r.at[layer, zz], sibling)

    def add_core(layer, u, n=17):
        b3, b2 = lax.rem(layer, 3), lax.rem(layer, 2)
        zz, lo = ORDER[u // 2], n * (u % 2)

        @on_second
        def _():
            if u % 2 == 0:
                wait_on(crecv.at[:, zz], c_r.at[layer, zz])

            def one(k, _):
                for yy in range(2):
                    for cc in range(2):
                        dW[b2, k, zz, yy, cc] = (
                            dW[b2, k, zz, yy, cc].astype(F32) + crecv[k, zz, yy, cc].astype(F32)
                        ).astype(BF)
                return 0

            lax.fori_loop(lo, lo + n, one, 0)
            remote(
                dW.at[b2, pl.ds(lo, n), zz, 1 - yi],
                yrecv.at[b3, pl.ds(lo, n), zz],
                y_s.at[layer],
                y_r.at[layer, u],
                across,
            )
            if u % 2 == 1:

                def give():
                    pl.semaphore_signal(
                        free.at[zz], inc=1, device_id=sibling, device_id_type=MESH
                    )

                when(layer > 0, give)

    def add_across(layer, u, n=17):
        b3, b2 = lax.rem(layer, 3), lax.rem(layer, 2)
        zz, lo = ORDER[u // 2], n * (u % 2)

        @on_second
        def _():
            wait_on(yrecv.at[b3, pl.ds(lo, n), zz], y_r.at[layer, u])

            def one(k, _):
                for cc in range(2):
                    dW[b2, k, zz, yi, cc] = (
                        dW[b2, k, zz, yi, cc].astype(F32) + yrecv[b3, k, zz, cc].astype(F32)
                    ).astype(BF)
                return 0

            lax.fori_loop(lo, lo + n, one, 0)

            @pl.when(zi != zz)
            def _():
                remote(
                    dW.at[b2, pl.ds(lo, n), zz, yi],
                    zrecv.at[b3, lax.rem(zi + 3 - zz, 4), pl.ds(lo, n)],
                    z_s.at[layer, u % 2],
                    z_r.at[layer, u % 2],
                    (zz * 4 + yi * 2 + 1, x),
                )

    def finish_sum(layer, half, n=17):
        b3, b2 = lax.rem(layer, 3), lax.rem(layer, 2)
        lo = n * half

        @on_second
        def _():
            wait_on(zrecv.at[b3, :, pl.ds(lo, n)], z_r.at[layer, half])
            if half == 0:

                def sent():
                    wait_on(fin.at[0], f_s.at[layer + 2, 0])
                    wait_on(fin.at[0], f_s.at[layer + 2, 1])
                    wait_on(fin.at[0], f_s.at[layer + 2, 2])

                when(layer + 2 <= 4, sent)

            def one(k, _):
                for cc in range(2):
                    v = dW[b2, k, zi, yi, cc].astype(F32)
                    for q in range(3):
                        v = v + zrecv[b3, q, k, cc].astype(F32)
                    if cc == 1:
                        fin[b3, k] = v.astype(BF)
                    else:
                        fin0[b2, k] = v.astype(BF)
                return 0

            lax.fori_loop(lo, lo + n, one, 0)
            mine = pl.ds(lo, n)
            remote(
                fin0.at[b2, mine],
                fin.at[b3, mine],
                f_s.at[layer, 0],
                n_r.at[layer, half],
                sibling,
            )
            remote(
                fin.at[b3, mine],
                xrecv.at[layer, mine],
                f_s.at[layer, 1],
                f_r.at[layer, half],
                partner,
            )
            remote(
                fin0.at[b2, mine],
                xrecv.at[layer, mine],
                f_s.at[layer, 2],
                f_r.at[layer, half],
                (t - 1, 1 - x),
            )

    def add_square(v):
        ss[...] += jnp.sum((v * v).reshape(-1, 8, 128), axis=0)

    def assemble(layer, put, n=17):
        rows = 32 if n == 17 else 24
        for half in range(2):

            @pl.when(ci == 0)
            def _():
                wait_on(fin.at[0, pl.ds(n * half, n)], n_r.at[layer, half])

            wait_on(xrecv.at[layer, pl.ds(n * half, n)], f_r.at[layer, half])
        for source, side in ((fin.at[lax.rem(layer, 3)], x), (xrecv.at[layer], 1 - x)):
            for b in range(2):
                lanes = pl.ds(128 * b, 128)
                def rest_row(k, _):
                    v = source[pl.ds(2 * k, 2), :, lanes].astype(F32).reshape(32, 128)
                    gst[2 * side + b, pl.ds(k, 32, stride=17), :] = v
                    return 0

                if n == 17:
                    lax.fori_loop(0, 17, rest_row, 0)
                else:
                    for k in range(17):
                        lo = 3 * (k // 2) + k % 2
                        v = source[pl.ds(lo, 2), :, lanes].astype(F32).reshape(32, 128)
                        v = v[8 * (k % 2) : 8 * (k % 2) + 24]
                        gst[2 * side + b, pl.ds(k, rows, stride=17), :] = v
        for b in range(4):
            add_square(gst[b, pl.ds(0, rows * 17), :])
            copy_in(gst.at[b, pl.ds(0, rows * 17)], put(b), g_s)

    def wait_assembled(rows):
        wait_on(gst.at[:, pl.ds(0, rows * 17)], g_s)

    def drain_sums(layer, n=17):
        @pl.when(ci == 0)
        def _():
            wait_on(crecv, c_s.at[layer])

        @on_second
        def _():
            wait_on(yrecv.at[0, pl.ds(0, 2 * n)], y_s.at[layer])
            for half in range(2):
                wait_on(zrecv.at[0, :, pl.ds(0, n)], z_s.at[layer, half])

    def put_rest(layer):
        return lambda b: gr_out.at[layer - 1, :, pl.ds(128 * b, 128)]

    def mixers_one():
        remote(Dm.at[:, :, 1 - ci], cm, m_s.at[0], m_r.at[0], sibling)

    def mixers_two():
        wait_on(cm, m_r.at[0])
        for zz in range(4):
            for yy in range(2):
                Dm[zz, yy, ci] = (Dm[zz, yy, ci].astype(F32) + cm[zz, yy].astype(F32)).astype(BF)
        remote(Dm.at[:, 1 - yi, ci], ym, m_s.at[1], m_r.at[1], across)

    def mixers_three():
        wait_on(ym, m_r.at[1])
        for zz in range(4):
            Dm[zz, yi, ci] = (Dm[zz, yi, ci].astype(F32) + ym[zz].astype(F32)).astype(BF)
        for q in range(3):
            zz = lax.rem(zi + 1 + q, 4)
            remote(Dm.at[zz, yi, ci], zm.at[q], m_s.at[2], m_r.at[2], (zz * 4 + yi * 2 + ci, x))

    def mixers_four():
        wait_on(zm, m_r.at[2])
        v = Dm[zi, yi, ci].astype(F32)
        for q in range(3):
            v = v + zm[q].astype(F32)
        fm[...] = v.astype(BF)
        remote(fm, xm, m_s.at[3], m_r.at[3], partner)

    def mixers_five():
        wait_on(xm, m_r.at[3])
        for b in range(2):
            lanes = pl.ds(128 * b, 128)
            gsm[2 * x + b] = fm[:, lanes].astype(F32)
            gsm[2 * (1 - x) + b] = xm[:, lanes].astype(F32)
        for b in range(4):
            add_square(gsm[b])
            for j in range(3):
                copy_in(
                    gsm.at[b, pl.ds(16 * j, 16)],
                    gmn_out.at[j, :, pl.ds(128 * b, 128)],
                    out_s.at[1],
                )
            for j in range(2):
                copy_in(
                    gsm.at[b, pl.ds(48 + 32 * j, 24)],
                    gmw_out.at[j, :, pl.ds(128 * b, 128)],
                    out_s.at[2],
                )

    def halos_out(layer):
        b2 = lax.rem(layer, 2)
        low, high = dzA.at[b2, pl.ds(HALO, HALO)], dzA.at[b2, pl.ds(1024, HALO)]
        above, below = dzA.at[b2, pl.ds(1088, HALO)], dzA.at[b2, pl.ds(0, HALO)]

        @pl.when(ci == 1)
        def _():
            remote(low, above, halo_s.at[layer, 0], halo_r.at[layer, 0], sibling)

        @pl.when((ci == 1) & (t < 15))
        def _():
            remote(high, rel.at[layer], halo_s.at[layer, 1], rel_r.at[layer], sibling)

        @pl.when((ci == 0) & (t > 0))
        def _():
            remote(low, above, halo_s.at[layer, 0], halo_r.at[layer, 0], (t - 1, x))

        @pl.when(ci == 0)
        def _():
            remote(high, below, halo_s.at[layer, 1], halo_r.at[layer, 1], sibling)

        @pl.when((ci == 0) & (t < 14))
        def _():
            wait_on(rel.at[layer], rel_r.at[layer])
            remote(rel.at[layer], below, rel_s.at[layer], halo_r.at[layer, 1], (t + 2, x))

    def halo_sent(layer):
        for side, edge in ((0, 0), (1, 15)):

            @pl.when(t != edge)
            def _():
                wait_on(dzA.at[0, pl.ds(0, HALO)], halo_s.at[layer, side])

    def output_gradient(layer, last):
        wait_on(Xl, load_s.at[2])
        if last:
            wait_on(y5, load_s.at[3])
            wait_on(sb.at[0], load_s.at[4])
        gain = norm[layer, pl.ds(0, 1), :]
        bias = norm[layer, pl.ds(1, 1), :]

        def one(b, acc):
            xh = Xl[rows_of(b), :]
            if last:
                y = y5[rows_of(b), :]
                d = sb[0, rows_of(b), :].astype(F32)
            else:
                y = gain * xh + bias
                d = da[rows_of(b), :] + pxr[1 - lax.rem(layer, 2), rows_of(b), :].astype(F32)
            sg = jax.nn.sigmoid(y)
            m = mask(b)
            if last:
                a = ((y * sg).reshape(16, 8, HALF) * m).reshape(128, HALF)
                for i in range(2):
                    stg[i, rows_of(b), :] = a[:, 128 * i : 128 * i + 128]
            v = (d * sg * (1.0 + y * (1.0 - sg))).reshape(16, 8, HALF) * m
            s0 = acc[0] + jnp.sum(v, axis=0)
            s1 = acc[1] + jnp.sum(v * xh.reshape(16, 8, HALF), axis=0)
            v = v.reshape(128, HALF)
            da[rows_of(b), :] = v
            if last:
                y5[rows_of(b), :] = v
            return s0, s1

        if last:
            s0, s1 = lax.fori_loop(0, 8, one, (zero, zero))
        else:
            s0, s1 = zero, zero
            for j in range(4):
                wait_on(pxr.at[0, pl.ds(0, 256)], px_r.at[layer + 1, j])
                s0, s1 = lax.fori_loop(2 * j, 2 * j + 2, one, (s0, s1))
        bsp[layer, pl.ds(0, 1), :] = jnp.sum(s0, axis=0, keepdims=True)
        bsp[layer, pl.ds(1, 1), :] = jnp.sum(s1, axis=0, keepdims=True)
        if last:
            for j in range(5):
                wait_on(xb.at[0], br_s.at[0])

                def branch(b, acc):
                    return acc + jnp.sum(
                        (da[rows_of(b), :] * xb[0, rows_of(b), :]).reshape(16, 8, HALF), axis=0
                    )

                sj = lax.fori_loop(0, 8, branch, zero)
                if j < 4:
                    copy_in(xh_in.at[6 + j], xb.at[0], br_s.at[0])
                bsp[layer, pl.ds(2 + j, 1), :] = jnp.sum(sj, axis=0, keepdims=True)
        share(bst, bsp, layer, 8 if last else 2, sems)

    def field_gradient(layer, last):
        shared(bst, layer, 8 if last else 2, sems)
        gain = norm[layer, pl.ds(0, 1), :]
        sums = lax.fori_loop(
            0, 16, lambda s, a: a + bst[layer, lax.div(s, 2), lax.rem(s, 2)], zero
        )
        ngr[layer, pl.ds(0, 1), :] = sums[1:2]
        ngr[layer, pl.ds(1, 1), :] = sums[0:1]
        if last:
            sums4[...] = sums
            for j in range(5):
                ngr[5 + j, pl.ds(0, 1), :] = sums[2 + j : 3 + j]
                ngr[5 + j, pl.ds(1, 1), :] = sums[0:1]
        r = rs[layer, pl.ds(0, 1), :]
        c0 = gain * sums[0:1] / count
        c1 = gain * sums[1:2] / count
        b2 = lax.rem(layer, 2)

        def dz_block(b, _):
            m = mask(b)
            v = (gain * da[rows_of(b), :]).reshape(16, 8, HALF)
            xh = Xl[rows_of(b), :].reshape(16, 8, HALF)
            v = r * (v - m * c0 - m * xh * c1)
            dzA[b2, pl.ds(pl.multiple_of(HALO + b * 128, 64), 128), :] = v.reshape(
                128, HALF
            ).astype(BF)
            return 0

        when(layer + 2 <= 4, lambda: halo_sent(layer + 2))
        lax.fori_loop(0, 8, dz_block, 0)
        halos_out(layer)

    def halo_arrived(layer):
        b2 = lax.rem(layer, 2)
        for side, edge in ((1, 0), (0, 15)):

            @pl.when(t != edge)
            def _():
                wait_on(dzA.at[b2, pl.ds(0, HALO)], halo_r.at[layer, side])

        def one(b, _):
            v = dzA[b2, pl.ds(pl.multiple_of(b * 128, 128), 144), :].astype(F32)
            dzB[pl.ds(pl.multiple_of(b * 128, 128), 128), :] = v[8:136].astype(BF)
            return 0

        lax.fori_loop(0, 9, one, 0)

    def shifted(b2, k, lo=0, rows=ROWS):
        o = 16 - k
        if o % 2 == 0:
            return dzA[b2, pl.ds(8 * o + lo, rows), :]
        return dzB[pl.ds(8 * (o - 1) + lo, rows), :]

    def data_tile(layer, half, j):
        b2 = lax.rem(layer, 2)
        lo = pl.multiple_of(256 * j, 256)
        acc = jnp.zeros((256, HALF), F32)
        for k in range(17):
            acc = acc + lax.dot_general(
                shifted(b2, k, lo, 256),
                Wl[b2, k, pl.ds(2 * half, 2)].reshape(HALF, HALF),
                (((1,), (1,)), ((), ())),
                preferred_element_type=F32,
            )
        return acc

    def weight_tap(h, dz):
        return lax.dot_general(
            Hl[h], dz, (((0,), (0,)), ((), ())), preferred_element_type=F32
        ).reshape(2, 2, 2, 32, HALF)

    def even_tap(b2, i):
        return dzA[b2, pl.ds(pl.multiple_of(128 - 16 * i, 16), ROWS), :]

    def odd_tap(i):
        return dzB[pl.ds(pl.multiple_of(112 - 16 * i, 16), ROWS), :]

    def weight_gradient(layer, h):
        b2 = lax.rem(layer, 2)

        def put(k, v):
            for part in range(2):
                dW[b2, 2 * k + part, pl.ds(2 * h, 2)] = v[
                    :, :, :, 16 * part : 16 * part + 16
                ].astype(BF)

        def pairs(q, _):
            for i in (4 * q, 4 * q + 1, 4 * q + 2, 4 * q + 3):
                put(2 * i, weight_tap(h, even_tap(b2, i)))
                put(2 * i + 1, weight_tap(h, odd_tap(i)))
            return 0

        lax.fori_loop(0, 2, pairs, 0)
        put(16, weight_tap(h, even_tap(b2, 8)))

    def first_weight_gradient(h):
        def put(at, v, blocks):
            for part in range(blocks):
                dW[0, at + part, pl.ds(2 * h, 2)] = v[
                    :, :, :, 16 * part : 16 * part + 16
                ].astype(BF)

        def pairs(q, _):
            for i in (2 * q, 2 * q + 1):
                v = [weight_tap(h, dz)[:, :, :, :24] for dz in (even_tap(0, i), odd_tap(i))]
                put(3 * i, jnp.concatenate(v, axis=3), 3)
            return 0

        lax.fori_loop(0, 4, pairs, 0)
        v = weight_tap(h, even_tap(0, 8))[:, :, :, :24]
        put(24, jnp.concatenate([v, jnp.zeros((2, 2, 2, 8, HALF), F32)], axis=3), 2)

    def load_branch(j):
        copy_in(xh_in.at[5 + j], xb.at[0], br_s.at[0])
        if j < 3:
            copy_in(nar_in.at[j], sb.at[0], br_s.at[2])
        elif j == 3:
            copy_in(wid_in, sb, br_s.at[2])
        else:
            copy_in(h_in.at[0], sb, br_s.at[2])

    def branch(j):
        field = 5 + j
        sums = sums4[...]
        wait_on(xb.at[0], br_s.at[0])
        wait_on(sb.at[0] if j < 3 else sb, br_s.at[2])
        gain = norm[field, pl.ds(0, 1), :]
        r = rs[field, pl.ds(0, 1), :]
        c0 = gain * sums[0:1] / count
        c1 = gain * sums[2 + j : 3 + j] / count

        def one(b, _):
            m = mask(b)
            v = (gain * y5[rows_of(b), :]).reshape(16, 8, HALF)
            xh = xb[0, rows_of(b), :].reshape(16, 8, HALF)
            v = r * (v - m * c0 - m * xh * c1)
            px[1, rows_of(b), :] = v.reshape(128, HALF).astype(BF)
            return 0

        lax.fori_loop(0, 8, one, 0)
        dv = px[1]
        if j < 3:
            v = lax.dot_general(
                sb[0], dv, (((0,), (0,)), ((), ())), preferred_element_type=F32
            )
            Dm[:, :, :, pl.ds(16 * j, 16), :] = v.reshape(4, 2, 2, 16, HALF).astype(BF)
            back = lax.dot_general(
                dv, wmn[j], (((1,), (1,)), ((), ())), preferred_element_type=F32
            )
            blocks = 2
        else:
            i = j - 3
            for h in range(2):
                v = lax.dot_general(
                    sb[h], dv, (((0,), (0,)), ((), ())), preferred_element_type=F32
                )
                Dm[pl.ds(2 * h, 2), :, :, pl.ds(48 + 32 * i, 32), :] = v.reshape(
                    2, 2, 2, 32, HALF
                ).astype(BF)
            wu = jnp.dot(perm[...], wmw[i], preferred_element_type=F32).astype(BF)
            back = lax.dot_general(
                dv, wu, (((1,), (1,)), ((), ())), preferred_element_type=F32
            )
            blocks = 3
        if j < 4:
            load_branch(j + 1)
        for b in range(8):
            m = mask(b)[:, :, :128]
            for i in range(blocks):
                v = back[128 * b : 128 * b + 128, 128 * i : 128 * i + 128]
                stg[i, pl.ds(128 * b, 128), :] = (v.reshape(16, 8, 128) * m).reshape(128, 128)
        if j < 3:

            def put_own(i, b, v):
                own_n[j, i, :, pl.ds(128 * b, 128)] = v

            def put_send(i, b, v):
                snd_n[j, i, :, pl.ds(128 * b, 128)] = v.astype(BF)

        else:

            def put_own(i, b, v):
                own_w[j - 3, i, :, pl.ds(128 * b, 128)] = v

            def put_send(i, b, v):
                snd_w[j - 3, i, :, pl.ds(128 * b, 128)] = v.astype(BF)

        unstage(blocks, put_own, put_send)
        if j < 3:
            remote(snd_n.at[j], rcv_n.at[j], sn_s.at[1 + j], sn_r.at[1 + j], partner)
        else:
            remote(snd_w.at[j - 3], rcv_w.at[j - 3], sn_s.at[1 + j], sn_r.at[1 + j], partner)

    def sources_narrow():
        for j in range(3):
            wait_on(rcv_n.at[j], sn_r.at[1 + j])
        own_n[...] = own_n[...] + rcv_n[...].astype(F32)
        copy_in(own_n, gn_out, out_s.at[3])

    def chain(layer, last):
        b2 = lax.rem(layer, 2)
        one = layer + 1
        two = lambda f: when(layer + 2 <= 4, lambda: f(layer + 2))
        load_w(layer - 1)
        output_gradient(layer, last)
        if last:
            send_mixed()
            load_branch(0)
        else:

            def two_a(older):
                add_across(older, 6)
                add_across(older, 7)

            two(two_a)
            add_core(one, 0)
            add_core(one, 1)
        field_gradient(layer, last)
        load_x(layer - 1)
        if not last:
            add_core(one, 2)
            add_core(one, 3)
        halo_arrived(layer)
        wait_on(Wl.at[0], w_s.at[b2])
        def other_tile(j, _):
            if not last:
                wait_on(px.at[0, pl.ds(0, 256)], px_s.at[j])
            rows = pl.ds(pl.multiple_of(256 * j, 256), 256)
            px[0, rows, :] = data_tile(layer, 1 - x, j).astype(BF)
            remote(px.at[0, rows], pxr.at[b2, rows], px_s.at[j], px_r.at[layer, j], partner)
            if not last:

                @pl.when(j == 1)
                def _():
                    add_core(one, 4)
                    add_core(one, 5)
                    add_across(one, 0)

            return 0

        lax.fori_loop(0, 4, other_tile, 0)
        if not last:
            two(lambda older: finish_sum(older, 0))
        def own_tile(j, _):
            da[pl.ds(pl.multiple_of(256 * j, 256), 256), :] = data_tile(layer, x, j)
            return 0

        lax.fori_loop(0, 4, own_tile, 0)
        if not last:
            add_core(one, 6)
            add_core(one, 7)
            add_across(one, 1)
            add_across(one, 2)
            two(lambda older: finish_sum(older, 1))
            two(drain_sums)
        wait_on(Hl, load_s.at[1])
        weight_gradient(layer, 0)
        send_core(layer, (0, 1))
        if not last:
            add_across(one, 3)
        weight_gradient(layer, 1)
        send_core(layer, (2, 3))
        load_h(layer - 1)
        if not last:
            add_across(one, 4)
            add_across(one, 5)

            def two_out(older):
                when(layer + 3 <= 4, lambda: wait_assembled(32))
                assemble(older, put_rest(older))

            two(two_out)

    ss[...] = jnp.zeros((8, 128), F32)
    chain(4, True)
    branch(0)

    def middle(i, _):
        layer = 3 - i
        chain(layer, False)

        @pl.when(layer == 3)
        def _():
            branch(1)
            branch(2)
            wait_on(mix_rcv, sn_r.at[0])
            copy_in(mix_rcv, mixed_out.at[:, :, other_cols], out_s.at[4])

        @pl.when(layer == 2)
        def _():
            branch(3)
            branch(4)
            mixers_one()
            sources_narrow()

        @pl.when(layer == 1)
        def _():
            mixers_two()

        return 0

    lax.fori_loop(0, 3, middle, 0)

    output_gradient(0, False)
    add_across(2, 6)
    add_across(2, 7)
    add_core(1, 0)
    add_core(1, 1)
    field_gradient(0, False)
    add_core(1, 2)
    add_core(1, 3)
    halo_arrived(0)
    wait_on(Hl, load_s.at[1])
    wait_on(Wl.at[0], w_s.at[0])
    add_core(1, 4)
    add_core(1, 5)
    add_across(1, 0)
    finish_sum(2, 0)
    finish_sum(2, 1)
    drain_sums(2)
    add_core(1, 6)
    add_core(1, 7)
    first_weight_gradient(0)
    send_core(0, (0, 1))
    add_across(1, 1)
    add_across(1, 2)
    first_weight_gradient(1)
    send_core(0, (2, 3))
    add_across(1, 3)
    mixers_three()

    remote(ngr, ngx, ng_s, ng_r, partner)

    for k in range(17):
        Wl[1, k, pl.ds(0, 3)] = (
            jnp.dot(perm[...], Wl[0, k].reshape(512, HALF), preferred_element_type=F32)
            .astype(BF)
            .reshape(3, 2, 2, 32, HALF)
        )
    add_across(1, 4)
    add_core(0, 0, 13)
    add_across(1, 5)
    add_core(0, 1, 13)
    mixers_four()
    for part in range(4):
        acc = jnp.zeros((HALF, 384), F32)
        for k in range(17):
            o = 16 - k
            lo = part * HALF
            lhs = (
                dzA[0, pl.ds(8 * o + lo, HALF), :]
                if o % 2 == 0
                else dzB[pl.ds(8 * (o - 1) + lo, HALF), :]
            )
            acc = acc + lax.dot_general(
                lhs,
                Wl[1, k, pl.ds(0, 3)].reshape(384, HALF),
                (((1,), (1,)), ((), ())),
                preferred_element_type=F32,
            )
        for half in range(2):
            m = mask(2 * part + half)[:, :, :128]
            for b in range(3):
                stg[b, pl.ds(part * HALF + half * 128, 128), :] = (
                    acc[128 * half : 128 * half + 128, 128 * b : 128 * b + 128].reshape(
                        16, 8, 128
                    )
                    * m
                ).reshape(128, 128)
        if part == 0:
            add_across(1, 6)
            add_core(0, 2, 13)
            add_core(0, 3, 13)
        if part == 1:
            add_across(1, 7)
            add_core(0, 4, 13)
            add_core(0, 5, 13)
        if part == 2:
            add_across(0, 0, 13)
            add_core(0, 6, 13)
            add_core(0, 7, 13)
        if part == 3:
            add_across(0, 1, 13)
            finish_sum(1, 0)
            finish_sum(1, 1)

    def put_own(i, b, v):
        lanes = pl.ds(128 * b, 128)
        own_w[1, i, :, lanes] = own_w[1, i, :, lanes] + v

    def put_send(i, b, v):
        snd_w[2, i, :, pl.ds(128 * b, 128)] = v.astype(BF)

    wait_on(mix_own, sn_s.at[0])
    unstage(3, put_own, put_send)
    remote(snd_w.at[2], rcv_w.at[2], sn_s.at[6], sn_r.at[6], partner)
    add_across(0, 2, 13)
    wait_assembled(32)
    assemble(2, put_rest(2))
    add_across(0, 3, 13)
    mixers_five()
    add_across(0, 4, 13)
    wait_assembled(32)
    assemble(1, put_rest(1))
    for j in range(2):
        wait_on(rcv_w.at[j], sn_r.at[4 + j])
    wait_on(rcv_w.at[2], sn_r.at[6])
    for j in range(2):
        v = own_w[j] + rcv_w[j].astype(F32)
        if j == 1:
            v = v + rcv_w[2].astype(F32)
        own_w[j] = v
    copy_in(own_w, gw_out, out_s.at[5])
    add_across(0, 5, 13)
    add_across(0, 6, 13)
    finish_sum(0, 0, 13)
    add_across(0, 7, 13)
    finish_sum(0, 1, 13)
    wait_on(ngx, ng_r)
    wait_assembled(32)
    assemble(0, lambda b: gf_out.at[:, pl.ds(128 * b, 128)], 13)

    bsp[5, :, pl.ds(0, 128)] = ss[...]
    share(bst, bsp, 5, 8, sems)
    mine, theirs = ngr[...], ngx[...]
    left = jnp.where(x == 0, mine, theirs)
    right = jnp.where(x == 0, theirs, mine)
    rows = lax.broadcasted_iota(jnp.int32, (10, 8, HALF), 1)
    left = jnp.where(rows < 2, left, 0.0)
    right = jnp.where(rows < 2, right, 0.0)
    for i in range(10):
        for row in range(2):
            for half, v in enumerate((left, right)):
                ng_out[row, pl.ds(i, 1), pl.ds(HALF * half, HALF)] = v[i, row : row + 1]
    norms = jnp.sum(left * left + right * right)
    shared(bst, 5, 8, sems)
    every = lax.fori_loop(0, 16, lambda s, a: a + bst[5, lax.div(s, 2), lax.rem(s, 2)], zero)
    total_out[...] = jnp.zeros((8, 128), F32) + (jnp.sum(every) + norms)

    wait_assembled(24)
    wait_on(mix_own, out_s.at[0])
    wait_on(mix_rcv, out_s.at[4])
    wait_on(own_n, out_s.at[3])
    wait_on(own_w, out_s.at[5])
    wait_on(gsm.at[:, pl.ds(0, 48)], out_s.at[1])
    wait_on(gsm.at[:, pl.ds(0, 48)], out_s.at[2])
    for j in range(4):
        wait_on(px.at[0, pl.ds(0, 256)], px_s.at[j])
    for j in range(3):
        wait_on(snd_n.at[0], sn_s.at[1 + j])
        wait_on(snd_w.at[0], sn_s.at[4 + j])
    wait_on(cm, m_s.at[0])
    wait_on(ym, m_s.at[1])
    wait_on(zm, m_s.at[2])
    wait_on(fm, m_s.at[3])
    wait_on(ngr, ng_s)
    drain_sums(1)
    drain_sums(0, 13)

    for layer in range(2):
        halo_sent(layer)

        @on_second
        def _():
            for i in range(3):
                wait_on(fin.at[0, pl.ds(0, 34 if layer else 26)], f_s.at[layer, i])

    for layer in range(5):

        @pl.when((ci == 0) & (t < 14))
        def _():
            wait_on(rel.at[0], rel_s.at[layer])

    for layer in range(6):
        share_drained(bst, bsp, layer, 2 if layer < 4 else 8, sems)


def run_backward(lens, norm, rs, perm, w, wmn, wmw, h, xh, y, nar, wid, cot):
    vm = pl.BlockSpec(memory_space=pltpu.VMEM)
    hb = pl.BlockSpec(memory_space=pl.ANY)
    dma = pltpu.SemaphoreType.DMA
    S = jax.ShapeDtypeStruct
    V = pltpu.VMEM
    return pl.pallas_call(
        backward_kernel,
        out_shape=(
            S((4, 128, 512), BF),
            S((3, 4, 128, HALF), F32),
            S((2, 4, 128, 384), F32),
            S((408, 512), F32),
            S((4, 544, 512), F32),
            S((3, 16, 512), F32),
            S((2, 24, 512), F32),
            S((2, 10, 512), F32),
            S((8, 128), F32),
        ),
        in_specs=[vm, vm, vm, vm, hb, vm, vm, hb, hb, hb, hb, hb, hb],
        out_specs=[hb] * 7 + [vm, vm],
        scratch_shapes=[
            V((2, 17, 4, 2, 2, 32, HALF), BF),
            V((2, ROWS, HALF), BF),
            V((ROWS, HALF), F32),
            V((1, ROWS, HALF), F32),
            V((2, ROWS, HALF), BF),
            V((ROWS, HALF), F32),
            V((ROWS, HALF), F32),
            V((2, 1168, HALF), BF),
            V((1152, HALF), BF),
            V((2, 34, 4, 2, 2, 16, HALF), BF),
            V((34, 4, 2, 2, 16, HALF), BF),
            V((3, 34, 4, 2, 16, HALF), BF),
            V((3, 3, 34, 2, 16, HALF), BF),
            V((3, 34, 16, HALF), BF),
            V((5, 34, 16, HALF), BF),
            V((2, ROWS, HALF), BF),
            V((2, ROWS, HALF), BF),
            V((3, ROWS, 128), F32),
            V((3, 4, 128, HALF), F32),
            V((2, 4, 128, 384), F32),
            V((3, 4, 128, HALF), BF),
            V((3, 4, 128, 384), BF),
            V((3, 4, 128, HALF), BF),
            V((3, 4, 128, 384), BF),
            V((4, 128, HALF), BF),
            V((4, 128, HALF), BF),
            V((4, 2, 2, 112, HALF), BF),
            V((4, 2, 112, HALF), BF),
            V((4, 112, HALF), BF),
            V((3, 112, HALF), BF),
            V((112, HALF), BF),
            V((112, HALF), BF),
            V((4, 544, 128), F32),
            V((4, 112, 128), F32),
            V((6, 8, 2, 8, HALF), F32),
            V((6, 8, HALF), F32),
            V((5, HALO, HALF), BF),
            V((2, 34, 16, HALF), BF),
            V((8, HALF), F32),
            V((10, 8, HALF), F32),
            V((10, 8, HALF), F32),
            V((8, 128), F32),
            dma((5,)),
            dma((2,)),
            dma((3,)),
            dma((5, 2)),
            dma((5, 2)),
            dma((5,)),
            dma((5,)),
            dma((6,)),
            dma((6,)),
            dma((6,)),
            dma((6,)),
            dma((6,)),
            dma((6,)),
            pltpu.SemaphoreType.REGULAR((4,)),
            dma((5,)),
            dma((5, 4)),
            dma((5,)),
            dma((5, 8)),
            dma((5, 2)),
            dma((5, 2)),
            dma((5, 3)),
            dma((5, 2)),
            dma((5, 2)),
            dma((4,)),
            dma((5, 4)),
            dma((4,)),
            dma((4,)),
            dma((7,)),
            dma((7,)),
            dma,
            dma((6,)),
            dma,
            dma,
        ],
        compiler_params=pltpu.CompilerParams(
            collective_id=1, has_side_effects=True, vmem_limit_bytes=63 << 20
        ),
        cost_estimate=pl.CostEstimate(flops=46 * 10**9, bytes_accessed=60 * 10**6, transcendentals=0),
    )(lens, norm, rs, perm, w, wmn, wmw, h, xh, y, nar, wid, cot)


def prepare(lengths, norm_params):
    x = lax.axis_index("batch")
    mine = jnp.broadcast_to(lengths.astype(F32)[:, None], (4, HALF))
    lens = jnp.zeros((8, HALF), F32)
    lens = lax.dynamic_update_slice(lens, mine, (4 * x, 0))
    half = lax.dynamic_slice(norm_params, (0, 0, x * HALF), (2, 10, HALF))
    norm = jnp.pad(jnp.transpose(half, (1, 0, 2)), ((0, 0), (0, 6), (0, 0)))
    places = np.arange(384)
    perm = np.zeros((384, 512), np.float32)
    perm[places, (places // 24) * 32 + places % 24] = 1.0
    return lens, norm, jnp.asarray(perm, BF)


def body_split(
    source_narrow,
    source_wide,
    lengths,
    cotangent,
    kernel_first,
    kernel_rest,
    mixer_narrow,
    mixer_wide,
    norm_params,
    moment_first,
    square_first,
    moment_rest,
    square_rest,
    moment_narrow,
    square_narrow,
    moment_wide,
    square_wide,
    moment_norm,
    square_norm,
):
    lens, norm, perm = prepare(lengths, norm_params)
    w, wmn, wmw, h, xh, y, nar, wid, cot, rs, lens = run_forward(
        lens,
        norm,
        perm,
        source_narrow,
        source_wide,
        cotangent,
        kernel_first,
        kernel_rest,
        mixer_narrow,
        mixer_wide,
    )
    mixed, gn, gw, gf, gr, gmn, gmw, ng, total = run_backward(
        lens, norm, rs, perm, w, wmn, wmw, h, xh, y, nar, wid, cot
    )
    grad_norm = jnp.sqrt(total[0, 0])
    clip = jnp.minimum(1.0, THRESHOLD / grad_norm)
    results = []
    for p, g, m, v in (
        (kernel_first, gf, moment_first, square_first),
        (kernel_rest, gr, moment_rest, square_rest),
        (mixer_narrow, gmn, moment_narrow, square_narrow),
        (mixer_wide, gmw, moment_wide, square_wide),
    ):
        results += adamw(p, clip * g, m, v, RATE_WEIGHT, DECAY)
    results += adamw(norm_params, clip * ng, moment_norm, square_norm, RATE_NORM, 0.0)
    return (mixed, gn, gw, grad_norm, *results)


def solution(mesh):
    in_specs = (
        P(None, "batch", "tm", None),
        P(None, "batch", "tm", None),
        P("batch"),
        P("batch", "tm", None),
        P("tm", None),
        P(None, "tm", None),
        P(None, "tm", None),
        P(None, "tm", None),
        P(),
        P("tm", None),
        P("tm", None),
        P(None, "tm", None),
        P(None, "tm", None),
        P(None, "tm", None),
        P(None, "tm", None),
        P(None, "tm", None),
        P(None, "tm", None),
        P(),
        P(),
    )
    out_specs = (
        P("batch", "tm", None),
        P(None, "batch", "tm", None),
        P(None, "batch", "tm", None),
        P(),
        P("tm", None),
        P("tm", None),
        P("tm", None),
        P(None, "tm", None),
        P(None, "tm", None),
        P(None, "tm", None),
        P(None, "tm", None),
        P(None, "tm", None),
        P(None, "tm", None),
        P(None, "tm", None),
        P(None, "tm", None),
        P(None, "tm", None),
        P(),
        P(),
        P(),
    )
    fits = mesh.shape["tm"] == 16 and mesh.shape["batch"] == 2
    chosen = body_split if fits else body
    return jax.shard_map(chosen, mesh=mesh, in_specs=in_specs, out_specs=out_specs, check_vma=False)
```
